32 devices in a mesh: depth: 4 (over z), row: 2 (over core), col: 4 (over y, x).
Axes of the slice: x: 2, y: 2, z: 4, core: 2. Of those that a mesh axis runs over, the one named last changes fastest.
Arguments:
- phase: float32 [4, 128, 512], P('depth', 'row', 'col'), may hold values from -1.8 to 1.8
- tilt: int32 [2, 2], replicated, may hold values from -6 to 6
- intensity: float32 [2, 128, 512], P(None, 'row', 'col'), may hold values from 0.3 to 1.5
Outputs:
- grad_phase: float32 [4, 128, 512], P('depth', 'row', 'col')
- exit_waves: float32 [2, 4, 2, 128, 512], P(None, 'depth', None, 'row', 'col')
The draws below stay inside these ranges and needn't reach their ends.
Inputs may be any that keep to these rules, and one draw needn't show every extreme that they name: `tilt`: whole numbers of phase cycles across the field.
All inputs are finite; a program needn't handle non-finite values.
Results may differ from the reference program's by a relative error of at most 0.0003.
Values sent between devices are 32-bit elements; how exact they have to be, the bound alone decides.
No kernel may reach another device: no remote copies, remote signals or barrier semaphores. Data moves between devices by JAX's collectives and lax.ppermute only.
A program may use at most 64 MiB of HBM per device.

```python
import math
import jax
import jax.numpy as jnp
from jax import lax

BATCH = 2
HALO = 32
FRESNEL = 64
NX = 128
NY = 512
SLICES = 4


def place_ends(result, rng, least, high):
    shape = result.shape
    place = [jax.random.randint(jax.random.fold_in(rng, axis), (), 0, shape[axis]) for axis in range(len(shape))]
    result = result.at[tuple(place)].set(least)
    longest = shape.index(max(shape))
    place[longest] = (place[longest] + 1) % shape[longest]
    return result.at[tuple(place)].set(high)


def block_levels(own_key, shape, cuts, least, largest):
    loudness = 1.0
    for dim, blocks in cuts:
        steps = jax.random.uniform(jax.random.fold_in(jax.random.fold_in(own_key, 6), dim), (blocks,), jnp.float32, least / len(cuts), largest / len(cuts))
        loudness = loudness * jnp.repeat(jnp.exp(steps), shape[dim] // blocks).reshape((-1,) + (1,) * (len(shape) - 1 - dim))
    return loudness


def bell_draw(stream_key, shape, deviation, most, cuts=(), kind=jnp.bfloat16):
    gain = block_levels(stream_key, shape, cuts, -0.22, 0.18) if cuts else 1.0
    drawn = jax.random.normal(stream_key, shape, jnp.float32) * deviation * gain
    return jnp.minimum(jnp.maximum(drawn, -most), most).astype(kind)


def setup_inputs(seed: int = 0) -> dict:
    keys = jax.random.split(jax.random.key(seed), 4)
    return {
        "phase": bell_draw(keys[0], (SLICES, NX, NY), 0.3, 1.8, ((0, 4), (1, 2), (2, 4)), jnp.float32),
        "tilt": place_ends(jax.random.randint(keys[1], (BATCH, 2), -6, 7), jax.random.fold_in(keys[1], 1), -6, 6).astype(jnp.int32),
        "intensity": jnp.clip(0.3 + 1.2 * jax.random.uniform(keys[2], (BATCH, NX, NY), jnp.float32) ** block_levels(keys[2], (BATCH, NX, NY), ((1, 2), (2, 4)), -0.2, 0.2), 0.3, 1.5),
    }


def kernel_taps():
    offset = jnp.arange(-HALO, HALO + 1).astype(jnp.float32)
    taper_dist = jnp.maximum(jnp.abs(offset) - 0.5 * HALO, 0.0)
    profile = jnp.cos(jnp.pi * taper_dist / (HALO + 2.0))
    weight = profile * profile / math.sqrt(FRESNEL)
    phase_angle = jnp.pi * offset * offset / FRESNEL
    return lax.complex(jnp.cos(phase_angle) * weight, jnp.sin(phase_angle) * weight)

def convolve_axis(current, kernel, axis_num):
    extent = current.shape[axis_num]
    fft_size = extent + 2 * HALO
    kernel_hat = jnp.fft.fft(kernel, fft_size)
    shaped = [1, 1]
    shaped[axis_num] = fft_size
    field_hat = jnp.fft.fft(current, fft_size, axis=axis_num)
    full_conv = jnp.fft.ifft(field_hat * kernel_hat.reshape(shaped), axis=axis_num)
    return lax.slice_in_dim(full_conv, HALO, HALO + extent, axis=axis_num)

def forward(phase_field, tilt):
    kernel = kernel_taps()
    row_pos = jnp.arange(NX).astype(jnp.float32)[:, None]
    col_pos = jnp.arange(NY).astype(jnp.float32)[None, :]
    tilt_f = tilt.astype(jnp.float32)
    results = []
    for tilt_index in range(BATCH):
        phase_angle = 2.0 * jnp.pi * (tilt_f[tilt_index, 0] * row_pos / NX + tilt_f[tilt_index, 1] * col_pos / NY)
        current = lax.complex(jnp.cos(phase_angle), jnp.sin(phase_angle))
        leaving = []
        for slice_index in range(SLICES):
            screen = lax.complex(jnp.cos(phase_field[slice_index]), jnp.sin(phase_field[slice_index]))
            current = current * screen
            current = convolve_axis(convolve_axis(current, kernel, 0), kernel, 1)
            leaving.append(jnp.stack([jnp.real(current), jnp.imag(current)]))
        results.append(jnp.stack(leaving))
    return jnp.stack(results)

def reference(phase, tilt, intensity):

    def misfit_loss(phase_field):
        exit_fields = forward(phase_field, tilt)
        final_wave = exit_fields[:, SLICES - 1]
        misfit = final_wave[:, 0] * final_wave[:, 0] + final_wave[:, 1] * final_wave[:, 1] - intensity
        return (0.5 * jnp.sum(misfit * misfit), exit_fields)
    loss_value, pullback, exit_fields = jax.vjp(misfit_loss, phase, has_aux=True)
    gradient = pullback(jnp.ones_like(loss_value))[0]
    return (gradient, exit_fields)
```

```python
import functools
import math

import jax
import jax.numpy as jnp
import numpy as np
from jax import lax
from jax.experimental import pallas as pl
from jax.experimental.pallas import tpu as pltpu
from jax.sharding import PartitionSpec as P

HALO = 32
FRESNEL = 64
LANES = 128
GATHER_BUDGET = 4 * 2**20
SIN = (
    0.9999999980536763,
    -0.1666666530009577,
    0.008333305907073658,
    -0.00019838908256358006,
    2.745822627876341e-06,
    -2.3043562782810933e-08,
)
COS = (
    0.9999999961345007,
    -0.4999999301617528,
    0.04166646215023687,
    -0.0013886696163545999,
    2.4695045482778703e-05,
    -2.5154931690000354e-07,
)


def horner(coefficients, square):
    total = jnp.full_like(square, coefficients[-1])
    for coefficient in coefficients[-2::-1]:
        total = total * square + coefficient
    return total


def cos_sin(angle):
    square = angle * angle
    return horner(COS, square), horner(SIN, square) * angle


def turn(fraction):
    half_cos, half_sin = cos_sin(fraction * math.pi)
    return half_cos * half_cos - half_sin * half_sin, 2.0 * half_cos * half_sin


def halves(value):
    high = value.astype(jnp.bfloat16)
    return high, (value - high.astype(jnp.float32)).astype(jnp.bfloat16)


def np_halves(matrix):
    high = matrix.astype(jnp.bfloat16)
    return high, (matrix - high.astype(np.float64)).astype(jnp.bfloat16)


def np_taps():
    offset = np.arange(-HALO, HALO + 1, dtype=np.float64)
    taper = np.maximum(np.abs(offset) - 0.5 * HALO, 0.0)
    weight = np.cos(np.pi * taper / (HALO + 2.0)) ** 2 / math.sqrt(FRESNEL)
    return weight * np.exp(1j * np.pi * offset * offset / FRESNEL)


def np_band(out_pos, in_pos):
    offset = out_pos[:, None] - in_pos[None, :]
    inside = np.abs(offset) <= HALO
    return np.where(inside, np_taps()[np.clip(offset, -HALO, HALO) + HALO], 0.0)


def row_constant(height):
    band = np_band(np.arange(height), np.arange(height))
    whole = np.block([[band.real, -band.imag], [band.imag, band.real]])
    high, low = np_halves(whole)
    return np.concatenate([high, high, low], axis=1)


def col_constant():
    lane = np.arange(LANES)
    edge_pos = np.where(lane < LANES // 2, lane + LANES, lane - LANES)
    parts = []
    for position in (lane, edge_pos):
        band = np_band(lane, position).T
        parts.append(np.block([[band.real, band.imag], [-band.imag, band.real]]))
    high, low = np_halves(np.concatenate(parts, axis=0))
    return np.concatenate([high, high, low], axis=0)


def wave_kernel(
    sections, tilt_ref, phase_ref, intensity_ref, row_ref, col_ref, grad_ref, exit_ref,
    cos_ref, sin_ref, u_high, u_low, a_high, a_low, v_ref, moved_ref,
):
    items, height, width = v_ref.shape[0], v_ref.shape[2], v_ref.shape[3]
    slices, tile_r, tile_c = grad_ref.shape
    rows, cols = height // tile_r, width // tile_c
    count = sections * slices
    blocks = width // LANES
    half = LANES // 2
    first = lax.axis_index("depth") * slices
    own_row = pl.multiple_of(lax.axis_index("row") * tile_r, tile_r)
    own_col = pl.multiple_of(lax.axis_index("col") * tile_c, tile_c)
    own = (pl.ds(own_row, tile_r), pl.ds(own_col, tile_c))

    def store_u(item, row, col, real, imag):
        for part, value in enumerate((real, imag)):
            high, low = halves(value)
            where = (item, pl.ds(part * height + row, value.shape[0]), pl.ds(col, value.shape[1]))
            u_high[where] = high
            u_low[where] = low

    def keep_moved(slice_index):
        @pl.when((slice_index >= first) & (slice_index < first + slices))
        def _():
            cos, sin = cos_ref[(slice_index,) + own], sin_ref[(slice_index,) + own]
            for item in range(items):
                real, imag = v_ref[(item, 0) + own], v_ref[(item, 1) + own]
                moved_ref[slice_index - first, item, 0] = cos * real - sin * imag
                moved_ref[slice_index - first, item, 1] = cos * imag + sin * real

    def transmit(slice_index):
        for item in range(items):
            for block in range(blocks):
                where = (slice(None), pl.ds(block * LANES, LANES))
                cos, sin = cos_ref[(slice_index,) + where], sin_ref[(slice_index,) + where]
                real, imag = v_ref[(item, 0) + where], v_ref[(item, 1) + where]
                store_u(item, 0, block * LANES, cos * real - sin * imag, cos * imag + sin * real)

    def propagate():
        for item in range(items):
            for start in range(0, width, 2 * LANES):
                where = (item, slice(None), pl.ds(start, 2 * LANES))
                high, low = u_high[where], u_low[where]
                done = jnp.dot(
                    row_ref[...],
                    jnp.concatenate([high, low, high], axis=0),
                    preferred_element_type=jnp.float32,
                )
                for part in range(2):
                    for sub in range(2):
                        block = start // LANES + sub
                        value = done[part * height : (part + 1) * height, sub * LANES : (sub + 1) * LANES]
                        for target, piece in zip((a_high, a_low), halves(value)):
                            target[item, block, :, pl.ds(part * LANES, LANES)] = piece
                            if block > 0:
                                target[item, block - 1, :, pl.ds((2 + part) * LANES, half)] = piece[:, :half]
                            if block < blocks - 1:
                                target[item, block + 1, :, pl.ds((2 + part) * LANES + half, half)] = piece[:, half:]
        for item in range(items):
            high = a_high[item].reshape(blocks * height, 4 * LANES)
            low = a_low[item].reshape(blocks * height, 4 * LANES)
            done = jnp.dot(
                jnp.concatenate([high, low, high], axis=1),
                col_ref[...],
                preferred_element_type=jnp.float32,
            )
            for block in range(blocks):
                for part in range(2):
                    v_ref[item, part, :, pl.ds(block * LANES, LANES)] = done[
                        block * height : (block + 1) * height, part * LANES : (part + 1) * LANES
                    ]

    for target in (a_high, a_low):
        for item in range(items):
            for part in range(2):
                target[item, 0, :, pl.ds((2 + part) * LANES + half, half)] = jnp.zeros((height, half), jnp.bfloat16)
                target[item, blocks - 1, :, pl.ds((2 + part) * LANES, half)] = jnp.zeros((height, half), jnp.bfloat16)

    def screens(slice_index, carry):
        section, inner = slice_index // slices, slice_index % slices
        for row in range(rows):
            for col in range(cols):
                cos, sin = cos_sin(phase_ref[section * (rows * cols) + row * cols + col, inner])
                where = (slice_index, pl.ds(row * tile_r, tile_r), pl.ds(col * tile_c, tile_c))
                cos_ref[where] = cos
                sin_ref[where] = sin
        return carry

    lax.fori_loop(0, count, screens, 0)

    def cycles(number, position, extent):
        fraction = (number * position).astype(jnp.float32) / extent
        return turn(fraction - jnp.round(fraction))

    for item in range(items):
        row_cos, row_sin = cycles(
            tilt_ref[item, 0], lax.broadcasted_iota(jnp.int32, (height, LANES), 0), float(height)
        )
        for block in range(blocks):
            col_cos, col_sin = cycles(
                tilt_ref[item, 1],
                lax.broadcasted_iota(jnp.int32, (8, LANES), 1) + block * LANES,
                float(width),
            )
            col_cos, col_sin = col_cos[:1], col_sin[:1]
            where = (slice(None), pl.ds(block * LANES, LANES))
            v_ref[(item, 0) + where] = row_cos * col_cos - row_sin * col_sin
            v_ref[(item, 1) + where] = row_sin * col_cos + row_cos * col_sin
    transmit(0)
    keep_moved(0)

    def step(tick, carry):
        propagate()

        @pl.when((tick >= first) & (tick < first + slices))
        def _():
            for item in range(items):
                for part in range(2):
                    exit_ref[item, tick - first, part] = v_ref[(item, part) + own]

        @pl.when(tick == count - 1)
        def _():
            for item in range(items):
                for row in range(rows):
                    for col in range(cols):
                        where = (pl.ds(row * tile_r, tile_r), pl.ds(col * tile_c, tile_c))
                        real, imag = v_ref[(item, 0) + where], v_ref[(item, 1) + where]
                        misfit = 2.0 * (real * real + imag * imag - intensity_ref[row * cols + col, item])
                        store_u(item, row * tile_r, col * tile_c, misfit * real, -misfit * imag)

        back = 2 * count - 1 - tick

        @pl.when((tick >= count) & (back < first + slices))
        def _():
            total = jnp.zeros((tile_r, tile_c), jnp.float32)
            for item in range(items):
                real, imag = v_ref[(item, 0) + own], v_ref[(item, 1) + own]
                total = total - (
                    imag * moved_ref[back - first, item, 0] + real * moved_ref[back - first, item, 1]
                )
            grad_ref[back - first] = total

        @pl.when((tick != count - 1) & (back > first))
        def _():
            transmit(jnp.where(tick < count, tick + 1, back))

        @pl.when(tick < count - 1)
        def _():
            keep_moved(tick + 1)

        return carry

    lax.fori_loop(0, 2 * count - first, step, 0)


def whole_field_body(sections, phase, tilt, intensity):
    slices, tile_r, tile_c = phase.shape
    items = tilt.shape[0]
    height = tile_r * lax.axis_size("row")
    width = tile_c * lax.axis_size("col")
    count = sections * slices
    blocks = width // LANES
    all_phase = lax.all_gather(phase, ("depth", "row", "col"))
    all_intensity = lax.all_gather(intensity, ("row", "col"))
    vmem = pl.BlockSpec(memory_space=pltpu.VMEM)
    field = (items, 2, height, width)
    gradient, leaving = pl.pallas_call(
        functools.partial(wave_kernel, sections),
        out_shape=(
            jax.ShapeDtypeStruct(phase.shape, jnp.float32),
            jax.ShapeDtypeStruct((items, slices, 2, tile_r, tile_c), jnp.float32),
        ),
        in_specs=[pl.BlockSpec(memory_space=pltpu.SMEM), vmem, vmem, vmem, vmem],
        out_specs=(vmem, vmem),
        scratch_shapes=[
            pltpu.VMEM((count, height, width), jnp.float32),
            pltpu.VMEM((count, height, width), jnp.float32),
            pltpu.VMEM((items, 2 * height, width), jnp.bfloat16),
            pltpu.VMEM((items, 2 * height, width), jnp.bfloat16),
            pltpu.VMEM((items, blocks, height, 4 * LANES), jnp.bfloat16),
            pltpu.VMEM((items, blocks, height, 4 * LANES), jnp.bfloat16),
            pltpu.VMEM(field, jnp.float32),
            pltpu.VMEM((slices, items, 2, tile_r, tile_c), jnp.float32),
        ],
        compiler_params=pltpu.CompilerParams(vmem_limit_bytes=40 * 2**20),
    )(tilt, all_phase, all_intensity, jnp.asarray(row_constant(height)), jnp.asarray(col_constant()))
    return gradient, leaving


def extended_2(cells, sides, width):
    for axis, dim in sides:
        count = lax.axis_size(axis)
        ends = count - 1
        head = lax.slice_in_dim(cells, 0, width, axis=dim)
        tail = lax.slice_in_dim(cells, cells.shape[dim] - width, cells.shape[dim], axis=dim)
        cells = jnp.concatenate(
            [
                lax.ppermute(tail, axis, [(i, (i + 1) % count) for i in range(ends)]),
                cells,
                lax.ppermute(head, axis, [((i + 1) % count, i) for i in range(ends)]),
            ],
            axis=dim,
        )
    return cells


def from_behind(value, axis, steps):
    count = lax.axis_size(axis)
    leading, last = (max(0, -steps), min(count, count - steps))
    return lax.ppermute(value, axis, [(source, source + steps) for source in range(leading, last)])


def band_matrix(block_size, margin, fresnel, adjoint):
    shape_full = (block_size, block_size + 2 * margin)
    out_idx = lax.broadcasted_iota(jnp.int32, shape_full, 0)
    in_idx = lax.broadcasted_iota(jnp.int32, shape_full, 1)
    offset = (out_idx + margin - in_idx).astype(jnp.float32)
    inside = jnp.abs(offset) <= margin
    taper_dist = jnp.maximum(jnp.abs(offset) - 0.5 * margin, 0.0)
    profile = jnp.cos(jnp.pi * taper_dist / (margin + 2.0))
    weight = profile * profile / math.sqrt(fresnel)
    phase_angle = jnp.pi * offset * offset / fresnel
    real_part = jnp.where(inside, jnp.cos(phase_angle) * weight, 0.0)
    imag_part = jnp.where(inside, jnp.sin(phase_angle) * weight, 0.0)
    if adjoint:
        imag_part = -imag_part
    upper = jnp.stack([real_part, -imag_part])
    lower = jnp.stack([imag_part, real_part])
    return jnp.stack([upper, lower])


def along_rows(extended, matrix):
    pieces = [jnp.einsum("pqij,gqjc->gpic", matrix, extended, precision=lax.Precision.HIGHEST)]
    return jnp.concatenate(pieces, axis=2)


def along_cols(extended, matrix, margin):
    block_size = matrix.shape[2]
    extent = extended.shape[3] - 2 * margin
    pieces = []
    for block_start in range(0, extent, block_size):
        window = extended[:, :, :, block_start : block_start + block_size + 2 * margin]
        pieces.append(
            jnp.einsum("pqij,gqrj->gpri", matrix, window, precision=lax.Precision.HIGHEST)
        )
    return jnp.concatenate(pieces, axis=3)


def propagate(current, row_matrix, col_matrix):
    with_rows = extended_2(current, (("row", 2),), HALO)
    row_done = along_rows(with_rows, row_matrix)
    with_cols = extended_2(row_done, (("col", 3),), HALO)
    return along_cols(with_cols, col_matrix, HALO)


def transmit(screen, current, adjoint):
    screen_re = screen[0][None]
    screen_im = screen[1][None]
    if adjoint:
        screen_im = -screen_im
    real_part = screen_re * current[:, 0] - screen_im * current[:, 1]
    imag_part = screen_re * current[:, 1] + screen_im * current[:, 0]
    return jnp.stack([real_part, imag_part], axis=1)


def store_item(store, current, first_item, slice_index, active):
    begin = (first_item, jnp.int32(slice_index), jnp.int32(0), jnp.int32(0), jnp.int32(0))
    sizes_now = (current.shape[0], 1) + current.shape[1:]
    previous = lax.dynamic_slice(store, begin, sizes_now)
    fresh = jnp.where(active, current[:, None], previous)
    return lax.dynamic_update_slice(store, fresh, begin)


def staged_body(phase, tilt, intensity):
    slices, tile_r, tile_c = phase.shape
    batch_size = tilt.shape[0]
    sections = lax.axis_size("depth")
    section_index = lax.axis_index("depth")
    group_size = 1
    groups = batch_size // group_size
    tick_count = sections + groups - 1
    block_r = 64
    block_c = 128
    fwd_rows = band_matrix(block_r, HALO, FRESNEL, False)
    fwd_cols = band_matrix(block_c, HALO, FRESNEL, False)
    adj_rows = band_matrix(block_r, HALO, FRESNEL, True)
    adj_cols = band_matrix(block_c, HALO, FRESNEL, True)
    row_pos = (
        lax.axis_index("row") * tile_r + lax.broadcasted_iota(jnp.int32, (tile_r, tile_c), 0)
    ).astype(jnp.float32)
    col_pos = (
        lax.axis_index("col") * tile_c + lax.broadcasted_iota(jnp.int32, (tile_r, tile_c), 1)
    ).astype(jnp.float32)
    height = float(tile_r * lax.axis_size("row"))
    width_all = float(tile_c * lax.axis_size("col"))
    tilt_f = tilt.astype(jnp.float32)
    phase_angle = (
        2.0
        * jnp.pi
        * (
            tilt_f[:, 0, None, None] * row_pos / height
            + tilt_f[:, 1, None, None] * col_pos / width_all
        )
    )
    incident = jnp.stack([jnp.cos(phase_angle), jnp.sin(phase_angle)], axis=1)
    screens = jnp.stack([jnp.cos(phase), jnp.sin(phase)], axis=1)

    def forward_tick(tick_now, carry):
        incoming, entering, leaving = carry
        group_index = tick_now - section_index
        active = (group_index >= 0) & (group_index < groups)
        first_item = jnp.clip(group_index, 0, groups - 1) * group_size
        current = jnp.where(
            section_index == 0,
            lax.dynamic_slice_in_dim(incident, first_item, group_size, 0),
            incoming,
        )
        entering = store_item(entering, current, first_item, 0, active)
        current = propagate(transmit(screens[0], current, False), fwd_rows, fwd_cols)
        leaving = store_item(leaving, current, first_item, 0, active)
        incoming = from_behind(current, "depth", 1)
        return (incoming, entering, leaving)

    store_zero = jnp.zeros((batch_size, slices, 2, tile_r, tile_c), jnp.float32)
    start_wave = jnp.zeros((group_size, 2, tile_r, tile_c), jnp.float32)
    _, entering, leaving = lax.fori_loop(
        0, tick_count, forward_tick, (start_wave, store_zero, store_zero)
    )
    final_wave = leaving[:, slices - 1]
    misfit = final_wave[:, 0] * final_wave[:, 0] + final_wave[:, 1] * final_wave[:, 1] - intensity
    seed_adjoint = 2.0 * misfit[:, None] * final_wave

    def backward_tick(tick_now, carry):
        incoming, gradient = carry
        group_index = tick_now - (sections - 1 - section_index)
        active = (group_index >= 0) & (group_index < groups)
        first_item = jnp.clip(group_index, 0, groups - 1) * group_size
        adjoint_wave = jnp.where(
            section_index == sections - 1,
            lax.dynamic_slice_in_dim(seed_adjoint, first_item, group_size, 0),
            incoming,
        )
        for slice_index in reversed(range(slices)):
            pulled = propagate(adjoint_wave, adj_rows, adj_cols)
            arrived = lax.dynamic_slice_in_dim(entering[:, slice_index], first_item, group_size, 0)
            moved = transmit(screens[slice_index], arrived, False)
            contribution = jnp.sum(pulled[:, 1] * moved[:, 0] - pulled[:, 0] * moved[:, 1], axis=0)
            gradient = gradient.at[slice_index].add(jnp.where(active, contribution, 0.0))
            adjoint_wave = transmit(screens[slice_index], pulled, True)
        incoming = from_behind(adjoint_wave, "depth", -1)
        return (incoming, gradient)

    grad_zero = jnp.zeros((slices, tile_r, tile_c), jnp.float32)
    _, gradient = lax.fori_loop(0, tick_count, backward_tick, (start_wave, grad_zero))
    return (gradient, leaving)


def fits_whole(phase_shape, batch, mesh):
    slices, height, width = phase_shape
    rows, cols = mesh.shape["row"], mesh.shape["col"]
    bytes_all = 4 * height * width * (slices + batch)
    return (
        bytes_all <= GATHER_BUDGET
        and height == LANES
        and (height // rows) % 16 == 0
        and (width // cols) % LANES == 0
        and width % (2 * LANES) == 0
    )


def solution(mesh):
    placed = (P("depth", "row", "col"), P(), P(None, "row", "col"))

    def run(phase, tilt, intensity):
        if fits_whole(phase.shape, tilt.shape[0], mesh):
            body = functools.partial(whole_field_body, mesh.shape["depth"])
        else:
            body = staged_body
        return jax.shard_map(
            body,
            mesh=mesh,
            in_specs=placed,
            out_specs=(P("depth", "row", "col"), P(None, "depth", None, "row", "col")),
            check_vma=False,
        )(phase, tilt, intensity)

    return run
```

```python
import math

import jax
import jax.numpy as jnp
import numpy as np
from jax import lax
from jax.experimental import pallas as pl
from jax.experimental.pallas import tpu as pltpu
from jax.sharding import PartitionSpec as P

HALO = 32
FRESNEL = 64
LANES = 128
GATHER_BUDGET = 4 * 2**20
SIN = (
    0.9999999980536763,
    -0.1666666530009577,
    0.008333305907073658,
    -0.00019838908256358006,
    2.745822627876341e-06,
    -2.3043562782810933e-08,
)
COS = (
    0.9999999961345007,
    -0.4999999301617528,
    0.04166646215023687,
    -0.0013886696163545999,
    2.4695045482778703e-05,
    -2.5154931690000354e-07,
)


def horner(coefficients, square):
    total = jnp.full_like(square, coefficients[-1])
    for coefficient in coefficients[-2::-1]:
        total = total * square + coefficient
    return total


def cos_sin(angle):
    square = angle * angle
    return horner(COS, square), horner(SIN, square) * angle


def turn(fraction):
    half_cos, half_sin = cos_sin(fraction * math.pi)
    return half_cos * half_cos - half_sin * half_sin, 2.0 * half_cos * half_sin


def halves(value):
    high = value.astype(jnp.bfloat16)
    return high, (value - high.astype(jnp.float32)).astype(jnp.bfloat16)


def np_halves(matrix):
    high = matrix.astype(jnp.bfloat16)
    return high, (matrix - high.astype(np.float64)).astype(jnp.bfloat16)


def np_taps():
    offset = np.arange(-HALO, HALO + 1, dtype=np.float64)
    taper = np.maximum(np.abs(offset) - 0.5 * HALO, 0.0)
    weight = np.cos(np.pi * taper / (HALO + 2.0)) ** 2 / math.sqrt(FRESNEL)
    return weight * np.exp(1j * np.pi * offset * offset / FRESNEL)


def np_band(out_pos, in_pos):
    offset = out_pos[:, None] - in_pos[None, :]
    inside = np.abs(offset) <= HALO
    return np.where(inside, np_taps()[np.clip(offset, -HALO, HALO) + HALO], 0.0)


def row_constant(height):
    band = np_band(np.arange(height), np.arange(height))
    whole = np.block([[band.real, -band.imag], [band.imag, band.real]])
    high, low = np_halves(whole)
    return np.concatenate([high, low], axis=1)


def col_constant():
    lane = np.arange(LANES)
    edge_pos = np.where(lane < LANES // 2, lane + LANES, lane - LANES)
    parts = []
    for position in (lane, edge_pos):
        band = np_band(lane, position).T
        parts.append(np.block([[band.real, band.imag], [-band.imag, band.real]]))
    high, low = np_halves(np.concatenate(parts, axis=0))
    return np.concatenate([high, low], axis=0)


def wave_kernel(
    tilt_ref, near_ref, far_ref, row_ref, col_ref, mine_ref, theirs_ref,
    cos_ref, sin_ref, u_high, u_low, a_high, a_low, v_ref, moved_ref,
):
    count, height, width = cos_ref.shape
    slices, _, tile_r, tile_c = mine_ref.shape
    cols = width // tile_c
    blocks = width // LANES
    half = LANES // 2
    core = lax.axis_index("row")
    first = lax.axis_index("depth") * slices
    near_row = pl.multiple_of(core * tile_r, tile_r)
    far_row = pl.multiple_of((1 - core) * tile_r, tile_r)
    own_col = pl.ds(pl.multiple_of(lax.axis_index("col") * tile_c, tile_c), tile_c)
    sides = ((near_ref, near_row), (far_ref, far_row))

    def store_u(row, col, real, imag):
        for part, value in enumerate((real, imag)):
            high, low = halves(value)
            where = (pl.ds(part * height + row, value.shape[0]), pl.ds(col, value.shape[1]))
            u_high[where] = high
            u_low[where] = low

    def turned(slice_index, where):
        cos, sin = cos_ref[(slice_index,) + where], sin_ref[(slice_index,) + where]
        real, imag = v_ref[(0,) + where], v_ref[(1,) + where]
        return cos * real - sin * imag, cos * imag + sin * real

    def keep_moved(slice_index):
        @pl.when((slice_index >= first) & (slice_index < first + slices))
        def _():
            real, imag = turned(slice_index, (slice(None), own_col))
            moved_ref[slice_index - first, 0] = real
            moved_ref[slice_index - first, 1] = imag

    def transmit(slice_index):
        for block in range(blocks):
            where = (slice(None), pl.ds(block * LANES, LANES))
            store_u(0, block * LANES, *turned(slice_index, where))

    def propagate():
        matrix = jnp.concatenate([row_ref[:, : 2 * height], row_ref[...]], axis=1)
        for start in range(0, width, 2 * LANES):
            where = (slice(None), pl.ds(start, 2 * LANES))
            high, low = u_high[where], u_low[where]
            done = jnp.dot(
                matrix,
                jnp.concatenate([high, low, high], axis=0),
                preferred_element_type=jnp.float32,
            )
            for part in range(2):
                for sub in range(2):
                    block = start // LANES + sub
                    value = done[part * height : (part + 1) * height, sub * LANES : (sub + 1) * LANES]
                    for target, piece in zip((a_high, a_low), halves(value)):
                        target[block, :, pl.ds(part * LANES, LANES)] = piece
                        if block > 0:
                            target[block - 1, :, pl.ds((2 + part) * LANES, half)] = piece[:, :half]
                        if block < blocks - 1:
                            target[block + 1, :, pl.ds((2 + part) * LANES + half, half)] = piece[:, half:]
        high = a_high[...].reshape(blocks * height, 4 * LANES)
        low = a_low[...].reshape(blocks * height, 4 * LANES)
        done = jnp.dot(
            jnp.concatenate([high, low, high], axis=1),
            jnp.concatenate([col_ref[: 4 * LANES], col_ref[...]], axis=0),
            preferred_element_type=jnp.float32,
        )
        for block in range(blocks):
            for part in range(2):
                v_ref[part, :, pl.ds(block * LANES, LANES)] = done[
                    block * height : (block + 1) * height, part * LANES : (part + 1) * LANES
                ]

    for target in (a_high, a_low):
        for part in range(2):
            target[0, :, pl.ds((2 + part) * LANES + half, half)] = jnp.zeros((height, half), jnp.bfloat16)
            target[blocks - 1, :, pl.ds((2 + part) * LANES, half)] = jnp.zeros((height, half), jnp.bfloat16)

    def screens(slice_index, carry):
        section, inner = slice_index // slices, slice_index % slices
        for side_ref, row in sides:
            for col in range(cols):
                cos, sin = cos_sin(side_ref[(section * cols + col) * slices + inner])
                where = (slice_index, pl.ds(row, tile_r), pl.ds(col * tile_c, tile_c))
                cos_ref[where] = cos
                sin_ref[where] = sin
        return carry

    lax.fori_loop(0, count, screens, 0)

    def cycles(number, position, extent):
        fraction = (number * position).astype(jnp.float32) / extent
        return turn(fraction - jnp.round(fraction))

    row_cos, row_sin = cycles(
        tilt_ref[core, 0], lax.broadcasted_iota(jnp.int32, (height, LANES), 0), float(height)
    )
    for block in range(blocks):
        col_cos, col_sin = cycles(
            tilt_ref[core, 1],
            lax.broadcasted_iota(jnp.int32, (8, LANES), 1) + block * LANES,
            float(width),
        )
        col_cos, col_sin = col_cos[:1], col_sin[:1]
        where = (slice(None), pl.ds(block * LANES, LANES))
        v_ref[(0,) + where] = row_cos * col_cos - row_sin * col_sin
        v_ref[(1,) + where] = row_sin * col_cos + row_cos * col_sin
    transmit(0)
    keep_moved(0)

    def step(tick, carry):
        propagate()

        @pl.when((tick >= first) & (tick < first + slices))
        def _():
            for target, row in ((mine_ref, near_row), (theirs_ref, far_row)):
                for part in range(2):
                    target[tick - first, part] = v_ref[part, pl.ds(row, tile_r), own_col]

        @pl.when(tick == count - 1)
        def _():
            for side_ref, row in sides:
                for col in range(cols):
                    where = (pl.ds(row, tile_r), pl.ds(col * tile_c, tile_c))
                    real, imag = v_ref[(0,) + where], v_ref[(1,) + where]
                    misfit = 2.0 * (real * real + imag * imag - side_ref[count * cols + col])
                    store_u(row, col * tile_c, misfit * real, -misfit * imag)

        back = 2 * count - 1 - tick

        @pl.when((tick >= count) & (back < first + slices))
        def _():
            for target, row in ((mine_ref, near_row), (theirs_ref, far_row)):
                where = (pl.ds(row, tile_r), own_col)
                here = (pl.ds(row, tile_r), slice(None))
                real, imag = v_ref[(0,) + where], v_ref[(1,) + where]
                target[back - first, 2] = -(
                    imag * moved_ref[(back - first, 0) + here] + real * moved_ref[(back - first, 1) + here]
                )

        @pl.when((tick != count - 1) & (back > first))
        def _():
            transmit(jnp.where(tick < count, tick + 1, back))

        @pl.when(tick < count - 1)
        def _():
            keep_moved(tick + 1)

        return carry

    lax.fori_loop(0, 2 * count - first, step, 0)


def spread(shard, axis):
    size = lax.axis_size(axis)
    return lax.all_to_all(jnp.broadcast_to(shard[None], (size,) + shard.shape), axis, 0, 0)


def swap_cores(value):
    return lax.ppermute(value, "row", [(0, 1), (1, 0)])


def whole_field_body(phase, tilt, intensity):
    slices, tile_r, tile_c = phase.shape
    sections, cols = lax.axis_size("depth"), lax.axis_size("col")
    core = lax.axis_index("row")
    height = tile_r * lax.axis_size("row")
    width = tile_c * cols
    count = sections * slices
    blocks = width // LANES
    plane = spread(jnp.concatenate([phase, intensity], axis=0), "col")
    near_phase = spread(plane[:, :slices], "depth").reshape(count * cols, tile_r, tile_c)

    def packed(item):
        chosen = lax.dynamic_index_in_dim(plane, slices + item, 1, keepdims=False)
        return jnp.concatenate([near_phase, chosen], axis=0)

    near, far = packed(core), swap_cores(packed(1 - core))
    vmem = pl.BlockSpec(memory_space=pltpu.VMEM)
    result = jax.ShapeDtypeStruct((slices, 3, tile_r, tile_c), jnp.float32)
    mine, theirs = pl.pallas_call(
        wave_kernel,
        out_shape=(result, result),
        in_specs=[pl.BlockSpec(memory_space=pltpu.SMEM), vmem, vmem, vmem, vmem],
        out_specs=(vmem, vmem),
        scratch_shapes=[
            pltpu.VMEM((count, height, width), jnp.float32),
            pltpu.VMEM((count, height, width), jnp.float32),
            pltpu.VMEM((2 * height, width), jnp.bfloat16),
            pltpu.VMEM((2 * height, width), jnp.bfloat16),
            pltpu.VMEM((blocks, height, 4 * LANES), jnp.bfloat16),
            pltpu.VMEM((blocks, height, 4 * LANES), jnp.bfloat16),
            pltpu.VMEM((2, height, width), jnp.float32),
            pltpu.VMEM((slices, 2, height, tile_c), jnp.float32),
        ],
        compiler_params=pltpu.CompilerParams(vmem_limit_bytes=24 * 2**20),
    )(tilt, near, far, jnp.asarray(row_constant(height)), jnp.asarray(col_constant()))
    received = swap_cores(theirs)
    gradient = mine[:, 2] + received[:, 2]
    waves = (mine[:, :2], received[:, :2])
    leaving = jnp.stack([jnp.where(core == 0, waves[0], waves[1]), jnp.where(core == 0, waves[1], waves[0])])
    return gradient, leaving


def extended_2(cells, sides, width):
    for axis, dim in sides:
        count = lax.axis_size(axis)
        ends = count - 1
        head = lax.slice_in_dim(cells, 0, width, axis=dim)
        tail = lax.slice_in_dim(cells, cells.shape[dim] - width, cells.shape[dim], axis=dim)
        cells = jnp.concatenate(
            [
                lax.ppermute(tail, axis, [(i, (i + 1) % count) for i in range(ends)]),
                cells,
                lax.ppermute(head, axis, [((i + 1) % count, i) for i in range(ends)]),
            ],
            axis=dim,
        )
    return cells


def from_behind(value, axis, steps):
    count = lax.axis_size(axis)
    leading, last = (max(0, -steps), min(count, count - steps))
    return lax.ppermute(value, axis, [(source, source + steps) for source in range(leading, last)])


def band_matrix(block_size, margin, fresnel, adjoint):
    shape_full = (block_size, block_size + 2 * margin)
    out_idx = lax.broadcasted_iota(jnp.int32, shape_full, 0)
    in_idx = lax.broadcasted_iota(jnp.int32, shape_full, 1)
    offset = (out_idx + margin - in_idx).astype(jnp.float32)
    inside = jnp.abs(offset) <= margin
    taper_dist = jnp.maximum(jnp.abs(offset) - 0.5 * margin, 0.0)
    profile = jnp.cos(jnp.pi * taper_dist / (margin + 2.0))
    weight = profile * profile / math.sqrt(fresnel)
    phase_angle = jnp.pi * offset * offset / fresnel
    real_part = jnp.where(inside, jnp.cos(phase_angle) * weight, 0.0)
    imag_part = jnp.where(inside, jnp.sin(phase_angle) * weight, 0.0)
    if adjoint:
        imag_part = -imag_part
    upper = jnp.stack([real_part, -imag_part])
    lower = jnp.stack([imag_part, real_part])
    return jnp.stack([upper, lower])


def along_rows(extended, matrix):
    pieces = [jnp.einsum("pqij,gqjc->gpic", matrix, extended, precision=lax.Precision.HIGHEST)]
    return jnp.concatenate(pieces, axis=2)


def along_cols(extended, matrix, margin):
    block_size = matrix.shape[2]
    extent = extended.shape[3] - 2 * margin
    pieces = []
    for block_start in range(0, extent, block_size):
        window = extended[:, :, :, block_start : block_start + block_size + 2 * margin]
        pieces.append(
            jnp.einsum("pqij,gqrj->gpri", matrix, window, precision=lax.Precision.HIGHEST)
        )
    return jnp.concatenate(pieces, axis=3)


def propagate(current, row_matrix, col_matrix):
    with_rows = extended_2(current, (("row", 2),), HALO)
    row_done = along_rows(with_rows, row_matrix)
    with_cols = extended_2(row_done, (("col", 3),), HALO)
    return along_cols(with_cols, col_matrix, HALO)


def transmit(screen, current, adjoint):
    screen_re = screen[0][None]
    screen_im = screen[1][None]
    if adjoint:
        screen_im = -screen_im
    real_part = screen_re * current[:, 0] - screen_im * current[:, 1]
    imag_part = screen_re * current[:, 1] + screen_im * current[:, 0]
    return jnp.stack([real_part, imag_part], axis=1)


def store_item(store, current, first_item, slice_index, active):
    begin = (first_item, jnp.int32(slice_index), jnp.int32(0), jnp.int32(0), jnp.int32(0))
    sizes_now = (current.shape[0], 1) + current.shape[1:]
    previous = lax.dynamic_slice(store, begin, sizes_now)
    fresh = jnp.where(active, current[:, None], previous)
    return lax.dynamic_update_slice(store, fresh, begin)


def staged_body(phase, tilt, intensity):
    slices, tile_r, tile_c = phase.shape
    batch_size = tilt.shape[0]
    sections = lax.axis_size("depth")
    section_index = lax.axis_index("depth")
    group_size = 1
    groups = batch_size // group_size
    tick_count = sections + groups - 1
    block_r = 64
    block_c = 128
    fwd_rows = band_matrix(block_r, HALO, FRESNEL, False)
    fwd_cols = band_matrix(block_c, HALO, FRESNEL, False)
    adj_rows = band_matrix(block_r, HALO, FRESNEL, True)
    adj_cols = band_matrix(block_c, HALO, FRESNEL, True)
    row_pos = (
        lax.axis_index("row") * tile_r + lax.broadcasted_iota(jnp.int32, (tile_r, tile_c), 0)
    ).astype(jnp.float32)
    col_pos = (
        lax.axis_index("col") * tile_c + lax.broadcasted_iota(jnp.int32, (tile_r, tile_c), 1)
    ).astype(jnp.float32)
    height = float(tile_r * lax.axis_size("row"))
    width_all = float(tile_c * lax.axis_size("col"))
    tilt_f = tilt.astype(jnp.float32)
    phase_angle = (
        2.0
        * jnp.pi
        * (
            tilt_f[:, 0, None, None] * row_pos / height
            + tilt_f[:, 1, None, None] * col_pos / width_all
        )
    )
    incident = jnp.stack([jnp.cos(phase_angle), jnp.sin(phase_angle)], axis=1)
    screens = jnp.stack([jnp.cos(phase), jnp.sin(phase)], axis=1)

    def forward_tick(tick_now, carry):
        incoming, entering, leaving = carry
        group_index = tick_now - section_index
        active = (group_index >= 0) & (group_index < groups)
        first_item = jnp.clip(group_index, 0, groups - 1) * group_size
        current = jnp.where(
            section_index == 0,
            lax.dynamic_slice_in_dim(incident, first_item, group_size, 0),
            incoming,
        )
        entering = store_item(entering, current, first_item, 0, active)
        current = propagate(transmit(screens[0], current, False), fwd_rows, fwd_cols)
        leaving = store_item(leaving, current, first_item, 0, active)
        incoming = from_behind(current, "depth", 1)
        return (incoming, entering, leaving)

    store_zero = jnp.zeros((batch_size, slices, 2, tile_r, tile_c), jnp.float32)
    start_wave = jnp.zeros((group_size, 2, tile_r, tile_c), jnp.float32)
    _, entering, leaving = lax.fori_loop(
        0, tick_count, forward_tick, (start_wave, store_zero, store_zero)
    )
    final_wave = leaving[:, slices - 1]
    misfit = final_wave[:, 0] * final_wave[:, 0] + final_wave[:, 1] * final_wave[:, 1] - intensity
    seed_adjoint = 2.0 * misfit[:, None] * final_wave

    def backward_tick(tick_now, carry):
        incoming, gradient = carry
        group_index = tick_now - (sections - 1 - section_index)
        active = (group_index >= 0) & (group_index < groups)
        first_item = jnp.clip(group_index, 0, groups - 1) * group_size
        adjoint_wave = jnp.where(
            section_index == sections - 1,
            lax.dynamic_slice_in_dim(seed_adjoint, first_item, group_size, 0),
            incoming,
        )
        for slice_index in reversed(range(slices)):
            pulled = propagate(adjoint_wave, adj_rows, adj_cols)
            arrived = lax.dynamic_slice_in_dim(entering[:, slice_index], first_item, group_size, 0)
            moved = transmit(screens[slice_index], arrived, False)
            contribution = jnp.sum(pulled[:, 1] * moved[:, 0] - pulled[:, 0] * moved[:, 1], axis=0)
            gradient = gradient.at[slice_index].add(jnp.where(active, contribution, 0.0))
            adjoint_wave = transmit(screens[slice_index], pulled, True)
        incoming = from_behind(adjoint_wave, "depth", -1)
        return (incoming, gradient)

    grad_zero = jnp.zeros((slices, tile_r, tile_c), jnp.float32)
    _, gradient = lax.fori_loop(0, tick_count, backward_tick, (start_wave, grad_zero))
    return (gradient, leaving)


def fits_whole(phase_shape, batch, mesh):
    slices, height, width = phase_shape
    rows, cols = mesh.shape["row"], mesh.shape["col"]
    bytes_all = 4 * height * width * (slices + batch)
    return (
        bytes_all <= GATHER_BUDGET
        and batch == rows == 2
        and height == LANES
        and (height // rows) % 16 == 0
        and (width // cols) % LANES == 0
        and width % (2 * LANES) == 0
    )


def solution(mesh):
    placed = (P("depth", "row", "col"), P(), P(None, "row", "col"))

    def run(phase, tilt, intensity):
        if fits_whole(phase.shape, tilt.shape[0], mesh):
            body = whole_field_body
        else:
            body = staged_body
        return jax.shard_map(
            body,
            mesh=mesh,
            in_specs=placed,
            out_specs=(P("depth", "row", "col"), P(None, "depth", None, "row", "col")),
            check_vma=False,
        )(phase, tilt, intensity)

    return run
```

```python
import math

import jax
import jax.numpy as jnp
import numpy as np
from jax import lax
from jax.experimental import pallas as pl
from jax.experimental.pallas import tpu as pltpu
from jax.sharding import PartitionSpec as P

HALO = 32
FRESNEL = 64
LANES = 128
GATHER_BUDGET = 4 * 2**20
SIN = (
    0.9999999980536763,
    -0.1666666530009577,
    0.008333305907073658,
    -0.00019838908256358006,
    2.745822627876341e-06,
    -2.3043562782810933e-08,
)
COS = (
    0.9999999961345007,
    -0.4999999301617528,
    0.04166646215023687,
    -0.0013886696163545999,
    2.4695045482778703e-05,
    -2.5154931690000354e-07,
)


def horner(coefficients, square):
    total = jnp.full_like(square, coefficients[-1])
    for coefficient in coefficients[-2::-1]:
        total = total * square + coefficient
    return total


def cos_sin(angle):
    square = angle * angle
    return horner(COS, square), horner(SIN, square) * angle


def turn(fraction):
    half_cos, half_sin = cos_sin(fraction * math.pi)
    return half_cos * half_cos - half_sin * half_sin, 2.0 * half_cos * half_sin


def halves(value):
    high = value.astype(jnp.bfloat16)
    return high, (value - high.astype(jnp.float32)).astype(jnp.bfloat16)


def np_halves(matrix):
    high = matrix.astype(jnp.bfloat16)
    return high, (matrix - high.astype(np.float64)).astype(jnp.bfloat16)


def np_taps():
    offset = np.arange(-HALO, HALO + 1, dtype=np.float64)
    taper = np.maximum(np.abs(offset) - 0.5 * HALO, 0.0)
    weight = np.cos(np.pi * taper / (HALO + 2.0)) ** 2 / math.sqrt(FRESNEL)
    return weight * np.exp(1j * np.pi * offset * offset / FRESNEL)


def np_band(out_pos, in_pos):
    offset = out_pos[:, None] - in_pos[None, :]
    inside = np.abs(offset) <= HALO
    return np.where(inside, np_taps()[np.clip(offset, -HALO, HALO) + HALO], 0.0)


def row_constant(height):
    band = np_band(np.arange(height), np.arange(height))
    whole = np.block([[band.real, -band.imag], [band.imag, band.real]])
    high, low = np_halves(whole)
    return np.concatenate([high, low], axis=1)


def col_constant():
    lane = np.arange(LANES)
    edge_pos = np.where(lane < LANES // 2, lane + LANES, lane - LANES)
    parts = []
    for position in (lane, edge_pos):
        band = np_band(lane, position).T
        parts.append(np.block([[band.real, band.imag], [-band.imag, band.real]]))
    high, low = np_halves(np.concatenate(parts, axis=0))
    return np.concatenate([high, low], axis=0)


def wave_kernel(
    tilt_ref, near_ref, far_ref, row_ref, col_ref, mine_ref, theirs_ref,
    cos_ref, sin_ref, u_high, u_low, a_high, a_low, v_ref, moved_ref,
):
    count, height, width = cos_ref.shape
    slices, _, tile_r, tile_c = mine_ref.shape
    cols = width // tile_c
    blocks = width // LANES
    half = LANES // 2
    core = lax.axis_index("row")
    first = lax.axis_index("depth") * slices
    near_row = pl.multiple_of(core * tile_r, tile_r)
    far_row = pl.multiple_of((1 - core) * tile_r, tile_r)
    own_col = pl.ds(pl.multiple_of(lax.axis_index("col") * tile_c, tile_c), tile_c)
    sides = ((near_ref, near_row), (far_ref, far_row))
    own_section, own_place = lax.axis_index("depth"), lax.axis_index("col")

    def store_u(row, col, real, imag):
        for part, value in enumerate((real, imag)):
            high, low = halves(value)
            where = (pl.ds(part * height + row, value.shape[0]), pl.ds(col, value.shape[1]))
            u_high[where] = high
            u_low[where] = low

    def turned(slice_index, where):
        cos, sin = cos_ref[(slice_index,) + where], sin_ref[(slice_index,) + where]
        real, imag = v_ref[(0,) + where], v_ref[(1,) + where]
        return cos * real - sin * imag, cos * imag + sin * real

    def keep_moved(slice_index):
        @pl.when((slice_index >= first) & (slice_index < first + slices))
        def _():
            real, imag = turned(slice_index, (slice(None), own_col))
            moved_ref[slice_index - first, 0] = real
            moved_ref[slice_index - first, 1] = imag

    def transmit(slice_index):
        for block in range(blocks):
            where = (slice(None), pl.ds(block * LANES, LANES))
            store_u(0, block * LANES, *turned(slice_index, where))

    def propagate():
        matrix = jnp.concatenate([row_ref[:, : 2 * height], row_ref[...]], axis=1)
        for start in range(0, width, 2 * LANES):
            where = (slice(None), pl.ds(start, 2 * LANES))
            high, low = u_high[where], u_low[where]
            done = jnp.dot(
                matrix,
                jnp.concatenate([high, low, high], axis=0),
                preferred_element_type=jnp.float32,
            )
            for part in range(2):
                for sub in range(2):
                    block = start // LANES + sub
                    value = done[part * height : (part + 1) * height, sub * LANES : (sub + 1) * LANES]
                    for target, piece in zip((a_high, a_low), halves(value)):
                        target[block, :, pl.ds(part * LANES, LANES)] = piece
                        if block > 0:
                            target[block - 1, :, pl.ds((2 + part) * LANES, half)] = piece[:, :half]
                        if block < blocks - 1:
                            target[block + 1, :, pl.ds((2 + part) * LANES + half, half)] = piece[:, half:]
        high = a_high[...].reshape(blocks * height, 4 * LANES)
        low = a_low[...].reshape(blocks * height, 4 * LANES)
        done = jnp.dot(
            jnp.concatenate([high, low, high], axis=1),
            jnp.concatenate([col_ref[: 4 * LANES], col_ref[...]], axis=0),
            preferred_element_type=jnp.float32,
        )
        for block in range(blocks):
            for part in range(2):
                v_ref[part, :, pl.ds(block * LANES, LANES)] = done[
                    block * height : (block + 1) * height, part * LANES : (part + 1) * LANES
                ]

    for target in (a_high, a_low):
        for part in range(2):
            target[0, :, pl.ds((2 + part) * LANES + half, half)] = jnp.zeros((height, half), jnp.bfloat16)
            target[blocks - 1, :, pl.ds((2 + part) * LANES, half)] = jnp.zeros((height, half), jnp.bfloat16)

    def screens(slice_index, carry):
        held = ((slice_index // slices) ^ own_section) * slices + slice_index % slices
        for side_ref, row in sides:
            for col in range(cols):
                cos, sin = cos_sin(side_ref[(col ^ own_place) * count + held])
                where = (slice_index, pl.ds(row, tile_r), pl.ds(col * tile_c, tile_c))
                cos_ref[where] = cos
                sin_ref[where] = sin
        return carry

    lax.fori_loop(0, count, screens, 0)

    def cycles(number, position, extent):
        fraction = (number * position).astype(jnp.float32) / extent
        return turn(fraction - jnp.round(fraction))

    row_cos, row_sin = cycles(
        tilt_ref[core, 0], lax.broadcasted_iota(jnp.int32, (height, LANES), 0), float(height)
    )
    for block in range(blocks):
        col_cos, col_sin = cycles(
            tilt_ref[core, 1],
            lax.broadcasted_iota(jnp.int32, (8, LANES), 1) + block * LANES,
            float(width),
        )
        col_cos, col_sin = col_cos[:1], col_sin[:1]
        where = (slice(None), pl.ds(block * LANES, LANES))
        v_ref[(0,) + where] = row_cos * col_cos - row_sin * col_sin
        v_ref[(1,) + where] = row_sin * col_cos + row_cos * col_sin
    transmit(0)
    keep_moved(0)

    def step(tick, carry):
        propagate()

        @pl.when((tick >= first) & (tick < first + slices))
        def _():
            for target, row in ((mine_ref, near_row), (theirs_ref, far_row)):
                for part in range(2):
                    target[tick - first, part] = v_ref[part, pl.ds(row, tile_r), own_col]

        @pl.when(tick == count - 1)
        def _():
            for side_ref, row in sides:
                for col in range(cols):
                    where = (pl.ds(row, tile_r), pl.ds(col * tile_c, tile_c))
                    real, imag = v_ref[(0,) + where], v_ref[(1,) + where]
                    misfit = 2.0 * (real * real + imag * imag - side_ref[count * cols + (col ^ own_place)])
                    store_u(row, col * tile_c, misfit * real, -misfit * imag)

        back = 2 * count - 1 - tick

        @pl.when((tick >= count) & (back < first + slices))
        def _():
            for target, row in ((mine_ref, near_row), (theirs_ref, far_row)):
                where = (pl.ds(row, tile_r), own_col)
                here = (pl.ds(row, tile_r), slice(None))
                real, imag = v_ref[(0,) + where], v_ref[(1,) + where]
                target[back - first, 2] = -(
                    imag * moved_ref[(back - first, 0) + here] + real * moved_ref[(back - first, 1) + here]
                )

        @pl.when((tick != count - 1) & (back > first))
        def _():
            transmit(jnp.where(tick < count, tick + 1, back))

        @pl.when(tick < count - 1)
        def _():
            keep_moved(tick + 1)

        return carry

    lax.fori_loop(0, 2 * count - first, step, 0)


def spread(shard, axis):
    size = lax.axis_size(axis)
    pieces = [shard]
    for bits in range(1, size):
        pieces.append(lax.ppermute(shard, axis, [(i, i ^ bits) for i in range(size)]))
    return jnp.stack(pieces)


def swap_cores(value):
    return lax.ppermute(value, "row", [(0, 1), (1, 0)])


def whole_field_body(phase, tilt, intensity):
    slices, tile_r, tile_c = phase.shape
    sections, cols = lax.axis_size("depth"), lax.axis_size("col")
    core = lax.axis_index("row")
    height = tile_r * lax.axis_size("row")
    width = tile_c * cols
    count = sections * slices
    blocks = width // LANES
    column = spread(phase, "depth").reshape(count, tile_r, tile_c)
    near_intensity = spread(intensity, "col")
    near_phase = spread(column, "col").reshape(cols * count, tile_r, tile_c)

    def packed(item):
        chosen = lax.dynamic_index_in_dim(near_intensity, item, 1, keepdims=False)
        return jnp.concatenate([near_phase, chosen], axis=0)

    near, far = packed(core), swap_cores(packed(1 - core))
    vmem = pl.BlockSpec(memory_space=pltpu.VMEM)
    result = jax.ShapeDtypeStruct((slices, 3, tile_r, tile_c), jnp.float32)
    mine, theirs = pl.pallas_call(
        wave_kernel,
        out_shape=(result, result),
        in_specs=[pl.BlockSpec(memory_space=pltpu.SMEM), vmem, vmem, vmem, vmem],
        out_specs=(vmem, vmem),
        scratch_shapes=[
            pltpu.VMEM((count, height, width), jnp.float32),
            pltpu.VMEM((count, height, width), jnp.float32),
            pltpu.VMEM((2 * height, width), jnp.bfloat16),
            pltpu.VMEM((2 * height, width), jnp.bfloat16),
            pltpu.VMEM((blocks, height, 4 * LANES), jnp.bfloat16),
            pltpu.VMEM((blocks, height, 4 * LANES), jnp.bfloat16),
            pltpu.VMEM((2, height, width), jnp.float32),
            pltpu.VMEM((slices, 2, height, tile_c), jnp.float32),
        ],
        compiler_params=pltpu.CompilerParams(vmem_limit_bytes=24 * 2**20),
    )(tilt, near, far, jnp.asarray(row_constant(height)), jnp.asarray(col_constant()))
    received = swap_cores(theirs)
    gradient = mine[:, 2] + received[:, 2]
    waves = (mine[:, :2], received[:, :2])
    leaving = jnp.stack([jnp.where(core == 0, waves[0], waves[1]), jnp.where(core == 0, waves[1], waves[0])])
    return gradient, leaving


def extended_2(cells, sides, width):
    for axis, dim in sides:
        count = lax.axis_size(axis)
        ends = count - 1
        head = lax.slice_in_dim(cells, 0, width, axis=dim)
        tail = lax.slice_in_dim(cells, cells.shape[dim] - width, cells.shape[dim], axis=dim)
        cells = jnp.concatenate(
            [
                lax.ppermute(tail, axis, [(i, (i + 1) % count) for i in range(ends)]),
                cells,
                lax.ppermute(head, axis, [((i + 1) % count, i) for i in range(ends)]),
            ],
            axis=dim,
        )
    return cells


def from_behind(value, axis, steps):
    count = lax.axis_size(axis)
    leading, last = (max(0, -steps), min(count, count - steps))
    return lax.ppermute(value, axis, [(source, source + steps) for source in range(leading, last)])


def band_matrix(block_size, margin, fresnel, adjoint):
    shape_full = (block_size, block_size + 2 * margin)
    out_idx = lax.broadcasted_iota(jnp.int32, shape_full, 0)
    in_idx = lax.broadcasted_iota(jnp.int32, shape_full, 1)
    offset = (out_idx + margin - in_idx).astype(jnp.float32)
    inside = jnp.abs(offset) <= margin
    taper_dist = jnp.maximum(jnp.abs(offset) - 0.5 * margin, 0.0)
    profile = jnp.cos(jnp.pi * taper_dist / (margin + 2.0))
    weight = profile * profile / math.sqrt(fresnel)
    phase_angle = jnp.pi * offset * offset / fresnel
    real_part = jnp.where(inside, jnp.cos(phase_angle) * weight, 0.0)
    imag_part = jnp.where(inside, jnp.sin(phase_angle) * weight, 0.0)
    if adjoint:
        imag_part = -imag_part
    upper = jnp.stack([real_part, -imag_part])
    lower = jnp.stack([imag_part, real_part])
    return jnp.stack([upper, lower])


def along_rows(extended, matrix):
    pieces = [jnp.einsum("pqij,gqjc->gpic", matrix, extended, precision=lax.Precision.HIGHEST)]
    return jnp.concatenate(pieces, axis=2)


def along_cols(extended, matrix, margin):
    block_size = matrix.shape[2]
    extent = extended.shape[3] - 2 * margin
    pieces = []
    for block_start in range(0, extent, block_size):
        window = extended[:, :, :, block_start : block_start + block_size + 2 * margin]
        pieces.append(
            jnp.einsum("pqij,gqrj->gpri", matrix, window, precision=lax.Precision.HIGHEST)
        )
    return jnp.concatenate(pieces, axis=3)


def propagate(current, row_matrix, col_matrix):
    with_rows = extended_2(current, (("row", 2),), HALO)
    row_done = along_rows(with_rows, row_matrix)
    with_cols = extended_2(row_done, (("col", 3),), HALO)
    return along_cols(with_cols, col_matrix, HALO)


def transmit(screen, current, adjoint):
    screen_re = screen[0][None]
    screen_im = screen[1][None]
    if adjoint:
        screen_im = -screen_im
    real_part = screen_re * current[:, 0] - screen_im * current[:, 1]
    imag_part = screen_re * current[:, 1] + screen_im * current[:, 0]
    return jnp.stack([real_part, imag_part], axis=1)


def store_item(store, current, first_item, slice_index, active):
    begin = (first_item, jnp.int32(slice_index), jnp.int32(0), jnp.int32(0), jnp.int32(0))
    sizes_now = (current.shape[0], 1) + current.shape[1:]
    previous = lax.dynamic_slice(store, begin, sizes_now)
    fresh = jnp.where(active, current[:, None], previous)
    return lax.dynamic_update_slice(store, fresh, begin)


def staged_body(phase, tilt, intensity):
    slices, tile_r, tile_c = phase.shape
    batch_size = tilt.shape[0]
    sections = lax.axis_size("depth")
    section_index = lax.axis_index("depth")
    group_size = 1
    groups = batch_size // group_size
    tick_count = sections + groups - 1
    block_r = 64
    block_c = 128
    fwd_rows = band_matrix(block_r, HALO, FRESNEL, False)
    fwd_cols = band_matrix(block_c, HALO, FRESNEL, False)
    adj_rows = band_matrix(block_r, HALO, FRESNEL, True)
    adj_cols = band_matrix(block_c, HALO, FRESNEL, True)
    row_pos = (
        lax.axis_index("row") * tile_r + lax.broadcasted_iota(jnp.int32, (tile_r, tile_c), 0)
    ).astype(jnp.float32)
    col_pos = (
        lax.axis_index("col") * tile_c + lax.broadcasted_iota(jnp.int32, (tile_r, tile_c), 1)
    ).astype(jnp.float32)
    height = float(tile_r * lax.axis_size("row"))
    width_all = float(tile_c * lax.axis_size("col"))
    tilt_f = tilt.astype(jnp.float32)
    phase_angle = (
        2.0
        * jnp.pi
        * (
            tilt_f[:, 0, None, None] * row_pos / height
            + tilt_f[:, 1, None, None] * col_pos / width_all
        )
    )
    incident = jnp.stack([jnp.cos(phase_angle), jnp.sin(phase_angle)], axis=1)
    screens = jnp.stack([jnp.cos(phase), jnp.sin(phase)], axis=1)

    def forward_tick(tick_now, carry):
        incoming, entering, leaving = carry
        group_index = tick_now - section_index
        active = (group_index >= 0) & (group_index < groups)
        first_item = jnp.clip(group_index, 0, groups - 1) * group_size
        current = jnp.where(
            section_index == 0,
            lax.dynamic_slice_in_dim(incident, first_item, group_size, 0),
            incoming,
        )
        entering = store_item(entering, current, first_item, 0, active)
        current = propagate(transmit(screens[0], current, False), fwd_rows, fwd_cols)
        leaving = store_item(leaving, current, first_item, 0, active)
        incoming = from_behind(current, "depth", 1)
        return (incoming, entering, leaving)

    store_zero = jnp.zeros((batch_size, slices, 2, tile_r, tile_c), jnp.float32)
    start_wave = jnp.zeros((group_size, 2, tile_r, tile_c), jnp.float32)
    _, entering, leaving = lax.fori_loop(
        0, tick_count, forward_tick, (start_wave, store_zero, store_zero)
    )
    final_wave = leaving[:, slices - 1]
    misfit = final_wave[:, 0] * final_wave[:, 0] + final_wave[:, 1] * final_wave[:, 1] - intensity
    seed_adjoint = 2.0 * misfit[:, None] * final_wave

    def backward_tick(tick_now, carry):
        incoming, gradient = carry
        group_index = tick_now - (sections - 1 - section_index)
        active = (group_index >= 0) & (group_index < groups)
        first_item = jnp.clip(group_index, 0, groups - 1) * group_size
        adjoint_wave = jnp.where(
            section_index == sections - 1,
            lax.dynamic_slice_in_dim(seed_adjoint, first_item, group_size, 0),
            incoming,
        )
        for slice_index in reversed(range(slices)):
            pulled = propagate(adjoint_wave, adj_rows, adj_cols)
            arrived = lax.dynamic_slice_in_dim(entering[:, slice_index], first_item, group_size, 0)
            moved = transmit(screens[slice_index], arrived, False)
            contribution = jnp.sum(pulled[:, 1] * moved[:, 0] - pulled[:, 0] * moved[:, 1], axis=0)
            gradient = gradient.at[slice_index].add(jnp.where(active, contribution, 0.0))
            adjoint_wave = transmit(screens[slice_index], pulled, True)
        incoming = from_behind(adjoint_wave, "depth", -1)
        return (incoming, gradient)

    grad_zero = jnp.zeros((slices, tile_r, tile_c), jnp.float32)
    _, gradient = lax.fori_loop(0, tick_count, backward_tick, (start_wave, grad_zero))
    return (gradient, leaving)


def fits_whole(phase_shape, batch, mesh):
    slices, height, width = phase_shape
    rows, cols, sections = mesh.shape["row"], mesh.shape["col"], mesh.shape["depth"]
    bytes_all = 4 * height * width * (slices + batch)
    return (
        bytes_all <= GATHER_BUDGET
        and batch == rows == 2
        and cols & (cols - 1) == 0
        and sections & (sections - 1) == 0
        and height == LANES
        and (height // rows) % 16 == 0
        and (width // cols) % LANES == 0
        and width % (2 * LANES) == 0
    )


def solution(mesh):
    placed = (P("depth", "row", "col"), P(), P(None, "row", "col"))

    def run(phase, tilt, intensity):
        if fits_whole(phase.shape, tilt.shape[0], mesh):
            body = whole_field_body
        else:
            body = staged_body
        return jax.shard_map(
            body,
            mesh=mesh,
            in_specs=placed,
            out_specs=(P("depth", "row", "col"), P(None, "depth", None, "row", "col")),
            check_vma=False,
        )(phase, tilt, intensity)

    return run
```

```python
import math

import jax
import jax.numpy as jnp
import numpy as np
from jax import lax
from jax.experimental import pallas as pl
from jax.experimental.pallas import tpu as pltpu
from jax.sharding import PartitionSpec as P

HALO = 32
FRESNEL = 64
LANES = 128
GATHER_BUDGET = 4 * 2**20
SIN = (
    0.9999999980536763,
    -0.1666666530009577,
    0.008333305907073658,
    -0.00019838908256358006,
    2.745822627876341e-06,
    -2.3043562782810933e-08,
)
COS = (
    0.9999999961345007,
    -0.4999999301617528,
    0.04166646215023687,
    -0.0013886696163545999,
    2.4695045482778703e-05,
    -2.5154931690000354e-07,
)


def horner(coefficients, square):
    total = jnp.full_like(square, coefficients[-1])
    for coefficient in coefficients[-2::-1]:
        total = total * square + coefficient
    return total


def cos_sin(angle):
    square = angle * angle
    return horner(COS, square), horner(SIN, square) * angle


def turn(fraction):
    half_cos, half_sin = cos_sin(fraction * math.pi)
    return half_cos * half_cos - half_sin * half_sin, 2.0 * half_cos * half_sin


def halves(value):
    high = value.astype(jnp.bfloat16)
    return high, (value - high.astype(jnp.float32)).astype(jnp.bfloat16)


def np_halves(matrix):
    high = matrix.astype(jnp.bfloat16)
    return high, (matrix - high.astype(np.float64)).astype(jnp.bfloat16)


def np_taps():
    offset = np.arange(-HALO, HALO + 1, dtype=np.float64)
    taper = np.maximum(np.abs(offset) - 0.5 * HALO, 0.0)
    weight = np.cos(np.pi * taper / (HALO + 2.0)) ** 2 / math.sqrt(FRESNEL)
    return weight * np.exp(1j * np.pi * offset * offset / FRESNEL)


def np_band(out_pos, in_pos):
    offset = out_pos[:, None] - in_pos[None, :]
    inside = np.abs(offset) <= HALO
    return np.where(inside, np_taps()[np.clip(offset, -HALO, HALO) + HALO], 0.0)


def row_constant(height):
    band = np_band(np.arange(height), np.arange(height))
    whole = np.block([[band.real, -band.imag], [band.imag, band.real]])
    high, low = np_halves(whole)
    return np.concatenate([high, low], axis=1)


def col_constant():
    lane = np.arange(LANES)
    edge_pos = np.where(lane < LANES // 2, lane + LANES, lane - LANES)
    parts = []
    for position in (lane, edge_pos):
        band = np_band(lane, position).T
        parts.append(np.block([[band.real, band.imag], [-band.imag, band.real]]))
    high, low = np_halves(np.concatenate(parts, axis=0))
    return np.concatenate([high, low], axis=0)


def advance(slice_index, cos_ref, sin_ref, row_ref, col_ref, v_ref, a_high, a_low):
    _, height, width = v_ref.shape
    blocks = width // LANES
    half = LANES // 2
    matrix = jnp.concatenate([row_ref[:, : 2 * height], row_ref[...]], axis=1)
    for start in range(0, width, 2 * LANES):
        where = (slice(None), pl.ds(start, 2 * LANES))
        cos, sin = cos_ref[(slice_index,) + where], sin_ref[(slice_index,) + where]
        real, imag = v_ref[(0,) + where], v_ref[(1,) + where]
        high, low = halves(jnp.concatenate([cos * real - sin * imag, cos * imag + sin * real], axis=0))
        done = jnp.dot(
            matrix, jnp.concatenate([high, low, high], axis=0), preferred_element_type=jnp.float32
        )
        for part in range(2):
            for sub in range(2):
                block = start // LANES + sub
                value = done[part * height : (part + 1) * height, sub * LANES : (sub + 1) * LANES]
                for target, piece in zip((a_high, a_low), halves(value)):
                    target[block, :, pl.ds(part * LANES, LANES)] = piece
                    if block > 0:
                        target[block - 1, :, pl.ds((2 + part) * LANES, half)] = piece[:, :half]
                    if block < blocks - 1:
                        target[block + 1, :, pl.ds((2 + part) * LANES + half, half)] = piece[:, half:]
    high = a_high[...].reshape(blocks * height, 4 * LANES)
    low = a_low[...].reshape(blocks * height, 4 * LANES)
    done = jnp.dot(
        jnp.concatenate([high, low, high], axis=1),
        jnp.concatenate([col_ref[: 4 * LANES], col_ref[...]], axis=0),
        preferred_element_type=jnp.float32,
    )
    for block in range(blocks):
        for part in range(2):
            v_ref[part, :, pl.ds(block * LANES, LANES)] = done[
                block * height : (block + 1) * height, part * LANES : (part + 1) * LANES
            ]


def clear_ends(a_high, a_low):
    blocks, height, _ = a_high.shape
    half = LANES // 2
    for target in (a_high, a_low):
        for part in range(2):
            target[0, :, pl.ds((2 + part) * LANES + half, half)] = jnp.zeros((height, half), jnp.bfloat16)
            target[blocks - 1, :, pl.ds((2 + part) * LANES, half)] = jnp.zeros((height, half), jnp.bfloat16)


def places(tile_r, tile_c):
    core = lax.axis_index("row")
    near = pl.ds(pl.multiple_of(core * tile_r, tile_r), tile_r)
    far = pl.ds(pl.multiple_of((1 - core) * tile_r, tile_r), tile_r)
    own_col = pl.ds(pl.multiple_of(lax.axis_index("col") * tile_c, tile_c), tile_c)
    return near, far, own_col


def wave_kernel(
    tilt_ref, near_own, far_own, near_rest, far_rest, row_ref, col_ref,
    mine_ref, theirs_ref, cos_ref, sin_ref, v_ref, moved_ref, a_high, a_low,
):
    slices, _, tile_r, tile_c = mine_ref.shape
    _, height, width = v_ref.shape
    cols = width // tile_c
    count = cos_ref.shape[0] - 1
    core, own_section, own_place = lax.axis_index("row"), lax.axis_index("depth"), lax.axis_index("col")
    first = own_section * slices
    near, far, own_col = places(tile_r, tile_c)
    clear_ends(a_high, a_low)

    def screens(col, carry):
        held = col ^ own_place
        own_cells = pl.ds(pl.multiple_of(col * tile_c, tile_c), tile_c)
        for bits in range(count // slices):
            for inner in range(slices):
                slice_index = (bits ^ own_section) * slices + inner
                sources = (near_own, far_own) if bits == 0 else (near_rest, far_rest)
                place = inner if bits == 0 else (bits - 1) * slices + inner
                for source, row in zip(sources, (near, far)):
                    cos, sin = cos_sin(source[held, place])
                    cos_ref[slice_index, row, own_cells] = cos
                    sin_ref[slice_index, row, own_cells] = sin
        return carry

    lax.fori_loop(0, cols, screens, 0)
    cos_ref[count] = jnp.ones((height, width), jnp.float32)
    sin_ref[count] = jnp.zeros((height, width), jnp.float32)

    def cycles(number, position, extent):
        fraction = (number * position).astype(jnp.float32) / extent
        return turn(fraction - jnp.round(fraction))

    row_cos, row_sin = cycles(
        tilt_ref[core, 0], lax.broadcasted_iota(jnp.int32, (height, LANES), 0), float(height)
    )
    for start in range(0, width, LANES):
        col_cos, col_sin = cycles(
            tilt_ref[core, 1], lax.broadcasted_iota(jnp.int32, (8, LANES), 1) + start, float(width)
        )
        col_cos, col_sin = col_cos[:1], col_sin[:1]
        v_ref[0, :, pl.ds(start, LANES)] = row_cos * col_cos - row_sin * col_sin
        v_ref[1, :, pl.ds(start, LANES)] = row_sin * col_cos + row_cos * col_sin

    def step(tick, carry):
        own = (tick >= first) & (tick < first + slices)
        behind = 2 * count - tick

        @pl.when(own)
        def _():
            cos, sin = cos_ref[tick, :, own_col], sin_ref[tick, :, own_col]
            real, imag = v_ref[0, :, own_col], v_ref[1, :, own_col]
            moved_ref[tick - first, 0] = cos * real - sin * imag
            moved_ref[tick - first, 1] = cos * imag + sin * real

        @pl.when(tick == count)
        def _():
            for row, measured in ((near, near_own), (far, far_own)):
                for col in range(cols):
                    where = (row, pl.ds(col * tile_c, tile_c))
                    place = slices + core if measured is near_own else slices
                    real, imag = v_ref[(0,) + where], v_ref[(1,) + where]
                    misfit = 2.0 * (real * real + imag * imag - measured[col ^ own_place, place])
                    v_ref[(0,) + where] = misfit * real
                    v_ref[(1,) + where] = -misfit * imag

        passed = jnp.where(tick < count, tick, jnp.minimum(behind, count))
        advance(passed, cos_ref, sin_ref, row_ref, col_ref, v_ref, a_high, a_low)

        @pl.when(own)
        def _():
            for target, row in ((mine_ref, near), (theirs_ref, far)):
                for part in range(2):
                    target[tick - first, part] = v_ref[part, row, own_col]

        @pl.when((tick >= count) & (behind - 1 < first + slices))
        def _():
            for target, row in ((mine_ref, near), (theirs_ref, far)):
                real, imag = v_ref[0, row, own_col], v_ref[1, row, own_col]
                moved = moved_ref[behind - 1 - first, 0, row], moved_ref[behind - 1 - first, 1, row]
                target[behind - 1 - first, 2] = -(imag * moved[0] + real * moved[1])

        return carry

    lax.fori_loop(0, 2 * count - first, step, 0)


def finish_kernel(mine_ref, received_ref, grad_ref, exit_ref, total_ref, sems):
    core = lax.axis_index("row")
    copies = []
    for source, item in ((mine_ref, core), (received_ref, 1 - core)):
        copies.append(pltpu.make_async_copy(source.at[:, pl.ds(0, 2)], exit_ref.at[item], sems.at[len(copies)]))
    for copy in copies:
        copy.start()
    total_ref[...] = mine_ref[:, 2] + received_ref[:, 2]
    copies.append(pltpu.make_async_copy(total_ref, grad_ref, sems.at[2]))
    copies[2].start()
    for copy in copies:
        copy.wait()


def spread(shard, axis):
    size = lax.axis_size(axis)
    return [lax.ppermute(shard, axis, [(i, i ^ bits) for i in range(size)]) for bits in range(1, size)]


def swap_cores(value):
    return lax.ppermute(value, "row", [(0, 1), (1, 0)])


def whole_field_body(phase, tilt, intensity):
    slices, tile_r, tile_c = phase.shape
    sections, cols = lax.axis_size("depth"), lax.axis_size("col")
    core = lax.axis_index("row")
    height = tile_r * lax.axis_size("row")
    width = tile_c * cols
    count = sections * slices
    blocks = width // LANES
    vmem = pl.BlockSpec(memory_space=pltpu.VMEM)
    smem = pl.BlockSpec(memory_space=pltpu.SMEM)
    result = jax.ShapeDtypeStruct((slices, 3, tile_r, tile_c), jnp.float32)

    other_depths = jnp.concatenate(spread(phase, "depth"), axis=0)
    packet = jnp.concatenate([phase, intensity], axis=0)
    near_own = jnp.stack([packet] + spread(packet, "col"))
    arriving = spread(other_depths, "col")
    arriving[0], near_own = lax.optimization_barrier((arriving[0], near_own))
    near_rest = jnp.stack([other_depths] + arriving)
    wanted = lax.dynamic_slice_in_dim(near_own, slices + 1 - core, 1, 1)
    far_own = swap_cores(jnp.concatenate([near_own[:, :slices], wanted], axis=1))
    far_rest = swap_cores(near_rest)

    halves_scratch = [pltpu.VMEM((blocks, height, 4 * LANES), jnp.bfloat16)] * 2
    screen_scratch = [pltpu.VMEM((count + 1, height, width), jnp.float32)] * 2
    mine, theirs = pl.pallas_call(
        wave_kernel,
        out_shape=(result, result),
        in_specs=[smem] + [vmem] * 6,
        out_specs=(vmem, vmem),
        scratch_shapes=screen_scratch
        + [pltpu.VMEM((2, height, width), jnp.float32), pltpu.VMEM((slices, 2, height, tile_c), jnp.float32)]
        + halves_scratch,
        compiler_params=pltpu.CompilerParams(vmem_limit_bytes=24 * 2**20),
    )(
        tilt, near_own, far_own, near_rest, far_rest,
        jnp.asarray(row_constant(height)), jnp.asarray(col_constant()),
    )
    hbm = pl.BlockSpec(memory_space=pl.ANY)
    return pl.pallas_call(
        finish_kernel,
        out_shape=(
            jax.ShapeDtypeStruct(phase.shape, jnp.float32),
            jax.ShapeDtypeStruct((2, slices, 2, tile_r, tile_c), jnp.float32),
        ),
        in_specs=[vmem, vmem],
        out_specs=(hbm, hbm),
        scratch_shapes=[pltpu.VMEM(phase.shape, jnp.float32), pltpu.SemaphoreType.DMA((3,))],
        compiler_params=pltpu.CompilerParams(vmem_limit_bytes=4 * 2**20),
    )(mine, swap_cores(theirs))


def extended_2(cells, sides, width):
    for axis, dim in sides:
        count = lax.axis_size(axis)
        ends = count - 1
        head = lax.slice_in_dim(cells, 0, width, axis=dim)
        tail = lax.slice_in_dim(cells, cells.shape[dim] - width, cells.shape[dim], axis=dim)
        cells = jnp.concatenate(
            [
                lax.ppermute(tail, axis, [(i, (i + 1) % count) for i in range(ends)]),
                cells,
                lax.ppermute(head, axis, [((i + 1) % count, i) for i in range(ends)]),
            ],
            axis=dim,
        )
    return cells


def from_behind(value, axis, steps):
    count = lax.axis_size(axis)
    leading, last = (max(0, -steps), min(count, count - steps))
    return lax.ppermute(value, axis, [(source, source + steps) for source in range(leading, last)])


def band_matrix(block_size, margin, fresnel, adjoint):
    shape_full = (block_size, block_size + 2 * margin)
    out_idx = lax.broadcasted_iota(jnp.int32, shape_full, 0)
    in_idx = lax.broadcasted_iota(jnp.int32, shape_full, 1)
    offset = (out_idx + margin - in_idx).astype(jnp.float32)
    inside = jnp.abs(offset) <= margin
    taper_dist = jnp.maximum(jnp.abs(offset) - 0.5 * margin, 0.0)
    profile = jnp.cos(jnp.pi * taper_dist / (margin + 2.0))
    weight = profile * profile / math.sqrt(fresnel)
    phase_angle = jnp.pi * offset * offset / fresnel
    real_part = jnp.where(inside, jnp.cos(phase_angle) * weight, 0.0)
    imag_part = jnp.where(inside, jnp.sin(phase_angle) * weight, 0.0)
    if adjoint:
        imag_part = -imag_part
    upper = jnp.stack([real_part, -imag_part])
    lower = jnp.stack([imag_part, real_part])
    return jnp.stack([upper, lower])


def along_rows(extended, matrix):
    pieces = [jnp.einsum("pqij,gqjc->gpic", matrix, extended, precision=lax.Precision.HIGHEST)]
    return jnp.concatenate(pieces, axis=2)


def along_cols(extended, matrix, margin):
    block_size = matrix.shape[2]
    extent = extended.shape[3] - 2 * margin
    pieces = []
    for block_start in range(0, extent, block_size):
        window = extended[:, :, :, block_start : block_start + block_size + 2 * margin]
        pieces.append(
            jnp.einsum("pqij,gqrj->gpri", matrix, window, precision=lax.Precision.HIGHEST)
        )
    return jnp.concatenate(pieces, axis=3)


def propagate(current, row_matrix, col_matrix):
    with_rows = extended_2(current, (("row", 2),), HALO)
    row_done = along_rows(with_rows, row_matrix)
    with_cols = extended_2(row_done, (("col", 3),), HALO)
    return along_cols(with_cols, col_matrix, HALO)


def transmit(screen, current, adjoint):
    screen_re = screen[0][None]
    screen_im = screen[1][None]
    if adjoint:
        screen_im = -screen_im
    real_part = screen_re * current[:, 0] - screen_im * current[:, 1]
    imag_part = screen_re * current[:, 1] + screen_im * current[:, 0]
    return jnp.stack([real_part, imag_part], axis=1)


def store_item(store, current, first_item, slice_index, active):
    begin = (first_item, jnp.int32(slice_index), jnp.int32(0), jnp.int32(0), jnp.int32(0))
    sizes_now = (current.shape[0], 1) + current.shape[1:]
    previous = lax.dynamic_slice(store, begin, sizes_now)
    fresh = jnp.where(active, current[:, None], previous)
    return lax.dynamic_update_slice(store, fresh, begin)


def staged_body(phase, tilt, intensity):
    slices, tile_r, tile_c = phase.shape
    batch_size = tilt.shape[0]
    sections = lax.axis_size("depth")
    section_index = lax.axis_index("depth")
    group_size = 1
    groups = batch_size // group_size
    tick_count = sections + groups - 1
    block_r = 64
    block_c = 128
    fwd_rows = band_matrix(block_r, HALO, FRESNEL, False)
    fwd_cols = band_matrix(block_c, HALO, FRESNEL, False)
    adj_rows = band_matrix(block_r, HALO, FRESNEL, True)
    adj_cols = band_matrix(block_c, HALO, FRESNEL, True)
    row_pos = (
        lax.axis_index("row") * tile_r + lax.broadcasted_iota(jnp.int32, (tile_r, tile_c), 0)
    ).astype(jnp.float32)
    col_pos = (
        lax.axis_index("col") * tile_c + lax.broadcasted_iota(jnp.int32, (tile_r, tile_c), 1)
    ).astype(jnp.float32)
    height = float(tile_r * lax.axis_size("row"))
    width_all = float(tile_c * lax.axis_size("col"))
    tilt_f = tilt.astype(jnp.float32)
    phase_angle = (
        2.0
        * jnp.pi
        * (
            tilt_f[:, 0, None, None] * row_pos / height
            + tilt_f[:, 1, None, None] * col_pos / width_all
        )
    )
    incident = jnp.stack([jnp.cos(phase_angle), jnp.sin(phase_angle)], axis=1)
    screens = jnp.stack([jnp.cos(phase), jnp.sin(phase)], axis=1)

    def forward_tick(tick_now, carry):
        incoming, entering, leaving = carry
        group_index = tick_now - section_index
        active = (group_index >= 0) & (group_index < groups)
        first_item = jnp.clip(group_index, 0, groups - 1) * group_size
        current = jnp.where(
            section_index == 0,
            lax.dynamic_slice_in_dim(incident, first_item, group_size, 0),
            incoming,
        )
        entering = store_item(entering, current, first_item, 0, active)
        current = propagate(transmit(screens[0], current, False), fwd_rows, fwd_cols)
        leaving = store_item(leaving, current, first_item, 0, active)
        incoming = from_behind(current, "depth", 1)
        return (incoming, entering, leaving)

    store_zero = jnp.zeros((batch_size, slices, 2, tile_r, tile_c), jnp.float32)
    start_wave = jnp.zeros((group_size, 2, tile_r, tile_c), jnp.float32)
    _, entering, leaving = lax.fori_loop(
        0, tick_count, forward_tick, (start_wave, store_zero, store_zero)
    )
    final_wave = leaving[:, slices - 1]
    misfit = final_wave[:, 0] * final_wave[:, 0] + final_wave[:, 1] * final_wave[:, 1] - intensity
    seed_adjoint = 2.0 * misfit[:, None] * final_wave

    def backward_tick(tick_now, carry):
        incoming, gradient = carry
        group_index = tick_now - (sections - 1 - section_index)
        active = (group_index >= 0) & (group_index < groups)
        first_item = jnp.clip(group_index, 0, groups - 1) * group_size
        adjoint_wave = jnp.where(
            section_index == sections - 1,
            lax.dynamic_slice_in_dim(seed_adjoint, first_item, group_size, 0),
            incoming,
        )
        for slice_index in reversed(range(slices)):
            pulled = propagate(adjoint_wave, adj_rows, adj_cols)
            arrived = lax.dynamic_slice_in_dim(entering[:, slice_index], first_item, group_size, 0)
            moved = transmit(screens[slice_index], arrived, False)
            contribution = jnp.sum(pulled[:, 1] * moved[:, 0] - pulled[:, 0] * moved[:, 1], axis=0)
            gradient = gradient.at[slice_index].add(jnp.where(active, contribution, 0.0))
            adjoint_wave = transmit(screens[slice_index], pulled, True)
        incoming = from_behind(adjoint_wave, "depth", -1)
        return (incoming, gradient)

    grad_zero = jnp.zeros((slices, tile_r, tile_c), jnp.float32)
    _, gradient = lax.fori_loop(0, tick_count, backward_tick, (start_wave, grad_zero))
    return (gradient, leaving)


def fits_whole(phase_shape, batch, mesh):
    slices, height, width = phase_shape
    rows, cols, sections = mesh.shape["row"], mesh.shape["col"], mesh.shape["depth"]
    bytes_all = 4 * height * width * (slices + batch)
    return (
        bytes_all <= GATHER_BUDGET
        and batch == rows == 2
        and cols & (cols - 1) == 0
        and sections & (sections - 1) == 0
        and height == LANES
        and (height // rows) % 16 == 0
        and (width // cols) % LANES == 0
        and width % (2 * LANES) == 0
    )


def solution(mesh):
    placed = (P("depth", "row", "col"), P(), P(None, "row", "col"))

    def run(phase, tilt, intensity):
        if fits_whole(phase.shape, tilt.shape[0], mesh):
            body = whole_field_body
        else:
            body = staged_body
        return jax.shard_map(
            body,
            mesh=mesh,
            in_specs=placed,
            out_specs=(P("depth", "row", "col"), P(None, "depth", None, "row", "col")),
            check_vma=False,
        )(phase, tilt, intensity)

    return run
```

```python
import math

import jax
import jax.numpy as jnp
import numpy as np
from jax import lax
from jax.experimental import pallas as pl
from jax.experimental.pallas import tpu as pltpu
from jax.sharding import PartitionSpec as P

HALO = 32
FRESNEL = 64
LANES = 128
GATHER_BUDGET = 4 * 2**20
SIN = (
    0.9999999980536763,
    -0.1666666530009577,
    0.008333305907073658,
    -0.00019838908256358006,
    2.745822627876341e-06,
    -2.3043562782810933e-08,
)
COS = (
    0.9999999961345007,
    -0.4999999301617528,
    0.04166646215023687,
    -0.0013886696163545999,
    2.4695045482778703e-05,
    -2.5154931690000354e-07,
)


def horner(coefficients, square):
    total = jnp.full_like(square, coefficients[-1])
    for coefficient in coefficients[-2::-1]:
        total = total * square + coefficient
    return total


def cos_sin(angle):
    square = angle * angle
    return horner(COS, square), horner(SIN, square) * angle


def turn(fraction):
    half_cos, half_sin = cos_sin(fraction * math.pi)
    return half_cos * half_cos - half_sin * half_sin, 2.0 * half_cos * half_sin


def halves(value):
    high = value.astype(jnp.bfloat16)
    return high, (value - high.astype(jnp.float32)).astype(jnp.bfloat16)


def np_halves(matrix):
    high = matrix.astype(jnp.bfloat16)
    return high, (matrix - high.astype(np.float64)).astype(jnp.bfloat16)


def np_taps():
    offset = np.arange(-HALO, HALO + 1, dtype=np.float64)
    taper = np.maximum(np.abs(offset) - 0.5 * HALO, 0.0)
    weight = np.cos(np.pi * taper / (HALO + 2.0)) ** 2 / math.sqrt(FRESNEL)
    return weight * np.exp(1j * np.pi * offset * offset / FRESNEL)


def np_band(out_pos, in_pos):
    offset = out_pos[:, None] - in_pos[None, :]
    inside = np.abs(offset) <= HALO
    return np.where(inside, np_taps()[np.clip(offset, -HALO, HALO) + HALO], 0.0)


def row_constant(height):
    matrices = []
    for core in range(2):
        pos = (np.arange(height) + core * (height // 2)) % height
        band = np_band(pos, pos)
        whole = np.block([[band.real, -band.imag], [band.imag, band.real]])
        matrices.append(np.concatenate(np_halves(whole), axis=1))
    return np.stack(matrices)


def col_constant():
    lane = np.arange(LANES)
    edge_pos = np.where(lane < LANES // 2, lane + LANES, lane - LANES)
    parts = []
    for position in (lane, edge_pos):
        band = np_band(lane, position).T
        parts.append(np.block([[band.real, band.imag], [-band.imag, band.real]]))
    high, low = np_halves(np.concatenate(parts, axis=0))
    return np.concatenate([high, low], axis=0)


def both_rows(near_ref, far_ref, where):
    return jnp.concatenate([near_ref[where], far_ref[where]], axis=0)


def block_turned(slice_index, block, screens, v_ref):
    near_cos, near_sin, far_cos, far_sin = screens
    cos = both_rows(near_cos, far_cos, (slice_index, block))
    sin = both_rows(near_sin, far_sin, (slice_index, block))
    real, imag = v_ref[block, 0], v_ref[block, 1]
    return cos * real - sin * imag, cos * imag + sin * real


def row_product(row_matrix, columns):
    high, low = halves(columns)
    whole = row_matrix.shape[0]
    return jnp.dot(
        jnp.concatenate([row_matrix[:, :whole], row_matrix], axis=1),
        jnp.concatenate([high, low, high], axis=0),
        preferred_element_type=jnp.float32,
    )


def col_product(high, low, col_high, col_low):
    return jnp.dot(
        jnp.concatenate([high, low, high], axis=1),
        jnp.concatenate([col_high, col_high, col_low], axis=0),
        preferred_element_type=jnp.float32,
    )


def advance(slice_index, start, size, screens, row_matrix, col_ref, v_ref, a_high, a_low):
    height = v_ref.shape[2]
    half = LANES // 2
    own, edge = pl.ds(0, 2 * LANES), pl.ds(2 * LANES, 2 * LANES)
    low_own, low_edge = pl.ds(4 * LANES, 2 * LANES), pl.ds(6 * LANES, 2 * LANES)
    chunks = [range(place, min(place + 2, size)) for place in range(0, size, 2)]
    for chunk in chunks:
        columns = jnp.concatenate(
            [jnp.concatenate(block_turned(slice_index, start + place, screens, v_ref), axis=0) for place in chunk],
            axis=1,
        )
        done = row_product(row_matrix, columns)
        for sub, place in enumerate(chunk):
            for part in range(2):
                value = done[part * height : (part + 1) * height, sub * LANES : (sub + 1) * LANES]
                for target, piece in zip((a_high, a_low), halves(value)):
                    target[place, :, pl.ds(part * LANES, LANES)] = piece
                    if place > 0:
                        target[place - 1, :, pl.ds((2 + part) * LANES, half)] = piece[:, :half]
                    if place < size - 1:
                        target[place + 1, :, pl.ds((2 + part) * LANES + half, half)] = piece[:, half:]
    parts = []
    for chunk in chunks:
        cells = pl.ds(chunk[0], len(chunk))
        rows = len(chunk) * height
        parts.append(
            col_product(
                a_high[cells, :, own].reshape(rows, 2 * LANES),
                a_low[cells, :, own].reshape(rows, 2 * LANES),
                col_ref[own],
                col_ref[low_own],
            )
        )
    cells, rows = pl.ds(0, size), size * height
    edges = col_product(
        a_high[cells, :, edge].reshape(rows, 2 * LANES),
        a_low[cells, :, edge].reshape(rows, 2 * LANES),
        col_ref[edge],
        col_ref[low_edge],
    )
    for chunk, done in zip(chunks, parts):
        for sub, place in enumerate(chunk):
            total = done[sub * height : (sub + 1) * height] + edges[place * height : (place + 1) * height]
            for part in range(2):
                v_ref[start + place, part] = total[:, part * LANES : (part + 1) * LANES]


def clear_edge(a_ref, place, right):
    half = LANES // 2
    for part in range(2):
        begin = (2 + part) * LANES + (0 if right else half)
        a_ref[place, :, pl.ds(begin, half)] = jnp.zeros((a_ref.shape[1], half), a_ref.dtype)


def prepare_kernel(tilt_ref, near_phase, wave_ref, cos_ref, sin_ref):
    blocks, _, height, _ = wave_ref.shape
    count = cos_ref.shape[0] - 1
    core, own_section, own_place = lax.axis_index("row"), lax.axis_index("depth"), lax.axis_index("col")

    def screens(col, carry):
        held = col ^ own_place
        for bits in range(count):
            cos_ref[bits ^ own_section, col], sin_ref[bits ^ own_section, col] = cos_sin(near_phase[held, bits])
        return carry

    lax.fori_loop(0, blocks, screens, 0)
    cos_ref[count] = jnp.ones(cos_ref.shape[1:], jnp.float32)
    sin_ref[count] = jnp.zeros(cos_ref.shape[1:], jnp.float32)

    def cycles(number, position, extent):
        fraction = (number * position).astype(jnp.float32) / extent
        return turn(fraction - jnp.round(fraction))

    row = lax.broadcasted_iota(jnp.int32, (height, LANES), 0) + core * (height // 2)
    row = jnp.where(row >= height, row - height, row)
    row_cos, row_sin = cycles(tilt_ref[core, 0], row, float(height))
    for block in range(blocks):
        col_cos, col_sin = cycles(
            tilt_ref[core, 1],
            lax.broadcasted_iota(jnp.int32, (8, LANES), 1) + block * LANES,
            float(blocks * LANES),
        )
        col_cos, col_sin = col_cos[:1], col_sin[:1]
        wave_ref[block, 0] = row_cos * col_cos - row_sin * col_sin
        wave_ref[block, 1] = row_sin * col_cos + row_cos * col_sin


def wave_kernel(
    wave_ref, near_cos, near_sin, near_measured, far_measured, far_phase, row_ref, col_ref,
    mine_ref, theirs_ref, far_cos, far_sin, v_ref, moved_ref, a_high, a_low,
):
    blocks, _, height, _ = v_ref.shape
    count = near_cos.shape[0] - 1
    core, own_section, own_place = lax.axis_index("row"), lax.axis_index("depth"), lax.axis_index("col")
    near, far = pl.ds(0, height // 2), pl.ds(height // 2, height // 2)
    screens = (near_cos, near_sin, far_cos, far_sin)
    row_matrix = row_ref.at[core]
    window = min(3, blocks)
    window_start = jnp.clip(own_place - 1, 0, blocks - window)

    def far_screens(slice_index):
        for col in range(blocks):
            angle = far_phase[col ^ own_place, slice_index ^ own_section]
            far_cos[slice_index, col], far_sin[slice_index, col] = cos_sin(angle)

    for target in (a_high, a_low):
        clear_edge(target, 0, False)
        clear_edge(target, blocks - 1, True)
    far_cos[count] = jnp.ones(far_cos.shape[1:], jnp.float32)
    far_sin[count] = jnp.zeros(far_cos.shape[1:], jnp.float32)
    v_ref[...] = wave_ref[...]
    far_screens(0)

    def forward(tick, carry):
        @pl.when(tick == own_section)
        def _():
            moved_ref[0], moved_ref[1] = block_turned(tick, own_place, screens, v_ref)

        advance(tick, 0, blocks, screens, row_matrix[...], col_ref, v_ref, a_high, a_low)
        far_screens(jnp.minimum(tick + 1, count - 1))

        @pl.when(tick == own_section)
        def _():
            for target, row in ((mine_ref, near), (theirs_ref, far)):
                for part in range(2):
                    target[0, part] = v_ref[own_place, part, row]

        return carry

    lax.fori_loop(0, count, forward, 0)

    for target in (a_high, a_low):
        clear_edge(target, window - 1, True)
    for place in range(window):
        block = window_start + place
        held = block ^ own_place
        for row, measured in ((near, near_measured[held, core]), (far, far_measured[held, 0])):
            real, imag = v_ref[block, 0, row], v_ref[block, 1, row]
            misfit = 2.0 * (real * real + imag * imag - measured)
            v_ref[block, 0, row] = misfit * real
            v_ref[block, 1, row] = -misfit * imag

    def backward(tick, carry):
        advance(count - tick, window_start, window, screens, row_matrix[...], col_ref, v_ref, a_high, a_low)
        return carry

    lax.fori_loop(0, count - 1 - own_section, backward, 0)

    left, right = jnp.maximum(own_place - 1, 0), jnp.minimum(own_place + 1, blocks - 1)
    lane = lax.broadcasted_iota(jnp.int32, (2 * height, LANES), 1)
    has_left, has_right = own_place > 0, own_place < blocks - 1
    behind = own_section + 1
    own_cells = jnp.concatenate(block_turned(behind, own_place, screens, v_ref), axis=0)
    left_cells = jnp.concatenate(block_turned(behind, left, screens, v_ref), axis=0)
    right_cells = jnp.concatenate(block_turned(behind, right, screens, v_ref), axis=0)
    edge_cells = jnp.where(
        lane < LANES // 2, jnp.where(has_right, right_cells, 0.0), jnp.where(has_left, left_cells, 0.0)
    )
    done = row_product(row_matrix[...], jnp.concatenate([own_cells, edge_cells], axis=1))
    quarters = [
        done[part * height : (part + 1) * height, sub * LANES : (sub + 1) * LANES]
        for sub in range(2)
        for part in range(2)
    ]
    high, low = halves(jnp.concatenate(quarters, axis=1))
    pulled = col_product(high, low, col_ref[: 4 * LANES], col_ref[4 * LANES :])
    gradient = -(pulled[:, LANES:] * moved_ref[0] + pulled[:, :LANES] * moved_ref[1])
    mine_ref[0, 2] = gradient[: height // 2]
    theirs_ref[0, 2] = gradient[height // 2 :]


def copy_kernel(from_ref, to_ref):
    to_ref[...] = from_ref[...]


def finish_kernel(mine_ref, received_ref, grad_ref, exit_ref, total_ref, sems):
    core = lax.axis_index("row")
    copies = []
    for source, item in ((mine_ref, core), (received_ref, 1 - core)):
        copies.append(pltpu.make_async_copy(source.at[:, pl.ds(0, 2)], exit_ref.at[item], sems.at[len(copies)]))
    for copy in copies:
        copy.start()
    total_ref[...] = mine_ref[:, 2] + received_ref[:, 2]
    copies.append(pltpu.make_async_copy(total_ref, grad_ref, sems.at[2]))
    copies[2].start()
    for copy in copies:
        copy.wait()


def spread(shard, axis):
    size = lax.axis_size(axis)
    return [lax.ppermute(shard, axis, [(i, i ^ bits) for i in range(size)]) for bits in range(1, size)]


def swap_cores(value):
    return lax.ppermute(value, "row", [(0, 1), (1, 0)])


def whole_field_body(phase, tilt, intensity):
    _, tile_r, tile_c = phase.shape
    count, blocks = lax.axis_size("depth"), lax.axis_size("col")
    core = lax.axis_index("row")
    height = 2 * tile_r
    vmem = pl.BlockSpec(memory_space=pltpu.VMEM)
    smem = pl.BlockSpec(memory_space=pltpu.SMEM)
    hbm = pl.BlockSpec(memory_space=pl.ANY)

    def array(*shape):
        return jax.ShapeDtypeStruct(shape, jnp.float32)

    def params(mebibytes):
        return pltpu.CompilerParams(vmem_limit_bytes=mebibytes * 2**20)

    own_phase = pl.pallas_call(
        copy_kernel,
        out_shape=array(*phase.shape),
        in_specs=[vmem],
        out_specs=vmem,
        compiler_params=params(1),
    )(phase)
    column = jnp.concatenate([own_phase] + spread(phase, "depth"), axis=0)
    near_measured = jnp.stack([intensity] + spread(intensity, "col"))
    far_measured = swap_cores(lax.dynamic_slice_in_dim(near_measured, 1 - core, 1, 1))
    arriving = spread(column, "col")
    arriving[0], far_measured = lax.optimization_barrier((arriving[0], far_measured))
    near_phase = jnp.stack([column] + arriving)
    far_phase = swap_cores(near_phase)

    half_screens = (count + 1, blocks, tile_r, tile_c)
    field = (blocks, 2, height, tile_c)
    wave, near_cos, near_sin = pl.pallas_call(
        prepare_kernel,
        out_shape=(array(*field), array(*half_screens), array(*half_screens)),
        in_specs=[smem, vmem],
        out_specs=(vmem,) * 3,
        compiler_params=params(8),
        cost_estimate=pl.CostEstimate(flops=5 * 10**8, bytes_accessed=2**20, transcendentals=0),
    )(tilt, near_phase)
    mine, theirs = pl.pallas_call(
        wave_kernel,
        out_shape=(array(1, 3, tile_r, tile_c),) * 2,
        in_specs=[vmem] * 8,
        out_specs=(vmem,) * 2,
        scratch_shapes=[pltpu.VMEM(half_screens, jnp.float32)] * 2
        + [pltpu.VMEM(field, jnp.float32), pltpu.VMEM((2, height, tile_c), jnp.float32)]
        + [pltpu.VMEM((blocks, height, 4 * LANES), jnp.bfloat16)] * 2,
        compiler_params=params(24),
    )(
        wave, near_cos, near_sin, near_measured, far_measured, far_phase,
        jnp.asarray(row_constant(height)), jnp.asarray(col_constant()),
    )
    return pl.pallas_call(
        finish_kernel,
        out_shape=(array(*phase.shape), array(2, 1, 2, tile_r, tile_c)),
        in_specs=[vmem, vmem],
        out_specs=(hbm, hbm),
        scratch_shapes=[pltpu.VMEM(phase.shape, jnp.float32), pltpu.SemaphoreType.DMA((3,))],
        compiler_params=params(4),
    )(mine, swap_cores(theirs))


def extended_2(cells, sides, width):
    for axis, dim in sides:
        count = lax.axis_size(axis)
        ends = count - 1
        head = lax.slice_in_dim(cells, 0, width, axis=dim)
        tail = lax.slice_in_dim(cells, cells.shape[dim] - width, cells.shape[dim], axis=dim)
        cells = jnp.concatenate(
            [
                lax.ppermute(tail, axis, [(i, (i + 1) % count) for i in range(ends)]),
                cells,
                lax.ppermute(head, axis, [((i + 1) % count, i) for i in range(ends)]),
            ],
            axis=dim,
        )
    return cells


def from_behind(value, axis, steps):
    count = lax.axis_size(axis)
    leading, last = (max(0, -steps), min(count, count - steps))
    return lax.ppermute(value, axis, [(source, source + steps) for source in range(leading, last)])


def band_matrix(block_size, margin, fresnel, adjoint):
    shape_full = (block_size, block_size + 2 * margin)
    out_idx = lax.broadcasted_iota(jnp.int32, shape_full, 0)
    in_idx = lax.broadcasted_iota(jnp.int32, shape_full, 1)
    offset = (out_idx + margin - in_idx).astype(jnp.float32)
    inside = jnp.abs(offset) <= margin
    taper_dist = jnp.maximum(jnp.abs(offset) - 0.5 * margin, 0.0)
    profile = jnp.cos(jnp.pi * taper_dist / (margin + 2.0))
    weight = profile * profile / math.sqrt(fresnel)
    phase_angle = jnp.pi * offset * offset / fresnel
    real_part = jnp.where(inside, jnp.cos(phase_angle) * weight, 0.0)
    imag_part = jnp.where(inside, jnp.sin(phase_angle) * weight, 0.0)
    if adjoint:
        imag_part = -imag_part
    upper = jnp.stack([real_part, -imag_part])
    lower = jnp.stack([imag_part, real_part])
    return jnp.stack([upper, lower])


def along_rows(extended, matrix):
    pieces = [jnp.einsum("pqij,gqjc->gpic", matrix, extended, precision=lax.Precision.HIGHEST)]
    return jnp.concatenate(pieces, axis=2)


def along_cols(extended, matrix, margin):
    block_size = matrix.shape[2]
    extent = extended.shape[3] - 2 * margin
    pieces = []
    for block_start in range(0, extent, block_size):
        window = extended[:, :, :, block_start : block_start + block_size + 2 * margin]
        pieces.append(
            jnp.einsum("pqij,gqrj->gpri", matrix, window, precision=lax.Precision.HIGHEST)
        )
    return jnp.concatenate(pieces, axis=3)


def propagate(current, row_matrix, col_matrix):
    with_rows = extended_2(current, (("row", 2),), HALO)
    row_done = along_rows(with_rows, row_matrix)
    with_cols = extended_2(row_done, (("col", 3),), HALO)
    return along_cols(with_cols, col_matrix, HALO)


def transmit(screen, current, adjoint):
    screen_re = screen[0][None]
    screen_im = screen[1][None]
    if adjoint:
        screen_im = -screen_im
    real_part = screen_re * current[:, 0] - screen_im * current[:, 1]
    imag_part = screen_re * current[:, 1] + screen_im * current[:, 0]
    return jnp.stack([real_part, imag_part], axis=1)


def store_item(store, current, first_item, slice_index, active):
    begin = (first_item, jnp.int32(slice_index), jnp.int32(0), jnp.int32(0), jnp.int32(0))
    sizes_now = (current.shape[0], 1) + current.shape[1:]
    previous = lax.dynamic_slice(store, begin, sizes_now)
    fresh = jnp.where(active, current[:, None], previous)
    return lax.dynamic_update_slice(store, fresh, begin)


def staged_body(phase, tilt, intensity):
    slices, tile_r, tile_c = phase.shape
    batch_size = tilt.shape[0]
    sections = lax.axis_size("depth")
    section_index = lax.axis_index("depth")
    group_size = 1
    groups = batch_size // group_size
    tick_count = sections + groups - 1
    block_r = 64
    block_c = 128
    fwd_rows = band_matrix(block_r, HALO, FRESNEL, False)
    fwd_cols = band_matrix(block_c, HALO, FRESNEL, False)
    adj_rows = band_matrix(block_r, HALO, FRESNEL, True)
    adj_cols = band_matrix(block_c, HALO, FRESNEL, True)
    row_pos = (
        lax.axis_index("row") * tile_r + lax.broadcasted_iota(jnp.int32, (tile_r, tile_c), 0)
    ).astype(jnp.float32)
    col_pos = (
        lax.axis_index("col") * tile_c + lax.broadcasted_iota(jnp.int32, (tile_r, tile_c), 1)
    ).astype(jnp.float32)
    height = float(tile_r * lax.axis_size("row"))
    width_all = float(tile_c * lax.axis_size("col"))
    tilt_f = tilt.astype(jnp.float32)
    phase_angle = (
        2.0
        * jnp.pi
        * (
            tilt_f[:, 0, None, None] * row_pos / height
            + tilt_f[:, 1, None, None] * col_pos / width_all
        )
    )
    incident = jnp.stack([jnp.cos(phase_angle), jnp.sin(phase_angle)], axis=1)
    screens = jnp.stack([jnp.cos(phase), jnp.sin(phase)], axis=1)

    def forward_tick(tick_now, carry):
        incoming, entering, leaving = carry
        group_index = tick_now - section_index
        active = (group_index >= 0) & (group_index < groups)
        first_item = jnp.clip(group_index, 0, groups - 1) * group_size
        current = jnp.where(
            section_index == 0,
            lax.dynamic_slice_in_dim(incident, first_item, group_size, 0),
            incoming,
        )
        entering = store_item(entering, current, first_item, 0, active)
        current = propagate(transmit(screens[0], current, False), fwd_rows, fwd_cols)
        leaving = store_item(leaving, current, first_item, 0, active)
        incoming = from_behind(current, "depth", 1)
        return (incoming, entering, leaving)

    store_zero = jnp.zeros((batch_size, slices, 2, tile_r, tile_c), jnp.float32)
    start_wave = jnp.zeros((group_size, 2, tile_r, tile_c), jnp.float32)
    _, entering, leaving = lax.fori_loop(
        0, tick_count, forward_tick, (start_wave, store_zero, store_zero)
    )
    final_wave = leaving[:, slices - 1]
    misfit = final_wave[:, 0] * final_wave[:, 0] + final_wave[:, 1] * final_wave[:, 1] - intensity
    seed_adjoint = 2.0 * misfit[:, None] * final_wave

    def backward_tick(tick_now, carry):
        incoming, gradient = carry
        group_index = tick_now - (sections - 1 - section_index)
        active = (group_index >= 0) & (group_index < groups)
        first_item = jnp.clip(group_index, 0, groups - 1) * group_size
        adjoint_wave = jnp.where(
            section_index == sections - 1,
            lax.dynamic_slice_in_dim(seed_adjoint, first_item, group_size, 0),
            incoming,
        )
        for slice_index in reversed(range(slices)):
            pulled = propagate(adjoint_wave, adj_rows, adj_cols)
            arrived = lax.dynamic_slice_in_dim(entering[:, slice_index], first_item, group_size, 0)
            moved = transmit(screens[slice_index], arrived, False)
            contribution = jnp.sum(pulled[:, 1] * moved[:, 0] - pulled[:, 0] * moved[:, 1], axis=0)
            gradient = gradient.at[slice_index].add(jnp.where(active, contribution, 0.0))
            adjoint_wave = transmit(screens[slice_index], pulled, True)
        incoming = from_behind(adjoint_wave, "depth", -1)
        return (incoming, gradient)

    grad_zero = jnp.zeros((slices, tile_r, tile_c), jnp.float32)
    _, gradient = lax.fori_loop(0, tick_count, backward_tick, (start_wave, grad_zero))
    return (gradient, leaving)


def fits_whole(phase_shape, batch, mesh):
    slices, height, width = phase_shape
    rows, cols, sections = mesh.shape["row"], mesh.shape["col"], mesh.shape["depth"]
    return (
        4 * height * width * (slices + batch) <= GATHER_BUDGET
        and batch == rows == 2
        and slices == sections
        and sections & (sections - 1) == 0
        and cols & (cols - 1) == 0
        and height == LANES
        and width == cols * LANES
        and cols > 1
        and sections > 1
        and sections * HALO <= LANES
    )


def solution(mesh):
    placed = (P("depth", "row", "col"), P(), P(None, "row", "col"))

    def run(phase, tilt, intensity):
        if fits_whole(phase.shape, tilt.shape[0], mesh):
            body = whole_field_body
        else:
            body = staged_body
        return jax.shard_map(
            body,
            mesh=mesh,
            in_specs=placed,
            out_specs=(P("depth", "row", "col"), P(None, "depth", None, "row", "col")),
            check_vma=False,
        )(phase, tilt, intensity)

    return run
```

```python
import math

import jax
import jax.numpy as jnp
import numpy as np
from jax import lax
from jax.experimental import pallas as pl
from jax.experimental.pallas import tpu as pltpu
from jax.sharding import PartitionSpec as P

HALO = 32
FRESNEL = 64
LANES = 128
GATHER_BUDGET = 4 * 2**20
SIN = (
    0.9999999980536763,
    -0.1666666530009577,
    0.008333305907073658,
    -0.00019838908256358006,
    2.745822627876341e-06,
    -2.3043562782810933e-08,
)
COS = (
    0.9999999961345007,
    -0.4999999301617528,
    0.04166646215023687,
    -0.0013886696163545999,
    2.4695045482778703e-05,
    -2.5154931690000354e-07,
)


def horner(coefficients, square):
    total = jnp.full_like(square, coefficients[-1])
    for coefficient in coefficients[-2::-1]:
        total = total * square + coefficient
    return total


def cos_sin(angle):
    square = angle * angle
    return horner(COS, square), horner(SIN, square) * angle


def turn(fraction):
    half_cos, half_sin = cos_sin(fraction * math.pi)
    return half_cos * half_cos - half_sin * half_sin, 2.0 * half_cos * half_sin


def halves(value):
    high = value.astype(jnp.bfloat16)
    return high, (value - high.astype(jnp.float32)).astype(jnp.bfloat16)


def np_halves(matrix):
    high = matrix.astype(jnp.bfloat16)
    return high, (matrix - high.astype(np.float64)).astype(jnp.bfloat16)


def np_taps():
    offset = np.arange(-HALO, HALO + 1, dtype=np.float64)
    taper = np.maximum(np.abs(offset) - 0.5 * HALO, 0.0)
    weight = np.cos(np.pi * taper / (HALO + 2.0)) ** 2 / math.sqrt(FRESNEL)
    return weight * np.exp(1j * np.pi * offset * offset / FRESNEL)


def np_band(out_pos, in_pos):
    offset = out_pos[:, None] - in_pos[None, :]
    inside = np.abs(offset) <= HALO
    return np.where(inside, np_taps()[np.clip(offset, -HALO, HALO) + HALO], 0.0)


def row_constant(height):
    matrices = []
    for core in range(2):
        pos = (np.arange(height) + core * (height // 2)) % height
        band = np_band(pos, pos)
        whole = np.block([[band.real, -band.imag], [band.imag, band.real]])
        matrices.append(np.concatenate(np_halves(whole), axis=1))
    return np.stack(matrices)


def col_constant():
    lane = np.arange(LANES)
    edge_pos = np.where(lane < LANES // 2, lane + LANES, lane - LANES)
    parts = []
    for position in (lane, edge_pos):
        band = np_band(lane, position).T
        parts.append(np.block([[band.real, band.imag], [-band.imag, band.real]]))
    high, low = np_halves(np.concatenate(parts, axis=0))
    return np.concatenate([high, low], axis=0)


def both_rows(near_ref, far_ref, where):
    return jnp.concatenate([near_ref[where], far_ref[where]], axis=0)


def block_turned(slice_index, block, screens, v_ref):
    near_cos, near_sin, far_cos, far_sin = screens
    cos = both_rows(near_cos, far_cos, (slice_index, block))
    sin = both_rows(near_sin, far_sin, (slice_index, block))
    real, imag = v_ref[block, 0], v_ref[block, 1]
    return cos * real - sin * imag, cos * imag + sin * real


def row_product(row_matrix, columns):
    high, low = halves(columns)
    whole = row_matrix.shape[0]
    return jnp.dot(
        jnp.concatenate([row_matrix[:, :whole], row_matrix], axis=1),
        jnp.concatenate([high, low, high], axis=0),
        preferred_element_type=jnp.float32,
    )


def col_product(high, low, col_high, col_low):
    return jnp.dot(
        jnp.concatenate([high, low, high], axis=1),
        jnp.concatenate([col_high, col_high, col_low], axis=0),
        preferred_element_type=jnp.float32,
    )


def advance(slice_index, start, size, screens, row_matrix, col_ref, v_ref, a_high, a_low):
    height = v_ref.shape[2]
    half = LANES // 2
    own, edge = pl.ds(0, 2 * LANES), pl.ds(2 * LANES, 2 * LANES)
    low_own, low_edge = pl.ds(4 * LANES, 2 * LANES), pl.ds(6 * LANES, 2 * LANES)
    chunks = [range(place, min(place + 2, size)) for place in range(0, size, 2)]
    for chunk in chunks:
        columns = jnp.concatenate(
            [jnp.concatenate(block_turned(slice_index, start + place, screens, v_ref), axis=0) for place in chunk],
            axis=1,
        )
        done = row_product(row_matrix, columns)
        for sub, place in enumerate(chunk):
            for part in range(2):
                value = done[part * height : (part + 1) * height, sub * LANES : (sub + 1) * LANES]
                for target, piece in zip((a_high, a_low), halves(value)):
                    target[place, :, pl.ds(part * LANES, LANES)] = piece
                    if place > 0:
                        target[place - 1, :, pl.ds((2 + part) * LANES, half)] = piece[:, :half]
                    if place < size - 1:
                        target[place + 1, :, pl.ds((2 + part) * LANES + half, half)] = piece[:, half:]
    parts = []
    for chunk in chunks:
        cells = pl.ds(chunk[0], len(chunk))
        rows = len(chunk) * height
        parts.append(
            col_product(
                a_high[cells, :, own].reshape(rows, 2 * LANES),
                a_low[cells, :, own].reshape(rows, 2 * LANES),
                col_ref[own],
                col_ref[low_own],
            )
        )
    cells, rows = pl.ds(0, size), size * height
    edges = col_product(
        a_high[cells, :, edge].reshape(rows, 2 * LANES),
        a_low[cells, :, edge].reshape(rows, 2 * LANES),
        col_ref[edge],
        col_ref[low_edge],
    )
    for chunk, done in zip(chunks, parts):
        for sub, place in enumerate(chunk):
            total = done[sub * height : (sub + 1) * height] + edges[place * height : (place + 1) * height]
            for part in range(2):
                v_ref[start + place, part] = total[:, part * LANES : (part + 1) * LANES]


def clear_edge(a_ref, place, right):
    half = LANES // 2
    for part in range(2):
        begin = (2 + part) * LANES + (0 if right else half)
        a_ref[place, :, pl.ds(begin, half)] = jnp.zeros((a_ref.shape[1], half), a_ref.dtype)


def prepare_kernel(tilt_ref, near_phase, all_measured, wave_ref, cos_ref, sin_ref, measured_ref):
    blocks, _, height, _ = wave_ref.shape
    count = cos_ref.shape[0] - 1
    core, own_section, own_place = lax.axis_index("row"), lax.axis_index("depth"), lax.axis_index("col")

    def screens(col, carry):
        held = col ^ own_place
        for bits in range(count):
            cos_ref[bits ^ own_section, col], sin_ref[bits ^ own_section, col] = cos_sin(near_phase[held, bits])
        measured_ref[col] = all_measured[held].reshape(height, LANES)
        return carry

    lax.fori_loop(0, blocks, screens, 0)
    cos_ref[count] = jnp.ones(cos_ref.shape[1:], jnp.float32)
    sin_ref[count] = jnp.zeros(cos_ref.shape[1:], jnp.float32)

    def cycles(number, position, extent):
        fraction = (number * position).astype(jnp.float32) / extent
        return turn(fraction - jnp.round(fraction))

    row = lax.broadcasted_iota(jnp.int32, (height, LANES), 0) + core * (height // 2)
    row = jnp.where(row >= height, row - height, row)
    row_cos, row_sin = cycles(tilt_ref[core, 0], row, float(height))
    for block in range(blocks):
        col_cos, col_sin = cycles(
            tilt_ref[core, 1],
            lax.broadcasted_iota(jnp.int32, (8, LANES), 1) + block * LANES,
            float(blocks * LANES),
        )
        col_cos, col_sin = col_cos[:1], col_sin[:1]
        wave_ref[block, 0] = row_cos * col_cos - row_sin * col_sin
        wave_ref[block, 1] = row_sin * col_cos + row_cos * col_sin


def wave_kernel(
    wave_ref, near_cos, near_sin, measured_ref, far_phase, row_ref, col_ref,
    mine_ref, theirs_ref, far_cos, far_sin, v_ref, moved_ref, a_high, a_low,
):
    blocks, _, height, _ = v_ref.shape
    count = near_cos.shape[0] - 1
    core, own_section, own_place = lax.axis_index("row"), lax.axis_index("depth"), lax.axis_index("col")
    near, far = pl.ds(0, height // 2), pl.ds(height // 2, height // 2)
    screens = (near_cos, near_sin, far_cos, far_sin)
    row_matrix = row_ref.at[core]
    window = min(3, blocks)
    window_start = jnp.clip(own_place - 1, 0, blocks - window)

    def far_screens(slice_index):
        for col in range(blocks):
            angle = far_phase[col ^ own_place, slice_index ^ own_section]
            far_cos[slice_index, col], far_sin[slice_index, col] = cos_sin(angle)

    for target in (a_high, a_low):
        clear_edge(target, 0, False)
        clear_edge(target, blocks - 1, True)
    far_cos[count] = jnp.ones(far_cos.shape[1:], jnp.float32)
    far_sin[count] = jnp.zeros(far_cos.shape[1:], jnp.float32)
    v_ref[...] = wave_ref[...]
    far_screens(0)

    def forward(tick, carry):
        @pl.when(tick == own_section)
        def _():
            moved_ref[0], moved_ref[1] = block_turned(tick, own_place, screens, v_ref)

        advance(tick, 0, blocks, screens, row_matrix[...], col_ref, v_ref, a_high, a_low)
        far_screens(jnp.minimum(tick + 1, count - 1))

        @pl.when(tick == own_section)
        def _():
            for target, row in ((mine_ref, near), (theirs_ref, far)):
                for part in range(2):
                    target[0, part] = v_ref[own_place, part, row]

        return carry

    lax.fori_loop(0, count, forward, 0)

    for target in (a_high, a_low):
        clear_edge(target, window - 1, True)
    for place in range(window):
        block = window_start + place
        real, imag = v_ref[block, 0], v_ref[block, 1]
        misfit = 2.0 * (real * real + imag * imag - measured_ref[block])
        v_ref[block, 0] = misfit * real
        v_ref[block, 1] = -misfit * imag

    def backward(tick, carry):
        advance(count - tick, window_start, window, screens, row_matrix[...], col_ref, v_ref, a_high, a_low)
        return carry

    lax.fori_loop(0, count - 1 - own_section, backward, 0)

    left, right = jnp.maximum(own_place - 1, 0), jnp.minimum(own_place + 1, blocks - 1)
    lane = lax.broadcasted_iota(jnp.int32, (2 * height, LANES), 1)
    has_left, has_right = own_place > 0, own_place < blocks - 1
    behind = own_section + 1
    own_cells = jnp.concatenate(block_turned(behind, own_place, screens, v_ref), axis=0)
    left_cells = jnp.concatenate(block_turned(behind, left, screens, v_ref), axis=0)
    right_cells = jnp.concatenate(block_turned(behind, right, screens, v_ref), axis=0)
    edge_cells = jnp.where(
        lane < LANES // 2, jnp.where(has_right, right_cells, 0.0), jnp.where(has_left, left_cells, 0.0)
    )
    done = row_product(row_matrix[...], jnp.concatenate([own_cells, edge_cells], axis=1))
    quarters = [
        done[part * height : (part + 1) * height, sub * LANES : (sub + 1) * LANES]
        for sub in range(2)
        for part in range(2)
    ]
    high, low = halves(jnp.concatenate(quarters, axis=1))
    pulled = col_product(high, low, col_ref[: 4 * LANES], col_ref[4 * LANES :])
    gradient = -(pulled[:, LANES:] * moved_ref[0] + pulled[:, :LANES] * moved_ref[1])
    mine_ref[0, 2] = gradient[: height // 2]
    theirs_ref[0, 2] = gradient[height // 2 :]


def copy_kernel(from_ref, to_ref):
    to_ref[...] = from_ref[...]


def finish_kernel(mine_ref, received_ref, grad_ref, exit_ref, total_ref, sems):
    core = lax.axis_index("row")
    copies = []
    for source, item in ((mine_ref, core), (received_ref, 1 - core)):
        copies.append(pltpu.make_async_copy(source.at[:, pl.ds(0, 2)], exit_ref.at[item], sems.at[len(copies)]))
    for copy in copies:
        copy.start()
    total_ref[...] = mine_ref[:, 2] + received_ref[:, 2]
    copies.append(pltpu.make_async_copy(total_ref, grad_ref, sems.at[2]))
    copies[2].start()
    for copy in copies:
        copy.wait()


def spread(shard, axis):
    size = lax.axis_size(axis)
    return [lax.ppermute(shard, axis, [(i, i ^ bits) for i in range(size)]) for bits in range(1, size)]


def swap_cores(value):
    return lax.ppermute(value, "row", [(0, 1), (1, 0)])


def whole_field_body(phase, tilt, intensity):
    _, tile_r, tile_c = phase.shape
    count, blocks = lax.axis_size("depth"), lax.axis_size("col")
    core = lax.axis_index("row")
    height = 2 * tile_r
    vmem = pl.BlockSpec(memory_space=pltpu.VMEM)
    smem = pl.BlockSpec(memory_space=pltpu.SMEM)
    hbm = pl.BlockSpec(memory_space=pl.ANY)

    def array(*shape):
        return jax.ShapeDtypeStruct(shape, jnp.float32)

    def params(mebibytes):
        return pltpu.CompilerParams(vmem_limit_bytes=mebibytes * 2**20)

    own_phase = pl.pallas_call(
        copy_kernel,
        out_shape=array(*phase.shape),
        in_specs=[vmem],
        out_specs=vmem,
        compiler_params=params(1),
    )(phase)
    column = jnp.concatenate([own_phase] + spread(phase, "depth"), axis=0)
    own_tilt = [lax.dynamic_index_in_dim(both, core, 0, False) for both in (intensity, swap_cores(intensity))]
    tile_measured = jnp.stack(own_tilt)
    near_phase = jnp.stack([column] + spread(column, "col"))
    all_measured = jnp.stack([tile_measured] + spread(tile_measured, "col"))
    far_phase = swap_cores(near_phase)

    half_screens = (count + 1, blocks, tile_r, tile_c)
    field = (blocks, 2, height, tile_c)
    wave, near_cos, near_sin, measured = pl.pallas_call(
        prepare_kernel,
        out_shape=(array(*field), array(*half_screens), array(*half_screens), array(blocks, height, tile_c)),
        in_specs=[smem, vmem, vmem],
        out_specs=(vmem,) * 4,
        compiler_params=params(8),
        cost_estimate=pl.CostEstimate(flops=4 * 10**9, bytes_accessed=2**20, transcendentals=0),
    )(tilt, near_phase, all_measured)
    mine, theirs = pl.pallas_call(
        wave_kernel,
        out_shape=(array(1, 3, tile_r, tile_c),) * 2,
        in_specs=[vmem] * 7,
        out_specs=(vmem,) * 2,
        scratch_shapes=[pltpu.VMEM(half_screens, jnp.float32)] * 2
        + [pltpu.VMEM(field, jnp.float32), pltpu.VMEM((2, height, tile_c), jnp.float32)]
        + [pltpu.VMEM((blocks, height, 4 * LANES), jnp.bfloat16)] * 2,
        compiler_params=params(24),
    )(
        wave, near_cos, near_sin, measured, far_phase,
        jnp.asarray(row_constant(height)), jnp.asarray(col_constant()),
    )
    return pl.pallas_call(
        finish_kernel,
        out_shape=(array(*phase.shape), array(2, 1, 2, tile_r, tile_c)),
        in_specs=[vmem, vmem],
        out_specs=(hbm, hbm),
        scratch_shapes=[pltpu.VMEM(phase.shape, jnp.float32), pltpu.SemaphoreType.DMA((3,))],
        compiler_params=params(4),
    )(mine, swap_cores(theirs))


def extended_2(cells, sides, width):
    for axis, dim in sides:
        count = lax.axis_size(axis)
        ends = count - 1
        head = lax.slice_in_dim(cells, 0, width, axis=dim)
        tail = lax.slice_in_dim(cells, cells.shape[dim] - width, cells.shape[dim], axis=dim)
        cells = jnp.concatenate(
            [
                lax.ppermute(tail, axis, [(i, (i + 1) % count) for i in range(ends)]),
                cells,
                lax.ppermute(head, axis, [((i + 1) % count, i) for i in range(ends)]),
            ],
            axis=dim,
        )
    return cells


def from_behind(value, axis, steps):
    count = lax.axis_size(axis)
    leading, last = (max(0, -steps), min(count, count - steps))
    return lax.ppermute(value, axis, [(source, source + steps) for source in range(leading, last)])


def band_matrix(block_size, margin, fresnel, adjoint):
    shape_full = (block_size, block_size + 2 * margin)
    out_idx = lax.broadcasted_iota(jnp.int32, shape_full, 0)
    in_idx = lax.broadcasted_iota(jnp.int32, shape_full, 1)
    offset = (out_idx + margin - in_idx).astype(jnp.float32)
    inside = jnp.abs(offset) <= margin
    taper_dist = jnp.maximum(jnp.abs(offset) - 0.5 * margin, 0.0)
    profile = jnp.cos(jnp.pi * taper_dist / (margin + 2.0))
    weight = profile * profile / math.sqrt(fresnel)
    phase_angle = jnp.pi * offset * offset / fresnel
    real_part = jnp.where(inside, jnp.cos(phase_angle) * weight, 0.0)
    imag_part = jnp.where(inside, jnp.sin(phase_angle) * weight, 0.0)
    if adjoint:
        imag_part = -imag_part
    upper = jnp.stack([real_part, -imag_part])
    lower = jnp.stack([imag_part, real_part])
    return jnp.stack([upper, lower])


def along_rows(extended, matrix):
    pieces = [jnp.einsum("pqij,gqjc->gpic", matrix, extended, precision=lax.Precision.HIGHEST)]
    return jnp.concatenate(pieces, axis=2)


def along_cols(extended, matrix, margin):
    block_size = matrix.shape[2]
    extent = extended.shape[3] - 2 * margin
    pieces = []
    for block_start in range(0, extent, block_size):
        window = extended[:, :, :, block_start : block_start + block_size + 2 * margin]
        pieces.append(
            jnp.einsum("pqij,gqrj->gpri", matrix, window, precision=lax.Precision.HIGHEST)
        )
    return jnp.concatenate(pieces, axis=3)


def propagate(current, row_matrix, col_matrix):
    with_rows = extended_2(current, (("row", 2),), HALO)
    row_done = along_rows(with_rows, row_matrix)
    with_cols = extended_2(row_done, (("col", 3),), HALO)
    return along_cols(with_cols, col_matrix, HALO)


def transmit(screen, current, adjoint):
    screen_re = screen[0][None]
    screen_im = screen[1][None]
    if adjoint:
        screen_im = -screen_im
    real_part = screen_re * current[:, 0] - screen_im * current[:, 1]
    imag_part = screen_re * current[:, 1] + screen_im * current[:, 0]
    return jnp.stack([real_part, imag_part], axis=1)


def store_item(store, current, first_item, slice_index, active):
    begin = (first_item, jnp.int32(slice_index), jnp.int32(0), jnp.int32(0), jnp.int32(0))
    sizes_now = (current.shape[0], 1) + current.shape[1:]
    previous = lax.dynamic_slice(store, begin, sizes_now)
    fresh = jnp.where(active, current[:, None], previous)
    return lax.dynamic_update_slice(store, fresh, begin)


def staged_body(phase, tilt, intensity):
    slices, tile_r, tile_c = phase.shape
    batch_size = tilt.shape[0]
    sections = lax.axis_size("depth")
    section_index = lax.axis_index("depth")
    group_size = 1
    groups = batch_size // group_size
    tick_count = sections + groups - 1
    block_r = 64
    block_c = 128
    fwd_rows = band_matrix(block_r, HALO, FRESNEL, False)
    fwd_cols = band_matrix(block_c, HALO, FRESNEL, False)
    adj_rows = band_matrix(block_r, HALO, FRESNEL, True)
    adj_cols = band_matrix(block_c, HALO, FRESNEL, True)
    row_pos = (
        lax.axis_index("row") * tile_r + lax.broadcasted_iota(jnp.int32, (tile_r, tile_c), 0)
    ).astype(jnp.float32)
    col_pos = (
        lax.axis_index("col") * tile_c + lax.broadcasted_iota(jnp.int32, (tile_r, tile_c), 1)
    ).astype(jnp.float32)
    height = float(tile_r * lax.axis_size("row"))
    width_all = float(tile_c * lax.axis_size("col"))
    tilt_f = tilt.astype(jnp.float32)
    phase_angle = (
        2.0
        * jnp.pi
        * (
            tilt_f[:, 0, None, None] * row_pos / height
            + tilt_f[:, 1, None, None] * col_pos / width_all
        )
    )
    incident = jnp.stack([jnp.cos(phase_angle), jnp.sin(phase_angle)], axis=1)
    screens = jnp.stack([jnp.cos(phase), jnp.sin(phase)], axis=1)

    def forward_tick(tick_now, carry):
        incoming, entering, leaving = carry
        group_index = tick_now - section_index
        active = (group_index >= 0) & (group_index < groups)
        first_item = jnp.clip(group_index, 0, groups - 1) * group_size
        current = jnp.where(
            section_index == 0,
            lax.dynamic_slice_in_dim(incident, first_item, group_size, 0),
            incoming,
        )
        entering = store_item(entering, current, first_item, 0, active)
        current = propagate(transmit(screens[0], current, False), fwd_rows, fwd_cols)
        leaving = store_item(leaving, current, first_item, 0, active)
        incoming = from_behind(current, "depth", 1)
        return (incoming, entering, leaving)

    store_zero = jnp.zeros((batch_size, slices, 2, tile_r, tile_c), jnp.float32)
    start_wave = jnp.zeros((group_size, 2, tile_r, tile_c), jnp.float32)
    _, entering, leaving = lax.fori_loop(
        0, tick_count, forward_tick, (start_wave, store_zero, store_zero)
    )
    final_wave = leaving[:, slices - 1]
    misfit = final_wave[:, 0] * final_wave[:, 0] + final_wave[:, 1] * final_wave[:, 1] - intensity
    seed_adjoint = 2.0 * misfit[:, None] * final_wave

    def backward_tick(tick_now, carry):
        incoming, gradient = carry
        group_index = tick_now - (sections - 1 - section_index)
        active = (group_index >= 0) & (group_index < groups)
        first_item = jnp.clip(group_index, 0, groups - 1) * group_size
        adjoint_wave = jnp.where(
            section_index == sections - 1,
            lax.dynamic_slice_in_dim(seed_adjoint, first_item, group_size, 0),
            incoming,
        )
        for slice_index in reversed(range(slices)):
            pulled = propagate(adjoint_wave, adj_rows, adj_cols)
            arrived = lax.dynamic_slice_in_dim(entering[:, slice_index], first_item, group_size, 0)
            moved = transmit(screens[slice_index], arrived, False)
            contribution = jnp.sum(pulled[:, 1] * moved[:, 0] - pulled[:, 0] * moved[:, 1], axis=0)
            gradient = gradient.at[slice_index].add(jnp.where(active, contribution, 0.0))
            adjoint_wave = transmit(screens[slice_index], pulled, True)
        incoming = from_behind(adjoint_wave, "depth", -1)
        return (incoming, gradient)

    grad_zero = jnp.zeros((slices, tile_r, tile_c), jnp.float32)
    _, gradient = lax.fori_loop(0, tick_count, backward_tick, (start_wave, grad_zero))
    return (gradient, leaving)


def fits_whole(phase_shape, batch, mesh):
    slices, height, width = phase_shape
    rows, cols, sections = mesh.shape["row"], mesh.shape["col"], mesh.shape["depth"]
    return (
        4 * height * width * (slices + batch) <= GATHER_BUDGET
        and batch == rows == 2
        and slices == sections
        and sections & (sections - 1) == 0
        and cols & (cols - 1) == 0
        and height == LANES
        and width == cols * LANES
        and cols > 1
        and sections > 1
        and sections * HALO <= LANES
    )


def solution(mesh):
    placed = (P("depth", "row", "col"), P(), P(None, "row", "col"))

    def run(phase, tilt, intensity):
        if fits_whole(phase.shape, tilt.shape[0], mesh):
            body = whole_field_body
        else:
            body = staged_body
        return jax.shard_map(
            body,
            mesh=mesh,
            in_specs=placed,
            out_specs=(P("depth", "row", "col"), P(None, "depth", None, "row", "col")),
            check_vma=False,
        )(phase, tilt, intensity)

    return run
```

```python
import math

import jax
import jax.numpy as jnp
import numpy as np
from jax import lax
from jax.experimental import pallas as pl
from jax.experimental.pallas import tpu as pltpu
from jax.sharding import PartitionSpec as P

HALO = 32
FRESNEL = 64
LANES = 128
GATHER_BUDGET = 4 * 2**20
SIN = (
    0.9999999980536763,
    -0.1666666530009577,
    0.008333305907073658,
    -0.00019838908256358006,
    2.745822627876341e-06,
    -2.3043562782810933e-08,
)
COS = (
    0.9999999961345007,
    -0.4999999301617528,
    0.04166646215023687,
    -0.0013886696163545999,
    2.4695045482778703e-05,
    -2.5154931690000354e-07,
)


def horner(coefficients, square):
    total = jnp.full_like(square, coefficients[-1])
    for coefficient in coefficients[-2::-1]:
        total = total * square + coefficient
    return total


def cos_sin(angle):
    square = angle * angle
    return horner(COS, square), horner(SIN, square) * angle


def turn(fraction):
    half_cos, half_sin = cos_sin(fraction * math.pi)
    return half_cos * half_cos - half_sin * half_sin, 2.0 * half_cos * half_sin


def halves(value):
    high = value.astype(jnp.bfloat16)
    return high, (value - high.astype(jnp.float32)).astype(jnp.bfloat16)


def np_halves(matrix):
    high = matrix.astype(jnp.bfloat16)
    return high, (matrix - high.astype(np.float64)).astype(jnp.bfloat16)


def np_taps():
    offset = np.arange(-HALO, HALO + 1, dtype=np.float64)
    taper = np.maximum(np.abs(offset) - 0.5 * HALO, 0.0)
    weight = np.cos(np.pi * taper / (HALO + 2.0)) ** 2 / math.sqrt(FRESNEL)
    return weight * np.exp(1j * np.pi * offset * offset / FRESNEL)


def np_band(out_pos, in_pos):
    offset = out_pos[:, None] - in_pos[None, :]
    inside = np.abs(offset) <= HALO
    return np.where(inside, np_taps()[np.clip(offset, -HALO, HALO) + HALO], 0.0)


def row_constant(height):
    matrices = []
    for core in range(2):
        pos = (np.arange(height) + core * (height // 2)) % height
        band = np_band(pos, pos)
        whole = np.block([[band.real, -band.imag], [band.imag, band.real]])
        matrices.append(np.concatenate(np_halves(whole), axis=1))
    return np.stack(matrices)


def col_constant():
    lane = np.arange(LANES)
    edge_pos = np.where(lane < LANES // 2, lane + LANES, lane - LANES)
    parts = []
    for position in (lane, edge_pos):
        band = np_band(lane, position).T
        parts.append(np.block([[band.real, band.imag], [-band.imag, band.real]]))
    high, low = np_halves(np.concatenate(parts, axis=0))
    return np.concatenate([high, low], axis=0)


def both_rows(near_ref, far_ref, where):
    return jnp.concatenate([near_ref[where], far_ref[where]], axis=0)


def block_turned(slice_index, block, screens, v_ref):
    near_cos, near_sin, far_cos, far_sin = screens
    cos = both_rows(near_cos, far_cos, (slice_index, block))
    sin = both_rows(near_sin, far_sin, (slice_index, block))
    real, imag = v_ref[block, 0], v_ref[block, 1]
    return cos * real - sin * imag, cos * imag + sin * real


def row_product(row_matrix, columns):
    high, low = halves(columns)
    whole = row_matrix.shape[0]
    return jnp.dot(
        jnp.concatenate([row_matrix[:, :whole], row_matrix], axis=1),
        jnp.concatenate([high, low, high], axis=0),
        preferred_element_type=jnp.float32,
    )


def col_product(high, low, col_high, col_low):
    return jnp.dot(
        jnp.concatenate([high, low, high], axis=1),
        jnp.concatenate([col_high, col_high, col_low], axis=0),
        preferred_element_type=jnp.float32,
    )


def advance(slice_index, start, size, screens, row_matrix, col_ref, v_ref, a_high, a_low):
    height = v_ref.shape[2]
    half = LANES // 2
    own, edge = pl.ds(0, 2 * LANES), pl.ds(2 * LANES, 2 * LANES)
    low_own, low_edge = pl.ds(4 * LANES, 2 * LANES), pl.ds(6 * LANES, 2 * LANES)
    chunks = [range(place, min(place + 2, size)) for place in range(0, size, 2)]
    for chunk in chunks:
        columns = jnp.concatenate(
            [jnp.concatenate(block_turned(slice_index, start + place, screens, v_ref), axis=0) for place in chunk],
            axis=1,
        )
        done = row_product(row_matrix, columns)
        for sub, place in enumerate(chunk):
            for part in range(2):
                value = done[part * height : (part + 1) * height, sub * LANES : (sub + 1) * LANES]
                for target, piece in zip((a_high, a_low), halves(value)):
                    target[place, :, pl.ds(part * LANES, LANES)] = piece
                    if place > 0:
                        target[place - 1, :, pl.ds((2 + part) * LANES, half)] = piece[:, :half]
                    if place < size - 1:
                        target[place + 1, :, pl.ds((2 + part) * LANES + half, half)] = piece[:, half:]
    parts = []
    for chunk in chunks:
        cells = pl.ds(chunk[0], len(chunk))
        rows = len(chunk) * height
        parts.append(
            col_product(
                a_high[cells, :, own].reshape(rows, 2 * LANES),
                a_low[cells, :, own].reshape(rows, 2 * LANES),
                col_ref[own],
                col_ref[low_own],
            )
        )
    cells, rows = pl.ds(0, size), size * height
    edges = col_product(
        a_high[cells, :, edge].reshape(rows, 2 * LANES),
        a_low[cells, :, edge].reshape(rows, 2 * LANES),
        col_ref[edge],
        col_ref[low_edge],
    )
    for chunk, done in zip(chunks, parts):
        for sub, place in enumerate(chunk):
            total = done[sub * height : (sub + 1) * height] + edges[place * height : (place + 1) * height]
            for part in range(2):
                v_ref[start + place, part] = total[:, part * LANES : (part + 1) * LANES]


def clear_edge(a_ref, place, right):
    half = LANES // 2
    for part in range(2):
        begin = (2 + part) * LANES + (0 if right else half)
        a_ref[place, :, pl.ds(begin, half)] = jnp.zeros((a_ref.shape[1], half), a_ref.dtype)


def prepare_kernel(tilt_ref, near_own, near_rest, wave_ref, cos_ref, sin_ref):
    blocks, _, height, _ = wave_ref.shape
    count = cos_ref.shape[0] - 1
    core, own_section, own_place = lax.axis_index("row"), lax.axis_index("depth"), lax.axis_index("col")

    def screens(col, carry):
        held = col ^ own_place
        for bits in range(count):
            angle = near_own[held, 0] if bits == 0 else near_rest[held, bits - 1]
            cos_ref[bits ^ own_section, col], sin_ref[bits ^ own_section, col] = cos_sin(angle)
        return carry

    lax.fori_loop(0, blocks, screens, 0)
    cos_ref[count] = jnp.ones(cos_ref.shape[1:], jnp.float32)
    sin_ref[count] = jnp.zeros(cos_ref.shape[1:], jnp.float32)

    def cycles(number, position, extent):
        fraction = (number * position).astype(jnp.float32) / extent
        return turn(fraction - jnp.round(fraction))

    row = lax.broadcasted_iota(jnp.int32, (height, LANES), 0) + core * (height // 2)
    row = jnp.where(row >= height, row - height, row)
    row_cos, row_sin = cycles(tilt_ref[core, 0], row, float(height))
    for block in range(blocks):
        col_cos, col_sin = cycles(
            tilt_ref[core, 1],
            lax.broadcasted_iota(jnp.int32, (8, LANES), 1) + block * LANES,
            float(blocks * LANES),
        )
        col_cos, col_sin = col_cos[:1], col_sin[:1]
        wave_ref[block, 0] = row_cos * col_cos - row_sin * col_sin
        wave_ref[block, 1] = row_sin * col_cos + row_cos * col_sin


def wave_kernel(
    wave_ref, near_cos, near_sin, near_own, far_own, far_rest, row_ref, col_ref,
    mine_ref, theirs_ref, far_cos, far_sin, v_ref, moved_ref, a_high, a_low,
):
    blocks, _, height, _ = v_ref.shape
    count = near_cos.shape[0] - 1
    core, own_section, own_place = lax.axis_index("row"), lax.axis_index("depth"), lax.axis_index("col")
    near, far = pl.ds(0, height // 2), pl.ds(height // 2, height // 2)
    screens = (near_cos, near_sin, far_cos, far_sin)
    row_matrix = row_ref.at[core]
    window = min(3, blocks)
    window_start = jnp.clip(own_place - 1, 0, blocks - window)

    def far_screens(slice_index):
        bits = slice_index ^ own_section
        for col in range(blocks):
            held = col ^ own_place
            angle = jnp.where(bits == 0, far_own[held, 0], far_rest[held, jnp.maximum(bits - 1, 0)])
            far_cos[slice_index, col], far_sin[slice_index, col] = cos_sin(angle)

    for target in (a_high, a_low):
        clear_edge(target, 0, False)
        clear_edge(target, blocks - 1, True)
    far_cos[count] = jnp.ones(far_cos.shape[1:], jnp.float32)
    far_sin[count] = jnp.zeros(far_cos.shape[1:], jnp.float32)
    v_ref[...] = wave_ref[...]
    far_screens(0)

    def forward(tick, carry):
        @pl.when(tick == own_section)
        def _():
            moved_ref[0], moved_ref[1] = block_turned(tick, own_place, screens, v_ref)

        advance(tick, 0, blocks, screens, row_matrix[...], col_ref, v_ref, a_high, a_low)
        far_screens(jnp.minimum(tick + 1, count - 1))

        @pl.when(tick == own_section)
        def _():
            for target, row in ((mine_ref, near), (theirs_ref, far)):
                for part in range(2):
                    target[0, part] = v_ref[own_place, part, row]

        return carry

    lax.fori_loop(0, count, forward, 0)

    for target in (a_high, a_low):
        clear_edge(target, window - 1, True)
    for place in range(window):
        block = window_start + place
        held = block ^ own_place
        for row, measured in ((near, near_own[held, 1 + core]), (far, far_own[held, 1])):
            real, imag = v_ref[block, 0, row], v_ref[block, 1, row]
            misfit = 2.0 * (real * real + imag * imag - measured)
            v_ref[block, 0, row] = misfit * real
            v_ref[block, 1, row] = -misfit * imag

    def backward(tick, carry):
        advance(count - tick, window_start, window, screens, row_matrix[...], col_ref, v_ref, a_high, a_low)
        return carry

    lax.fori_loop(0, count - 1 - own_section, backward, 0)

    left, right = jnp.maximum(own_place - 1, 0), jnp.minimum(own_place + 1, blocks - 1)
    lane = lax.broadcasted_iota(jnp.int32, (2 * height, LANES), 1)
    has_left, has_right = own_place > 0, own_place < blocks - 1
    behind = own_section + 1
    own_cells = jnp.concatenate(block_turned(behind, own_place, screens, v_ref), axis=0)
    left_cells = jnp.concatenate(block_turned(behind, left, screens, v_ref), axis=0)
    right_cells = jnp.concatenate(block_turned(behind, right, screens, v_ref), axis=0)
    edge_cells = jnp.where(
        lane < LANES // 2, jnp.where(has_right, right_cells, 0.0), jnp.where(has_left, left_cells, 0.0)
    )
    done = row_product(row_matrix[...], jnp.concatenate([own_cells, edge_cells], axis=1))
    quarters = [
        done[part * height : (part + 1) * height, sub * LANES : (sub + 1) * LANES]
        for sub in range(2)
        for part in range(2)
    ]
    high, low = halves(jnp.concatenate(quarters, axis=1))
    pulled = col_product(high, low, col_ref[: 4 * LANES], col_ref[4 * LANES :])
    gradient = -(pulled[:, LANES:] * moved_ref[0] + pulled[:, :LANES] * moved_ref[1])
    mine_ref[0, 2] = gradient[: height // 2]
    theirs_ref[0, 2] = gradient[height // 2 :]


def finish_kernel(mine_ref, received_ref, grad_ref, exit_ref, total_ref, sems):
    core = lax.axis_index("row")
    copies = []
    for source, item in ((mine_ref, core), (received_ref, 1 - core)):
        copies.append(pltpu.make_async_copy(source.at[:, pl.ds(0, 2)], exit_ref.at[item], sems.at[len(copies)]))
    for copy in copies:
        copy.start()
    total_ref[...] = mine_ref[:, 2] + received_ref[:, 2]
    copies.append(pltpu.make_async_copy(total_ref, grad_ref, sems.at[2]))
    copies[2].start()
    for copy in copies:
        copy.wait()


def spread(shard, axis, reach=None):
    size = lax.axis_size(axis)
    reach = size if reach is None else reach
    pieces = []
    for bits in range(1, size):
        pairs = [(i, i ^ bits) for i in range(size) if abs(i - (i ^ bits)) <= reach]
        pieces.append(lax.ppermute(shard, axis, pairs) if pairs else jnp.zeros_like(shard))
    return pieces


def swap_cores(value):
    return lax.ppermute(value, "row", [(0, 1), (1, 0)])


def whole_field_body(phase, tilt, intensity):
    _, tile_r, tile_c = phase.shape
    count, blocks = lax.axis_size("depth"), lax.axis_size("col")
    core = lax.axis_index("row")
    height = 2 * tile_r
    vmem = pl.BlockSpec(memory_space=pltpu.VMEM)
    smem = pl.BlockSpec(memory_space=pltpu.SMEM)
    hbm = pl.BlockSpec(memory_space=pl.ANY)

    def array(*shape):
        return jax.ShapeDtypeStruct(shape, jnp.float32)

    def params(mebibytes):
        return pltpu.CompilerParams(vmem_limit_bytes=mebibytes * 2**20)

    other_depths = spread(phase, "depth")
    other_depths[0], measured, slab = lax.optimization_barrier((other_depths[0], intensity, phase))
    other_depths = jnp.concatenate(other_depths, axis=0)
    packet = jnp.concatenate([slab, measured], axis=0)
    near_own = [packet]
    for bits in range(1, blocks):
        pairs = [(i, i ^ bits) for i in range(blocks)]
        close = [(i, j) for i, j in pairs if abs(i - j) <= 1]
        if close:
            near_own.append(lax.ppermute(packet, "col", close))
        else:
            further = [(i, j) for i, j in pairs if abs(i - j) <= 2]
            arrived = lax.ppermute(slab, "col", further) if further else jnp.zeros_like(slab)
            near_own.append(jnp.concatenate([arrived, jnp.zeros_like(measured)], axis=0))
    near_own = jnp.stack(near_own)
    arriving = spread(other_depths, "col", 2)
    arriving[0], near_own = lax.optimization_barrier((arriving[0], near_own))
    near_rest = jnp.stack([other_depths] + arriving)
    wanted = lax.dynamic_slice_in_dim(near_own, 2 - core, 1, 1)
    far_own = swap_cores(jnp.concatenate([near_own[:, :1], wanted], axis=1))
    far_rest = swap_cores(near_rest)

    half_screens = (count + 1, blocks, tile_r, tile_c)
    field = (blocks, 2, height, tile_c)
    wave, near_cos, near_sin = pl.pallas_call(
        prepare_kernel,
        out_shape=(array(*field), array(*half_screens), array(*half_screens)),
        in_specs=[smem, vmem, vmem],
        out_specs=(vmem,) * 3,
        compiler_params=params(8),
        cost_estimate=pl.CostEstimate(flops=5 * 10**8, bytes_accessed=2**20, transcendentals=0),
    )(tilt, near_own, near_rest)
    mine, theirs = pl.pallas_call(
        wave_kernel,
        out_shape=(array(1, 3, tile_r, tile_c),) * 2,
        in_specs=[vmem] * 8,
        out_specs=(vmem,) * 2,
        scratch_shapes=[pltpu.VMEM(half_screens, jnp.float32)] * 2
        + [pltpu.VMEM(field, jnp.float32), pltpu.VMEM((2, height, tile_c), jnp.float32)]
        + [pltpu.VMEM((blocks, height, 4 * LANES), jnp.bfloat16)] * 2,
        compiler_params=params(24),
    )(
        wave, near_cos, near_sin, near_own, far_own, far_rest,
        jnp.asarray(row_constant(height)), jnp.asarray(col_constant()),
    )
    return pl.pallas_call(
        finish_kernel,
        out_shape=(array(*phase.shape), array(2, 1, 2, tile_r, tile_c)),
        in_specs=[vmem, vmem],
        out_specs=(hbm, hbm),
        scratch_shapes=[pltpu.VMEM(phase.shape, jnp.float32), pltpu.SemaphoreType.DMA((3,))],
        compiler_params=params(4),
    )(mine, swap_cores(theirs))


def extended_2(cells, sides, width):
    for axis, dim in sides:
        count = lax.axis_size(axis)
        ends = count - 1
        head = lax.slice_in_dim(cells, 0, width, axis=dim)
        tail = lax.slice_in_dim(cells, cells.shape[dim] - width, cells.shape[dim], axis=dim)
        cells = jnp.concatenate(
            [
                lax.ppermute(tail, axis, [(i, (i + 1) % count) for i in range(ends)]),
                cells,
                lax.ppermute(head, axis, [((i + 1) % count, i) for i in range(ends)]),
            ],
            axis=dim,
        )
    return cells


def from_behind(value, axis, steps):
    count = lax.axis_size(axis)
    leading, last = (max(0, -steps), min(count, count - steps))
    return lax.ppermute(value, axis, [(source, source + steps) for source in range(leading, last)])


def band_matrix(block_size, margin, fresnel, adjoint):
    shape_full = (block_size, block_size + 2 * margin)
    out_idx = lax.broadcasted_iota(jnp.int32, shape_full, 0)
    in_idx = lax.broadcasted_iota(jnp.int32, shape_full, 1)
    offset = (out_idx + margin - in_idx).astype(jnp.float32)
    inside = jnp.abs(offset) <= margin
    taper_dist = jnp.maximum(jnp.abs(offset) - 0.5 * margin, 0.0)
    profile = jnp.cos(jnp.pi * taper_dist / (margin + 2.0))
    weight = profile * profile / math.sqrt(fresnel)
    phase_angle = jnp.pi * offset * offset / fresnel
    real_part = jnp.where(inside, jnp.cos(phase_angle) * weight, 0.0)
    imag_part = jnp.where(inside, jnp.sin(phase_angle) * weight, 0.0)
    if adjoint:
        imag_part = -imag_part
    upper = jnp.stack([real_part, -imag_part])
    lower = jnp.stack([imag_part, real_part])
    return jnp.stack([upper, lower])


def along_rows(extended, matrix):
    pieces = [jnp.einsum("pqij,gqjc->gpic", matrix, extended, precision=lax.Precision.HIGHEST)]
    return jnp.concatenate(pieces, axis=2)


def along_cols(extended, matrix, margin):
    block_size = matrix.shape[2]
    extent = extended.shape[3] - 2 * margin
    pieces = []
    for block_start in range(0, extent, block_size):
        window = extended[:, :, :, block_start : block_start + block_size + 2 * margin]
        pieces.append(
            jnp.einsum("pqij,gqrj->gpri", matrix, window, precision=lax.Precision.HIGHEST)
        )
    return jnp.concatenate(pieces, axis=3)


def propagate(current, row_matrix, col_matrix):
    with_rows = extended_2(current, (("row", 2),), HALO)
    row_done = along_rows(with_rows, row_matrix)
    with_cols = extended_2(row_done, (("col", 3),), HALO)
    return along_cols(with_cols, col_matrix, HALO)


def transmit(screen, current, adjoint):
    screen_re = screen[0][None]
    screen_im = screen[1][None]
    if adjoint:
        screen_im = -screen_im
    real_part = screen_re * current[:, 0] - screen_im * current[:, 1]
    imag_part = screen_re * current[:, 1] + screen_im * current[:, 0]
    return jnp.stack([real_part, imag_part], axis=1)


def store_item(store, current, first_item, slice_index, active):
    begin = (first_item, jnp.int32(slice_index), jnp.int32(0), jnp.int32(0), jnp.int32(0))
    sizes_now = (current.shape[0], 1) + current.shape[1:]
    previous = lax.dynamic_slice(store, begin, sizes_now)
    fresh = jnp.where(active, current[:, None], previous)
    return lax.dynamic_update_slice(store, fresh, begin)


def staged_body(phase, tilt, intensity):
    slices, tile_r, tile_c = phase.shape
    batch_size = tilt.shape[0]
    sections = lax.axis_size("depth")
    section_index = lax.axis_index("depth")
    group_size = 1
    groups = batch_size // group_size
    tick_count = sections + groups - 1
    block_r = 64
    block_c = 128
    fwd_rows = band_matrix(block_r, HALO, FRESNEL, False)
    fwd_cols = band_matrix(block_c, HALO, FRESNEL, False)
    adj_rows = band_matrix(block_r, HALO, FRESNEL, True)
    adj_cols = band_matrix(block_c, HALO, FRESNEL, True)
    row_pos = (
        lax.axis_index("row") * tile_r + lax.broadcasted_iota(jnp.int32, (tile_r, tile_c), 0)
    ).astype(jnp.float32)
    col_pos = (
        lax.axis_index("col") * tile_c + lax.broadcasted_iota(jnp.int32, (tile_r, tile_c), 1)
    ).astype(jnp.float32)
    height = float(tile_r * lax.axis_size("row"))
    width_all = float(tile_c * lax.axis_size("col"))
    tilt_f = tilt.astype(jnp.float32)
    phase_angle = (
        2.0
        * jnp.pi
        * (
            tilt_f[:, 0, None, None] * row_pos / height
            + tilt_f[:, 1, None, None] * col_pos / width_all
        )
    )
    incident = jnp.stack([jnp.cos(phase_angle), jnp.sin(phase_angle)], axis=1)
    screens = jnp.stack([jnp.cos(phase), jnp.sin(phase)], axis=1)

    def forward_tick(tick_now, carry):
        incoming, entering, leaving = carry
        group_index = tick_now - section_index
        active = (group_index >= 0) & (group_index < groups)
        first_item = jnp.clip(group_index, 0, groups - 1) * group_size
        current = jnp.where(
            section_index == 0,
            lax.dynamic_slice_in_dim(incident, first_item, group_size, 0),
            incoming,
        )
        entering = store_item(entering, current, first_item, 0, active)
        current = propagate(transmit(screens[0], current, False), fwd_rows, fwd_cols)
        leaving = store_item(leaving, current, first_item, 0, active)
        incoming = from_behind(current, "depth", 1)
        return (incoming, entering, leaving)

    store_zero = jnp.zeros((batch_size, slices, 2, tile_r, tile_c), jnp.float32)
    start_wave = jnp.zeros((group_size, 2, tile_r, tile_c), jnp.float32)
    _, entering, leaving = lax.fori_loop(
        0, tick_count, forward_tick, (start_wave, store_zero, store_zero)
    )
    final_wave = leaving[:, slices - 1]
    misfit = final_wave[:, 0] * final_wave[:, 0] + final_wave[:, 1] * final_wave[:, 1] - intensity
    seed_adjoint = 2.0 * misfit[:, None] * final_wave

    def backward_tick(tick_now, carry):
        incoming, gradient = carry
        group_index = tick_now - (sections - 1 - section_index)
        active = (group_index >= 0) & (group_index < groups)
        first_item = jnp.clip(group_index, 0, groups - 1) * group_size
        adjoint_wave = jnp.where(
            section_index == sections - 1,
            lax.dynamic_slice_in_dim(seed_adjoint, first_item, group_size, 0),
            incoming,
        )
        for slice_index in reversed(range(slices)):
            pulled = propagate(adjoint_wave, adj_rows, adj_cols)
            arrived = lax.dynamic_slice_in_dim(entering[:, slice_index], first_item, group_size, 0)
            moved = transmit(screens[slice_index], arrived, False)
            contribution = jnp.sum(pulled[:, 1] * moved[:, 0] - pulled[:, 0] * moved[:, 1], axis=0)
            gradient = gradient.at[slice_index].add(jnp.where(active, contribution, 0.0))
            adjoint_wave = transmit(screens[slice_index], pulled, True)
        incoming = from_behind(adjoint_wave, "depth", -1)
        return (incoming, gradient)

    grad_zero = jnp.zeros((slices, tile_r, tile_c), jnp.float32)
    _, gradient = lax.fori_loop(0, tick_count, backward_tick, (start_wave, grad_zero))
    return (gradient, leaving)


def fits_whole(phase_shape, batch, mesh):
    slices, height, width = phase_shape
    rows, cols, sections = mesh.shape["row"], mesh.shape["col"], mesh.shape["depth"]
    return (
        4 * height * width * (slices + batch) <= GATHER_BUDGET
        and batch == rows == 2
        and slices == sections
        and sections & (sections - 1) == 0
        and cols & (cols - 1) == 0
        and height == LANES
        and width == cols * LANES
        and cols > 1
        and sections > 1
        and sections * HALO <= LANES
    )


def solution(mesh):
    placed = (P("depth", "row", "col"), P(), P(None, "row", "col"))

    def run(phase, tilt, intensity):
        if fits_whole(phase.shape, tilt.shape[0], mesh):
            body = whole_field_body
        else:
            body = staged_body
        return jax.shard_map(
            body,
            mesh=mesh,
            in_specs=placed,
            out_specs=(P("depth", "row", "col"), P(None, "depth", None, "row", "col")),
            check_vma=False,
        )(phase, tilt, intensity)

    return run
```

```python
import math

import jax
import jax.numpy as jnp
import numpy as np
from jax import lax
from jax.experimental import pallas as pl
from jax.experimental.pallas import tpu as pltpu
from jax.sharding import PartitionSpec as P

HALO = 32
FRESNEL = 64
LANES = 128
GATHER_BUDGET = 4 * 2**20
SIN = (
    0.9999999980536763,
    -0.1666666530009577,
    0.008333305907073658,
    -0.00019838908256358006,
    2.745822627876341e-06,
    -2.3043562782810933e-08,
)
COS = (
    0.9999999961345007,
    -0.4999999301617528,
    0.04166646215023687,
    -0.0013886696163545999,
    2.4695045482778703e-05,
    -2.5154931690000354e-07,
)


def horner(coefficients, square):
    total = jnp.full_like(square, coefficients[-1])
    for coefficient in coefficients[-2::-1]:
        total = total * square + coefficient
    return total


def cos_sin(angle):
    square = angle * angle
    return horner(COS, square), horner(SIN, square) * angle


def turn(fraction):
    half_cos, half_sin = cos_sin(fraction * math.pi)
    return half_cos * half_cos - half_sin * half_sin, 2.0 * half_cos * half_sin


def halves(value):
    high = value.astype(jnp.bfloat16)
    return high, (value - high.astype(jnp.float32)).astype(jnp.bfloat16)


def np_halves(matrix):
    high = matrix.astype(jnp.bfloat16)
    return high, (matrix - high.astype(np.float64)).astype(jnp.bfloat16)


def np_taps():
    offset = np.arange(-HALO, HALO + 1, dtype=np.float64)
    taper = np.maximum(np.abs(offset) - 0.5 * HALO, 0.0)
    weight = np.cos(np.pi * taper / (HALO + 2.0)) ** 2 / math.sqrt(FRESNEL)
    return weight * np.exp(1j * np.pi * offset * offset / FRESNEL)


def np_band(out_pos, in_pos):
    offset = out_pos[:, None] - in_pos[None, :]
    inside = np.abs(offset) <= HALO
    return np.where(inside, np_taps()[np.clip(offset, -HALO, HALO) + HALO], 0.0)


def row_constant(height):
    matrices = []
    for core in range(2):
        pos = (np.arange(height) + core * (height // 2)) % height
        band = np_band(pos, pos)
        whole = np.block([[band.real, -band.imag], [band.imag, band.real]])
        matrices.append(np.concatenate(np_halves(whole), axis=1))
    return np.stack(matrices)


def col_constant():
    lane = np.arange(LANES)
    edge_pos = np.where(lane < LANES // 2, lane + LANES, lane - LANES)
    parts = []
    for position in (lane, edge_pos):
        band = np_band(lane, position).T
        parts.append(np.block([[band.real, band.imag], [-band.imag, band.real]]))
    high, low = np_halves(np.concatenate(parts, axis=0))
    return np.concatenate([high, low], axis=0)


def both_rows(near_ref, far_ref, where):
    return jnp.concatenate([near_ref[where], far_ref[where]], axis=0)


def block_turned(slice_index, block, screens, v_ref):
    near_cos, near_sin, far_cos, far_sin = screens
    cos = both_rows(near_cos, far_cos, (slice_index, block))
    sin = both_rows(near_sin, far_sin, (slice_index, block))
    real, imag = v_ref[block, 0], v_ref[block, 1]
    return cos * real - sin * imag, cos * imag + sin * real


def row_product(row_matrix, columns):
    high, low = halves(columns)
    whole = row_matrix.shape[0]
    return jnp.dot(
        jnp.concatenate([row_matrix[:, :whole], row_matrix], axis=1),
        jnp.concatenate([high, low, high], axis=0),
        preferred_element_type=jnp.float32,
    )


def col_product(high, low, col_high, col_low):
    return jnp.dot(
        jnp.concatenate([high, low, high], axis=1),
        jnp.concatenate([col_high, col_high, col_low], axis=0),
        preferred_element_type=jnp.float32,
    )


def advance(slice_index, start, size, screens, row_matrix, col_ref, v_ref, a_high, a_low):
    height = v_ref.shape[2]
    half = LANES // 2
    own, edge = pl.ds(0, 2 * LANES), pl.ds(2 * LANES, 2 * LANES)
    low_own, low_edge = pl.ds(4 * LANES, 2 * LANES), pl.ds(6 * LANES, 2 * LANES)
    chunks = [range(place, min(place + 2, size)) for place in range(0, size, 2)]
    for chunk in chunks:
        columns = jnp.concatenate(
            [jnp.concatenate(block_turned(slice_index, start + place, screens, v_ref), axis=0) for place in chunk],
            axis=1,
        )
        done = row_product(row_matrix, columns)
        for sub, place in enumerate(chunk):
            for part in range(2):
                value = done[part * height : (part + 1) * height, sub * LANES : (sub + 1) * LANES]
                for target, piece in zip((a_high, a_low), halves(value)):
                    target[place, :, pl.ds(part * LANES, LANES)] = piece
                    if place > 0:
                        target[place - 1, :, pl.ds((2 + part) * LANES, half)] = piece[:, :half]
                    if place < size - 1:
                        target[place + 1, :, pl.ds((2 + part) * LANES + half, half)] = piece[:, half:]
    parts = []
    for chunk in chunks:
        cells = pl.ds(chunk[0], len(chunk))
        rows = len(chunk) * height
        parts.append(
            col_product(
                a_high[cells, :, own].reshape(rows, 2 * LANES),
                a_low[cells, :, own].reshape(rows, 2 * LANES),
                col_ref[own],
                col_ref[low_own],
            )
        )
    cells, rows = pl.ds(0, size), size * height
    edges = col_product(
        a_high[cells, :, edge].reshape(rows, 2 * LANES),
        a_low[cells, :, edge].reshape(rows, 2 * LANES),
        col_ref[edge],
        col_ref[low_edge],
    )
    for chunk, done in zip(chunks, parts):
        for sub, place in enumerate(chunk):
            total = done[sub * height : (sub + 1) * height] + edges[place * height : (place + 1) * height]
            for part in range(2):
                v_ref[start + place, part] = total[:, part * LANES : (part + 1) * LANES]


def clear_edge(a_ref, place, right):
    half = LANES // 2
    for part in range(2):
        begin = (2 + part) * LANES + (0 if right else half)
        a_ref[place, :, pl.ds(begin, half)] = jnp.zeros((a_ref.shape[1], half), a_ref.dtype)


def prepare_kernel(tilt_ref, near_own, near_rest, wave_ref, cos_ref, sin_ref):
    blocks, _, height, _ = wave_ref.shape
    count = cos_ref.shape[0] - 1
    core, own_section, own_place = lax.axis_index("row"), lax.axis_index("depth"), lax.axis_index("col")

    def screens(col, carry):
        held = col ^ own_place
        for bits in range(count):
            angle = near_own[held, 0] if bits == 0 else near_rest[held, bits - 1]
            cos_ref[bits ^ own_section, col], sin_ref[bits ^ own_section, col] = cos_sin(angle)
        return carry

    lax.fori_loop(0, blocks, screens, 0)
    cos_ref[count] = jnp.ones(cos_ref.shape[1:], jnp.float32)
    sin_ref[count] = jnp.zeros(cos_ref.shape[1:], jnp.float32)

    def cycles(number, position, extent):
        fraction = (number * position).astype(jnp.float32) / extent
        return turn(fraction - jnp.round(fraction))

    row = lax.broadcasted_iota(jnp.int32, (height, LANES), 0) + core * (height // 2)
    row = jnp.where(row >= height, row - height, row)
    row_cos, row_sin = cycles(tilt_ref[core, 0], row, float(height))
    for block in range(blocks):
        col_cos, col_sin = cycles(
            tilt_ref[core, 1],
            lax.broadcasted_iota(jnp.int32, (8, LANES), 1) + block * LANES,
            float(blocks * LANES),
        )
        col_cos, col_sin = col_cos[:1], col_sin[:1]
        wave_ref[block, 0] = row_cos * col_cos - row_sin * col_sin
        wave_ref[block, 1] = row_sin * col_cos + row_cos * col_sin


def wave_kernel(
    wave_ref, near_cos, near_sin, near_own, far_own, far_rest, row_ref, col_ref,
    mine_ref, theirs_ref, far_cos, far_sin, v_ref, moved_ref, a_high, a_low,
):
    blocks, _, height, _ = v_ref.shape
    count = near_cos.shape[0] - 1
    core, own_section, own_place = lax.axis_index("row"), lax.axis_index("depth"), lax.axis_index("col")
    near, far = pl.ds(0, height // 2), pl.ds(height // 2, height // 2)
    screens = (near_cos, near_sin, far_cos, far_sin)
    row_matrix = row_ref.at[core]
    window = min(3, blocks)
    window_start = jnp.clip(own_place - 1, 0, blocks - window)

    def far_screens(slice_index):
        bits = slice_index ^ own_section
        for col in range(blocks):
            held = col ^ own_place
            angle = jnp.where(bits == 0, far_own[held, 0], far_rest[held, jnp.maximum(bits - 1, 0)])
            far_cos[slice_index, col], far_sin[slice_index, col] = cos_sin(angle)

    for target in (a_high, a_low):
        clear_edge(target, 0, False)
        clear_edge(target, blocks - 1, True)
    far_cos[count] = jnp.ones(far_cos.shape[1:], jnp.float32)
    far_sin[count] = jnp.zeros(far_cos.shape[1:], jnp.float32)
    v_ref[...] = wave_ref[...]
    far_screens(0)

    def forward(tick, carry):
        @pl.when(tick == own_section)
        def _():
            moved_ref[0], moved_ref[1] = block_turned(tick, own_place, screens, v_ref)

        advance(tick, 0, blocks, screens, row_matrix[...], col_ref, v_ref, a_high, a_low)
        far_screens(jnp.minimum(tick + 1, count - 1))

        @pl.when(tick == own_section)
        def _():
            for target, row in ((mine_ref, near), (theirs_ref, far)):
                for part in range(2):
                    target[0, part] = v_ref[own_place, part, row]

        return carry

    lax.fori_loop(0, count, forward, 0)

    for target in (a_high, a_low):
        clear_edge(target, window - 1, True)
    for place in range(window):
        block = window_start + place
        held = block ^ own_place
        for row, measured in ((near, near_own[held, 1 + core]), (far, far_own[held, 1])):
            real, imag = v_ref[block, 0, row], v_ref[block, 1, row]
            misfit = 2.0 * (real * real + imag * imag - measured)
            v_ref[block, 0, row] = misfit * real
            v_ref[block, 1, row] = -misfit * imag

    def backward(tick, carry):
        advance(count - tick, window_start, window, screens, row_matrix[...], col_ref, v_ref, a_high, a_low)
        return carry

    lax.fori_loop(0, count - 1 - own_section, backward, 0)

    left, right = jnp.maximum(own_place - 1, 0), jnp.minimum(own_place + 1, blocks - 1)
    lane = lax.broadcasted_iota(jnp.int32, (2 * height, LANES), 1)
    has_left, has_right = own_place > 0, own_place < blocks - 1
    behind = own_section + 1
    own_cells = jnp.concatenate(block_turned(behind, own_place, screens, v_ref), axis=0)
    left_cells = jnp.concatenate(block_turned(behind, left, screens, v_ref), axis=0)
    right_cells = jnp.concatenate(block_turned(behind, right, screens, v_ref), axis=0)
    edge_cells = jnp.where(
        lane < LANES // 2, jnp.where(has_right, right_cells, 0.0), jnp.where(has_left, left_cells, 0.0)
    )
    done = row_product(row_matrix[...], jnp.concatenate([own_cells, edge_cells], axis=1))
    quarters = [
        done[part * height : (part + 1) * height, sub * LANES : (sub + 1) * LANES]
        for sub in range(2)
        for part in range(2)
    ]
    high, low = halves(jnp.concatenate(quarters, axis=1))
    pulled = col_product(high, low, col_ref[: 4 * LANES], col_ref[4 * LANES :])
    gradient = -(pulled[:, LANES:] * moved_ref[0] + pulled[:, :LANES] * moved_ref[1])
    mine_ref[0, 2] = gradient[: height // 2]
    theirs_ref[0, 2] = gradient[height // 2 :]


def finish_kernel(mine_ref, received_ref, grad_ref, exit_ref, total_ref, sems):
    core = lax.axis_index("row")
    copies = []
    for source, item in ((mine_ref, core), (received_ref, 1 - core)):
        copies.append(pltpu.make_async_copy(source.at[:, pl.ds(0, 2)], exit_ref.at[item], sems.at[len(copies)]))
    for copy in copies:
        copy.start()
    total_ref[...] = mine_ref[:, 2] + received_ref[:, 2]
    copies.append(pltpu.make_async_copy(total_ref, grad_ref, sems.at[2]))
    copies[2].start()
    for copy in copies:
        copy.wait()


def spread(shard, axis):
    size = lax.axis_size(axis)
    return [lax.ppermute(shard, axis, [(i, i ^ bits) for i in range(size)]) for bits in range(1, size)]


def exchange(value, bits):
    return lax.ppermute(value, "col", [(i, i ^ bits) for i in range(4)])


def swap_cores(value):
    return lax.ppermute(value, "row", [(0, 1), (1, 0)])


def whole_field_body(phase, tilt, intensity):
    _, tile_r, tile_c = phase.shape
    count, blocks = lax.axis_size("depth"), lax.axis_size("col")
    core = lax.axis_index("row")
    height = 2 * tile_r
    vmem = pl.BlockSpec(memory_space=pltpu.VMEM)
    smem = pl.BlockSpec(memory_space=pltpu.SMEM)
    hbm = pl.BlockSpec(memory_space=pl.ANY)

    def array(*shape):
        return jax.ShapeDtypeStruct(shape, jnp.float32)

    def params(mebibytes):
        return pltpu.CompilerParams(vmem_limit_bytes=mebibytes * 2**20)

    other_depths = spread(phase, "depth")
    other_depths[0], measured, slab = lax.optimization_barrier((other_depths[0], intensity, phase))
    packet = jnp.concatenate([slab, measured], axis=0)
    packet_x, packet_y = exchange(packet, 1), exchange(packet, 2)
    other_depths[-1], packet_x = lax.optimization_barrier((other_depths[-1], packet_x))
    other_depths = jnp.concatenate(other_depths, axis=0)
    near_own = jnp.stack([packet, packet_x, packet_y, exchange(packet_y, 1)])
    rest_x, rest_y = exchange(other_depths, 1), exchange(other_depths, 2)
    rest_corner = exchange(rest_x, 2)
    rest_x, near_own = lax.optimization_barrier((rest_x, near_own))
    near_rest = jnp.stack([other_depths, rest_x, rest_y, rest_corner])
    wanted = lax.dynamic_slice_in_dim(near_own, 2 - core, 1, 1)
    far_own = swap_cores(jnp.concatenate([near_own[:, :1], wanted], axis=1))
    far_rest = swap_cores(near_rest)

    half_screens = (count + 1, blocks, tile_r, tile_c)
    field = (blocks, 2, height, tile_c)
    wave, near_cos, near_sin = pl.pallas_call(
        prepare_kernel,
        out_shape=(array(*field), array(*half_screens), array(*half_screens)),
        in_specs=[smem, vmem, vmem],
        out_specs=(vmem,) * 3,
        compiler_params=params(8),
        cost_estimate=pl.CostEstimate(flops=5 * 10**8, bytes_accessed=2**20, transcendentals=0),
    )(tilt, near_own, near_rest)
    mine, theirs = pl.pallas_call(
        wave_kernel,
        out_shape=(array(1, 3, tile_r, tile_c),) * 2,
        in_specs=[vmem] * 8,
        out_specs=(vmem,) * 2,
        scratch_shapes=[pltpu.VMEM(half_screens, jnp.float32)] * 2
        + [pltpu.VMEM(field, jnp.float32), pltpu.VMEM((2, height, tile_c), jnp.float32)]
        + [pltpu.VMEM((blocks, height, 4 * LANES), jnp.bfloat16)] * 2,
        compiler_params=params(24),
    )(
        wave, near_cos, near_sin, near_own, far_own, far_rest,
        jnp.asarray(row_constant(height)), jnp.asarray(col_constant()),
    )
    return pl.pallas_call(
        finish_kernel,
        out_shape=(array(*phase.shape), array(2, 1, 2, tile_r, tile_c)),
        in_specs=[vmem, vmem],
        out_specs=(hbm, hbm),
        scratch_shapes=[pltpu.VMEM(phase.shape, jnp.float32), pltpu.SemaphoreType.DMA((3,))],
        compiler_params=params(4),
    )(mine, swap_cores(theirs))


def extended_2(cells, sides, width):
    for axis, dim in sides:
        count = lax.axis_size(axis)
        ends = count - 1
        head = lax.slice_in_dim(cells, 0, width, axis=dim)
        tail = lax.slice_in_dim(cells, cells.shape[dim] - width, cells.shape[dim], axis=dim)
        cells = jnp.concatenate(
            [
                lax.ppermute(tail, axis, [(i, (i + 1) % count) for i in range(ends)]),
                cells,
                lax.ppermute(head, axis, [((i + 1) % count, i) for i in range(ends)]),
            ],
            axis=dim,
        )
    return cells


def from_behind(value, axis, steps):
    count = lax.axis_size(axis)
    leading, last = (max(0, -steps), min(count, count - steps))
    return lax.ppermute(value, axis, [(source, source + steps) for source in range(leading, last)])


def band_matrix(block_size, margin, fresnel, adjoint):
    shape_full = (block_size, block_size + 2 * margin)
    out_idx = lax.broadcasted_iota(jnp.int32, shape_full, 0)
    in_idx = lax.broadcasted_iota(jnp.int32, shape_full, 1)
    offset = (out_idx + margin - in_idx).astype(jnp.float32)
    inside = jnp.abs(offset) <= margin
    taper_dist = jnp.maximum(jnp.abs(offset) - 0.5 * margin, 0.0)
    profile = jnp.cos(jnp.pi * taper_dist / (margin + 2.0))
    weight = profile * profile / math.sqrt(fresnel)
    phase_angle = jnp.pi * offset * offset / fresnel
    real_part = jnp.where(inside, jnp.cos(phase_angle) * weight, 0.0)
    imag_part = jnp.where(inside, jnp.sin(phase_angle) * weight, 0.0)
    if adjoint:
        imag_part = -imag_part
    upper = jnp.stack([real_part, -imag_part])
    lower = jnp.stack([imag_part, real_part])
    return jnp.stack([upper, lower])


def along_rows(extended, matrix):
    pieces = [jnp.einsum("pqij,gqjc->gpic", matrix, extended, precision=lax.Precision.HIGHEST)]
    return jnp.concatenate(pieces, axis=2)


def along_cols(extended, matrix, margin):
    block_size = matrix.shape[2]
    extent = extended.shape[3] - 2 * margin
    pieces = []
    for block_start in range(0, extent, block_size):
        window = extended[:, :, :, block_start : block_start + block_size + 2 * margin]
        pieces.append(
            jnp.einsum("pqij,gqrj->gpri", matrix, window, precision=lax.Precision.HIGHEST)
        )
    return jnp.concatenate(pieces, axis=3)


def propagate(current, row_matrix, col_matrix):
    with_rows = extended_2(current, (("row", 2),), HALO)
    row_done = along_rows(with_rows, row_matrix)
    with_cols = extended_2(row_done, (("col", 3),), HALO)
    return along_cols(with_cols, col_matrix, HALO)


def transmit(screen, current, adjoint):
    screen_re = screen[0][None]
    screen_im = screen[1][None]
    if adjoint:
        screen_im = -screen_im
    real_part = screen_re * current[:, 0] - screen_im * current[:, 1]
    imag_part = screen_re * current[:, 1] + screen_im * current[:, 0]
    return jnp.stack([real_part, imag_part], axis=1)


def store_item(store, current, first_item, slice_index, active):
    begin = (first_item, jnp.int32(slice_index), jnp.int32(0), jnp.int32(0), jnp.int32(0))
    sizes_now = (current.shape[0], 1) + current.shape[1:]
    previous = lax.dynamic_slice(store, begin, sizes_now)
    fresh = jnp.where(active, current[:, None], previous)
    return lax.dynamic_update_slice(store, fresh, begin)


def staged_body(phase, tilt, intensity):
    slices, tile_r, tile_c = phase.shape
    batch_size = tilt.shape[0]
    sections = lax.axis_size("depth")
    section_index = lax.axis_index("depth")
    group_size = 1
    groups = batch_size // group_size
    tick_count = sections + groups - 1
    block_r = 64
    block_c = 128
    fwd_rows = band_matrix(block_r, HALO, FRESNEL, False)
    fwd_cols = band_matrix(block_c, HALO, FRESNEL, False)
    adj_rows = band_matrix(block_r, HALO, FRESNEL, True)
    adj_cols = band_matrix(block_c, HALO, FRESNEL, True)
    row_pos = (
        lax.axis_index("row") * tile_r + lax.broadcasted_iota(jnp.int32, (tile_r, tile_c), 0)
    ).astype(jnp.float32)
    col_pos = (
        lax.axis_index("col") * tile_c + lax.broadcasted_iota(jnp.int32, (tile_r, tile_c), 1)
    ).astype(jnp.float32)
    height = float(tile_r * lax.axis_size("row"))
    width_all = float(tile_c * lax.axis_size("col"))
    tilt_f = tilt.astype(jnp.float32)
    phase_angle = (
        2.0
        * jnp.pi
        * (
            tilt_f[:, 0, None, None] * row_pos / height
            + tilt_f[:, 1, None, None] * col_pos / width_all
        )
    )
    incident = jnp.stack([jnp.cos(phase_angle), jnp.sin(phase_angle)], axis=1)
    screens = jnp.stack([jnp.cos(phase), jnp.sin(phase)], axis=1)

    def forward_tick(tick_now, carry):
        incoming, entering, leaving = carry
        group_index = tick_now - section_index
        active = (group_index >= 0) & (group_index < groups)
        first_item = jnp.clip(group_index, 0, groups - 1) * group_size
        current = jnp.where(
            section_index == 0,
            lax.dynamic_slice_in_dim(incident, first_item, group_size, 0),
            incoming,
        )
        entering = store_item(entering, current, first_item, 0, active)
        current = propagate(transmit(screens[0], current, False), fwd_rows, fwd_cols)
        leaving = store_item(leaving, current, first_item, 0, active)
        incoming = from_behind(current, "depth", 1)
        return (incoming, entering, leaving)

    store_zero = jnp.zeros((batch_size, slices, 2, tile_r, tile_c), jnp.float32)
    start_wave = jnp.zeros((group_size, 2, tile_r, tile_c), jnp.float32)
    _, entering, leaving = lax.fori_loop(
        0, tick_count, forward_tick, (start_wave, store_zero, store_zero)
    )
    final_wave = leaving[:, slices - 1]
    misfit = final_wave[:, 0] * final_wave[:, 0] + final_wave[:, 1] * final_wave[:, 1] - intensity
    seed_adjoint = 2.0 * misfit[:, None] * final_wave

    def backward_tick(tick_now, carry):
        incoming, gradient = carry
        group_index = tick_now - (sections - 1 - section_index)
        active = (group_index >= 0) & (group_index < groups)
        first_item = jnp.clip(group_index, 0, groups - 1) * group_size
        adjoint_wave = jnp.where(
            section_index == sections - 1,
            lax.dynamic_slice_in_dim(seed_adjoint, first_item, group_size, 0),
            incoming,
        )
        for slice_index in reversed(range(slices)):
            pulled = propagate(adjoint_wave, adj_rows, adj_cols)
            arrived = lax.dynamic_slice_in_dim(entering[:, slice_index], first_item, group_size, 0)
            moved = transmit(screens[slice_index], arrived, False)
            contribution = jnp.sum(pulled[:, 1] * moved[:, 0] - pulled[:, 0] * moved[:, 1], axis=0)
            gradient = gradient.at[slice_index].add(jnp.where(active, contribution, 0.0))
            adjoint_wave = transmit(screens[slice_index], pulled, True)
        incoming = from_behind(adjoint_wave, "depth", -1)
        return (incoming, gradient)

    grad_zero = jnp.zeros((slices, tile_r, tile_c), jnp.float32)
    _, gradient = lax.fori_loop(0, tick_count, backward_tick, (start_wave, grad_zero))
    return (gradient, leaving)


def fits_whole(phase_shape, batch, mesh):
    slices, height, width = phase_shape
    rows, cols, sections = mesh.shape["row"], mesh.shape["col"], mesh.shape["depth"]
    return (
        4 * height * width * (slices + batch) <= GATHER_BUDGET
        and batch == rows == 2
        and slices == sections
        and sections & (sections - 1) == 0
        and cols == 4
        and height == LANES
        and width == cols * LANES
        and sections > 1
        and sections * HALO <= LANES
    )


def solution(mesh):
    placed = (P("depth", "row", "col"), P(), P(None, "row", "col"))

    def run(phase, tilt, intensity):
        if fits_whole(phase.shape, tilt.shape[0], mesh):
            body = whole_field_body
        else:
            body = staged_body
        return jax.shard_map(
            body,
            mesh=mesh,
            in_specs=placed,
            out_specs=(P("depth", "row", "col"), P(None, "depth", None, "row", "col")),
            check_vma=False,
        )(phase, tilt, intensity)

    return run
```

```python
import math

import jax
import jax.numpy as jnp
import numpy as np
from jax import lax
from jax.experimental import pallas as pl
from jax.experimental.pallas import tpu as pltpu
from jax.sharding import PartitionSpec as P

HALO = 32
FRESNEL = 64
LANES = 128
GATHER_BUDGET = 4 * 2**20
SIN = (
    0.9999999980536763,
    -0.1666666530009577,
    0.008333305907073658,
    -0.00019838908256358006,
    2.745822627876341e-06,
    -2.3043562782810933e-08,
)
COS = (
    0.9999999961345007,
    -0.4999999301617528,
    0.04166646215023687,
    -0.0013886696163545999,
    2.4695045482778703e-05,
    -2.5154931690000354e-07,
)


def horner(coefficients, square):
    total = jnp.full_like(square, coefficients[-1])
    for coefficient in coefficients[-2::-1]:
        total = total * square + coefficient
    return total


def cos_sin(angle):
    square = angle * angle
    return horner(COS, square), horner(SIN, square) * angle


def turn(fraction):
    half_cos, half_sin = cos_sin(fraction * math.pi)
    return half_cos * half_cos - half_sin * half_sin, 2.0 * half_cos * half_sin


def halves(value):
    high = value.astype(jnp.bfloat16)
    return high, (value - high.astype(jnp.float32)).astype(jnp.bfloat16)


def np_halves(matrix):
    high = matrix.astype(jnp.bfloat16)
    return high, (matrix - high.astype(np.float64)).astype(jnp.bfloat16)


def np_taps():
    offset = np.arange(-HALO, HALO + 1, dtype=np.float64)
    taper = np.maximum(np.abs(offset) - 0.5 * HALO, 0.0)
    weight = np.cos(np.pi * taper / (HALO + 2.0)) ** 2 / math.sqrt(FRESNEL)
    return weight * np.exp(1j * np.pi * offset * offset / FRESNEL)


def np_band(out_pos, in_pos):
    offset = out_pos[:, None] - in_pos[None, :]
    inside = np.abs(offset) <= HALO
    return np.where(inside, np_taps()[np.clip(offset, -HALO, HALO) + HALO], 0.0)


def row_constant(height):
    matrices = []
    for core in range(2):
        pos = (np.arange(height) + core * (height // 2)) % height
        band = np_band(pos, pos)
        whole = np.block([[band.real, -band.imag], [band.imag, band.real]])
        matrices.append(np.concatenate(np_halves(whole), axis=1))
    return np.stack(matrices)


def col_constant():
    lane = np.arange(LANES)
    edge_pos = np.where(lane < LANES // 2, lane + LANES, lane - LANES)
    parts = []
    for position in (lane, edge_pos):
        band = np_band(lane, position).T
        parts.append(np.block([[band.real, band.imag], [-band.imag, band.real]]))
    high, low = np_halves(np.concatenate(parts, axis=0))
    return np.concatenate([high, low], axis=0)


def both_rows(near_ref, far_ref, where):
    return jnp.concatenate([near_ref[where], far_ref[where]], axis=0)


def block_turned(slice_index, block, screens, wave_ref, place):
    near_cos, near_sin, far_cos, far_sin = screens
    cos = both_rows(near_cos, far_cos, (slice_index, block))
    sin = both_rows(near_sin, far_sin, (slice_index, block))
    real, imag = wave_ref[place, 0], wave_ref[place, 1]
    return cos * real - sin * imag, cos * imag + sin * real


def row_product(row_matrix, columns):
    high, low = halves(columns)
    whole = row_matrix.shape[0]
    return jnp.dot(
        jnp.concatenate([row_matrix[:, :whole], row_matrix], axis=1),
        jnp.concatenate([high, low, high], axis=0),
        preferred_element_type=jnp.float32,
    )


def col_product(high, low, col_high, col_low):
    return jnp.dot(
        jnp.concatenate([high, low, high], axis=1),
        jnp.concatenate([col_high, col_high, col_low], axis=0),
        preferred_element_type=jnp.float32,
    )


def advance(slice_index, start, size, screens, row_matrix, col_ref, from_ref, to_ref, a_high, a_low):
    height = from_ref.shape[2]
    half = LANES // 2
    own, edge = pl.ds(0, 2 * LANES), pl.ds(2 * LANES, 2 * LANES)
    low_own, low_edge = pl.ds(4 * LANES, 2 * LANES), pl.ds(6 * LANES, 2 * LANES)
    chunks = [range(place, min(place + 2, size)) for place in range(0, size, 2)]
    for chunk in chunks:
        columns = jnp.concatenate(
            [
                jnp.concatenate(block_turned(slice_index, start + place, screens, from_ref, place), axis=0)
                for place in chunk
            ],
            axis=1,
        )
        done = row_product(row_matrix, columns)
        for sub, place in enumerate(chunk):
            for part in range(2):
                value = done[part * height : (part + 1) * height, sub * LANES : (sub + 1) * LANES]
                for target, piece in zip((a_high, a_low), halves(value)):
                    target[place, :, pl.ds(part * LANES, LANES)] = piece
                    if place > 0:
                        target[place - 1, :, pl.ds((2 + part) * LANES, half)] = piece[:, :half]
                    if place < size - 1:
                        target[place + 1, :, pl.ds((2 + part) * LANES + half, half)] = piece[:, half:]
    parts = []
    for chunk in chunks:
        cells = pl.ds(chunk[0], len(chunk))
        rows = len(chunk) * height
        parts.append(
            col_product(
                a_high[cells, :, own].reshape(rows, 2 * LANES),
                a_low[cells, :, own].reshape(rows, 2 * LANES),
                col_ref[own],
                col_ref[low_own],
            )
        )
    for chunk, done in zip(chunks, parts):
        cells = pl.ds(chunk[0], len(chunk))
        rows = len(chunk) * height
        total = done + col_product(
            a_high[cells, :, edge].reshape(rows, 2 * LANES),
            a_low[cells, :, edge].reshape(rows, 2 * LANES),
            col_ref[edge],
            col_ref[low_edge],
        )
        for sub, place in enumerate(chunk):
            for part in range(2):
                to_ref[place, part] = total[sub * height : (sub + 1) * height, part * LANES : (part + 1) * LANES]


def clear_edge(a_ref, place, right):
    half = LANES // 2
    for part in range(2):
        begin = (2 + part) * LANES + (0 if right else half)
        a_ref[place, :, pl.ds(begin, half)] = jnp.zeros((a_ref.shape[1], half), a_ref.dtype)


def prepare_kernel(tilt_ref, near_own, near_rest, wave_ref, cos_ref, sin_ref):
    blocks, _, height, _ = wave_ref.shape
    count = cos_ref.shape[0] - 1
    core, own_section, own_place = lax.axis_index("row"), lax.axis_index("depth"), lax.axis_index("col")

    def screens(col, carry):
        held = col ^ own_place
        for bits in range(count):
            angle = near_own[held, 0] if bits == 0 else near_rest[held, bits - 1]
            cos_ref[bits ^ own_section, col], sin_ref[bits ^ own_section, col] = cos_sin(angle)
        return carry

    lax.fori_loop(0, blocks, screens, 0)
    cos_ref[count] = jnp.ones(cos_ref.shape[1:], jnp.float32)
    sin_ref[count] = jnp.zeros(cos_ref.shape[1:], jnp.float32)

    def cycles(number, position, extent):
        fraction = (number * position).astype(jnp.float32) / extent
        return turn(fraction - jnp.round(fraction))

    row = lax.broadcasted_iota(jnp.int32, (height, LANES), 0) + core * (height // 2)
    row = jnp.where(row >= height, row - height, row)
    row_cos, row_sin = cycles(tilt_ref[core, 0], row, float(height))
    for block in range(blocks):
        col_cos, col_sin = cycles(
            tilt_ref[core, 1],
            lax.broadcasted_iota(jnp.int32, (8, LANES), 1) + block * LANES,
            float(blocks * LANES),
        )
        col_cos, col_sin = col_cos[:1], col_sin[:1]
        wave_ref[block, 0] = row_cos * col_cos - row_sin * col_sin
        wave_ref[block, 1] = row_sin * col_cos + row_cos * col_sin


def wave_kernel(
    wave_ref, near_cos, near_sin, near_own, far_own, far_rest, row_ref, col_ref,
    mine_ref, theirs_ref, far_cos, far_sin, even_ref, odd_ref, moved_ref, left_ref, grad_ref,
    even_high, even_low, odd_high, odd_low,
):
    blocks, _, height, _ = wave_ref.shape
    count = near_cos.shape[0] - 1
    core, own_section, own_place = lax.axis_index("row"), lax.axis_index("depth"), lax.axis_index("col")
    near, far = pl.ds(0, height // 2), pl.ds(height // 2, height // 2)
    screens = (near_cos, near_sin, far_cos, far_sin)
    row_matrix = row_ref[core]
    window = min(3, blocks)
    window_start = jnp.clip(own_place - 1, 0, blocks - window)
    own_in_window = own_place - window_start
    waves = (even_ref, odd_ref)
    sums = ((even_high, even_low), (odd_high, odd_low))

    def far_screens(slice_index):
        bits = slice_index ^ own_section
        for col in range(blocks):
            held = col ^ own_place
            angle = jnp.where(bits == 0, far_own[held, 0], far_rest[held, jnp.maximum(bits - 1, 0)])
            far_cos[slice_index, col], far_sin[slice_index, col] = cos_sin(angle)

    for pair in sums:
        for target in pair:
            clear_edge(target, 0, False)
            clear_edge(target, blocks - 1, True)
    far_cos[count] = jnp.ones(far_cos.shape[1:], jnp.float32)
    far_sin[count] = jnp.zeros(far_cos.shape[1:], jnp.float32)
    far_screens(0)

    for tick in range(count):
        source, target = wave_ref if tick == 0 else waves[tick % 2], waves[(tick + 1) % 2]
        moved_ref[tick, 0], moved_ref[tick, 1] = block_turned(tick, own_place, screens, source, own_place)
        advance(tick, 0, blocks, screens, row_matrix, col_ref, source, target, *sums[tick % 2])
        if tick + 1 < count:
            far_screens(tick + 1)
        left_ref[tick] = target[own_place]

    last = waves[count % 2]
    source = waves[(count + 1) % 2]
    for pair in sums:
        for target in pair:
            clear_edge(target, window - 1, True)
    for place in range(window):
        block = window_start + place
        held = block ^ own_place
        measured = jnp.concatenate([near_own[held, 1 + core], far_own[held, 1]], axis=0)
        real, imag = last[block, 0], last[block, 1]
        misfit = 2.0 * (real * real + imag * imag - measured)
        source[place, 0] = misfit * real
        source[place, 1] = -misfit * imag

    for tick in range(count - 1):
        source, target = waves[(count + 1 + tick) % 2], waves[(count + tick) % 2]
        advance(
            count - tick, window_start, window, screens, row_matrix, col_ref, source, target, *sums[tick % 2]
        )
        arrived = count - 1 - tick
        pulled = target[own_in_window, 0], target[own_in_window, 1]
        grad_ref[arrived] = -(pulled[1] * moved_ref[arrived, 0] + pulled[0] * moved_ref[arrived, 1])

    source = waves[(2 * count) % 2]
    left, right = jnp.maximum(own_place - 1, 0), jnp.minimum(own_place + 1, blocks - 1)
    lane = lax.broadcasted_iota(jnp.int32, (2 * height, LANES), 1)
    has_left, has_right = own_place > 0, own_place < blocks - 1

    def cells(block):
        return jnp.concatenate(block_turned(1, block, screens, source, block - window_start), axis=0)

    edge_cells = jnp.where(
        lane < LANES // 2, jnp.where(has_right, cells(right), 0.0), jnp.where(has_left, cells(left), 0.0)
    )
    done = row_product(row_matrix, jnp.concatenate([cells(own_place), edge_cells], axis=1))
    quarters = [
        done[part * height : (part + 1) * height, sub * LANES : (sub + 1) * LANES]
        for sub in range(2)
        for part in range(2)
    ]
    high, low = halves(jnp.concatenate(quarters, axis=1))
    pulled = col_product(high, low, col_ref[: 4 * LANES], col_ref[4 * LANES :])
    grad_ref[0] = -(pulled[:, LANES:] * moved_ref[0, 0] + pulled[:, :LANES] * moved_ref[0, 1])

    for target, row in ((mine_ref, near), (theirs_ref, far)):
        for part in range(2):
            target[0, part] = left_ref[own_section, part, row]
        target[0, 2] = grad_ref[own_section, row]


def finish_kernel(mine_ref, received_ref, grad_ref, exit_ref, total_ref, sems):
    core = lax.axis_index("row")
    copies = []
    for source, item in ((mine_ref, core), (received_ref, 1 - core)):
        copies.append(pltpu.make_async_copy(source.at[:, pl.ds(0, 2)], exit_ref.at[item], sems.at[len(copies)]))
    for copy in copies:
        copy.start()
    total_ref[...] = mine_ref[:, 2] + received_ref[:, 2]
    copies.append(pltpu.make_async_copy(total_ref, grad_ref, sems.at[2]))
    copies[2].start()
    for copy in copies:
        copy.wait()


def spread(shard, axis, reach=None):
    size = lax.axis_size(axis)
    reach = size if reach is None else reach
    pieces = []
    for bits in range(1, size):
        pairs = [(i, i ^ bits) for i in range(size) if abs(i - (i ^ bits)) <= reach]
        pieces.append(lax.ppermute(shard, axis, pairs) if pairs else jnp.zeros_like(shard))
    return pieces


def swap_cores(value):
    return lax.ppermute(value, "row", [(0, 1), (1, 0)])


def whole_field_body(phase, tilt, intensity):
    _, tile_r, tile_c = phase.shape
    count, blocks = lax.axis_size("depth"), lax.axis_size("col")
    core = lax.axis_index("row")
    height = 2 * tile_r
    vmem = pl.BlockSpec(memory_space=pltpu.VMEM)
    smem = pl.BlockSpec(memory_space=pltpu.SMEM)
    hbm = pl.BlockSpec(memory_space=pl.ANY)

    def array(*shape):
        return jax.ShapeDtypeStruct(shape, jnp.float32)

    def params(mebibytes):
        return pltpu.CompilerParams(vmem_limit_bytes=mebibytes * 2**20)

    other_depths = spread(phase, "depth")
    other_depths[0], measured, slab = lax.optimization_barrier((other_depths[0], intensity, phase))
    other_depths = jnp.concatenate(other_depths, axis=0)
    packet = jnp.concatenate([slab, measured], axis=0)
    near_own = [packet]
    for bits in range(1, blocks):
        pairs = [(i, i ^ bits) for i in range(blocks)]
        close = [(i, j) for i, j in pairs if abs(i - j) <= 1]
        if close:
            near_own.append(lax.ppermute(packet, "col", close))
        else:
            further = [(i, j) for i, j in pairs if abs(i - j) <= 2]
            arrived = lax.ppermute(slab, "col", further) if further else jnp.zeros_like(slab)
            near_own.append(jnp.concatenate([arrived, jnp.zeros_like(measured)], axis=0))
    near_own = jnp.stack(near_own)
    arriving = spread(other_depths, "col", 2)
    arriving[0], near_own = lax.optimization_barrier((arriving[0], near_own))
    near_rest = jnp.stack([other_depths] + arriving)
    wanted = lax.dynamic_slice_in_dim(near_own, 2 - core, 1, 1)
    far_own = swap_cores(jnp.concatenate([near_own[:, :1], wanted], axis=1))
    far_rest = swap_cores(near_rest)

    half_screens = (count + 1, blocks, tile_r, tile_c)
    field = (blocks, 2, height, tile_c)
    wave, near_cos, near_sin = pl.pallas_call(
        prepare_kernel,
        out_shape=(array(*field), array(*half_screens), array(*half_screens)),
        in_specs=[smem, vmem, vmem],
        out_specs=(vmem,) * 3,
        compiler_params=params(8),
        cost_estimate=pl.CostEstimate(flops=5 * 10**8, bytes_accessed=2**20, transcendentals=0),
    )(tilt, near_own, near_rest)
    mine, theirs = pl.pallas_call(
        wave_kernel,
        out_shape=(array(1, 3, tile_r, tile_c),) * 2,
        in_specs=[vmem] * 8,
        out_specs=(vmem,) * 2,
        scratch_shapes=[pltpu.VMEM(half_screens, jnp.float32)] * 2
        + [pltpu.VMEM(field, jnp.float32)] * 2
        + [pltpu.VMEM((count, 2, height, tile_c), jnp.float32)] * 2
        + [pltpu.VMEM((count, height, tile_c), jnp.float32)]
        + [pltpu.VMEM((blocks, height, 4 * LANES), jnp.bfloat16)] * 4,
        compiler_params=params(24),
    )(
        wave, near_cos, near_sin, near_own, far_own, far_rest,
        jnp.asarray(row_constant(height)), jnp.asarray(col_constant()),
    )
    return pl.pallas_call(
        finish_kernel,
        out_shape=(array(*phase.shape), array(2, 1, 2, tile_r, tile_c)),
        in_specs=[vmem, vmem],
        out_specs=(hbm, hbm),
        scratch_shapes=[pltpu.VMEM(phase.shape, jnp.float32), pltpu.SemaphoreType.DMA((3,))],
        compiler_params=params(4),
    )(mine, swap_cores(theirs))


def extended_2(cells, sides, width):
    for axis, dim in sides:
        count = lax.axis_size(axis)
        ends = count - 1
        head = lax.slice_in_dim(cells, 0, width, axis=dim)
        tail = lax.slice_in_dim(cells, cells.shape[dim] - width, cells.shape[dim], axis=dim)
        cells = jnp.concatenate(
            [
                lax.ppermute(tail, axis, [(i, (i + 1) % count) for i in range(ends)]),
                cells,
                lax.ppermute(head, axis, [((i + 1) % count, i) for i in range(ends)]),
            ],
            axis=dim,
        )
    return cells


def from_behind(value, axis, steps):
    count = lax.axis_size(axis)
    leading, last = (max(0, -steps), min(count, count - steps))
    return lax.ppermute(value, axis, [(source, source + steps) for source in range(leading, last)])


def band_matrix(block_size, margin, fresnel, adjoint):
    shape_full = (block_size, block_size + 2 * margin)
    out_idx = lax.broadcasted_iota(jnp.int32, shape_full, 0)
    in_idx = lax.broadcasted_iota(jnp.int32, shape_full, 1)
    offset = (out_idx + margin - in_idx).astype(jnp.float32)
    inside = jnp.abs(offset) <= margin
    taper_dist = jnp.maximum(jnp.abs(offset) - 0.5 * margin, 0.0)
    profile = jnp.cos(jnp.pi * taper_dist / (margin + 2.0))
    weight = profile * profile / math.sqrt(fresnel)
    phase_angle = jnp.pi * offset * offset / fresnel
    real_part = jnp.where(inside, jnp.cos(phase_angle) * weight, 0.0)
    imag_part = jnp.where(inside, jnp.sin(phase_angle) * weight, 0.0)
    if adjoint:
        imag_part = -imag_part
    upper = jnp.stack([real_part, -imag_part])
    lower = jnp.stack([imag_part, real_part])
    return jnp.stack([upper, lower])


def along_rows(extended, matrix):
    pieces = [jnp.einsum("pqij,gqjc->gpic", matrix, extended, precision=lax.Precision.HIGHEST)]
    return jnp.concatenate(pieces, axis=2)


def along_cols(extended, matrix, margin):
    block_size = matrix.shape[2]
    extent = extended.shape[3] - 2 * margin
    pieces = []
    for block_start in range(0, extent, block_size):
        window = extended[:, :, :, block_start : block_start + block_size + 2 * margin]
        pieces.append(
            jnp.einsum("pqij,gqrj->gpri", matrix, window, precision=lax.Precision.HIGHEST)
        )
    return jnp.concatenate(pieces, axis=3)


def propagate(current, row_matrix, col_matrix):
    with_rows = extended_2(current, (("row", 2),), HALO)
    row_done = along_rows(with_rows, row_matrix)
    with_cols = extended_2(row_done, (("col", 3),), HALO)
    return along_cols(with_cols, col_matrix, HALO)


def transmit(screen, current, adjoint):
    screen_re = screen[0][None]
    screen_im = screen[1][None]
    if adjoint:
        screen_im = -screen_im
    real_part = screen_re * current[:, 0] - screen_im * current[:, 1]
    imag_part = screen_re * current[:, 1] + screen_im * current[:, 0]
    return jnp.stack([real_part, imag_part], axis=1)


def store_item(store, current, first_item, slice_index, active):
    begin = (first_item, jnp.int32(slice_index), jnp.int32(0), jnp.int32(0), jnp.int32(0))
    sizes_now = (current.shape[0], 1) + current.shape[1:]
    previous = lax.dynamic_slice(store, begin, sizes_now)
    fresh = jnp.where(active, current[:, None], previous)
    return lax.dynamic_update_slice(store, fresh, begin)


def staged_body(phase, tilt, intensity):
    slices, tile_r, tile_c = phase.shape
    batch_size = tilt.shape[0]
    sections = lax.axis_size("depth")
    section_index = lax.axis_index("depth")
    group_size = 1
    groups = batch_size // group_size
    tick_count = sections + groups - 1
    block_r = 64
    block_c = 128
    fwd_rows = band_matrix(block_r, HALO, FRESNEL, False)
    fwd_cols = band_matrix(block_c, HALO, FRESNEL, False)
    adj_rows = band_matrix(block_r, HALO, FRESNEL, True)
    adj_cols = band_matrix(block_c, HALO, FRESNEL, True)
    row_pos = (
        lax.axis_index("row") * tile_r + lax.broadcasted_iota(jnp.int32, (tile_r, tile_c), 0)
    ).astype(jnp.float32)
    col_pos = (
        lax.axis_index("col") * tile_c + lax.broadcasted_iota(jnp.int32, (tile_r, tile_c), 1)
    ).astype(jnp.float32)
    height = float(tile_r * lax.axis_size("row"))
    width_all = float(tile_c * lax.axis_size("col"))
    tilt_f = tilt.astype(jnp.float32)
    phase_angle = (
        2.0
        * jnp.pi
        * (
            tilt_f[:, 0, None, None] * row_pos / height
            + tilt_f[:, 1, None, None] * col_pos / width_all
        )
    )
    incident = jnp.stack([jnp.cos(phase_angle), jnp.sin(phase_angle)], axis=1)
    screens = jnp.stack([jnp.cos(phase), jnp.sin(phase)], axis=1)

    def forward_tick(tick_now, carry):
        incoming, entering, leaving = carry
        group_index = tick_now - section_index
        active = (group_index >= 0) & (group_index < groups)
        first_item = jnp.clip(group_index, 0, groups - 1) * group_size
        current = jnp.where(
            section_index == 0,
            lax.dynamic_slice_in_dim(incident, first_item, group_size, 0),
            incoming,
        )
        entering = store_item(entering, current, first_item, 0, active)
        current = propagate(transmit(screens[0], current, False), fwd_rows, fwd_cols)
        leaving = store_item(leaving, current, first_item, 0, active)
        incoming = from_behind(current, "depth", 1)
        return (incoming, entering, leaving)

    store_zero = jnp.zeros((batch_size, slices, 2, tile_r, tile_c), jnp.float32)
    start_wave = jnp.zeros((group_size, 2, tile_r, tile_c), jnp.float32)
    _, entering, leaving = lax.fori_loop(
        0, tick_count, forward_tick, (start_wave, store_zero, store_zero)
    )
    final_wave = leaving[:, slices - 1]
    misfit = final_wave[:, 0] * final_wave[:, 0] + final_wave[:, 1] * final_wave[:, 1] - intensity
    seed_adjoint = 2.0 * misfit[:, None] * final_wave

    def backward_tick(tick_now, carry):
        incoming, gradient = carry
        group_index = tick_now - (sections - 1 - section_index)
        active = (group_index >= 0) & (group_index < groups)
        first_item = jnp.clip(group_index, 0, groups - 1) * group_size
        adjoint_wave = jnp.where(
            section_index == sections - 1,
            lax.dynamic_slice_in_dim(seed_adjoint, first_item, group_size, 0),
            incoming,
        )
        for slice_index in reversed(range(slices)):
            pulled = propagate(adjoint_wave, adj_rows, adj_cols)
            arrived = lax.dynamic_slice_in_dim(entering[:, slice_index], first_item, group_size, 0)
            moved = transmit(screens[slice_index], arrived, False)
            contribution = jnp.sum(pulled[:, 1] * moved[:, 0] - pulled[:, 0] * moved[:, 1], axis=0)
            gradient = gradient.at[slice_index].add(jnp.where(active, contribution, 0.0))
            adjoint_wave = transmit(screens[slice_index], pulled, True)
        incoming = from_behind(adjoint_wave, "depth", -1)
        return (incoming, gradient)

    grad_zero = jnp.zeros((slices, tile_r, tile_c), jnp.float32)
    _, gradient = lax.fori_loop(0, tick_count, backward_tick, (start_wave, grad_zero))
    return (gradient, leaving)


def fits_whole(phase_shape, batch, mesh):
    slices, height, width = phase_shape
    rows, cols, sections = mesh.shape["row"], mesh.shape["col"], mesh.shape["depth"]
    return (
        4 * height * width * (slices + batch) <= GATHER_BUDGET
        and batch == rows == 2
        and slices == sections
        and sections & (sections - 1) == 0
        and cols & (cols - 1) == 0
        and height == LANES
        and width == cols * LANES
        and cols > 1
        and sections > 1
        and sections * HALO <= LANES
    )


def solution(mesh):
    placed = (P("depth", "row", "col"), P(), P(None, "row", "col"))

    def run(phase, tilt, intensity):
        if fits_whole(phase.shape, tilt.shape[0], mesh):
            body = whole_field_body
        else:
            body = staged_body
        return jax.shard_map(
            body,
            mesh=mesh,
            in_specs=placed,
            out_specs=(P("depth", "row", "col"), P(None, "depth", None, "row", "col")),
            check_vma=False,
        )(phase, tilt, intensity)

    return run
```

```python
import math

import jax
import jax.numpy as jnp
import numpy as np
from jax import lax
from jax.experimental import pallas as pl
from jax.experimental.pallas import tpu as pltpu
from jax.sharding import PartitionSpec as P

HALO = 32
FRESNEL = 64
LANES = 128
GATHER_BUDGET = 4 * 2**20
SIN = (
    0.9999999980536763,
    -0.1666666530009577,
    0.008333305907073658,
    -0.00019838908256358006,
    2.745822627876341e-06,
    -2.3043562782810933e-08,
)
COS = (
    0.9999999961345007,
    -0.4999999301617528,
    0.04166646215023687,
    -0.0013886696163545999,
    2.4695045482778703e-05,
    -2.5154931690000354e-07,
)


def horner(coefficients, square):
    total = jnp.full_like(square, coefficients[-1])
    for coefficient in coefficients[-2::-1]:
        total = total * square + coefficient
    return total


def cos_sin(angle):
    square = angle * angle
    return horner(COS, square), horner(SIN, square) * angle


def turn(fraction):
    half_cos, half_sin = cos_sin(fraction * math.pi)
    return half_cos * half_cos - half_sin * half_sin, 2.0 * half_cos * half_sin


def halves(value):
    high = value.astype(jnp.bfloat16)
    return high, (value - high.astype(jnp.float32)).astype(jnp.bfloat16)


def np_halves(matrix):
    high = matrix.astype(jnp.bfloat16)
    return high, (matrix - high.astype(np.float64)).astype(jnp.bfloat16)


def np_taps():
    offset = np.arange(-HALO, HALO + 1, dtype=np.float64)
    taper = np.maximum(np.abs(offset) - 0.5 * HALO, 0.0)
    weight = np.cos(np.pi * taper / (HALO + 2.0)) ** 2 / math.sqrt(FRESNEL)
    return weight * np.exp(1j * np.pi * offset * offset / FRESNEL)


def np_band(out_pos, in_pos):
    offset = out_pos[:, None] - in_pos[None, :]
    inside = np.abs(offset) <= HALO
    return np.where(inside, np_taps()[np.clip(offset, -HALO, HALO) + HALO], 0.0)


def row_constant(height):
    matrices = []
    for core in range(2):
        pos = (np.arange(height) + core * (height // 2)) % height
        band = np_band(pos, pos)
        whole = np.block([[band.real, -band.imag], [band.imag, band.real]])
        matrices.append(np.concatenate(np_halves(whole), axis=1))
    return np.stack(matrices)


def col_constant():
    lane = np.arange(LANES)
    edge_pos = np.where(lane < LANES // 2, lane + LANES, lane - LANES)
    parts = []
    for position in (lane, edge_pos):
        band = np_band(lane, position).T
        parts.append(np.block([[band.real, band.imag], [-band.imag, band.real]]))
    high, low = np_halves(np.concatenate(parts, axis=0))
    return np.concatenate([high, low], axis=0)


def both_rows(near_ref, far_ref, where):
    return jnp.concatenate([near_ref[where], far_ref[where]], axis=0)


def block_turned(slice_index, block, screens, wave_ref, place):
    near_cos, near_sin, far_cos, far_sin = screens
    cos = both_rows(near_cos, far_cos, (slice_index, block))
    sin = both_rows(near_sin, far_sin, (slice_index, block))
    real, imag = wave_ref[place, 0], wave_ref[place, 1]
    return cos * real - sin * imag, cos * imag + sin * real


def row_product(row_matrix, columns):
    high, low = halves(columns)
    whole = row_matrix.shape[0]
    return jnp.dot(
        jnp.concatenate([row_matrix[:, :whole], row_matrix], axis=1),
        jnp.concatenate([high, low, high], axis=0),
        preferred_element_type=jnp.float32,
    )


def col_product(high, low, col_high, col_low):
    return jnp.dot(
        jnp.concatenate([high, low, high], axis=1),
        jnp.concatenate([col_high, col_high, col_low], axis=0),
        preferred_element_type=jnp.float32,
    )


def advance(slice_index, start, size, screens, row_matrix, col_ref, from_ref, to_ref, a_high, a_low):
    height = from_ref.shape[2]
    half = LANES // 2
    columns = [
        jnp.concatenate(block_turned(slice_index, start + place, screens, from_ref, place), axis=0)
        for place in range(size)
    ]
    done = row_product(row_matrix, jnp.concatenate(columns, axis=1))
    for place in range(size):
        for part in range(2):
            value = done[part * height : (part + 1) * height, place * LANES : (place + 1) * LANES]
            for target, piece in zip((a_high, a_low), halves(value)):
                target[place, :, pl.ds(part * LANES, LANES)] = piece
                if place > 0:
                    target[place - 1, :, pl.ds((2 + part) * LANES, half)] = piece[:, :half]
                if place < size - 1:
                    target[place + 1, :, pl.ds((2 + part) * LANES + half, half)] = piece[:, half:]
    cells, rows = pl.ds(0, size), size * height
    total = col_product(
        a_high[cells].reshape(rows, 4 * LANES),
        a_low[cells].reshape(rows, 4 * LANES),
        col_ref[: 4 * LANES],
        col_ref[4 * LANES :],
    )
    for place in range(size):
        for part in range(2):
            to_ref[place, part] = total[place * height : (place + 1) * height, part * LANES : (part + 1) * LANES]


def clear_edge(a_ref, place, right):
    half = LANES // 2
    for part in range(2):
        begin = (2 + part) * LANES + (0 if right else half)
        a_ref[place, :, pl.ds(begin, half)] = jnp.zeros((a_ref.shape[1], half), a_ref.dtype)


def prepare_kernel(tilt_ref, near_own, near_rest, wave_ref, cos_ref, sin_ref):
    blocks, _, height, _ = wave_ref.shape
    count = cos_ref.shape[0] - 1
    core, own_section, own_place = lax.axis_index("row"), lax.axis_index("depth"), lax.axis_index("col")

    def screens(col, carry):
        held = col ^ own_place
        for bits in range(count):
            angle = near_own[held, 0] if bits == 0 else near_rest[held, bits - 1]
            cos_ref[bits ^ own_section, col], sin_ref[bits ^ own_section, col] = cos_sin(angle)
        return carry

    lax.fori_loop(0, blocks, screens, 0)
    cos_ref[count] = jnp.ones(cos_ref.shape[1:], jnp.float32)
    sin_ref[count] = jnp.zeros(cos_ref.shape[1:], jnp.float32)

    def cycles(number, position, extent):
        fraction = (number * position).astype(jnp.float32) / extent
        return turn(fraction - jnp.round(fraction))

    row = lax.broadcasted_iota(jnp.int32, (height, LANES), 0) + core * (height // 2)
    row = jnp.where(row >= height, row - height, row)
    row_cos, row_sin = cycles(tilt_ref[core, 0], row, float(height))
    for block in range(blocks):
        col_cos, col_sin = cycles(
            tilt_ref[core, 1],
            lax.broadcasted_iota(jnp.int32, (8, LANES), 1) + block * LANES,
            float(blocks * LANES),
        )
        col_cos, col_sin = col_cos[:1], col_sin[:1]
        wave_ref[block, 0] = row_cos * col_cos - row_sin * col_sin
        wave_ref[block, 1] = row_sin * col_cos + row_cos * col_sin


def wave_kernel(
    wave_ref, near_cos, near_sin, near_own, far_own, far_rest, row_ref, col_ref,
    mine_ref, theirs_ref, far_cos, far_sin, even_ref, odd_ref, moved_ref, left_ref, grad_ref,
    even_high, even_low, odd_high, odd_low,
):
    blocks, _, height, _ = wave_ref.shape
    count = near_cos.shape[0] - 1
    core, own_section, own_place = lax.axis_index("row"), lax.axis_index("depth"), lax.axis_index("col")
    near, far = pl.ds(0, height // 2), pl.ds(height // 2, height // 2)
    screens = (near_cos, near_sin, far_cos, far_sin)
    row_matrix = row_ref[core]
    window = min(3, blocks)
    window_start = jnp.clip(own_place - 1, 0, blocks - window)
    own_in_window = own_place - window_start
    waves = (even_ref, odd_ref)
    sums = ((even_high, even_low), (odd_high, odd_low))

    def far_screens(slice_index):
        bits = slice_index ^ own_section
        for col in range(blocks):
            held = col ^ own_place
            angle = jnp.where(bits == 0, far_own[held, 0], far_rest[held, jnp.maximum(bits - 1, 0)])
            far_cos[slice_index, col], far_sin[slice_index, col] = cos_sin(angle)

    for pair in sums:
        for target in pair:
            clear_edge(target, 0, False)
            clear_edge(target, blocks - 1, True)
    far_cos[count] = jnp.ones(far_cos.shape[1:], jnp.float32)
    far_sin[count] = jnp.zeros(far_cos.shape[1:], jnp.float32)
    far_screens(0)

    for tick in range(count):
        source, target = wave_ref if tick == 0 else waves[tick % 2], waves[(tick + 1) % 2]
        moved_ref[tick, 0], moved_ref[tick, 1] = block_turned(tick, own_place, screens, source, own_place)
        advance(tick, 0, blocks, screens, row_matrix, col_ref, source, target, *sums[tick % 2])
        if tick + 1 < count:
            far_screens(tick + 1)
        left_ref[tick] = target[own_place]

    last = waves[count % 2]
    source = waves[(count + 1) % 2]
    for pair in sums:
        for target in pair:
            clear_edge(target, window - 1, True)
    for place in range(window):
        block = window_start + place
        held = block ^ own_place
        measured = jnp.concatenate([near_own[held, 1 + core], far_own[held, 1]], axis=0)
        real, imag = last[block, 0], last[block, 1]
        misfit = 2.0 * (real * real + imag * imag - measured)
        source[place, 0] = misfit * real
        source[place, 1] = -misfit * imag

    for tick in range(count - 1):
        source, target = waves[(count + 1 + tick) % 2], waves[(count + tick) % 2]
        advance(
            count - tick, window_start, window, screens, row_matrix, col_ref, source, target, *sums[tick % 2]
        )
        arrived = count - 1 - tick
        pulled = target[own_in_window, 0], target[own_in_window, 1]
        grad_ref[arrived] = -(pulled[1] * moved_ref[arrived, 0] + pulled[0] * moved_ref[arrived, 1])

    source = waves[(2 * count) % 2]
    left, right = jnp.maximum(own_place - 1, 0), jnp.minimum(own_place + 1, blocks - 1)
    lane = lax.broadcasted_iota(jnp.int32, (2 * height, LANES), 1)
    has_left, has_right = own_place > 0, own_place < blocks - 1

    def cells(block):
        return jnp.concatenate(block_turned(1, block, screens, source, block - window_start), axis=0)

    edge_cells = jnp.where(
        lane < LANES // 2, jnp.where(has_right, cells(right), 0.0), jnp.where(has_left, cells(left), 0.0)
    )
    done = row_product(row_matrix, jnp.concatenate([cells(own_place), edge_cells], axis=1))
    quarters = [
        done[part * height : (part + 1) * height, sub * LANES : (sub + 1) * LANES]
        for sub in range(2)
        for part in range(2)
    ]
    high, low = halves(jnp.concatenate(quarters, axis=1))
    pulled = col_product(high, low, col_ref[: 4 * LANES], col_ref[4 * LANES :])
    grad_ref[0] = -(pulled[:, LANES:] * moved_ref[0, 0] + pulled[:, :LANES] * moved_ref[0, 1])

    for target, row in ((mine_ref, near), (theirs_ref, far)):
        for part in range(2):
            target[0, part] = left_ref[own_section, part, row]
        target[0, 2] = grad_ref[own_section, row]


def finish_kernel(mine_ref, received_ref, grad_ref, exit_ref, total_ref, sems):
    core = lax.axis_index("row")
    copies = []
    for source, item in ((mine_ref, core), (received_ref, 1 - core)):
        copies.append(pltpu.make_async_copy(source.at[:, pl.ds(0, 2)], exit_ref.at[item], sems.at[len(copies)]))
    for copy in copies:
        copy.start()
    total_ref[...] = mine_ref[:, 2] + received_ref[:, 2]
    copies.append(pltpu.make_async_copy(total_ref, grad_ref, sems.at[2]))
    copies[2].start()
    for copy in copies:
        copy.wait()


def spread(shard, axis, reach=None):
    size = lax.axis_size(axis)
    reach = size if reach is None else reach
    pieces = []
    for bits in range(1, size):
        pairs = [(i, i ^ bits) for i in range(size) if abs(i - (i ^ bits)) <= reach]
        pieces.append(lax.ppermute(shard, axis, pairs) if pairs else jnp.zeros_like(shard))
    return pieces


def swap_cores(value):
    return lax.ppermute(value, "row", [(0, 1), (1, 0)])


def whole_field_body(phase, tilt, intensity):
    _, tile_r, tile_c = phase.shape
    count, blocks = lax.axis_size("depth"), lax.axis_size("col")
    core = lax.axis_index("row")
    height = 2 * tile_r
    vmem = pl.BlockSpec(memory_space=pltpu.VMEM)
    smem = pl.BlockSpec(memory_space=pltpu.SMEM)
    hbm = pl.BlockSpec(memory_space=pl.ANY)

    def array(*shape):
        return jax.ShapeDtypeStruct(shape, jnp.float32)

    def params(mebibytes):
        return pltpu.CompilerParams(vmem_limit_bytes=mebibytes * 2**20)

    other_depths = spread(phase, "depth")
    other_depths[0], measured, slab = lax.optimization_barrier((other_depths[0], intensity, phase))
    other_depths = jnp.concatenate(other_depths, axis=0)
    packet = jnp.concatenate([slab, measured], axis=0)
    near_own = [packet]
    for bits in range(1, blocks):
        pairs = [(i, i ^ bits) for i in range(blocks)]
        close = [(i, j) for i, j in pairs if abs(i - j) <= 1]
        if close:
            near_own.append(lax.ppermute(packet, "col", close))
        else:
            further = [(i, j) for i, j in pairs if abs(i - j) <= 2]
            arrived = lax.ppermute(slab, "col", further) if further else jnp.zeros_like(slab)
            near_own.append(jnp.concatenate([arrived, jnp.zeros_like(measured)], axis=0))
    near_own = jnp.stack(near_own)
    arriving = spread(other_depths, "col", 2)
    arriving[0], near_own = lax.optimization_barrier((arriving[0], near_own))
    near_rest = jnp.stack([other_depths] + arriving)
    wanted = lax.dynamic_slice_in_dim(near_own, 2 - core, 1, 1)
    far_own = swap_cores(jnp.concatenate([near_own[:, :1], wanted], axis=1))
    far_rest = swap_cores(near_rest)

    half_screens = (count + 1, blocks, tile_r, tile_c)
    field = (blocks, 2, height, tile_c)
    wave, near_cos, near_sin = pl.pallas_call(
        prepare_kernel,
        out_shape=(array(*field), array(*half_screens), array(*half_screens)),
        in_specs=[smem, vmem, vmem],
        out_specs=(vmem,) * 3,
        compiler_params=params(8),
        cost_estimate=pl.CostEstimate(flops=5 * 10**8, bytes_accessed=2**20, transcendentals=0),
    )(tilt, near_own, near_rest)
    mine, theirs = pl.pallas_call(
        wave_kernel,
        out_shape=(array(1, 3, tile_r, tile_c),) * 2,
        in_specs=[vmem] * 8,
        out_specs=(vmem,) * 2,
        scratch_shapes=[pltpu.VMEM(half_screens, jnp.float32)] * 2
        + [pltpu.VMEM(field, jnp.float32)] * 2
        + [pltpu.VMEM((count, 2, height, tile_c), jnp.float32)] * 2
        + [pltpu.VMEM((count, height, tile_c), jnp.float32)]
        + [pltpu.VMEM((blocks, height, 4 * LANES), jnp.bfloat16)] * 4,
        compiler_params=params(24),
    )(
        wave, near_cos, near_sin, near_own, far_own, far_rest,
        jnp.asarray(row_constant(height)), jnp.asarray(col_constant()),
    )
    return pl.pallas_call(
        finish_kernel,
        out_shape=(array(*phase.shape), array(2, 1, 2, tile_r, tile_c)),
        in_specs=[vmem, vmem],
        out_specs=(hbm, hbm),
        scratch_shapes=[pltpu.VMEM(phase.shape, jnp.float32), pltpu.SemaphoreType.DMA((3,))],
        compiler_params=params(4),
    )(mine, swap_cores(theirs))


def extended_2(cells, sides, width):
    for axis, dim in sides:
        count = lax.axis_size(axis)
        ends = count - 1
        head = lax.slice_in_dim(cells, 0, width, axis=dim)
        tail = lax.slice_in_dim(cells, cells.shape[dim] - width, cells.shape[dim], axis=dim)
        cells = jnp.concatenate(
            [
                lax.ppermute(tail, axis, [(i, (i + 1) % count) for i in range(ends)]),
                cells,
                lax.ppermute(head, axis, [((i + 1) % count, i) for i in range(ends)]),
            ],
            axis=dim,
        )
    return cells


def from_behind(value, axis, steps):
    count = lax.axis_size(axis)
    leading, last = (max(0, -steps), min(count, count - steps))
    return lax.ppermute(value, axis, [(source, source + steps) for source in range(leading, last)])


def band_matrix(block_size, margin, fresnel, adjoint):
    shape_full = (block_size, block_size + 2 * margin)
    out_idx = lax.broadcasted_iota(jnp.int32, shape_full, 0)
    in_idx = lax.broadcasted_iota(jnp.int32, shape_full, 1)
    offset = (out_idx + margin - in_idx).astype(jnp.float32)
    inside = jnp.abs(offset) <= margin
    taper_dist = jnp.maximum(jnp.abs(offset) - 0.5 * margin, 0.0)
    profile = jnp.cos(jnp.pi * taper_dist / (margin + 2.0))
    weight = profile * profile / math.sqrt(fresnel)
    phase_angle = jnp.pi * offset * offset / fresnel
    real_part = jnp.where(inside, jnp.cos(phase_angle) * weight, 0.0)
    imag_part = jnp.where(inside, jnp.sin(phase_angle) * weight, 0.0)
    if adjoint:
        imag_part = -imag_part
    upper = jnp.stack([real_part, -imag_part])
    lower = jnp.stack([imag_part, real_part])
    return jnp.stack([upper, lower])


def along_rows(extended, matrix):
    pieces = [jnp.einsum("pqij,gqjc->gpic", matrix, extended, precision=lax.Precision.HIGHEST)]
    return jnp.concatenate(pieces, axis=2)


def along_cols(extended, matrix, margin):
    block_size = matrix.shape[2]
    extent = extended.shape[3] - 2 * margin
    pieces = []
    for block_start in range(0, extent, block_size):
        window = extended[:, :, :, block_start : block_start + block_size + 2 * margin]
        pieces.append(
            jnp.einsum("pqij,gqrj->gpri", matrix, window, precision=lax.Precision.HIGHEST)
        )
    return jnp.concatenate(pieces, axis=3)


def propagate(current, row_matrix, col_matrix):
    with_rows = extended_2(current, (("row", 2),), HALO)
    row_done = along_rows(with_rows, row_matrix)
    with_cols = extended_2(row_done, (("col", 3),), HALO)
    return along_cols(with_cols, col_matrix, HALO)


def transmit(screen, current, adjoint):
    screen_re = screen[0][None]
    screen_im = screen[1][None]
    if adjoint:
        screen_im = -screen_im
    real_part = screen_re * current[:, 0] - screen_im * current[:, 1]
    imag_part = screen_re * current[:, 1] + screen_im * current[:, 0]
    return jnp.stack([real_part, imag_part], axis=1)


def store_item(store, current, first_item, slice_index, active):
    begin = (first_item, jnp.int32(slice_index), jnp.int32(0), jnp.int32(0), jnp.int32(0))
    sizes_now = (current.shape[0], 1) + current.shape[1:]
    previous = lax.dynamic_slice(store, begin, sizes_now)
    fresh = jnp.where(active, current[:, None], previous)
    return lax.dynamic_update_slice(store, fresh, begin)


def staged_body(phase, tilt, intensity):
    slices, tile_r, tile_c = phase.shape
    batch_size = tilt.shape[0]
    sections = lax.axis_size("depth")
    section_index = lax.axis_index("depth")
    group_size = 1
    groups = batch_size // group_size
    tick_count = sections + groups - 1
    block_r = 64
    block_c = 128
    fwd_rows = band_matrix(block_r, HALO, FRESNEL, False)
    fwd_cols = band_matrix(block_c, HALO, FRESNEL, False)
    adj_rows = band_matrix(block_r, HALO, FRESNEL, True)
    adj_cols = band_matrix(block_c, HALO, FRESNEL, True)
    row_pos = (
        lax.axis_index("row") * tile_r + lax.broadcasted_iota(jnp.int32, (tile_r, tile_c), 0)
    ).astype(jnp.float32)
    col_pos = (
        lax.axis_index("col") * tile_c + lax.broadcasted_iota(jnp.int32, (tile_r, tile_c), 1)
    ).astype(jnp.float32)
    height = float(tile_r * lax.axis_size("row"))
    width_all = float(tile_c * lax.axis_size("col"))
    tilt_f = tilt.astype(jnp.float32)
    phase_angle = (
        2.0
        * jnp.pi
        * (
            tilt_f[:, 0, None, None] * row_pos / height
            + tilt_f[:, 1, None, None] * col_pos / width_all
        )
    )
    incident = jnp.stack([jnp.cos(phase_angle), jnp.sin(phase_angle)], axis=1)
    screens = jnp.stack([jnp.cos(phase), jnp.sin(phase)], axis=1)

    def forward_tick(tick_now, carry):
        incoming, entering, leaving = carry
        group_index = tick_now - section_index
        active = (group_index >= 0) & (group_index < groups)
        first_item = jnp.clip(group_index, 0, groups - 1) * group_size
        current = jnp.where(
            section_index == 0,
            lax.dynamic_slice_in_dim(incident, first_item, group_size, 0),
            incoming,
        )
        entering = store_item(entering, current, first_item, 0, active)
        current = propagate(transmit(screens[0], current, False), fwd_rows, fwd_cols)
        leaving = store_item(leaving, current, first_item, 0, active)
        incoming = from_behind(current, "depth", 1)
        return (incoming, entering, leaving)

    store_zero = jnp.zeros((batch_size, slices, 2, tile_r, tile_c), jnp.float32)
    start_wave = jnp.zeros((group_size, 2, tile_r, tile_c), jnp.float32)
    _, entering, leaving = lax.fori_loop(
        0, tick_count, forward_tick, (start_wave, store_zero, store_zero)
    )
    final_wave = leaving[:, slices - 1]
    misfit = final_wave[:, 0] * final_wave[:, 0] + final_wave[:, 1] * final_wave[:, 1] - intensity
    seed_adjoint = 2.0 * misfit[:, None] * final_wave

    def backward_tick(tick_now, carry):
        incoming, gradient = carry
        group_index = tick_now - (sections - 1 - section_index)
        active = (group_index >= 0) & (group_index < groups)
        first_item = jnp.clip(group_index, 0, groups - 1) * group_size
        adjoint_wave = jnp.where(
            section_index == sections - 1,
            lax.dynamic_slice_in_dim(seed_adjoint, first_item, group_size, 0),
            incoming,
        )
        for slice_index in reversed(range(slices)):
            pulled = propagate(adjoint_wave, adj_rows, adj_cols)
            arrived = lax.dynamic_slice_in_dim(entering[:, slice_index], first_item, group_size, 0)
            moved = transmit(screens[slice_index], arrived, False)
            contribution = jnp.sum(pulled[:, 1] * moved[:, 0] - pulled[:, 0] * moved[:, 1], axis=0)
            gradient = gradient.at[slice_index].add(jnp.where(active, contribution, 0.0))
            adjoint_wave = transmit(screens[slice_index], pulled, True)
        incoming = from_behind(adjoint_wave, "depth", -1)
        return (incoming, gradient)

    grad_zero = jnp.zeros((slices, tile_r, tile_c), jnp.float32)
    _, gradient = lax.fori_loop(0, tick_count, backward_tick, (start_wave, grad_zero))
    return (gradient, leaving)


def fits_whole(phase_shape, batch, mesh):
    slices, height, width = phase_shape
    rows, cols, sections = mesh.shape["row"], mesh.shape["col"], mesh.shape["depth"]
    return (
        4 * height * width * (slices + batch) <= GATHER_BUDGET
        and batch == rows == 2
        and slices == sections
        and sections & (sections - 1) == 0
        and cols & (cols - 1) == 0
        and height == LANES
        and width == cols * LANES
        and cols > 1
        and sections > 1
        and sections * HALO <= LANES
    )


def solution(mesh):
    placed = (P("depth", "row", "col"), P(), P(None, "row", "col"))

    def run(phase, tilt, intensity):
        if fits_whole(phase.shape, tilt.shape[0], mesh):
            body = whole_field_body
        else:
            body = staged_body
        return jax.shard_map(
            body,
            mesh=mesh,
            in_specs=placed,
            out_specs=(P("depth", "row", "col"), P(None, "depth", None, "row", "col")),
            check_vma=False,
        )(phase, tilt, intensity)

    return run
```

```python
import math

import jax
import jax.numpy as jnp
import numpy as np
from jax import lax
from jax.experimental import pallas as pl
from jax.experimental.pallas import tpu as pltpu
from jax.sharding import PartitionSpec as P

HALO = 32
FRESNEL = 64
LANES = 128
GATHER_BUDGET = 4 * 2**20
SIN = (
    0.9999999980536763,
    -0.1666666530009577,
    0.008333305907073658,
    -0.00019838908256358006,
    2.745822627876341e-06,
    -2.3043562782810933e-08,
)
COS = (
    0.9999999961345007,
    -0.4999999301617528,
    0.04166646215023687,
    -0.0013886696163545999,
    2.4695045482778703e-05,
    -2.5154931690000354e-07,
)


def horner(coefficients, square):
    total = jnp.full_like(square, coefficients[-1])
    for coefficient in coefficients[-2::-1]:
        total = total * square + coefficient
    return total


def cos_sin(angle):
    square = angle * angle
    return horner(COS, square), horner(SIN, square) * angle


def turn(fraction):
    half_cos, half_sin = cos_sin(fraction * math.pi)
    return half_cos * half_cos - half_sin * half_sin, 2.0 * half_cos * half_sin


def halves(value):
    high = value.astype(jnp.bfloat16)
    return high, (value - high.astype(jnp.float32)).astype(jnp.bfloat16)


def np_halves(matrix):
    high = matrix.astype(jnp.bfloat16)
    return high, (matrix - high.astype(np.float64)).astype(jnp.bfloat16)


def np_taps():
    offset = np.arange(-HALO, HALO + 1, dtype=np.float64)
    taper = np.maximum(np.abs(offset) - 0.5 * HALO, 0.0)
    weight = np.cos(np.pi * taper / (HALO + 2.0)) ** 2 / math.sqrt(FRESNEL)
    return weight * np.exp(1j * np.pi * offset * offset / FRESNEL)


def np_band(out_pos, in_pos):
    offset = out_pos[:, None] - in_pos[None, :]
    inside = np.abs(offset) <= HALO
    return np.where(inside, np_taps()[np.clip(offset, -HALO, HALO) + HALO], 0.0)


def row_constant(height):
    matrices = []
    for core in range(2):
        pos = (np.arange(height) + core * (height // 2)) % height
        band = np_band(pos, pos)
        whole = np.block([[band.real, -band.imag], [band.imag, band.real]])
        matrices.append(np.concatenate(np_halves(whole), axis=1))
    return np.stack(matrices)


def col_constant():
    lane = np.arange(LANES)
    edge_pos = np.where(lane < LANES // 2, lane + LANES, lane - LANES)
    parts = []
    for position in (lane, edge_pos):
        band = np_band(lane, position).T
        parts.append(np.block([[band.real, band.imag], [-band.imag, band.real]]))
    return np.concatenate(np_halves(np.concatenate(parts, axis=0)), axis=1)


def both_rows(near_ref, far_ref, where):
    return jnp.concatenate([near_ref[where], far_ref[where]], axis=0)


def block_turned(slice_index, block, screens, wave_ref, place):
    near_cos, near_sin, far_cos, far_sin = screens
    cos = both_rows(near_cos, far_cos, (slice_index, block))
    sin = both_rows(near_sin, far_sin, (slice_index, block))
    real, imag = wave_ref[place, 0], wave_ref[place, 1]
    return cos * real - sin * imag, cos * imag + sin * real


def row_product(row_matrix, columns):
    high, low = halves(columns)
    whole, width = columns.shape
    wide = jnp.dot(
        row_matrix[:, :whole], jnp.concatenate([high, low], axis=1), preferred_element_type=jnp.float32
    )
    rest = jnp.dot(row_matrix[:, whole:], high, preferred_element_type=jnp.float32)
    return wide[:, :width] + wide[:, width:] + rest


def col_product(high, low, col_ref):
    wide = jnp.dot(high, col_ref[...], preferred_element_type=jnp.float32)
    rest = jnp.dot(low, col_ref[:, : 2 * LANES], preferred_element_type=jnp.float32)
    return wide[:, : 2 * LANES] + wide[:, 2 * LANES :] + rest


def advance(slice_index, start, size, screens, row_matrix, col_ref, from_ref, to_ref, a_high, a_low):
    height = from_ref.shape[2]
    half = LANES // 2
    chunks = [range(place, min(place + 2, size)) for place in range(0, size, 2)]
    for chunk in chunks:
        columns = jnp.concatenate(
            [
                jnp.concatenate(block_turned(slice_index, start + place, screens, from_ref, place), axis=0)
                for place in chunk
            ],
            axis=1,
        )
        done = row_product(row_matrix, columns)
        for sub, place in enumerate(chunk):
            for part in range(2):
                value = done[part * height : (part + 1) * height, sub * LANES : (sub + 1) * LANES]
                for target, piece in zip((a_high, a_low), halves(value)):
                    target[place, :, pl.ds(part * LANES, LANES)] = piece
                    if place > 0:
                        target[place - 1, :, pl.ds((2 + part) * LANES, half)] = piece[:, :half]
                    if place < size - 1:
                        target[place + 1, :, pl.ds((2 + part) * LANES + half, half)] = piece[:, half:]
    for chunk in chunks:
        cells = pl.ds(chunk[0], len(chunk))
        rows = len(chunk) * height
        total = col_product(
            a_high[cells].reshape(rows, 4 * LANES), a_low[cells].reshape(rows, 4 * LANES), col_ref
        )
        for sub, place in enumerate(chunk):
            for part in range(2):
                to_ref[place, part] = total[sub * height : (sub + 1) * height, part * LANES : (part + 1) * LANES]


def clear_edge(a_ref, place, right):
    half = LANES // 2
    for part in range(2):
        begin = (2 + part) * LANES + (0 if right else half)
        a_ref[place, :, pl.ds(begin, half)] = jnp.zeros((a_ref.shape[1], half), a_ref.dtype)


def prepare_kernel(tilt_ref, near_own, near_rest, wave_ref, cos_ref, sin_ref):
    blocks, _, height, _ = wave_ref.shape
    count = cos_ref.shape[0] - 1
    core, own_section, own_place = lax.axis_index("row"), lax.axis_index("depth"), lax.axis_index("col")

    def screens(col, carry):
        held = col ^ own_place
        for bits in range(count):
            angle = near_own[held, 0] if bits == 0 else near_rest[held, bits - 1]
            cos_ref[bits ^ own_section, col], sin_ref[bits ^ own_section, col] = cos_sin(angle)
        return carry

    lax.fori_loop(0, blocks, screens, 0)
    cos_ref[count] = jnp.ones(cos_ref.shape[1:], jnp.float32)
    sin_ref[count] = jnp.zeros(cos_ref.shape[1:], jnp.float32)

    def cycles(number, position, extent):
        fraction = (number * position).astype(jnp.float32) / extent
        return turn(fraction - jnp.round(fraction))

    row = lax.broadcasted_iota(jnp.int32, (height, LANES), 0) + core * (height // 2)
    row = jnp.where(row >= height, row - height, row)
    row_cos, row_sin = cycles(tilt_ref[core, 0], row, float(height))
    for block in range(blocks):
        col_cos, col_sin = cycles(
            tilt_ref[core, 1],
            lax.broadcasted_iota(jnp.int32, (8, LANES), 1) + block * LANES,
            float(blocks * LANES),
        )
        col_cos, col_sin = col_cos[:1], col_sin[:1]
        wave_ref[block, 0] = row_cos * col_cos - row_sin * col_sin
        wave_ref[block, 1] = row_sin * col_cos + row_cos * col_sin


def wave_kernel(
    wave_ref, near_cos, near_sin, near_own, far_own, far_rest, row_ref, col_ref,
    mine_ref, theirs_ref, far_cos, far_sin, even_ref, odd_ref, moved_ref, left_ref, grad_ref,
    even_high, even_low, odd_high, odd_low,
):
    blocks, _, height, _ = wave_ref.shape
    count = near_cos.shape[0] - 1
    core, own_section, own_place = lax.axis_index("row"), lax.axis_index("depth"), lax.axis_index("col")
    near, far = pl.ds(0, height // 2), pl.ds(height // 2, height // 2)
    screens = (near_cos, near_sin, far_cos, far_sin)
    row_matrix = row_ref[core]
    window = min(3, blocks)
    window_start = jnp.clip(own_place - 1, 0, blocks - window)
    own_in_window = own_place - window_start
    waves = (even_ref, odd_ref)
    sums = ((even_high, even_low), (odd_high, odd_low))

    def far_screens(slice_index):
        bits = slice_index ^ own_section
        for col in range(blocks):
            held = col ^ own_place
            angle = jnp.where(bits == 0, far_own[held, 0], far_rest[held, jnp.maximum(bits - 1, 0)])
            far_cos[slice_index, col], far_sin[slice_index, col] = cos_sin(angle)

    for pair in sums:
        for target in pair:
            clear_edge(target, 0, False)
            clear_edge(target, blocks - 1, True)
    far_cos[count] = jnp.ones(far_cos.shape[1:], jnp.float32)
    far_sin[count] = jnp.zeros(far_cos.shape[1:], jnp.float32)
    far_screens(0)

    for tick in range(count):
        source, target = wave_ref if tick == 0 else waves[tick % 2], waves[(tick + 1) % 2]
        moved_ref[tick, 0], moved_ref[tick, 1] = block_turned(tick, own_place, screens, source, own_place)
        advance(tick, 0, blocks, screens, row_matrix, col_ref, source, target, *sums[tick % 2])
        if tick + 1 < count:
            far_screens(tick + 1)
        left_ref[tick] = target[own_place]

    last = waves[count % 2]
    source = waves[(count + 1) % 2]
    for pair in sums:
        for target in pair:
            clear_edge(target, window - 1, True)
    for place in range(window):
        block = window_start + place
        held = block ^ own_place
        measured = jnp.concatenate([near_own[held, 1 + core], far_own[held, 1]], axis=0)
        real, imag = last[block, 0], last[block, 1]
        misfit = 2.0 * (real * real + imag * imag - measured)
        source[place, 0] = misfit * real
        source[place, 1] = -misfit * imag

    for tick in range(count - 1):
        source, target = waves[(count + 1 + tick) % 2], waves[(count + tick) % 2]
        advance(
            count - tick, window_start, window, screens, row_matrix, col_ref, source, target, *sums[tick % 2]
        )
        arrived = count - 1 - tick
        pulled = target[own_in_window, 0], target[own_in_window, 1]
        grad_ref[arrived] = -(pulled[1] * moved_ref[arrived, 0] + pulled[0] * moved_ref[arrived, 1])

    source = waves[(2 * count) % 2]
    left, right = jnp.maximum(own_place - 1, 0), jnp.minimum(own_place + 1, blocks - 1)
    lane = lax.broadcasted_iota(jnp.int32, (2 * height, LANES), 1)
    has_left, has_right = own_place > 0, own_place < blocks - 1

    def cells(block):
        return jnp.concatenate(block_turned(1, block, screens, source, block - window_start), axis=0)

    edge_cells = jnp.where(
        lane < LANES // 2, jnp.where(has_right, cells(right), 0.0), jnp.where(has_left, cells(left), 0.0)
    )
    done = row_product(row_matrix, jnp.concatenate([cells(own_place), edge_cells], axis=1))
    quarters = [
        done[part * height : (part + 1) * height, sub * LANES : (sub + 1) * LANES]
        for sub in range(2)
        for part in range(2)
    ]
    high, low = halves(jnp.concatenate(quarters, axis=1))
    pulled = col_product(high, low, col_ref)
    grad_ref[0] = -(pulled[:, LANES:] * moved_ref[0, 0] + pulled[:, :LANES] * moved_ref[0, 1])

    for target, row in ((mine_ref, near), (theirs_ref, far)):
        for part in range(2):
            target[0, part] = left_ref[own_section, part, row]
        target[0, 2] = grad_ref[own_section, row]


def finish_kernel(mine_ref, received_ref, grad_ref, exit_ref, total_ref, sems):
    core = lax.axis_index("row")
    copies = []
    for source, item in ((mine_ref, core), (received_ref, 1 - core)):
        copies.append(pltpu.make_async_copy(source.at[:, pl.ds(0, 2)], exit_ref.at[item], sems.at[len(copies)]))
    for copy in copies:
        copy.start()
    total_ref[...] = mine_ref[:, 2] + received_ref[:, 2]
    copies.append(pltpu.make_async_copy(total_ref, grad_ref, sems.at[2]))
    copies[2].start()
    for copy in copies:
        copy.wait()


def spread(shard, axis, reach=None):
    size = lax.axis_size(axis)
    reach = size if reach is None else reach
    pieces = []
    for bits in range(1, size):
        pairs = [(i, i ^ bits) for i in range(size) if abs(i - (i ^ bits)) <= reach]
        pieces.append(lax.ppermute(shard, axis, pairs) if pairs else jnp.zeros_like(shard))
    return pieces


def swap_cores(value):
    return lax.ppermute(value, "row", [(0, 1), (1, 0)])


def whole_field_body(phase, tilt, intensity):
    _, tile_r, tile_c = phase.shape
    count, blocks = lax.axis_size("depth"), lax.axis_size("col")
    core = lax.axis_index("row")
    height = 2 * tile_r
    vmem = pl.BlockSpec(memory_space=pltpu.VMEM)
    smem = pl.BlockSpec(memory_space=pltpu.SMEM)
    hbm = pl.BlockSpec(memory_space=pl.ANY)

    def array(*shape):
        return jax.ShapeDtypeStruct(shape, jnp.float32)

    def params(mebibytes):
        return pltpu.CompilerParams(vmem_limit_bytes=mebibytes * 2**20)

    other_depths = spread(phase, "depth")
    other_depths[0], measured, slab = lax.optimization_barrier((other_depths[0], intensity, phase))
    other_depths = jnp.concatenate(other_depths, axis=0)
    packet = jnp.concatenate([slab, measured], axis=0)
    near_own = [packet]
    for bits in range(1, blocks):
        pairs = [(i, i ^ bits) for i in range(blocks)]
        close = [(i, j) for i, j in pairs if abs(i - j) <= 1]
        if close:
            near_own.append(lax.ppermute(packet, "col", close))
        else:
            further = [(i, j) for i, j in pairs if abs(i - j) <= 2]
            arrived = lax.ppermute(slab, "col", further) if further else jnp.zeros_like(slab)
            near_own.append(jnp.concatenate([arrived, jnp.zeros_like(measured)], axis=0))
    near_own = jnp.stack(near_own)
    arriving = spread(other_depths, "col", 2)
    arriving[0], near_own = lax.optimization_barrier((arriving[0], near_own))
    near_rest = jnp.stack([other_depths] + arriving)
    wanted = lax.dynamic_slice_in_dim(near_own, 2 - core, 1, 1)
    far_own = swap_cores(jnp.concatenate([near_own[:, :1], wanted], axis=1))
    far_rest = swap_cores(near_rest)

    half_screens = (count + 1, blocks, tile_r, tile_c)
    field = (blocks, 2, height, tile_c)
    wave, near_cos, near_sin = pl.pallas_call(
        prepare_kernel,
        out_shape=(array(*field), array(*half_screens), array(*half_screens)),
        in_specs=[smem, vmem, vmem],
        out_specs=(vmem,) * 3,
        compiler_params=params(8),
        cost_estimate=pl.CostEstimate(flops=5 * 10**8, bytes_accessed=2**20, transcendentals=0),
    )(tilt, near_own, near_rest)
    mine, theirs = pl.pallas_call(
        wave_kernel,
        out_shape=(array(1, 3, tile_r, tile_c),) * 2,
        in_specs=[vmem] * 8,
        out_specs=(vmem,) * 2,
        scratch_shapes=[pltpu.VMEM(half_screens, jnp.float32)] * 2
        + [pltpu.VMEM(field, jnp.float32)] * 2
        + [pltpu.VMEM((count, 2, height, tile_c), jnp.float32)] * 2
        + [pltpu.VMEM((count, height, tile_c), jnp.float32)]
        + [pltpu.VMEM((blocks, height, 4 * LANES), jnp.bfloat16)] * 4,
        compiler_params=params(24),
    )(
        wave, near_cos, near_sin, near_own, far_own, far_rest,
        jnp.asarray(row_constant(height)), jnp.asarray(col_constant()),
    )
    return pl.pallas_call(
        finish_kernel,
        out_shape=(array(*phase.shape), array(2, 1, 2, tile_r, tile_c)),
        in_specs=[vmem, vmem],
        out_specs=(hbm, hbm),
        scratch_shapes=[pltpu.VMEM(phase.shape, jnp.float32), pltpu.SemaphoreType.DMA((3,))],
        compiler_params=params(4),
    )(mine, swap_cores(theirs))


def extended_2(cells, sides, width):
    for axis, dim in sides:
        count = lax.axis_size(axis)
        ends = count - 1
        head = lax.slice_in_dim(cells, 0, width, axis=dim)
        tail = lax.slice_in_dim(cells, cells.shape[dim] - width, cells.shape[dim], axis=dim)
        cells = jnp.concatenate(
            [
                lax.ppermute(tail, axis, [(i, (i + 1) % count) for i in range(ends)]),
                cells,
                lax.ppermute(head, axis, [((i + 1) % count, i) for i in range(ends)]),
            ],
            axis=dim,
        )
    return cells


def from_behind(value, axis, steps):
    count = lax.axis_size(axis)
    leading, last = (max(0, -steps), min(count, count - steps))
    return lax.ppermute(value, axis, [(source, source + steps) for source in range(leading, last)])


def band_matrix(block_size, margin, fresnel, adjoint):
    shape_full = (block_size, block_size + 2 * margin)
    out_idx = lax.broadcasted_iota(jnp.int32, shape_full, 0)
    in_idx = lax.broadcasted_iota(jnp.int32, shape_full, 1)
    offset = (out_idx + margin - in_idx).astype(jnp.float32)
    inside = jnp.abs(offset) <= margin
    taper_dist = jnp.maximum(jnp.abs(offset) - 0.5 * margin, 0.0)
    profile = jnp.cos(jnp.pi * taper_dist / (margin + 2.0))
    weight = profile * profile / math.sqrt(fresnel)
    phase_angle = jnp.pi * offset * offset / fresnel
    real_part = jnp.where(inside, jnp.cos(phase_angle) * weight, 0.0)
    imag_part = jnp.where(inside, jnp.sin(phase_angle) * weight, 0.0)
    if adjoint:
        imag_part = -imag_part
    upper = jnp.stack([real_part, -imag_part])
    lower = jnp.stack([imag_part, real_part])
    return jnp.stack([upper, lower])


def along_rows(extended, matrix):
    pieces = [jnp.einsum("pqij,gqjc->gpic", matrix, extended, precision=lax.Precision.HIGHEST)]
    return jnp.concatenate(pieces, axis=2)


def along_cols(extended, matrix, margin):
    block_size = matrix.shape[2]
    extent = extended.shape[3] - 2 * margin
    pieces = []
    for block_start in range(0, extent, block_size):
        window = extended[:, :, :, block_start : block_start + block_size + 2 * margin]
        pieces.append(
            jnp.einsum("pqij,gqrj->gpri", matrix, window, precision=lax.Precision.HIGHEST)
        )
    return jnp.concatenate(pieces, axis=3)


def propagate(current, row_matrix, col_matrix):
    with_rows = extended_2(current, (("row", 2),), HALO)
    row_done = along_rows(with_rows, row_matrix)
    with_cols = extended_2(row_done, (("col", 3),), HALO)
    return along_cols(with_cols, col_matrix, HALO)


def transmit(screen, current, adjoint):
    screen_re = screen[0][None]
    screen_im = screen[1][None]
    if adjoint:
        screen_im = -screen_im
    real_part = screen_re * current[:, 0] - screen_im * current[:, 1]
    imag_part = screen_re * current[:, 1] + screen_im * current[:, 0]
    return jnp.stack([real_part, imag_part], axis=1)


def store_item(store, current, first_item, slice_index, active):
    begin = (first_item, jnp.int32(slice_index), jnp.int32(0), jnp.int32(0), jnp.int32(0))
    sizes_now = (current.shape[0], 1) + current.shape[1:]
    previous = lax.dynamic_slice(store, begin, sizes_now)
    fresh = jnp.where(active, current[:, None], previous)
    return lax.dynamic_update_slice(store, fresh, begin)


def staged_body(phase, tilt, intensity):
    slices, tile_r, tile_c = phase.shape
    batch_size = tilt.shape[0]
    sections = lax.axis_size("depth")
    section_index = lax.axis_index("depth")
    group_size = 1
    groups = batch_size // group_size
    tick_count = sections + groups - 1
    block_r = 64
    block_c = 128
    fwd_rows = band_matrix(block_r, HALO, FRESNEL, False)
    fwd_cols = band_matrix(block_c, HALO, FRESNEL, False)
    adj_rows = band_matrix(block_r, HALO, FRESNEL, True)
    adj_cols = band_matrix(block_c, HALO, FRESNEL, True)
    row_pos = (
        lax.axis_index("row") * tile_r + lax.broadcasted_iota(jnp.int32, (tile_r, tile_c), 0)
    ).astype(jnp.float32)
    col_pos = (
        lax.axis_index("col") * tile_c + lax.broadcasted_iota(jnp.int32, (tile_r, tile_c), 1)
    ).astype(jnp.float32)
    height = float(tile_r * lax.axis_size("row"))
    width_all = float(tile_c * lax.axis_size("col"))
    tilt_f = tilt.astype(jnp.float32)
    phase_angle = (
        2.0
        * jnp.pi
        * (
            tilt_f[:, 0, None, None] * row_pos / height
            + tilt_f[:, 1, None, None] * col_pos / width_all
        )
    )
    incident = jnp.stack([jnp.cos(phase_angle), jnp.sin(phase_angle)], axis=1)
    screens = jnp.stack([jnp.cos(phase), jnp.sin(phase)], axis=1)

    def forward_tick(tick_now, carry):
        incoming, entering, leaving = carry
        group_index = tick_now - section_index
        active = (group_index >= 0) & (group_index < groups)
        first_item = jnp.clip(group_index, 0, groups - 1) * group_size
        current = jnp.where(
            section_index == 0,
            lax.dynamic_slice_in_dim(incident, first_item, group_size, 0),
            incoming,
        )
        entering = store_item(entering, current, first_item, 0, active)
        current = propagate(transmit(screens[0], current, False), fwd_rows, fwd_cols)
        leaving = store_item(leaving, current, first_item, 0, active)
        incoming = from_behind(current, "depth", 1)
        return (incoming, entering, leaving)

    store_zero = jnp.zeros((batch_size, slices, 2, tile_r, tile_c), jnp.float32)
    start_wave = jnp.zeros((group_size, 2, tile_r, tile_c), jnp.float32)
    _, entering, leaving = lax.fori_loop(
        0, tick_count, forward_tick, (start_wave, store_zero, store_zero)
    )
    final_wave = leaving[:, slices - 1]
    misfit = final_wave[:, 0] * final_wave[:, 0] + final_wave[:, 1] * final_wave[:, 1] - intensity
    seed_adjoint = 2.0 * misfit[:, None] * final_wave

    def backward_tick(tick_now, carry):
        incoming, gradient = carry
        group_index = tick_now - (sections - 1 - section_index)
        active = (group_index >= 0) & (group_index < groups)
        first_item = jnp.clip(group_index, 0, groups - 1) * group_size
        adjoint_wave = jnp.where(
            section_index == sections - 1,
            lax.dynamic_slice_in_dim(seed_adjoint, first_item, group_size, 0),
            incoming,
        )
        for slice_index in reversed(range(slices)):
            pulled = propagate(adjoint_wave, adj_rows, adj_cols)
            arrived = lax.dynamic_slice_in_dim(entering[:, slice_index], first_item, group_size, 0)
            moved = transmit(screens[slice_index], arrived, False)
            contribution = jnp.sum(pulled[:, 1] * moved[:, 0] - pulled[:, 0] * moved[:, 1], axis=0)
            gradient = gradient.at[slice_index].add(jnp.where(active, contribution, 0.0))
            adjoint_wave = transmit(screens[slice_index], pulled, True)
        incoming = from_behind(adjoint_wave, "depth", -1)
        return (incoming, gradient)

    grad_zero = jnp.zeros((slices, tile_r, tile_c), jnp.float32)
    _, gradient = lax.fori_loop(0, tick_count, backward_tick, (start_wave, grad_zero))
    return (gradient, leaving)


def fits_whole(phase_shape, batch, mesh):
    slices, height, width = phase_shape
    rows, cols, sections = mesh.shape["row"], mesh.shape["col"], mesh.shape["depth"]
    return (
        4 * height * width * (slices + batch) <= GATHER_BUDGET
        and batch == rows == 2
        and slices == sections
        and sections & (sections - 1) == 0
        and cols & (cols - 1) == 0
        and height == LANES
        and width == cols * LANES
        and cols > 1
        and sections > 1
        and sections * HALO <= LANES
    )


def solution(mesh):
    placed = (P("depth", "row", "col"), P(), P(None, "row", "col"))

    def run(phase, tilt, intensity):
        if fits_whole(phase.shape, tilt.shape[0], mesh):
            body = whole_field_body
        else:
            body = staged_body
        return jax.shard_map(
            body,
            mesh=mesh,
            in_specs=placed,
            out_specs=(P("depth", "row", "col"), P(None, "depth", None, "row", "col")),
            check_vma=False,
        )(phase, tilt, intensity)

    return run
```

```python
import math

import jax
import jax.numpy as jnp
import numpy as np
from jax import lax
from jax.experimental import pallas as pl
from jax.experimental.pallas import tpu as pltpu
from jax.sharding import PartitionSpec as P

HALO = 32
FRESNEL = 64
LANES = 128
GATHER_BUDGET = 4 * 2**20
SIN = (
    0.9999999980536763,
    -0.1666666530009577,
    0.008333305907073658,
    -0.00019838908256358006,
    2.745822627876341e-06,
    -2.3043562782810933e-08,
)
COS = (
    0.9999999961345007,
    -0.4999999301617528,
    0.04166646215023687,
    -0.0013886696163545999,
    2.4695045482778703e-05,
    -2.5154931690000354e-07,
)


def horner(coefficients, square):
    total = jnp.full_like(square, coefficients[-1])
    for coefficient in coefficients[-2::-1]:
        total = total * square + coefficient
    return total


def cos_sin(angle):
    square = angle * angle
    return horner(COS, square), horner(SIN, square) * angle


def turn(fraction):
    half_cos, half_sin = cos_sin(fraction * math.pi)
    return half_cos * half_cos - half_sin * half_sin, 2.0 * half_cos * half_sin


def halves(value):
    high = value.astype(jnp.bfloat16)
    return high, (value - high.astype(jnp.float32)).astype(jnp.bfloat16)


def np_halves(matrix):
    high = matrix.astype(jnp.bfloat16)
    return high, (matrix - high.astype(np.float64)).astype(jnp.bfloat16)


def np_taps():
    offset = np.arange(-HALO, HALO + 1, dtype=np.float64)
    taper = np.maximum(np.abs(offset) - 0.5 * HALO, 0.0)
    weight = np.cos(np.pi * taper / (HALO + 2.0)) ** 2 / math.sqrt(FRESNEL)
    return weight * np.exp(1j * np.pi * offset * offset / FRESNEL)


def np_band(out_pos, in_pos):
    offset = out_pos[:, None] - in_pos[None, :]
    inside = np.abs(offset) <= HALO
    return np.where(inside, np_taps()[np.clip(offset, -HALO, HALO) + HALO], 0.0)


def row_constant(height):
    matrices = []
    for core in range(2):
        pos = (np.arange(height) + core * (height // 2)) % height
        band = np_band(pos, pos)
        whole = np.block([[band.real, -band.imag], [band.imag, band.real]])
        matrices.append(np.concatenate(np_halves(whole), axis=1))
    return np.stack(matrices)


def col_constant():
    lane = np.arange(LANES)
    turned = np.where((lane >= HALO) & (lane < LANES - HALO), lane ^ (LANES // 2), lane)
    edge_pos = np.where(turned < LANES // 2, turned + LANES, turned - LANES)
    parts = []
    for position in (lane, edge_pos):
        band = np_band(lane, position).T
        parts.append(np.block([[band.real, band.imag], [-band.imag, band.real]]))
    return np.concatenate(np_halves(np.concatenate(parts, axis=0)), axis=1)


def both_rows(near_ref, far_ref, where):
    return jnp.concatenate([near_ref[where], far_ref[where]], axis=0)


def block_turned(slice_index, block, screens, wave_ref, place):
    near_cos, near_sin, far_cos, far_sin = screens
    cos = both_rows(near_cos, far_cos, (slice_index, block))
    sin = both_rows(near_sin, far_sin, (slice_index, block))
    real, imag = wave_ref[place, 0], wave_ref[place, 1]
    return cos * real - sin * imag, cos * imag + sin * real


def row_product(row_matrix, columns):
    high, low = halves(columns)
    whole, width = columns.shape
    wide = jnp.dot(
        row_matrix[:, :whole], jnp.concatenate([high, low], axis=1), preferred_element_type=jnp.float32
    )
    rest = jnp.dot(row_matrix[:, whole:], high, preferred_element_type=jnp.float32)
    return wide[:, :width] + wide[:, width:] + rest


def col_product(high, low, col_ref):
    wide = jnp.dot(high, col_ref[...], preferred_element_type=jnp.float32)
    rest = jnp.dot(low, col_ref[: 2 * LANES, : 2 * LANES], preferred_element_type=jnp.float32)
    return wide[:, : 2 * LANES] + wide[:, 2 * LANES :] + rest


def three_parts(value):
    high = value.astype(jnp.bfloat16)
    rest = value - high.astype(jnp.float32)
    return high, rest.astype(jnp.bfloat16), pltpu.roll(rest, LANES // 2, 1).astype(jnp.bfloat16)


def advance(slice_index, start, size, screens, row_matrix, col_ref, from_ref, to_ref, a_high, a_low):
    height = from_ref.shape[2]
    chunks = [range(place, min(place + 2, size)) for place in range(0, size, 2)]
    for chunk in chunks:
        columns = jnp.concatenate(
            [
                jnp.concatenate(block_turned(slice_index, start + place, screens, from_ref, place), axis=0)
                for place in chunk
            ],
            axis=1,
        )
        done = row_product(row_matrix, columns)
        for sub, place in enumerate(chunk):
            for part in range(2):
                value = done[part * height : (part + 1) * height, sub * LANES : (sub + 1) * LANES]
                high, low, turned = three_parts(value)
                cells = pl.ds(part * LANES, LANES)
                a_high[place, :, cells] = high
                a_low[place, :, cells] = low
                edge = (2 + part) * LANES
                if place > 0:
                    a_high[place - 1, :, pl.ds(edge, HALO)] = high[:, :HALO]
                    a_high[place - 1, :, pl.ds(edge + 2 * HALO, HALO)] = turned[:, 2 * HALO : 3 * HALO]
                if place < size - 1:
                    a_high[place + 1, :, pl.ds(edge + 3 * HALO, HALO)] = high[:, 3 * HALO :]
                    a_high[place + 1, :, pl.ds(edge + HALO, HALO)] = turned[:, HALO : 2 * HALO]
    for chunk in chunks:
        cells = pl.ds(chunk[0], len(chunk))
        rows = len(chunk) * height
        total = col_product(
            a_high[cells].reshape(rows, 4 * LANES), a_low[cells].reshape(rows, 2 * LANES), col_ref
        )
        for sub, place in enumerate(chunk):
            for part in range(2):
                to_ref[place, part] = total[sub * height : (sub + 1) * height, part * LANES : (part + 1) * LANES]


def clear_edge(a_ref, place, right):
    for part in range(2):
        for begin in (0, 2 * HALO) if right else (HALO, 3 * HALO):
            a_ref[place, :, pl.ds((2 + part) * LANES + begin, HALO)] = jnp.zeros((a_ref.shape[1], HALO), a_ref.dtype)


def prepare_kernel(tilt_ref, near_own, near_rest, wave_ref, cos_ref, sin_ref):
    blocks, _, height, _ = wave_ref.shape
    count = cos_ref.shape[0] - 1
    core, own_section, own_place = lax.axis_index("row"), lax.axis_index("depth"), lax.axis_index("col")

    def screens(col, carry):
        held = col ^ own_place
        for bits in range(count):
            angle = near_own[held, 0] if bits == 0 else near_rest[held, bits - 1]
            cos_ref[bits ^ own_section, col], sin_ref[bits ^ own_section, col] = cos_sin(angle)
        return carry

    lax.fori_loop(0, blocks, screens, 0)
    cos_ref[count] = jnp.ones(cos_ref.shape[1:], jnp.float32)
    sin_ref[count] = jnp.zeros(cos_ref.shape[1:], jnp.float32)

    def cycles(number, position, extent):
        fraction = (number * position).astype(jnp.float32) / extent
        return turn(fraction - jnp.round(fraction))

    row = lax.broadcasted_iota(jnp.int32, (height, LANES), 0) + core * (height // 2)
    row = jnp.where(row >= height, row - height, row)
    row_cos, row_sin = cycles(tilt_ref[core, 0], row, float(height))
    for block in range(blocks):
        col_cos, col_sin = cycles(
            tilt_ref[core, 1],
            lax.broadcasted_iota(jnp.int32, (8, LANES), 1) + block * LANES,
            float(blocks * LANES),
        )
        col_cos, col_sin = col_cos[:1], col_sin[:1]
        wave_ref[block, 0] = row_cos * col_cos - row_sin * col_sin
        wave_ref[block, 1] = row_sin * col_cos + row_cos * col_sin


def wave_kernel(
    wave_ref, near_cos, near_sin, near_own, far_own, far_rest, row_ref, col_ref,
    mine_ref, theirs_ref, far_cos, far_sin, even_ref, odd_ref, moved_ref, left_ref, grad_ref,
    even_high, even_low, odd_high, odd_low,
):
    blocks, _, height, _ = wave_ref.shape
    count = near_cos.shape[0] - 1
    core, own_section, own_place = lax.axis_index("row"), lax.axis_index("depth"), lax.axis_index("col")
    near, far = pl.ds(0, height // 2), pl.ds(height // 2, height // 2)
    screens = (near_cos, near_sin, far_cos, far_sin)
    row_matrix = row_ref[core]
    window = min(3, blocks)
    window_start = jnp.clip(own_place - 1, 0, blocks - window)
    own_in_window = own_place - window_start
    waves = (even_ref, odd_ref)
    sums = ((even_high, even_low), (odd_high, odd_low))

    def far_screens(slice_index):
        bits = slice_index ^ own_section
        for col in range(blocks):
            held = col ^ own_place
            angle = jnp.where(bits == 0, far_own[held, 0], far_rest[held, jnp.maximum(bits - 1, 0)])
            far_cos[slice_index, col], far_sin[slice_index, col] = cos_sin(angle)

    for target, _ in sums:
        clear_edge(target, 0, False)
        clear_edge(target, blocks - 1, True)
    far_cos[count] = jnp.ones(far_cos.shape[1:], jnp.float32)
    far_sin[count] = jnp.zeros(far_cos.shape[1:], jnp.float32)
    far_screens(0)

    for tick in range(count):
        source, target = wave_ref if tick == 0 else waves[tick % 2], waves[(tick + 1) % 2]
        moved_ref[tick, 0], moved_ref[tick, 1] = block_turned(tick, own_place, screens, source, own_place)
        advance(tick, 0, blocks, screens, row_matrix, col_ref, source, target, *sums[tick % 2])
        if tick + 1 < count:
            far_screens(tick + 1)
        left_ref[tick] = target[own_place]

    last = waves[count % 2]
    source = waves[(count + 1) % 2]
    for target, _ in sums:
        clear_edge(target, window - 1, True)
    for place in range(window):
        block = window_start + place
        held = block ^ own_place
        measured = jnp.concatenate([near_own[held, 1 + core], far_own[held, 1]], axis=0)
        real, imag = last[block, 0], last[block, 1]
        misfit = 2.0 * (real * real + imag * imag - measured)
        source[place, 0] = misfit * real
        source[place, 1] = -misfit * imag

    for tick in range(count - 1):
        source, target = waves[(count + 1 + tick) % 2], waves[(count + tick) % 2]
        advance(
            count - tick, window_start, window, screens, row_matrix, col_ref, source, target, *sums[tick % 2]
        )
        arrived = count - 1 - tick
        pulled = target[own_in_window, 0], target[own_in_window, 1]
        grad_ref[arrived] = -(pulled[1] * moved_ref[arrived, 0] + pulled[0] * moved_ref[arrived, 1])

    source = waves[(2 * count) % 2]
    left, right = jnp.maximum(own_place - 1, 0), jnp.minimum(own_place + 1, blocks - 1)
    lane = lax.broadcasted_iota(jnp.int32, (2 * height, LANES), 1)
    has_left, has_right = own_place > 0, own_place < blocks - 1

    def cells(block):
        return jnp.concatenate(block_turned(1, block, screens, source, block - window_start), axis=0)

    edge_cells = jnp.where(
        lane < LANES // 2, jnp.where(has_right, cells(right), 0.0), jnp.where(has_left, cells(left), 0.0)
    )
    done = row_product(row_matrix, jnp.concatenate([cells(own_place), edge_cells], axis=1))
    lane = lax.broadcasted_iota(jnp.int32, (height, LANES), 1)
    between = (lane >= HALO) & (lane < LANES - HALO)
    highs, lows, edges = [], [], []
    for part in range(2):
        high, low, _ = three_parts(done[part * height : (part + 1) * height, :LANES])
        highs.append(high)
        lows.append(low)
        value = done[part * height : (part + 1) * height, LANES:]
        whole_high = value.astype(jnp.bfloat16).astype(jnp.float32)
        edge = jnp.where(between, pltpu.roll(value - whole_high, LANES // 2, 1), whole_high)
        edges.append(edge.astype(jnp.bfloat16))
    pulled = col_product(jnp.concatenate(highs + edges, axis=1), jnp.concatenate(lows, axis=1), col_ref)
    grad_ref[0] = -(pulled[:, LANES:] * moved_ref[0, 0] + pulled[:, :LANES] * moved_ref[0, 1])

    for target, row in ((mine_ref, near), (theirs_ref, far)):
        for part in range(2):
            target[0, part] = left_ref[own_section, part, row]
        target[0, 2] = grad_ref[own_section, row]


def finish_kernel(mine_ref, received_ref, grad_ref, exit_ref, total_ref, sems):
    core = lax.axis_index("row")
    copies = []
    for source, item in ((mine_ref, core), (received_ref, 1 - core)):
        copies.append(pltpu.make_async_copy(source.at[:, pl.ds(0, 2)], exit_ref.at[item], sems.at[len(copies)]))
    for copy in copies:
        copy.start()
    total_ref[...] = mine_ref[:, 2] + received_ref[:, 2]
    copies.append(pltpu.make_async_copy(total_ref, grad_ref, sems.at[2]))
    copies[2].start()
    for copy in copies:
        copy.wait()


def spread(shard, axis, reach=None):
    size = lax.axis_size(axis)
    reach = size if reach is None else reach
    pieces = []
    for bits in range(1, size):
        pairs = [(i, i ^ bits) for i in range(size) if abs(i - (i ^ bits)) <= reach]
        pieces.append(lax.ppermute(shard, axis, pairs) if pairs else jnp.zeros_like(shard))
    return pieces


def swap_cores(value):
    return lax.ppermute(value, "row", [(0, 1), (1, 0)])


def whole_field_body(phase, tilt, intensity):
    _, tile_r, tile_c = phase.shape
    count, blocks = lax.axis_size("depth"), lax.axis_size("col")
    core = lax.axis_index("row")
    height = 2 * tile_r
    vmem = pl.BlockSpec(memory_space=pltpu.VMEM)
    smem = pl.BlockSpec(memory_space=pltpu.SMEM)
    hbm = pl.BlockSpec(memory_space=pl.ANY)

    def array(*shape):
        return jax.ShapeDtypeStruct(shape, jnp.float32)

    def params(mebibytes):
        return pltpu.CompilerParams(vmem_limit_bytes=mebibytes * 2**20)

    other_depths = spread(phase, "depth")
    other_depths[0], measured, slab = lax.optimization_barrier((other_depths[0], intensity, phase))
    other_depths = jnp.concatenate(other_depths, axis=0)
    packet = jnp.concatenate([slab, measured], axis=0)
    near_own = [packet]
    for bits in range(1, blocks):
        pairs = [(i, i ^ bits) for i in range(blocks)]
        close = [(i, j) for i, j in pairs if abs(i - j) <= 1]
        if close:
            near_own.append(lax.ppermute(packet, "col", close))
        else:
            further = [(i, j) for i, j in pairs if abs(i - j) <= 2]
            arrived = lax.ppermute(slab, "col", further) if further else jnp.zeros_like(slab)
            near_own.append(jnp.concatenate([arrived, jnp.zeros_like(measured)], axis=0))
    near_own = jnp.stack(near_own)
    arriving = spread(other_depths, "col", 2)
    arriving[0], near_own = lax.optimization_barrier((arriving[0], near_own))
    near_rest = jnp.stack([other_depths] + arriving)
    wanted = lax.dynamic_slice_in_dim(near_own, 2 - core, 1, 1)
    far_own = swap_cores(jnp.concatenate([near_own[:, :1], wanted], axis=1))
    far_rest = swap_cores(near_rest)

    half_screens = (count + 1, blocks, tile_r, tile_c)
    field = (blocks, 2, height, tile_c)
    wave, near_cos, near_sin = pl.pallas_call(
        prepare_kernel,
        out_shape=(array(*field), array(*half_screens), array(*half_screens)),
        in_specs=[smem, vmem, vmem],
        out_specs=(vmem,) * 3,
        compiler_params=params(8),
        cost_estimate=pl.CostEstimate(flops=5 * 10**8, bytes_accessed=2**20, transcendentals=0),
    )(tilt, near_own, near_rest)
    mine, theirs = pl.pallas_call(
        wave_kernel,
        out_shape=(array(1, 3, tile_r, tile_c),) * 2,
        in_specs=[vmem] * 8,
        out_specs=(vmem,) * 2,
        scratch_shapes=[pltpu.VMEM(half_screens, jnp.float32)] * 2
        + [pltpu.VMEM(field, jnp.float32)] * 2
        + [pltpu.VMEM((count, 2, height, tile_c), jnp.float32)] * 2
        + [pltpu.VMEM((count, height, tile_c), jnp.float32)]
        + [pltpu.VMEM((blocks, height, parts * LANES), jnp.bfloat16) for parts in (4, 2, 4, 2)],
        compiler_params=params(24),
    )(
        wave, near_cos, near_sin, near_own, far_own, far_rest,
        jnp.asarray(row_constant(height)), jnp.asarray(col_constant()),
    )
    return pl.pallas_call(
        finish_kernel,
        out_shape=(array(*phase.shape), array(2, 1, 2, tile_r, tile_c)),
        in_specs=[vmem, vmem],
        out_specs=(hbm, hbm),
        scratch_shapes=[pltpu.VMEM(phase.shape, jnp.float32), pltpu.SemaphoreType.DMA((3,))],
        compiler_params=params(4),
    )(mine, swap_cores(theirs))


def extended_2(cells, sides, width):
    for axis, dim in sides:
        count = lax.axis_size(axis)
        ends = count - 1
        head = lax.slice_in_dim(cells, 0, width, axis=dim)
        tail = lax.slice_in_dim(cells, cells.shape[dim] - width, cells.shape[dim], axis=dim)
        cells = jnp.concatenate(
            [
                lax.ppermute(tail, axis, [(i, (i + 1) % count) for i in range(ends)]),
                cells,
                lax.ppermute(head, axis, [((i + 1) % count, i) for i in range(ends)]),
            ],
            axis=dim,
        )
    return cells


def from_behind(value, axis, steps):
    count = lax.axis_size(axis)
    leading, last = (max(0, -steps), min(count, count - steps))
    return lax.ppermute(value, axis, [(source, source + steps) for source in range(leading, last)])


def band_matrix(block_size, margin, fresnel, adjoint):
    shape_full = (block_size, block_size + 2 * margin)
    out_idx = lax.broadcasted_iota(jnp.int32, shape_full, 0)
    in_idx = lax.broadcasted_iota(jnp.int32, shape_full, 1)
    offset = (out_idx + margin - in_idx).astype(jnp.float32)
    inside = jnp.abs(offset) <= margin
    taper_dist = jnp.maximum(jnp.abs(offset) - 0.5 * margin, 0.0)
    profile = jnp.cos(jnp.pi * taper_dist / (margin + 2.0))
    weight = profile * profile / math.sqrt(fresnel)
    phase_angle = jnp.pi * offset * offset / fresnel
    real_part = jnp.where(inside, jnp.cos(phase_angle) * weight, 0.0)
    imag_part = jnp.where(inside, jnp.sin(phase_angle) * weight, 0.0)
    if adjoint:
        imag_part = -imag_part
    upper = jnp.stack([real_part, -imag_part])
    lower = jnp.stack([imag_part, real_part])
    return jnp.stack([upper, lower])


def along_rows(extended, matrix):
    pieces = [jnp.einsum("pqij,gqjc->gpic", matrix, extended, precision=lax.Precision.HIGHEST)]
    return jnp.concatenate(pieces, axis=2)


def along_cols(extended, matrix, margin):
    block_size = matrix.shape[2]
    extent = extended.shape[3] - 2 * margin
    pieces = []
    for block_start in range(0, extent, block_size):
        window = extended[:, :, :, block_start : block_start + block_size + 2 * margin]
        pieces.append(
            jnp.einsum("pqij,gqrj->gpri", matrix, window, precision=lax.Precision.HIGHEST)
        )
    return jnp.concatenate(pieces, axis=3)


def propagate(current, row_matrix, col_matrix):
    with_rows = extended_2(current, (("row", 2),), HALO)
    row_done = along_rows(with_rows, row_matrix)
    with_cols = extended_2(row_done, (("col", 3),), HALO)
    return along_cols(with_cols, col_matrix, HALO)


def transmit(screen, current, adjoint):
    screen_re = screen[0][None]
    screen_im = screen[1][None]
    if adjoint:
        screen_im = -screen_im
    real_part = screen_re * current[:, 0] - screen_im * current[:, 1]
    imag_part = screen_re * current[:, 1] + screen_im * current[:, 0]
    return jnp.stack([real_part, imag_part], axis=1)


def store_item(store, current, first_item, slice_index, active):
    begin = (first_item, jnp.int32(slice_index), jnp.int32(0), jnp.int32(0), jnp.int32(0))
    sizes_now = (current.shape[0], 1) + current.shape[1:]
    previous = lax.dynamic_slice(store, begin, sizes_now)
    fresh = jnp.where(active, current[:, None], previous)
    return lax.dynamic_update_slice(store, fresh, begin)


def staged_body(phase, tilt, intensity):
    slices, tile_r, tile_c = phase.shape
    batch_size = tilt.shape[0]
    sections = lax.axis_size("depth")
    section_index = lax.axis_index("depth")
    group_size = 1
    groups = batch_size // group_size
    tick_count = sections + groups - 1
    block_r = 64
    block_c = 128
    fwd_rows = band_matrix(block_r, HALO, FRESNEL, False)
    fwd_cols = band_matrix(block_c, HALO, FRESNEL, False)
    adj_rows = band_matrix(block_r, HALO, FRESNEL, True)
    adj_cols = band_matrix(block_c, HALO, FRESNEL, True)
    row_pos = (
        lax.axis_index("row") * tile_r + lax.broadcasted_iota(jnp.int32, (tile_r, tile_c), 0)
    ).astype(jnp.float32)
    col_pos = (
        lax.axis_index("col") * tile_c + lax.broadcasted_iota(jnp.int32, (tile_r, tile_c), 1)
    ).astype(jnp.float32)
    height = float(tile_r * lax.axis_size("row"))
    width_all = float(tile_c * lax.axis_size("col"))
    tilt_f = tilt.astype(jnp.float32)
    phase_angle = (
        2.0
        * jnp.pi
        * (
            tilt_f[:, 0, None, None] * row_pos / height
            + tilt_f[:, 1, None, None] * col_pos / width_all
        )
    )
    incident = jnp.stack([jnp.cos(phase_angle), jnp.sin(phase_angle)], axis=1)
    screens = jnp.stack([jnp.cos(phase), jnp.sin(phase)], axis=1)

    def forward_tick(tick_now, carry):
        incoming, entering, leaving = carry
        group_index = tick_now - section_index
        active = (group_index >= 0) & (group_index < groups)
        first_item = jnp.clip(group_index, 0, groups - 1) * group_size
        current = jnp.where(
            section_index == 0,
            lax.dynamic_slice_in_dim(incident, first_item, group_size, 0),
            incoming,
        )
        entering = store_item(entering, current, first_item, 0, active)
        current = propagate(transmit(screens[0], current, False), fwd_rows, fwd_cols)
        leaving = store_item(leaving, current, first_item, 0, active)
        incoming = from_behind(current, "depth", 1)
        return (incoming, entering, leaving)

    store_zero = jnp.zeros((batch_size, slices, 2, tile_r, tile_c), jnp.float32)
    start_wave = jnp.zeros((group_size, 2, tile_r, tile_c), jnp.float32)
    _, entering, leaving = lax.fori_loop(
        0, tick_count, forward_tick, (start_wave, store_zero, store_zero)
    )
    final_wave = leaving[:, slices - 1]
    misfit = final_wave[:, 0] * final_wave[:, 0] + final_wave[:, 1] * final_wave[:, 1] - intensity
    seed_adjoint = 2.0 * misfit[:, None] * final_wave

    def backward_tick(tick_now, carry):
        incoming, gradient = carry
        group_index = tick_now - (sections - 1 - section_index)
        active = (group_index >= 0) & (group_index < groups)
        first_item = jnp.clip(group_index, 0, groups - 1) * group_size
        adjoint_wave = jnp.where(
            section_index == sections - 1,
            lax.dynamic_slice_in_dim(seed_adjoint, first_item, group_size, 0),
            incoming,
        )
        for slice_index in reversed(range(slices)):
            pulled = propagate(adjoint_wave, adj_rows, adj_cols)
            arrived = lax.dynamic_slice_in_dim(entering[:, slice_index], first_item, group_size, 0)
            moved = transmit(screens[slice_index], arrived, False)
            contribution = jnp.sum(pulled[:, 1] * moved[:, 0] - pulled[:, 0] * moved[:, 1], axis=0)
            gradient = gradient.at[slice_index].add(jnp.where(active, contribution, 0.0))
            adjoint_wave = transmit(screens[slice_index], pulled, True)
        incoming = from_behind(adjoint_wave, "depth", -1)
        return (incoming, gradient)

    grad_zero = jnp.zeros((slices, tile_r, tile_c), jnp.float32)
    _, gradient = lax.fori_loop(0, tick_count, backward_tick, (start_wave, grad_zero))
    return (gradient, leaving)


def fits_whole(phase_shape, batch, mesh):
    slices, height, width = phase_shape
    rows, cols, sections = mesh.shape["row"], mesh.shape["col"], mesh.shape["depth"]
    return (
        4 * height * width * (slices + batch) <= GATHER_BUDGET
        and batch == rows == 2
        and slices == sections
        and sections & (sections - 1) == 0
        and cols & (cols - 1) == 0
        and height == LANES
        and width == cols * LANES
        and cols > 1
        and sections > 1
        and sections * HALO <= LANES
    )


def solution(mesh):
    placed = (P("depth", "row", "col"), P(), P(None, "row", "col"))

    def run(phase, tilt, intensity):
        if fits_whole(phase.shape, tilt.shape[0], mesh):
            body = whole_field_body
        else:
            body = staged_body
        return jax.shard_map(
            body,
            mesh=mesh,
            in_specs=placed,
            out_specs=(P("depth", "row", "col"), P(None, "depth", None, "row", "col")),
            check_vma=False,
        )(phase, tilt, intensity)

    return run
```

```python
import math

import jax
import jax.numpy as jnp
import numpy as np
from jax import lax
from jax.experimental import pallas as pl
from jax.experimental.pallas import tpu as pltpu
from jax.sharding import PartitionSpec as P

HALO = 32
FRESNEL = 64
LANES = 128
GATHER_BUDGET = 4 * 2**20
SIN = (
    0.9999999980536763,
    -0.1666666530009577,
    0.008333305907073658,
    -0.00019838908256358006,
    2.745822627876341e-06,
    -2.3043562782810933e-08,
)
COS = (
    0.9999999961345007,
    -0.4999999301617528,
    0.04166646215023687,
    -0.0013886696163545999,
    2.4695045482778703e-05,
    -2.5154931690000354e-07,
)


def horner(coefficients, square):
    total = jnp.full_like(square, coefficients[-1])
    for coefficient in coefficients[-2::-1]:
        total = total * square + coefficient
    return total


def cos_sin(angle):
    square = angle * angle
    return horner(COS, square), horner(SIN, square) * angle


def turn(fraction):
    half_cos, half_sin = cos_sin(fraction * math.pi)
    return half_cos * half_cos - half_sin * half_sin, 2.0 * half_cos * half_sin


def halves(value):
    high = value.astype(jnp.bfloat16)
    return high, (value - high.astype(jnp.float32)).astype(jnp.bfloat16)


def np_halves(matrix):
    high = matrix.astype(jnp.bfloat16)
    return high, (matrix - high.astype(np.float64)).astype(jnp.bfloat16)


def np_taps():
    offset = np.arange(-HALO, HALO + 1, dtype=np.float64)
    taper = np.maximum(np.abs(offset) - 0.5 * HALO, 0.0)
    weight = np.cos(np.pi * taper / (HALO + 2.0)) ** 2 / math.sqrt(FRESNEL)
    return weight * np.exp(1j * np.pi * offset * offset / FRESNEL)


def np_band(out_pos, in_pos):
    offset = out_pos[:, None] - in_pos[None, :]
    inside = np.abs(offset) <= HALO
    return np.where(inside, np_taps()[np.clip(offset, -HALO, HALO) + HALO], 0.0)


def row_constant(height):
    matrices = []
    for core in range(2):
        pos = (np.arange(height) + core * (height // 2)) % height
        band = np_band(pos, pos)
        whole = np.block([[band.real, -band.imag], [band.imag, band.real]])
        matrices.append(np.concatenate(np_halves(whole), axis=1))
    return np.stack(matrices)


def col_constant():
    lane = np.arange(LANES)
    turned = np.where((lane >= HALO) & (lane < LANES - HALO), lane ^ (LANES // 2), lane)
    edge_pos = np.where(turned < LANES // 2, turned + LANES, turned - LANES)
    parts = []
    for position in (lane, edge_pos):
        band = np_band(lane, position).T
        parts.append(np.block([[band.real, band.imag], [-band.imag, band.real]]))
    return np.concatenate(np_halves(np.concatenate(parts, axis=0)), axis=1)


def both_rows(near_ref, far_ref, where):
    return jnp.concatenate([near_ref[where], far_ref[where]], axis=0)


def turned(slice_index, block, screens, wave):
    near_cos, near_sin, far_cos, far_sin = screens
    cos = both_rows(near_cos, far_cos, (slice_index, block))
    sin = both_rows(near_sin, far_sin, (slice_index, block))
    real, imag = wave
    return cos * real - sin * imag, cos * imag + sin * real


def row_product(row_matrix, columns):
    high, low = halves(columns)
    whole, width = columns.shape
    wide = jnp.dot(
        row_matrix[:, :whole], jnp.concatenate([high, low], axis=1), preferred_element_type=jnp.float32
    )
    rest = jnp.dot(row_matrix[:, whole:], high, preferred_element_type=jnp.float32)
    return wide[:, :width] + wide[:, width:] + rest


def col_product(high, low, col_ref):
    wide = jnp.dot(high, col_ref[...], preferred_element_type=jnp.float32)
    rest = jnp.dot(low, col_ref[: 2 * LANES, : 2 * LANES], preferred_element_type=jnp.float32)
    return wide[:, : 2 * LANES] + wide[:, 2 * LANES :] + rest


def three_parts(value):
    high = value.astype(jnp.bfloat16)
    rest = value - high.astype(jnp.float32)
    return high, rest.astype(jnp.bfloat16), pltpu.roll(rest, LANES // 2, 1).astype(jnp.bfloat16)


def advance(slice_index, start, waves, screens, row_matrix, col_ref, edge_ref):
    size, height = len(waves), waves[0][0].shape[0]
    chunks = [range(place, min(place + 2, size)) for place in range(0, size, 2)]
    highs, lows = [], []
    for chunk in chunks:
        columns = [
            jnp.concatenate(turned(slice_index, start + place, screens, waves[place]), axis=0) for place in chunk
        ]
        done = row_product(row_matrix, jnp.concatenate(columns, axis=1))
        for sub, place in enumerate(chunk):
            own_high, own_low = [], []
            for part in range(2):
                value = done[part * height : (part + 1) * height, sub * LANES : (sub + 1) * LANES]
                high, low, swung = three_parts(value)
                own_high.append(high)
                own_low.append(low)
                edge = part * LANES
                if place > 0:
                    edge_ref[place - 1, :, pl.ds(edge, HALO)] = high[:, :HALO]
                    edge_ref[place - 1, :, pl.ds(edge + 2 * HALO, HALO)] = swung[:, 2 * HALO : 3 * HALO]
                if place < size - 1:
                    edge_ref[place + 1, :, pl.ds(edge + 3 * HALO, HALO)] = high[:, 3 * HALO :]
                    edge_ref[place + 1, :, pl.ds(edge + HALO, HALO)] = swung[:, HALO : 2 * HALO]
            highs.append(jnp.concatenate(own_high, axis=1))
            lows.append(jnp.concatenate(own_low, axis=1))
    results = []
    for chunk in chunks:
        rows = len(chunk) * height
        edges = edge_ref[pl.ds(chunk[0], len(chunk))].reshape(rows, 2 * LANES)
        own = jnp.concatenate([highs[place] for place in chunk], axis=0)
        total = col_product(
            jnp.concatenate([own, edges], axis=1),
            jnp.concatenate([lows[place] for place in chunk], axis=0),
            col_ref,
        )
        for sub in range(len(chunk)):
            block = total[sub * height : (sub + 1) * height]
            results.append((block[:, :LANES], block[:, LANES:]))
    return results


def clear_edge(edge_ref, place, right):
    for part in range(2):
        for begin in (0, 2 * HALO) if right else (HALO, 3 * HALO):
            cells = pl.ds(part * LANES + begin, HALO)
            edge_ref[place, :, cells] = jnp.zeros((edge_ref.shape[1], HALO), edge_ref.dtype)


def keep(wave_ref, waves):
    for place, wave in enumerate(waves):
        wave_ref[place, 0], wave_ref[place, 1] = wave


def prepare_kernel(tilt_ref, near_own, near_rest, wave_ref, cos_ref, sin_ref):
    blocks, _, height, _ = wave_ref.shape
    count = cos_ref.shape[0] - 1
    core, own_section, own_place = lax.axis_index("row"), lax.axis_index("depth"), lax.axis_index("col")

    def screens(col, carry):
        held = col ^ own_place
        for bits in range(count):
            angle = near_own[held, 0] if bits == 0 else near_rest[held, bits - 1]
            cos_ref[bits ^ own_section, col], sin_ref[bits ^ own_section, col] = cos_sin(angle)
        return carry

    lax.fori_loop(0, blocks, screens, 0)
    cos_ref[count] = jnp.ones(cos_ref.shape[1:], jnp.float32)
    sin_ref[count] = jnp.zeros(cos_ref.shape[1:], jnp.float32)

    def cycles(number, position, extent):
        fraction = (number * position).astype(jnp.float32) / extent
        return turn(fraction - jnp.round(fraction))

    row = lax.broadcasted_iota(jnp.int32, (height, LANES), 0) + core * (height // 2)
    row = jnp.where(row >= height, row - height, row)
    row_cos, row_sin = cycles(tilt_ref[core, 0], row, float(height))
    for block in range(blocks):
        col_cos, col_sin = cycles(
            tilt_ref[core, 1],
            lax.broadcasted_iota(jnp.int32, (8, LANES), 1) + block * LANES,
            float(blocks * LANES),
        )
        col_cos, col_sin = col_cos[:1], col_sin[:1]
        wave_ref[block, 0] = row_cos * col_cos - row_sin * col_sin
        wave_ref[block, 1] = row_sin * col_cos + row_cos * col_sin


def wave_kernel(
    wave_ref, near_cos, near_sin, near_own, far_own, far_rest, row_ref, col_ref,
    mine_ref, theirs_ref, far_cos, far_sin, kept_ref, moved_ref, left_ref, grad_ref, even_edge, odd_edge,
):
    blocks, _, height, _ = wave_ref.shape
    count = near_cos.shape[0] - 1
    core, own_section, own_place = lax.axis_index("row"), lax.axis_index("depth"), lax.axis_index("col")
    near, far = pl.ds(0, height // 2), pl.ds(height // 2, height // 2)
    screens = (near_cos, near_sin, far_cos, far_sin)
    row_matrix = row_ref[core]
    window = min(3, blocks)
    window_start = jnp.clip(own_place - 1, 0, blocks - window)
    own_in_window = own_place - window_start
    edges = (even_edge, odd_edge)

    def far_screens(slice_index):
        bits = slice_index ^ own_section
        for col in range(blocks):
            held = col ^ own_place
            angle = jnp.where(bits == 0, far_own[held, 0], far_rest[held, jnp.maximum(bits - 1, 0)])
            far_cos[slice_index, col], far_sin[slice_index, col] = cos_sin(angle)

    for edge_ref in edges:
        clear_edge(edge_ref, 0, False)
        clear_edge(edge_ref, blocks - 1, True)
    far_cos[count] = jnp.ones(far_cos.shape[1:], jnp.float32)
    far_sin[count] = jnp.zeros(far_cos.shape[1:], jnp.float32)
    far_screens(0)

    waves = [(wave_ref[place, 0], wave_ref[place, 1]) for place in range(blocks)]
    for tick in range(count):
        entering = (wave_ref if tick == 0 else kept_ref)[own_place]
        moved_ref[tick, 0], moved_ref[tick, 1] = turned(tick, own_place, screens, (entering[0], entering[1]))
        waves = advance(tick, 0, waves, screens, row_matrix, col_ref, edges[tick % 2])
        if tick + 1 < count:
            far_screens(tick + 1)
        keep(kept_ref, waves)
        left_ref[tick] = kept_ref[own_place]

    for edge_ref in edges:
        clear_edge(edge_ref, window - 1, True)
    waves = []
    for place in range(window):
        block = window_start + place
        held = block ^ own_place
        measured = jnp.concatenate([near_own[held, 1 + core], far_own[held, 1]], axis=0)
        real, imag = kept_ref[block, 0], kept_ref[block, 1]
        misfit = 2.0 * (real * real + imag * imag - measured)
        waves.append((misfit * real, -misfit * imag))

    for tick in range(count - 1):
        waves = advance(count - tick, window_start, waves, screens, row_matrix, col_ref, edges[tick % 2])
        keep(kept_ref, waves)
        arrived = count - 1 - tick
        pulled = kept_ref[own_in_window]
        grad_ref[arrived] = -(pulled[1] * moved_ref[arrived, 0] + pulled[0] * moved_ref[arrived, 1])

    left, right = jnp.maximum(own_place - 1, 0), jnp.minimum(own_place + 1, blocks - 1)
    lane = lax.broadcasted_iota(jnp.int32, (2 * height, LANES), 1)
    has_left, has_right = own_place > 0, own_place < blocks - 1

    def cells(block):
        wave = kept_ref[block - window_start]
        return jnp.concatenate(turned(1, block, screens, (wave[0], wave[1])), axis=0)

    edge_cells = jnp.where(
        lane < LANES // 2, jnp.where(has_right, cells(right), 0.0), jnp.where(has_left, cells(left), 0.0)
    )
    done = row_product(row_matrix, jnp.concatenate([cells(own_place), edge_cells], axis=1))
    lane = lax.broadcasted_iota(jnp.int32, (height, LANES), 1)
    between = (lane >= HALO) & (lane < LANES - HALO)
    highs, lows, edges = [], [], []
    for part in range(2):
        high, low, _ = three_parts(done[part * height : (part + 1) * height, :LANES])
        highs.append(high)
        lows.append(low)
        value = done[part * height : (part + 1) * height, LANES:]
        whole_high = value.astype(jnp.bfloat16).astype(jnp.float32)
        edge = jnp.where(between, pltpu.roll(value - whole_high, LANES // 2, 1), whole_high)
        edges.append(edge.astype(jnp.bfloat16))
    pulled = col_product(jnp.concatenate(highs + edges, axis=1), jnp.concatenate(lows, axis=1), col_ref)
    grad_ref[0] = -(pulled[:, LANES:] * moved_ref[0, 0] + pulled[:, :LANES] * moved_ref[0, 1])

    for target, row in ((mine_ref, near), (theirs_ref, far)):
        for part in range(2):
            target[0, part] = left_ref[own_section, part, row]
        target[0, 2] = grad_ref[own_section, row]


def finish_kernel(mine_ref, received_ref, grad_ref, exit_ref, total_ref, sems):
    core = lax.axis_index("row")
    copies = []
    for source, item in ((mine_ref, core), (received_ref, 1 - core)):
        copies.append(pltpu.make_async_copy(source.at[:, pl.ds(0, 2)], exit_ref.at[item], sems.at[len(copies)]))
    for copy in copies:
        copy.start()
    total_ref[...] = mine_ref[:, 2] + received_ref[:, 2]
    copies.append(pltpu.make_async_copy(total_ref, grad_ref, sems.at[2]))
    copies[2].start()
    for copy in copies:
        copy.wait()


def spread(shard, axis, reach=None):
    size = lax.axis_size(axis)
    reach = size if reach is None else reach
    pieces = []
    for bits in range(1, size):
        pairs = [(i, i ^ bits) for i in range(size) if abs(i - (i ^ bits)) <= reach]
        pieces.append(lax.ppermute(shard, axis, pairs) if pairs else jnp.zeros_like(shard))
    return pieces


def swap_cores(value):
    return lax.ppermute(value, "row", [(0, 1), (1, 0)])


def whole_field_body(phase, tilt, intensity):
    _, tile_r, tile_c = phase.shape
    count, blocks = lax.axis_size("depth"), lax.axis_size("col")
    core = lax.axis_index("row")
    height = 2 * tile_r
    vmem = pl.BlockSpec(memory_space=pltpu.VMEM)
    smem = pl.BlockSpec(memory_space=pltpu.SMEM)
    hbm = pl.BlockSpec(memory_space=pl.ANY)

    def array(*shape):
        return jax.ShapeDtypeStruct(shape, jnp.float32)

    def params(mebibytes):
        return pltpu.CompilerParams(vmem_limit_bytes=mebibytes * 2**20)

    other_depths = spread(phase, "depth")
    other_depths[0], measured, slab = lax.optimization_barrier((other_depths[0], intensity, phase))
    other_depths = jnp.concatenate(other_depths, axis=0)
    packet = jnp.concatenate([slab, measured], axis=0)
    near_own = [packet]
    for bits in range(1, blocks):
        pairs = [(i, i ^ bits) for i in range(blocks)]
        close = [(i, j) for i, j in pairs if abs(i - j) <= 1]
        if close:
            near_own.append(lax.ppermute(packet, "col", close))
        else:
            further = [(i, j) for i, j in pairs if abs(i - j) <= 2]
            arrived = lax.ppermute(slab, "col", further) if further else jnp.zeros_like(slab)
            near_own.append(jnp.concatenate([arrived, jnp.zeros_like(measured)], axis=0))
    near_own = jnp.stack(near_own)
    arriving = spread(other_depths, "col", 2)
    arriving[0], near_own = lax.optimization_barrier((arriving[0], near_own))
    near_rest = jnp.stack([other_depths] + arriving)
    wanted = lax.dynamic_slice_in_dim(near_own, 2 - core, 1, 1)
    far_own = swap_cores(jnp.concatenate([near_own[:, :1], wanted], axis=1))
    far_rest = swap_cores(near_rest)

    half_screens = (count + 1, blocks, tile_r, tile_c)
    field = (blocks, 2, height, tile_c)
    wave, near_cos, near_sin = pl.pallas_call(
        prepare_kernel,
        out_shape=(array(*field), array(*half_screens), array(*half_screens)),
        in_specs=[smem, vmem, vmem],
        out_specs=(vmem,) * 3,
        compiler_params=params(8),
        cost_estimate=pl.CostEstimate(flops=5 * 10**8, bytes_accessed=2**20, transcendentals=0),
    )(tilt, near_own, near_rest)
    mine, theirs = pl.pallas_call(
        wave_kernel,
        out_shape=(array(1, 3, tile_r, tile_c),) * 2,
        in_specs=[vmem] * 8,
        out_specs=(vmem,) * 2,
        scratch_shapes=[pltpu.VMEM(half_screens, jnp.float32)] * 2
        + [pltpu.VMEM(field, jnp.float32)]
        + [pltpu.VMEM((count, 2, height, tile_c), jnp.float32)] * 2
        + [pltpu.VMEM((count, height, tile_c), jnp.float32)]
        + [pltpu.VMEM((blocks, height, 2 * LANES), jnp.bfloat16)] * 2,
        compiler_params=params(24),
    )(
        wave, near_cos, near_sin, near_own, far_own, far_rest,
        jnp.asarray(row_constant(height)), jnp.asarray(col_constant()),
    )
    return pl.pallas_call(
        finish_kernel,
        out_shape=(array(*phase.shape), array(2, 1, 2, tile_r, tile_c)),
        in_specs=[vmem, vmem],
        out_specs=(hbm, hbm),
        scratch_shapes=[pltpu.VMEM(phase.shape, jnp.float32), pltpu.SemaphoreType.DMA((3,))],
        compiler_params=params(4),
    )(mine, swap_cores(theirs))


def extended_2(cells, sides, width):
    for axis, dim in sides:
        count = lax.axis_size(axis)
        ends = count - 1
        head = lax.slice_in_dim(cells, 0, width, axis=dim)
        tail = lax.slice_in_dim(cells, cells.shape[dim] - width, cells.shape[dim], axis=dim)
        cells = jnp.concatenate(
            [
                lax.ppermute(tail, axis, [(i, (i + 1) % count) for i in range(ends)]),
                cells,
                lax.ppermute(head, axis, [((i + 1) % count, i) for i in range(ends)]),
            ],
            axis=dim,
        )
    return cells


def from_behind(value, axis, steps):
    count = lax.axis_size(axis)
    leading, last = (max(0, -steps), min(count, count - steps))
    return lax.ppermute(value, axis, [(source, source + steps) for source in range(leading, last)])


def band_matrix(block_size, margin, fresnel, adjoint):
    shape_full = (block_size, block_size + 2 * margin)
    out_idx = lax.broadcasted_iota(jnp.int32, shape_full, 0)
    in_idx = lax.broadcasted_iota(jnp.int32, shape_full, 1)
    offset = (out_idx + margin - in_idx).astype(jnp.float32)
    inside = jnp.abs(offset) <= margin
    taper_dist = jnp.maximum(jnp.abs(offset) - 0.5 * margin, 0.0)
    profile = jnp.cos(jnp.pi * taper_dist / (margin + 2.0))
    weight = profile * profile / math.sqrt(fresnel)
    phase_angle = jnp.pi * offset * offset / fresnel
    real_part = jnp.where(inside, jnp.cos(phase_angle) * weight, 0.0)
    imag_part = jnp.where(inside, jnp.sin(phase_angle) * weight, 0.0)
    if adjoint:
        imag_part = -imag_part
    upper = jnp.stack([real_part, -imag_part])
    lower = jnp.stack([imag_part, real_part])
    return jnp.stack([upper, lower])


def along_rows(extended, matrix):
    pieces = [jnp.einsum("pqij,gqjc->gpic", matrix, extended, precision=lax.Precision.HIGHEST)]
    return jnp.concatenate(pieces, axis=2)


def along_cols(extended, matrix, margin):
    block_size = matrix.shape[2]
    extent = extended.shape[3] - 2 * margin
    pieces = []
    for block_start in range(0, extent, block_size):
        window = extended[:, :, :, block_start : block_start + block_size + 2 * margin]
        pieces.append(
            jnp.einsum("pqij,gqrj->gpri", matrix, window, precision=lax.Precision.HIGHEST)
        )
    return jnp.concatenate(pieces, axis=3)


def propagate(current, row_matrix, col_matrix):
    with_rows = extended_2(current, (("row", 2),), HALO)
    row_done = along_rows(with_rows, row_matrix)
    with_cols = extended_2(row_done, (("col", 3),), HALO)
    return along_cols(with_cols, col_matrix, HALO)


def transmit(screen, current, adjoint):
    screen_re = screen[0][None]
    screen_im = screen[1][None]
    if adjoint:
        screen_im = -screen_im
    real_part = screen_re * current[:, 0] - screen_im * current[:, 1]
    imag_part = screen_re * current[:, 1] + screen_im * current[:, 0]
    return jnp.stack([real_part, imag_part], axis=1)


def store_item(store, current, first_item, slice_index, active):
    begin = (first_item, jnp.int32(slice_index), jnp.int32(0), jnp.int32(0), jnp.int32(0))
    sizes_now = (current.shape[0], 1) + current.shape[1:]
    previous = lax.dynamic_slice(store, begin, sizes_now)
    fresh = jnp.where(active, current[:, None], previous)
    return lax.dynamic_update_slice(store, fresh, begin)


def staged_body(phase, tilt, intensity):
    slices, tile_r, tile_c = phase.shape
    batch_size = tilt.shape[0]
    sections = lax.axis_size("depth")
    section_index = lax.axis_index("depth")
    group_size = 1
    groups = batch_size // group_size
    tick_count = sections + groups - 1
    block_r = 64
    block_c = 128
    fwd_rows = band_matrix(block_r, HALO, FRESNEL, False)
    fwd_cols = band_matrix(block_c, HALO, FRESNEL, False)
    adj_rows = band_matrix(block_r, HALO, FRESNEL, True)
    adj_cols = band_matrix(block_c, HALO, FRESNEL, True)
    row_pos = (
        lax.axis_index("row") * tile_r + lax.broadcasted_iota(jnp.int32, (tile_r, tile_c), 0)
    ).astype(jnp.float32)
    col_pos = (
        lax.axis_index("col") * tile_c + lax.broadcasted_iota(jnp.int32, (tile_r, tile_c), 1)
    ).astype(jnp.float32)
    height = float(tile_r * lax.axis_size("row"))
    width_all = float(tile_c * lax.axis_size("col"))
    tilt_f = tilt.astype(jnp.float32)
    phase_angle = (
        2.0
        * jnp.pi
        * (
            tilt_f[:, 0, None, None] * row_pos / height
            + tilt_f[:, 1, None, None] * col_pos / width_all
        )
    )
    incident = jnp.stack([jnp.cos(phase_angle), jnp.sin(phase_angle)], axis=1)
    screens = jnp.stack([jnp.cos(phase), jnp.sin(phase)], axis=1)

    def forward_tick(tick_now, carry):
        incoming, entering, leaving = carry
        group_index = tick_now - section_index
        active = (group_index >= 0) & (group_index < groups)
        first_item = jnp.clip(group_index, 0, groups - 1) * group_size
        current = jnp.where(
            section_index == 0,
            lax.dynamic_slice_in_dim(incident, first_item, group_size, 0),
            incoming,
        )
        entering = store_item(entering, current, first_item, 0, active)
        current = propagate(transmit(screens[0], current, False), fwd_rows, fwd_cols)
        leaving = store_item(leaving, current, first_item, 0, active)
        incoming = from_behind(current, "depth", 1)
        return (incoming, entering, leaving)

    store_zero = jnp.zeros((batch_size, slices, 2, tile_r, tile_c), jnp.float32)
    start_wave = jnp.zeros((group_size, 2, tile_r, tile_c), jnp.float32)
    _, entering, leaving = lax.fori_loop(
        0, tick_count, forward_tick, (start_wave, store_zero, store_zero)
    )
    final_wave = leaving[:, slices - 1]
    misfit = final_wave[:, 0] * final_wave[:, 0] + final_wave[:, 1] * final_wave[:, 1] - intensity
    seed_adjoint = 2.0 * misfit[:, None] * final_wave

    def backward_tick(tick_now, carry):
        incoming, gradient = carry
        group_index = tick_now - (sections - 1 - section_index)
        active = (group_index >= 0) & (group_index < groups)
        first_item = jnp.clip(group_index, 0, groups - 1) * group_size
        adjoint_wave = jnp.where(
            section_index == sections - 1,
            lax.dynamic_slice_in_dim(seed_adjoint, first_item, group_size, 0),
            incoming,
        )
        for slice_index in reversed(range(slices)):
            pulled = propagate(adjoint_wave, adj_rows, adj_cols)
            arrived = lax.dynamic_slice_in_dim(entering[:, slice_index], first_item, group_size, 0)
            moved = transmit(screens[slice_index], arrived, False)
            contribution = jnp.sum(pulled[:, 1] * moved[:, 0] - pulled[:, 0] * moved[:, 1], axis=0)
            gradient = gradient.at[slice_index].add(jnp.where(active, contribution, 0.0))
            adjoint_wave = transmit(screens[slice_index], pulled, True)
        incoming = from_behind(adjoint_wave, "depth", -1)
        return (incoming, gradient)

    grad_zero = jnp.zeros((slices, tile_r, tile_c), jnp.float32)
    _, gradient = lax.fori_loop(0, tick_count, backward_tick, (start_wave, grad_zero))
    return (gradient, leaving)


def fits_whole(phase_shape, batch, mesh):
    slices, height, width = phase_shape
    rows, cols, sections = mesh.shape["row"], mesh.shape["col"], mesh.shape["depth"]
    return (
        4 * height * width * (slices + batch) <= GATHER_BUDGET
        and batch == rows == 2
        and slices == sections
        and sections & (sections - 1) == 0
        and cols & (cols - 1) == 0
        and height == LANES
        and width == cols * LANES
        and cols > 1
        and sections > 1
        and sections * HALO <= LANES
    )


def solution(mesh):
    placed = (P("depth", "row", "col"), P(), P(None, "row", "col"))

    def run(phase, tilt, intensity):
        if fits_whole(phase.shape, tilt.shape[0], mesh):
            body = whole_field_body
        else:
            body = staged_body
        return jax.shard_map(
            body,
            mesh=mesh,
            in_specs=placed,
            out_specs=(P("depth", "row", "col"), P(None, "depth", None, "row", "col")),
            check_vma=False,
        )(phase, tilt, intensity)

    return run
```

```python
import math

import jax
import jax.numpy as jnp
import numpy as np
from jax import lax
from jax.experimental import pallas as pl
from jax.experimental.pallas import tpu as pltpu
from jax.sharding import PartitionSpec as P

HALO = 32
FRESNEL = 64
LANES = 128
GATHER_BUDGET = 4 * 2**20
SIN = (
    0.9999999980536763,
    -0.1666666530009577,
    0.008333305907073658,
    -0.00019838908256358006,
    2.745822627876341e-06,
    -2.3043562782810933e-08,
)
COS = (
    0.9999999961345007,
    -0.4999999301617528,
    0.04166646215023687,
    -0.0013886696163545999,
    2.4695045482778703e-05,
    -2.5154931690000354e-07,
)


def horner(coefficients, square):
    total = jnp.full_like(square, coefficients[-1])
    for coefficient in coefficients[-2::-1]:
        total = total * square + coefficient
    return total


def cos_sin(angle):
    square = angle * angle
    return horner(COS, square), horner(SIN, square) * angle


def turn(fraction):
    half_cos, half_sin = cos_sin(fraction * math.pi)
    return half_cos * half_cos - half_sin * half_sin, 2.0 * half_cos * half_sin


def halves(value):
    high = value.astype(jnp.bfloat16)
    return high, (value - high.astype(jnp.float32)).astype(jnp.bfloat16)


def np_halves(matrix):
    high = matrix.astype(jnp.bfloat16)
    return high, (matrix - high.astype(np.float64)).astype(jnp.bfloat16)


def np_taps():
    offset = np.arange(-HALO, HALO + 1, dtype=np.float64)
    taper = np.maximum(np.abs(offset) - 0.5 * HALO, 0.0)
    weight = np.cos(np.pi * taper / (HALO + 2.0)) ** 2 / math.sqrt(FRESNEL)
    return weight * np.exp(1j * np.pi * offset * offset / FRESNEL)


def np_band(out_pos, in_pos):
    offset = out_pos[:, None] - in_pos[None, :]
    inside = np.abs(offset) <= HALO
    return np.where(inside, np_taps()[np.clip(offset, -HALO, HALO) + HALO], 0.0)


def row_constant(height):
    matrices = []
    for core in range(2):
        pos = (np.arange(height) + core * (height // 2)) % height
        band = np_band(pos, pos)
        whole = np.block([[band.real, -band.imag], [band.imag, band.real]])
        matrices.append(np.concatenate(np_halves(whole), axis=1))
    return np.stack(matrices)


def col_constant():
    lane = np.arange(LANES)
    turned = np.where((lane >= HALO) & (lane < LANES - HALO), lane ^ (LANES // 2), lane)
    edge_pos = np.where(turned < LANES // 2, turned + LANES, turned - LANES)
    parts = []
    for position in (lane, edge_pos):
        band = np_band(lane, position).T
        parts.append(np.block([[band.real, band.imag], [-band.imag, band.real]]))
    return np.concatenate(np_halves(np.concatenate(parts, axis=0)), axis=1)


def both_rows(near_ref, far_ref, where):
    return jnp.concatenate([near_ref[where], far_ref[where]], axis=0)


def turned(slice_index, block, screens, wave):
    near_cos, near_sin, far_cos, far_sin = screens
    cos = both_rows(near_cos, far_cos, (slice_index, block))
    sin = both_rows(near_sin, far_sin, (slice_index, block))
    real, imag = wave
    return cos * real - sin * imag, cos * imag + sin * real


def row_product(row_matrix, columns):
    high, low = halves(columns)
    whole, width = columns.shape
    wide = jnp.dot(
        row_matrix[:, :whole], jnp.concatenate([high, low], axis=1), preferred_element_type=jnp.float32
    )
    rest = jnp.dot(row_matrix[:, whole:], high, preferred_element_type=jnp.float32)
    return wide[:, :width] + wide[:, width:] + rest


def col_product(high, low, col_ref):
    wide = jnp.dot(high, col_ref[...], preferred_element_type=jnp.float32)
    rest = jnp.dot(low, col_ref[: 2 * LANES, : 2 * LANES], preferred_element_type=jnp.float32)
    return wide[:, : 2 * LANES] + wide[:, 2 * LANES :] + rest


def three_parts(value):
    high = value.astype(jnp.bfloat16)
    rest = value - high.astype(jnp.float32)
    return high, rest.astype(jnp.bfloat16), pltpu.roll(rest, LANES // 2, 1).astype(jnp.bfloat16)


def advance(slice_index, start, waves, screens, row_matrix, col_ref, edge_ref):
    size, height = len(waves), waves[0][0].shape[0]
    chunks = [range(place, min(place + 2, size)) for place in range(0, size, 2)]
    highs, lows = [], []
    for chunk in chunks:
        columns = [
            jnp.concatenate(turned(slice_index, start + place, screens, waves[place]), axis=0) for place in chunk
        ]
        done = row_product(row_matrix, jnp.concatenate(columns, axis=1))
        for sub, place in enumerate(chunk):
            own_high, own_low = [], []
            for part in range(2):
                value = done[part * height : (part + 1) * height, sub * LANES : (sub + 1) * LANES]
                high, low, swung = three_parts(value)
                own_high.append(high)
                own_low.append(low)
                edge = part * LANES
                if place > 0:
                    edge_ref[place - 1, :, pl.ds(edge, HALO)] = high[:, :HALO]
                    edge_ref[place - 1, :, pl.ds(edge + 2 * HALO, HALO)] = swung[:, 2 * HALO : 3 * HALO]
                if place < size - 1:
                    edge_ref[place + 1, :, pl.ds(edge + 3 * HALO, HALO)] = high[:, 3 * HALO :]
                    edge_ref[place + 1, :, pl.ds(edge + HALO, HALO)] = swung[:, HALO : 2 * HALO]
            highs.append(jnp.concatenate(own_high, axis=1))
            lows.append(jnp.concatenate(own_low, axis=1))
    results = []
    for chunk in chunks:
        rows = len(chunk) * height
        edges = edge_ref[pl.ds(chunk[0], len(chunk))].reshape(rows, 2 * LANES)
        own = jnp.concatenate([highs[place] for place in chunk], axis=0)
        total = col_product(
            jnp.concatenate([own, edges], axis=1),
            jnp.concatenate([lows[place] for place in chunk], axis=0),
            col_ref,
        )
        for sub in range(len(chunk)):
            block = total[sub * height : (sub + 1) * height]
            results.append((block[:, :LANES], block[:, LANES:]))
    return results


def clear_edge(edge_ref, place, right):
    for part in range(2):
        for begin in (0, 2 * HALO) if right else (HALO, 3 * HALO):
            cells = pl.ds(part * LANES + begin, HALO)
            edge_ref[place, :, cells] = jnp.zeros((edge_ref.shape[1], HALO), edge_ref.dtype)


def keep(wave_ref, waves):
    for place, wave in enumerate(waves):
        wave_ref[place, 0], wave_ref[place, 1] = wave


def prepare_kernel(tilt_ref, near_own, near_rest, wave_ref, cos_ref, sin_ref):
    blocks, _, height, _ = wave_ref.shape
    count = cos_ref.shape[0] - 1
    core, own_section, own_place = lax.axis_index("row"), lax.axis_index("depth"), lax.axis_index("col")

    def screens(col, carry):
        held = col ^ own_place
        for bits in range(count):
            angle = near_own[held, 0] if bits == 0 else near_rest[held, bits - 1]
            cos_ref[bits ^ own_section, col], sin_ref[bits ^ own_section, col] = cos_sin(angle)
        return carry

    lax.fori_loop(0, blocks, screens, 0)
    cos_ref[count] = jnp.ones(cos_ref.shape[1:], jnp.float32)
    sin_ref[count] = jnp.zeros(cos_ref.shape[1:], jnp.float32)

    def cycles(number, position, extent):
        fraction = (number * position).astype(jnp.float32) / extent
        return turn(fraction - jnp.round(fraction))

    row = lax.broadcasted_iota(jnp.int32, (height, LANES), 0) + core * (height // 2)
    row = jnp.where(row >= height, row - height, row)
    row_cos, row_sin = cycles(tilt_ref[core, 0], row, float(height))
    for block in range(blocks):
        col_cos, col_sin = cycles(
            tilt_ref[core, 1],
            lax.broadcasted_iota(jnp.int32, (8, LANES), 1) + block * LANES,
            float(blocks * LANES),
        )
        col_cos, col_sin = col_cos[:1], col_sin[:1]
        wave_ref[block, 0] = row_cos * col_cos - row_sin * col_sin
        wave_ref[block, 1] = row_sin * col_cos + row_cos * col_sin


def wave_kernel(
    wave_ref, near_cos, near_sin, near_own, far_own, far_rest, row_ref, col_ref,
    mine_ref, theirs_ref, far_cos, far_sin, kept_ref, moved_ref, left_ref, grad_ref, edge_ref,
):
    blocks, _, height, _ = wave_ref.shape
    count = near_cos.shape[0] - 1
    core, own_section, own_place = lax.axis_index("row"), lax.axis_index("depth"), lax.axis_index("col")
    near, far = pl.ds(0, height // 2), pl.ds(height // 2, height // 2)
    screens = (near_cos, near_sin, far_cos, far_sin)
    row_matrix = row_ref.at[core]
    window = min(3, blocks)
    window_start = jnp.clip(own_place - 1, 0, blocks - window)
    own_in_window = own_place - window_start

    def far_screens(slice_index):
        bits = slice_index ^ own_section
        for col in range(blocks):
            held = col ^ own_place
            angle = jnp.where(bits == 0, far_own[held, 0], far_rest[held, jnp.maximum(bits - 1, 0)])
            far_cos[slice_index, col], far_sin[slice_index, col] = cos_sin(angle)

    clear_edge(edge_ref, 0, False)
    clear_edge(edge_ref, blocks - 1, True)
    far_cos[count] = jnp.ones(far_cos.shape[1:], jnp.float32)
    far_sin[count] = jnp.zeros(far_cos.shape[1:], jnp.float32)
    far_screens(0)

    def held_waves(size):
        return [(kept_ref[place, 0], kept_ref[place, 1]) for place in range(size)]

    def forward(tick, carry):
        entering = kept_ref[own_place]
        moved_ref[tick, 0], moved_ref[tick, 1] = turned(tick, own_place, screens, (entering[0], entering[1]))
        waves = advance(tick, 0, held_waves(blocks), screens, row_matrix[...], col_ref, edge_ref)
        far_screens(jnp.minimum(tick + 1, count - 1))
        keep(kept_ref, waves)
        left_ref[tick] = kept_ref[own_place]
        return carry

    kept_ref[...] = wave_ref[...]
    lax.fori_loop(0, count, forward, 0)

    clear_edge(edge_ref, window - 1, True)
    waves = []
    for place in range(window):
        block = window_start + place
        held = block ^ own_place
        measured = jnp.concatenate([near_own[held, 1 + core], far_own[held, 1]], axis=0)
        real, imag = kept_ref[block, 0], kept_ref[block, 1]
        misfit = 2.0 * (real * real + imag * imag - measured)
        waves.append((misfit * real, -misfit * imag))

    keep(kept_ref, waves)

    def backward(tick, carry):
        waves = advance(
            count - tick, window_start, held_waves(window), screens, row_matrix[...], col_ref, edge_ref
        )
        keep(kept_ref, waves)
        arrived = count - 1 - tick
        pulled = kept_ref[own_in_window]
        grad_ref[arrived] = -(pulled[1] * moved_ref[arrived, 0] + pulled[0] * moved_ref[arrived, 1])
        return carry

    lax.fori_loop(0, count - 1, backward, 0)

    left, right = jnp.maximum(own_place - 1, 0), jnp.minimum(own_place + 1, blocks - 1)
    lane = lax.broadcasted_iota(jnp.int32, (2 * height, LANES), 1)
    has_left, has_right = own_place > 0, own_place < blocks - 1

    def cells(block):
        wave = kept_ref[block - window_start]
        return jnp.concatenate(turned(1, block, screens, (wave[0], wave[1])), axis=0)

    edge_cells = jnp.where(
        lane < LANES // 2, jnp.where(has_right, cells(right), 0.0), jnp.where(has_left, cells(left), 0.0)
    )
    done = row_product(row_matrix[...], jnp.concatenate([cells(own_place), edge_cells], axis=1))
    lane = lax.broadcasted_iota(jnp.int32, (height, LANES), 1)
    between = (lane >= HALO) & (lane < LANES - HALO)
    highs, lows, edges = [], [], []
    for part in range(2):
        high, low, _ = three_parts(done[part * height : (part + 1) * height, :LANES])
        highs.append(high)
        lows.append(low)
        value = done[part * height : (part + 1) * height, LANES:]
        whole_high = value.astype(jnp.bfloat16).astype(jnp.float32)
        edge = jnp.where(between, pltpu.roll(value - whole_high, LANES // 2, 1), whole_high)
        edges.append(edge.astype(jnp.bfloat16))
    pulled = col_product(jnp.concatenate(highs + edges, axis=1), jnp.concatenate(lows, axis=1), col_ref)
    grad_ref[0] = -(pulled[:, LANES:] * moved_ref[0, 0] + pulled[:, :LANES] * moved_ref[0, 1])

    for target, row in ((mine_ref, near), (theirs_ref, far)):
        for part in range(2):
            target[0, part] = left_ref[own_section, part, row]
        target[0, 2] = grad_ref[own_section, row]


def finish_kernel(mine_ref, received_ref, grad_ref, exit_ref, total_ref, sems):
    core = lax.axis_index("row")
    copies = []
    for source, item in ((mine_ref, core), (received_ref, 1 - core)):
        copies.append(pltpu.make_async_copy(source.at[:, pl.ds(0, 2)], exit_ref.at[item], sems.at[len(copies)]))
    for copy in copies:
        copy.start()
    total_ref[...] = mine_ref[:, 2] + received_ref[:, 2]
    copies.append(pltpu.make_async_copy(total_ref, grad_ref, sems.at[2]))
    copies[2].start()
    for copy in copies:
        copy.wait()


def spread(shard, axis, reach=None):
    size = lax.axis_size(axis)
    reach = size if reach is None else reach
    pieces = []
    for bits in range(1, size):
        pairs = [(i, i ^ bits) for i in range(size) if abs(i - (i ^ bits)) <= reach]
        pieces.append(lax.ppermute(shard, axis, pairs) if pairs else jnp.zeros_like(shard))
    return pieces


def swap_cores(value):
    return lax.ppermute(value, "row", [(0, 1), (1, 0)])


def whole_field_body(phase, tilt, intensity):
    _, tile_r, tile_c = phase.shape
    count, blocks = lax.axis_size("depth"), lax.axis_size("col")
    core = lax.axis_index("row")
    height = 2 * tile_r
    vmem = pl.BlockSpec(memory_space=pltpu.VMEM)
    smem = pl.BlockSpec(memory_space=pltpu.SMEM)
    hbm = pl.BlockSpec(memory_space=pl.ANY)

    def array(*shape):
        return jax.ShapeDtypeStruct(shape, jnp.float32)

    def params(mebibytes):
        return pltpu.CompilerParams(vmem_limit_bytes=mebibytes * 2**20)

    other_depths = spread(phase, "depth")
    other_depths[0], measured, slab = lax.optimization_barrier((other_depths[0], intensity, phase))
    other_depths = jnp.concatenate(other_depths, axis=0)
    packet = jnp.concatenate([slab, measured], axis=0)
    near_own = [packet]
    for bits in range(1, blocks):
        pairs = [(i, i ^ bits) for i in range(blocks)]
        close = [(i, j) for i, j in pairs if abs(i - j) <= 1]
        if close:
            near_own.append(lax.ppermute(packet, "col", close))
        else:
            further = [(i, j) for i, j in pairs if abs(i - j) <= 2]
            arrived = lax.ppermute(slab, "col", further) if further else jnp.zeros_like(slab)
            near_own.append(jnp.concatenate([arrived, jnp.zeros_like(measured)], axis=0))
    near_own = jnp.stack(near_own)
    arriving = spread(other_depths, "col", 2)
    arriving[0], near_own = lax.optimization_barrier((arriving[0], near_own))
    near_rest = jnp.stack([other_depths] + arriving)
    wanted = lax.dynamic_slice_in_dim(near_own, 2 - core, 1, 1)
    far_own = swap_cores(jnp.concatenate([near_own[:, :1], wanted], axis=1))
    far_rest = swap_cores(near_rest)

    half_screens = (count + 1, blocks, tile_r, tile_c)
    field = (blocks, 2, height, tile_c)
    wave, near_cos, near_sin = pl.pallas_call(
        prepare_kernel,
        out_shape=(array(*field), array(*half_screens), array(*half_screens)),
        in_specs=[smem, vmem, vmem],
        out_specs=(vmem,) * 3,
        compiler_params=params(8),
        cost_estimate=pl.CostEstimate(flops=5 * 10**8, bytes_accessed=2**20, transcendentals=0),
    )(tilt, near_own, near_rest)
    mine, theirs = pl.pallas_call(
        wave_kernel,
        out_shape=(array(1, 3, tile_r, tile_c),) * 2,
        in_specs=[vmem] * 8,
        out_specs=(vmem,) * 2,
        scratch_shapes=[pltpu.VMEM(half_screens, jnp.float32)] * 2
        + [pltpu.VMEM(field, jnp.float32)]
        + [pltpu.VMEM((count, 2, height, tile_c), jnp.float32)] * 2
        + [pltpu.VMEM((count, height, tile_c), jnp.float32)]
        + [pltpu.VMEM((blocks, height, 2 * LANES), jnp.bfloat16)],
        compiler_params=params(24),
    )(
        wave, near_cos, near_sin, near_own, far_own, far_rest,
        jnp.asarray(row_constant(height)), jnp.asarray(col_constant()),
    )
    return pl.pallas_call(
        finish_kernel,
        out_shape=(array(*phase.shape), array(2, 1, 2, tile_r, tile_c)),
        in_specs=[vmem, vmem],
        out_specs=(hbm, hbm),
        scratch_shapes=[pltpu.VMEM(phase.shape, jnp.float32), pltpu.SemaphoreType.DMA((3,))],
        compiler_params=params(4),
    )(mine, swap_cores(theirs))


def extended_2(cells, sides, width):
    for axis, dim in sides:
        count = lax.axis_size(axis)
        ends = count - 1
        head = lax.slice_in_dim(cells, 0, width, axis=dim)
        tail = lax.slice_in_dim(cells, cells.shape[dim] - width, cells.shape[dim], axis=dim)
        cells = jnp.concatenate(
            [
                lax.ppermute(tail, axis, [(i, (i + 1) % count) for i in range(ends)]),
                cells,
                lax.ppermute(head, axis, [((i + 1) % count, i) for i in range(ends)]),
            ],
            axis=dim,
        )
    return cells


def from_behind(value, axis, steps):
    count = lax.axis_size(axis)
    leading, last = (max(0, -steps), min(count, count - steps))
    return lax.ppermute(value, axis, [(source, source + steps) for source in range(leading, last)])


def band_matrix(block_size, margin, fresnel, adjoint):
    shape_full = (block_size, block_size + 2 * margin)
    out_idx = lax.broadcasted_iota(jnp.int32, shape_full, 0)
    in_idx = lax.broadcasted_iota(jnp.int32, shape_full, 1)
    offset = (out_idx + margin - in_idx).astype(jnp.float32)
    inside = jnp.abs(offset) <= margin
    taper_dist = jnp.maximum(jnp.abs(offset) - 0.5 * margin, 0.0)
    profile = jnp.cos(jnp.pi * taper_dist / (margin + 2.0))
    weight = profile * profile / math.sqrt(fresnel)
    phase_angle = jnp.pi * offset * offset / fresnel
    real_part = jnp.where(inside, jnp.cos(phase_angle) * weight, 0.0)
    imag_part = jnp.where(inside, jnp.sin(phase_angle) * weight, 0.0)
    if adjoint:
        imag_part = -imag_part
    upper = jnp.stack([real_part, -imag_part])
    lower = jnp.stack([imag_part, real_part])
    return jnp.stack([upper, lower])


def along_rows(extended, matrix):
    pieces = [jnp.einsum("pqij,gqjc->gpic", matrix, extended, precision=lax.Precision.HIGHEST)]
    return jnp.concatenate(pieces, axis=2)


def along_cols(extended, matrix, margin):
    block_size = matrix.shape[2]
    extent = extended.shape[3] - 2 * margin
    pieces = []
    for block_start in range(0, extent, block_size):
        window = extended[:, :, :, block_start : block_start + block_size + 2 * margin]
        pieces.append(
            jnp.einsum("pqij,gqrj->gpri", matrix, window, precision=lax.Precision.HIGHEST)
        )
    return jnp.concatenate(pieces, axis=3)


def propagate(current, row_matrix, col_matrix):
    with_rows = extended_2(current, (("row", 2),), HALO)
    row_done = along_rows(with_rows, row_matrix)
    with_cols = extended_2(row_done, (("col", 3),), HALO)
    return along_cols(with_cols, col_matrix, HALO)


def transmit(screen, current, adjoint):
    screen_re = screen[0][None]
    screen_im = screen[1][None]
    if adjoint:
        screen_im = -screen_im
    real_part = screen_re * current[:, 0] - screen_im * current[:, 1]
    imag_part = screen_re * current[:, 1] + screen_im * current[:, 0]
    return jnp.stack([real_part, imag_part], axis=1)


def store_item(store, current, first_item, slice_index, active):
    begin = (first_item, jnp.int32(slice_index), jnp.int32(0), jnp.int32(0), jnp.int32(0))
    sizes_now = (current.shape[0], 1) + current.shape[1:]
    previous = lax.dynamic_slice(store, begin, sizes_now)
    fresh = jnp.where(active, current[:, None], previous)
    return lax.dynamic_update_slice(store, fresh, begin)


def staged_body(phase, tilt, intensity):
    slices, tile_r, tile_c = phase.shape
    batch_size = tilt.shape[0]
    sections = lax.axis_size("depth")
    section_index = lax.axis_index("depth")
    group_size = 1
    groups = batch_size // group_size
    tick_count = sections + groups - 1
    block_r = 64
    block_c = 128
    fwd_rows = band_matrix(block_r, HALO, FRESNEL, False)
    fwd_cols = band_matrix(block_c, HALO, FRESNEL, False)
    adj_rows = band_matrix(block_r, HALO, FRESNEL, True)
    adj_cols = band_matrix(block_c, HALO, FRESNEL, True)
    row_pos = (
        lax.axis_index("row") * tile_r + lax.broadcasted_iota(jnp.int32, (tile_r, tile_c), 0)
    ).astype(jnp.float32)
    col_pos = (
        lax.axis_index("col") * tile_c + lax.broadcasted_iota(jnp.int32, (tile_r, tile_c), 1)
    ).astype(jnp.float32)
    height = float(tile_r * lax.axis_size("row"))
    width_all = float(tile_c * lax.axis_size("col"))
    tilt_f = tilt.astype(jnp.float32)
    phase_angle = (
        2.0
        * jnp.pi
        * (
            tilt_f[:, 0, None, None] * row_pos / height
            + tilt_f[:, 1, None, None] * col_pos / width_all
        )
    )
    incident = jnp.stack([jnp.cos(phase_angle), jnp.sin(phase_angle)], axis=1)
    screens = jnp.stack([jnp.cos(phase), jnp.sin(phase)], axis=1)

    def forward_tick(tick_now, carry):
        incoming, entering, leaving = carry
        group_index = tick_now - section_index
        active = (group_index >= 0) & (group_index < groups)
        first_item = jnp.clip(group_index, 0, groups - 1) * group_size
        current = jnp.where(
            section_index == 0,
            lax.dynamic_slice_in_dim(incident, first_item, group_size, 0),
            incoming,
        )
        entering = store_item(entering, current, first_item, 0, active)
        current = propagate(transmit(screens[0], current, False), fwd_rows, fwd_cols)
        leaving = store_item(leaving, current, first_item, 0, active)
        incoming = from_behind(current, "depth", 1)
        return (incoming, entering, leaving)

    store_zero = jnp.zeros((batch_size, slices, 2, tile_r, tile_c), jnp.float32)
    start_wave = jnp.zeros((group_size, 2, tile_r, tile_c), jnp.float32)
    _, entering, leaving = lax.fori_loop(
        0, tick_count, forward_tick, (start_wave, store_zero, store_zero)
    )
    final_wave = leaving[:, slices - 1]
    misfit = final_wave[:, 0] * final_wave[:, 0] + final_wave[:, 1] * final_wave[:, 1] - intensity
    seed_adjoint = 2.0 * misfit[:, None] * final_wave

    def backward_tick(tick_now, carry):
        incoming, gradient = carry
        group_index = tick_now - (sections - 1 - section_index)
        active = (group_index >= 0) & (group_index < groups)
        first_item = jnp.clip(group_index, 0, groups - 1) * group_size
        adjoint_wave = jnp.where(
            section_index == sections - 1,
            lax.dynamic_slice_in_dim(seed_adjoint, first_item, group_size, 0),
            incoming,
        )
        for slice_index in reversed(range(slices)):
            pulled = propagate(adjoint_wave, adj_rows, adj_cols)
            arrived = lax.dynamic_slice_in_dim(entering[:, slice_index], first_item, group_size, 0)
            moved = transmit(screens[slice_index], arrived, False)
            contribution = jnp.sum(pulled[:, 1] * moved[:, 0] - pulled[:, 0] * moved[:, 1], axis=0)
            gradient = gradient.at[slice_index].add(jnp.where(active, contribution, 0.0))
            adjoint_wave = transmit(screens[slice_index], pulled, True)
        incoming = from_behind(adjoint_wave, "depth", -1)
        return (incoming, gradient)

    grad_zero = jnp.zeros((slices, tile_r, tile_c), jnp.float32)
    _, gradient = lax.fori_loop(0, tick_count, backward_tick, (start_wave, grad_zero))
    return (gradient, leaving)


def fits_whole(phase_shape, batch, mesh):
    slices, height, width = phase_shape
    rows, cols, sections = mesh.shape["row"], mesh.shape["col"], mesh.shape["depth"]
    return (
        4 * height * width * (slices + batch) <= GATHER_BUDGET
        and batch == rows == 2
        and slices == sections
        and sections & (sections - 1) == 0
        and cols & (cols - 1) == 0
        and height == LANES
        and width == cols * LANES
        and cols > 1
        and sections > 1
        and sections * HALO <= LANES
    )


def solution(mesh):
    placed = (P("depth", "row", "col"), P(), P(None, "row", "col"))

    def run(phase, tilt, intensity):
        if fits_whole(phase.shape, tilt.shape[0], mesh):
            body = whole_field_body
        else:
            body = staged_body
        return jax.shard_map(
            body,
            mesh=mesh,
            in_specs=placed,
            out_specs=(P("depth", "row", "col"), P(None, "depth", None, "row", "col")),
            check_vma=False,
        )(phase, tilt, intensity)

    return run
```

```python
import math

import jax
import jax.numpy as jnp
import numpy as np
from jax import lax
from jax.experimental import pallas as pl
from jax.experimental.pallas import tpu as pltpu
from jax.sharding import PartitionSpec as P

HALO = 32
FRESNEL = 64
LANES = 128
GATHER_BUDGET = 4 * 2**20
SIN = (
    0.9999999980536763,
    -0.1666666530009577,
    0.008333305907073658,
    -0.00019838908256358006,
    2.745822627876341e-06,
    -2.3043562782810933e-08,
)
COS = (
    0.9999999961345007,
    -0.4999999301617528,
    0.04166646215023687,
    -0.0013886696163545999,
    2.4695045482778703e-05,
    -2.5154931690000354e-07,
)


def horner(coefficients, square):
    total = jnp.full_like(square, coefficients[-1])
    for coefficient in coefficients[-2::-1]:
        total = total * square + coefficient
    return total


def cos_sin(angle):
    square = angle * angle
    return horner(COS, square), horner(SIN, square) * angle


def turn(fraction):
    half_cos, half_sin = cos_sin(fraction * math.pi)
    return half_cos * half_cos - half_sin * half_sin, 2.0 * half_cos * half_sin


def halves(value):
    high = value.astype(jnp.bfloat16)
    return high, (value - high.astype(jnp.float32)).astype(jnp.bfloat16)


def np_halves(matrix):
    high = matrix.astype(jnp.bfloat16)
    return high, (matrix - high.astype(np.float64)).astype(jnp.bfloat16)


def np_taps():
    offset = np.arange(-HALO, HALO + 1, dtype=np.float64)
    taper = np.maximum(np.abs(offset) - 0.5 * HALO, 0.0)
    weight = np.cos(np.pi * taper / (HALO + 2.0)) ** 2 / math.sqrt(FRESNEL)
    return weight * np.exp(1j * np.pi * offset * offset / FRESNEL)


def np_band(out_pos, in_pos):
    offset = out_pos[:, None] - in_pos[None, :]
    inside = np.abs(offset) <= HALO
    return np.where(inside, np_taps()[np.clip(offset, -HALO, HALO) + HALO], 0.0)


def row_constant(height):
    matrices = []
    for core in range(2):
        pos = (np.arange(height) + core * (height // 2)) % height
        band = np_band(pos, pos)
        whole = np.block([[band.real, -band.imag], [band.imag, band.real]])
        matrices.append(np.concatenate(np_halves(whole), axis=1))
    return np.stack(matrices)


def col_constant():
    lane = np.arange(LANES)
    turned = np.where((lane >= HALO) & (lane < LANES - HALO), lane ^ (LANES // 2), lane)
    edge_pos = np.where(turned < LANES // 2, turned + LANES, turned - LANES)
    parts = []
    for position in (lane, edge_pos):
        band = np_band(lane, position).T
        parts.append(np.block([[band.real, band.imag], [-band.imag, band.real]]))
    return np.concatenate(np_halves(np.concatenate(parts, axis=0)), axis=1)


def both_rows(near_ref, far_ref, where):
    return jnp.concatenate([near_ref[where], far_ref[where]], axis=0)


def turned(slice_index, block, screens, wave):
    near_cos, near_sin, far_cos, far_sin = screens
    cos = both_rows(near_cos, far_cos, (slice_index, block))
    sin = both_rows(near_sin, far_sin, (slice_index, block))
    real, imag = wave
    return cos * real - sin * imag, cos * imag + sin * real


def row_product(row_matrix, columns):
    high, low = halves(columns)
    whole, width = columns.shape
    wide = jnp.dot(
        row_matrix[:, :whole], jnp.concatenate([high, low], axis=1), preferred_element_type=jnp.float32
    )
    rest = jnp.dot(row_matrix[:, whole:], high, preferred_element_type=jnp.float32)
    return wide[:, :width] + wide[:, width:] + rest


def col_product(high, low, col_ref):
    wide = jnp.dot(high, col_ref[...], preferred_element_type=jnp.float32)
    rest = jnp.dot(low, col_ref[: 2 * LANES, : 2 * LANES], preferred_element_type=jnp.float32)
    return wide[:, : 2 * LANES] + wide[:, 2 * LANES :] + rest


def three_parts(value):
    high = value.astype(jnp.bfloat16)
    rest = value - high.astype(jnp.float32)
    return high, rest.astype(jnp.bfloat16), pltpu.roll(rest, LANES // 2, 1).astype(jnp.bfloat16)


def advance(slice_index, start, waves, screens, row_matrix, col_ref, edge_ref):
    size, height = len(waves), waves[0][0].shape[0]
    chunks = [range(place, min(place + 2, size)) for place in range(0, size, 2)]
    highs, lows = [], []
    for chunk in chunks:
        columns = [
            jnp.concatenate(turned(slice_index, start + place, screens, waves[place]), axis=0) for place in chunk
        ]
        done = row_product(row_matrix, jnp.concatenate(columns, axis=1))
        for sub, place in enumerate(chunk):
            own_high, own_low = [], []
            for part in range(2):
                value = done[part * height : (part + 1) * height, sub * LANES : (sub + 1) * LANES]
                high, low, swung = three_parts(value)
                own_high.append(high)
                own_low.append(low)
                edge = part * LANES
                if place > 0:
                    edge_ref[place - 1, :, pl.ds(edge, HALO)] = high[:, :HALO]
                    edge_ref[place - 1, :, pl.ds(edge + 2 * HALO, HALO)] = swung[:, 2 * HALO : 3 * HALO]
                if place < size - 1:
                    edge_ref[place + 1, :, pl.ds(edge + 3 * HALO, HALO)] = high[:, 3 * HALO :]
                    edge_ref[place + 1, :, pl.ds(edge + HALO, HALO)] = swung[:, HALO : 2 * HALO]
            highs.append(jnp.concatenate(own_high, axis=1))
            lows.append(jnp.concatenate(own_low, axis=1))
    results = []
    for chunk in chunks:
        rows = len(chunk) * height
        edges = edge_ref[pl.ds(chunk[0], len(chunk))].reshape(rows, 2 * LANES)
        own = jnp.concatenate([highs[place] for place in chunk], axis=0)
        total = col_product(
            jnp.concatenate([own, edges], axis=1),
            jnp.concatenate([lows[place] for place in chunk], axis=0),
            col_ref,
        )
        for sub in range(len(chunk)):
            block = total[sub * height : (sub + 1) * height]
            results.append((block[:, :LANES], block[:, LANES:]))
    return results


def clear_edge(edge_ref, place, right):
    for part in range(2):
        for begin in (0, 2 * HALO) if right else (HALO, 3 * HALO):
            cells = pl.ds(part * LANES + begin, HALO)
            edge_ref[place, :, cells] = jnp.zeros((edge_ref.shape[1], HALO), edge_ref.dtype)


def keep(wave_ref, waves):
    for place, wave in enumerate(waves):
        wave_ref[place, 0], wave_ref[place, 1] = wave


def prepare_kernel(tilt_ref, near_own, near_rest, wave_ref, cos_ref, sin_ref):
    blocks, _, height, _ = wave_ref.shape
    count = cos_ref.shape[0] - 1
    core, own_section, own_place = lax.axis_index("row"), lax.axis_index("depth"), lax.axis_index("col")

    def screens(col, carry):
        held = col ^ own_place
        for bits in range(count):
            angle = near_own[held, 0] if bits == 0 else near_rest[held, bits - 1]
            cos_ref[bits ^ own_section, col], sin_ref[bits ^ own_section, col] = cos_sin(angle)
        return carry

    lax.fori_loop(0, blocks, screens, 0)
    cos_ref[count] = jnp.ones(cos_ref.shape[1:], jnp.float32)
    sin_ref[count] = jnp.zeros(cos_ref.shape[1:], jnp.float32)

    def cycles(number, position, extent):
        fraction = (number * position).astype(jnp.float32) / extent
        return turn(fraction - jnp.round(fraction))

    row = lax.broadcasted_iota(jnp.int32, (height, LANES), 0) + core * (height // 2)
    row = jnp.where(row >= height, row - height, row)
    row_cos, row_sin = cycles(tilt_ref[core, 0], row, float(height))
    for block in range(blocks):
        col_cos, col_sin = cycles(
            tilt_ref[core, 1],
            lax.broadcasted_iota(jnp.int32, (8, LANES), 1) + block * LANES,
            float(blocks * LANES),
        )
        col_cos, col_sin = col_cos[:1], col_sin[:1]
        wave_ref[block, 0] = row_cos * col_cos - row_sin * col_sin
        wave_ref[block, 1] = row_sin * col_cos + row_cos * col_sin


def wave_kernel(
    wave_ref, near_cos, near_sin, near_own, far_own, far_rest, row_ref, col_ref,
    mine_ref, theirs_ref, far_cos, far_sin, kept_ref, moved_ref, left_ref, grad_ref, even_edge, odd_edge,
):
    blocks, _, height, _ = wave_ref.shape
    count = near_cos.shape[0] - 1
    core, own_section, own_place = lax.axis_index("row"), lax.axis_index("depth"), lax.axis_index("col")
    near, far = pl.ds(0, height // 2), pl.ds(height // 2, height // 2)
    screens = (near_cos, near_sin, far_cos, far_sin)
    row_matrix = row_ref[core]
    window = min(3, blocks)
    window_start = jnp.clip(own_place - 1, 0, blocks - window)
    own_in_window = own_place - window_start
    edges = (even_edge, odd_edge)

    def far_screens(slice_index):
        bits = slice_index ^ own_section
        for col in range(blocks):
            held = col ^ own_place
            angle = jnp.where(bits == 0, far_own[held, 0], far_rest[held, jnp.maximum(bits - 1, 0)])
            far_cos[slice_index, col], far_sin[slice_index, col] = cos_sin(angle)

    for edge_ref in edges:
        clear_edge(edge_ref, 0, False)
        clear_edge(edge_ref, blocks - 1, True)
    far_cos[count] = jnp.ones(far_cos.shape[1:], jnp.float32)
    far_sin[count] = jnp.zeros(far_cos.shape[1:], jnp.float32)
    far_screens(0)

    waves = [(wave_ref[place, 0], wave_ref[place, 1]) for place in range(blocks)]
    for tick in range(count):
        entering = (wave_ref if tick == 0 else kept_ref)[own_place]
        moved_ref[tick, 0], moved_ref[tick, 1] = turned(tick, own_place, screens, (entering[0], entering[1]))
        waves = advance(tick, 0, waves, screens, row_matrix, col_ref, edges[tick % 2])
        if tick + 1 < count:
            far_screens(tick + 1)
        keep(kept_ref, waves)
        left_ref[tick] = kept_ref[own_place]

    for edge_ref in edges:
        clear_edge(edge_ref, window - 1, True)
    waves = []
    for place in range(window):
        block = window_start + place
        held = block ^ own_place
        measured = jnp.concatenate([near_own[held, 1 + core], far_own[held, 1]], axis=0)
        real, imag = kept_ref[block, 0], kept_ref[block, 1]
        misfit = 2.0 * (real * real + imag * imag - measured)
        waves.append((misfit * real, -misfit * imag))

    for tick in range(count - 1):
        waves = advance(count - tick, window_start, waves, screens, row_matrix, col_ref, edges[tick % 2])
        keep(kept_ref, waves)
        arrived = count - 1 - tick
        pulled = kept_ref[own_in_window]
        grad_ref[arrived] = -(pulled[1] * moved_ref[arrived, 0] + pulled[0] * moved_ref[arrived, 1])

    left, right = jnp.maximum(own_place - 1, 0), jnp.minimum(own_place + 1, blocks - 1)
    lane = lax.broadcasted_iota(jnp.int32, (2 * height, LANES), 1)
    has_left, has_right = own_place > 0, own_place < blocks - 1

    def cells(block):
        wave = kept_ref[block - window_start]
        return jnp.concatenate(turned(1, block, screens, (wave[0], wave[1])), axis=0)

    edge_cells = jnp.where(
        lane < LANES // 2, jnp.where(has_right, cells(right), 0.0), jnp.where(has_left, cells(left), 0.0)
    )
    done = row_product(row_matrix, jnp.concatenate([cells(own_place), edge_cells], axis=1))
    lane = lax.broadcasted_iota(jnp.int32, (height, LANES), 1)
    between = (lane >= HALO) & (lane < LANES - HALO)
    highs, lows, edges = [], [], []
    for part in range(2):
        high, low, _ = three_parts(done[part * height : (part + 1) * height, :LANES])
        highs.append(high)
        lows.append(low)
        value = done[part * height : (part + 1) * height, LANES:]
        whole_high = value.astype(jnp.bfloat16).astype(jnp.float32)
        edge = jnp.where(between, pltpu.roll(value - whole_high, LANES // 2, 1), whole_high)
        edges.append(edge.astype(jnp.bfloat16))
    pulled = col_product(jnp.concatenate(highs + edges, axis=1), jnp.concatenate(lows, axis=1), col_ref)
    grad_ref[0] = -(pulled[:, LANES:] * moved_ref[0, 0] + pulled[:, :LANES] * moved_ref[0, 1])

    for target, row in ((mine_ref, near), (theirs_ref, far)):
        for part in range(2):
            target[0, part] = left_ref[own_section, part, row]
        target[0, 2] = grad_ref[own_section, row]


def finish_kernel(mine_ref, received_ref, grad_ref, exit_ref, total_ref, sems):
    core = lax.axis_index("row")
    copies = []
    for source, item in ((mine_ref, core), (received_ref, 1 - core)):
        copies.append(pltpu.make_async_copy(source.at[:, pl.ds(0, 2)], exit_ref.at[item], sems.at[len(copies)]))
    for copy in copies:
        copy.start()
    total_ref[...] = mine_ref[:, 2] + received_ref[:, 2]
    copies.append(pltpu.make_async_copy(total_ref, grad_ref, sems.at[2]))
    copies[2].start()
    for copy in copies:
        copy.wait()


def spread(shard, axis):
    size = lax.axis_size(axis)
    return [lax.ppermute(shard, axis, [(i, i ^ bits) for i in range(size)]) for bits in range(1, size)]


def exchange(value, pairs):
    return lax.ppermute(value, "col", pairs)


def swap_cores(value):
    return lax.ppermute(value, "row", [(0, 1), (1, 0)])


def whole_field_body(phase, tilt, intensity):
    _, tile_r, tile_c = phase.shape
    count, blocks = lax.axis_size("depth"), lax.axis_size("col")
    core = lax.axis_index("row")
    height = 2 * tile_r
    vmem = pl.BlockSpec(memory_space=pltpu.VMEM)
    smem = pl.BlockSpec(memory_space=pltpu.SMEM)
    hbm = pl.BlockSpec(memory_space=pl.ANY)

    def array(*shape):
        return jax.ShapeDtypeStruct(shape, jnp.float32)

    def params(mebibytes):
        return pltpu.CompilerParams(vmem_limit_bytes=mebibytes * 2**20)

    other_depths = spread(phase, "depth")
    other_depths[0], measured, slab = lax.optimization_barrier((other_depths[0], intensity, phase))
    other_depths = jnp.concatenate(other_depths, axis=0)
    packet = jnp.concatenate([slab, measured], axis=0)
    by_one, by_two, corner = [(i, i ^ 1) for i in range(4)], [(i, i ^ 2) for i in range(4)], [(1, 2), (2, 1)]
    packet_near, packet_corner = exchange(packet, by_one), exchange(packet, corner)
    whole_column = exchange(jnp.concatenate([slab, other_depths], axis=0), by_two)
    packet_next = jnp.concatenate([whole_column[:1], jnp.zeros_like(measured)], axis=0)
    near_own = jnp.stack([packet, packet_near, packet_next, packet_corner])
    arriving = [exchange(other_depths, by_one), whole_column[1:], exchange(other_depths, corner)]
    arriving[0], near_own = lax.optimization_barrier((arriving[0], near_own))
    near_rest = jnp.stack([other_depths] + arriving)
    wanted = lax.dynamic_slice_in_dim(near_own, 2 - core, 1, 1)
    far_own = swap_cores(jnp.concatenate([near_own[:, :1], wanted], axis=1))
    far_rest = swap_cores(near_rest)

    half_screens = (count + 1, blocks, tile_r, tile_c)
    field = (blocks, 2, height, tile_c)
    wave, near_cos, near_sin = pl.pallas_call(
        prepare_kernel,
        out_shape=(array(*field), array(*half_screens), array(*half_screens)),
        in_specs=[smem, vmem, vmem],
        out_specs=(vmem,) * 3,
        compiler_params=params(8),
        cost_estimate=pl.CostEstimate(flops=5 * 10**8, bytes_accessed=2**20, transcendentals=0),
    )(tilt, near_own, near_rest)
    mine, theirs = pl.pallas_call(
        wave_kernel,
        out_shape=(array(1, 3, tile_r, tile_c),) * 2,
        in_specs=[vmem] * 8,
        out_specs=(vmem,) * 2,
        scratch_shapes=[pltpu.VMEM(half_screens, jnp.float32)] * 2
        + [pltpu.VMEM(field, jnp.float32)]
        + [pltpu.VMEM((count, 2, height, tile_c), jnp.float32)] * 2
        + [pltpu.VMEM((count, height, tile_c), jnp.float32)]
        + [pltpu.VMEM((blocks, height, 2 * LANES), jnp.bfloat16)] * 2,
        compiler_params=params(24),
    )(
        wave, near_cos, near_sin, near_own, far_own, far_rest,
        jnp.asarray(row_constant(height)), jnp.asarray(col_constant()),
    )
    return pl.pallas_call(
        finish_kernel,
        out_shape=(array(*phase.shape), array(2, 1, 2, tile_r, tile_c)),
        in_specs=[vmem, vmem],
        out_specs=(hbm, hbm),
        scratch_shapes=[pltpu.VMEM(phase.shape, jnp.float32), pltpu.SemaphoreType.DMA((3,))],
        compiler_params=params(4),
    )(mine, swap_cores(theirs))


def extended_2(cells, sides, width):
    for axis, dim in sides:
        count = lax.axis_size(axis)
        ends = count - 1
        head = lax.slice_in_dim(cells, 0, width, axis=dim)
        tail = lax.slice_in_dim(cells, cells.shape[dim] - width, cells.shape[dim], axis=dim)
        cells = jnp.concatenate(
            [
                lax.ppermute(tail, axis, [(i, (i + 1) % count) for i in range(ends)]),
                cells,
                lax.ppermute(head, axis, [((i + 1) % count, i) for i in range(ends)]),
            ],
            axis=dim,
        )
    return cells


def from_behind(value, axis, steps):
    count = lax.axis_size(axis)
    leading, last = (max(0, -steps), min(count, count - steps))
    return lax.ppermute(value, axis, [(source, source + steps) for source in range(leading, last)])


def band_matrix(block_size, margin, fresnel, adjoint):
    shape_full = (block_size, block_size + 2 * margin)
    out_idx = lax.broadcasted_iota(jnp.int32, shape_full, 0)
    in_idx = lax.broadcasted_iota(jnp.int32, shape_full, 1)
    offset = (out_idx + margin - in_idx).astype(jnp.float32)
    inside = jnp.abs(offset) <= margin
    taper_dist = jnp.maximum(jnp.abs(offset) - 0.5 * margin, 0.0)
    profile = jnp.cos(jnp.pi * taper_dist / (margin + 2.0))
    weight = profile * profile / math.sqrt(fresnel)
    phase_angle = jnp.pi * offset * offset / fresnel
    real_part = jnp.where(inside, jnp.cos(phase_angle) * weight, 0.0)
    imag_part = jnp.where(inside, jnp.sin(phase_angle) * weight, 0.0)
    if adjoint:
        imag_part = -imag_part
    upper = jnp.stack([real_part, -imag_part])
    lower = jnp.stack([imag_part, real_part])
    return jnp.stack([upper, lower])


def along_rows(extended, matrix):
    pieces = [jnp.einsum("pqij,gqjc->gpic", matrix, extended, precision=lax.Precision.HIGHEST)]
    return jnp.concatenate(pieces, axis=2)


def along_cols(extended, matrix, margin):
    block_size = matrix.shape[2]
    extent = extended.shape[3] - 2 * margin
    pieces = []
    for block_start in range(0, extent, block_size):
        window = extended[:, :, :, block_start : block_start + block_size + 2 * margin]
        pieces.append(
            jnp.einsum("pqij,gqrj->gpri", matrix, window, precision=lax.Precision.HIGHEST)
        )
    return jnp.concatenate(pieces, axis=3)


def propagate(current, row_matrix, col_matrix):
    with_rows = extended_2(current, (("row", 2),), HALO)
    row_done = along_rows(with_rows, row_matrix)
    with_cols = extended_2(row_done, (("col", 3),), HALO)
    return along_cols(with_cols, col_matrix, HALO)


def transmit(screen, current, adjoint):
    screen_re = screen[0][None]
    screen_im = screen[1][None]
    if adjoint:
        screen_im = -screen_im
    real_part = screen_re * current[:, 0] - screen_im * current[:, 1]
    imag_part = screen_re * current[:, 1] + screen_im * current[:, 0]
    return jnp.stack([real_part, imag_part], axis=1)


def store_item(store, current, first_item, slice_index, active):
    begin = (first_item, jnp.int32(slice_index), jnp.int32(0), jnp.int32(0), jnp.int32(0))
    sizes_now = (current.shape[0], 1) + current.shape[1:]
    previous = lax.dynamic_slice(store, begin, sizes_now)
    fresh = jnp.where(active, current[:, None], previous)
    return lax.dynamic_update_slice(store, fresh, begin)


def staged_body(phase, tilt, intensity):
    slices, tile_r, tile_c = phase.shape
    batch_size = tilt.shape[0]
    sections = lax.axis_size("depth")
    section_index = lax.axis_index("depth")
    group_size = 1
    groups = batch_size // group_size
    tick_count = sections + groups - 1
    block_r = 64
    block_c = 128
    fwd_rows = band_matrix(block_r, HALO, FRESNEL, False)
    fwd_cols = band_matrix(block_c, HALO, FRESNEL, False)
    adj_rows = band_matrix(block_r, HALO, FRESNEL, True)
    adj_cols = band_matrix(block_c, HALO, FRESNEL, True)
    row_pos = (
        lax.axis_index("row") * tile_r + lax.broadcasted_iota(jnp.int32, (tile_r, tile_c), 0)
    ).astype(jnp.float32)
    col_pos = (
        lax.axis_index("col") * tile_c + lax.broadcasted_iota(jnp.int32, (tile_r, tile_c), 1)
    ).astype(jnp.float32)
    height = float(tile_r * lax.axis_size("row"))
    width_all = float(tile_c * lax.axis_size("col"))
    tilt_f = tilt.astype(jnp.float32)
    phase_angle = (
        2.0
        * jnp.pi
        * (
            tilt_f[:, 0, None, None] * row_pos / height
            + tilt_f[:, 1, None, None] * col_pos / width_all
        )
    )
    incident = jnp.stack([jnp.cos(phase_angle), jnp.sin(phase_angle)], axis=1)
    screens = jnp.stack([jnp.cos(phase), jnp.sin(phase)], axis=1)

    def forward_tick(tick_now, carry):
        incoming, entering, leaving = carry
        group_index = tick_now - section_index
        active = (group_index >= 0) & (group_index < groups)
        first_item = jnp.clip(group_index, 0, groups - 1) * group_size
        current = jnp.where(
            section_index == 0,
            lax.dynamic_slice_in_dim(incident, first_item, group_size, 0),
            incoming,
        )
        entering = store_item(entering, current, first_item, 0, active)
        current = propagate(transmit(screens[0], current, False), fwd_rows, fwd_cols)
        leaving = store_item(leaving, current, first_item, 0, active)
        incoming = from_behind(current, "depth", 1)
        return (incoming, entering, leaving)

    store_zero = jnp.zeros((batch_size, slices, 2, tile_r, tile_c), jnp.float32)
    start_wave = jnp.zeros((group_size, 2, tile_r, tile_c), jnp.float32)
    _, entering, leaving = lax.fori_loop(
        0, tick_count, forward_tick, (start_wave, store_zero, store_zero)
    )
    final_wave = leaving[:, slices - 1]
    misfit = final_wave[:, 0] * final_wave[:, 0] + final_wave[:, 1] * final_wave[:, 1] - intensity
    seed_adjoint = 2.0 * misfit[:, None] * final_wave

    def backward_tick(tick_now, carry):
        incoming, gradient = carry
        group_index = tick_now - (sections - 1 - section_index)
        active = (group_index >= 0) & (group_index < groups)
        first_item = jnp.clip(group_index, 0, groups - 1) * group_size
        adjoint_wave = jnp.where(
            section_index == sections - 1,
            lax.dynamic_slice_in_dim(seed_adjoint, first_item, group_size, 0),
            incoming,
        )
        for slice_index in reversed(range(slices)):
            pulled = propagate(adjoint_wave, adj_rows, adj_cols)
            arrived = lax.dynamic_slice_in_dim(entering[:, slice_index], first_item, group_size, 0)
            moved = transmit(screens[slice_index], arrived, False)
            contribution = jnp.sum(pulled[:, 1] * moved[:, 0] - pulled[:, 0] * moved[:, 1], axis=0)
            gradient = gradient.at[slice_index].add(jnp.where(active, contribution, 0.0))
            adjoint_wave = transmit(screens[slice_index], pulled, True)
        incoming = from_behind(adjoint_wave, "depth", -1)
        return (incoming, gradient)

    grad_zero = jnp.zeros((slices, tile_r, tile_c), jnp.float32)
    _, gradient = lax.fori_loop(0, tick_count, backward_tick, (start_wave, grad_zero))
    return (gradient, leaving)


def fits_whole(phase_shape, batch, mesh):
    slices, height, width = phase_shape
    rows, cols, sections = mesh.shape["row"], mesh.shape["col"], mesh.shape["depth"]
    return (
        4 * height * width * (slices + batch) <= GATHER_BUDGET
        and batch == rows == 2
        and slices == sections
        and sections & (sections - 1) == 0
        and cols == 4
        and height == LANES
        and width == cols * LANES
        and sections > 1
        and sections * HALO <= LANES
    )


def solution(mesh):
    placed = (P("depth", "row", "col"), P(), P(None, "row", "col"))

    def run(phase, tilt, intensity):
        if fits_whole(phase.shape, tilt.shape[0], mesh):
            body = whole_field_body
        else:
            body = staged_body
        return jax.shard_map(
            body,
            mesh=mesh,
            in_specs=placed,
            out_specs=(P("depth", "row", "col"), P(None, "depth", None, "row", "col")),
            check_vma=False,
        )(phase, tilt, intensity)

    return run
```

```python
import math

import jax
import jax.numpy as jnp
import numpy as np
from jax import lax
from jax.experimental import pallas as pl
from jax.experimental.pallas import tpu as pltpu
from jax.sharding import PartitionSpec as P

HALO = 32
FRESNEL = 64
LANES = 128
GATHER_BUDGET = 4 * 2**20
SIN = (
    0.9999999980536763,
    -0.1666666530009577,
    0.008333305907073658,
    -0.00019838908256358006,
    2.745822627876341e-06,
    -2.3043562782810933e-08,
)
COS = (
    0.9999999961345007,
    -0.4999999301617528,
    0.04166646215023687,
    -0.0013886696163545999,
    2.4695045482778703e-05,
    -2.5154931690000354e-07,
)


def horner(coefficients, square):
    total = jnp.full_like(square, coefficients[-1])
    for coefficient in coefficients[-2::-1]:
        total = total * square + coefficient
    return total


def cos_sin(angle):
    square = angle * angle
    return horner(COS, square), horner(SIN, square) * angle


def turn(fraction):
    half_cos, half_sin = cos_sin(fraction * math.pi)
    return half_cos * half_cos - half_sin * half_sin, 2.0 * half_cos * half_sin


def halves(value):
    high = value.astype(jnp.bfloat16)
    return high, (value - high.astype(jnp.float32)).astype(jnp.bfloat16)


def np_halves(matrix):
    high = matrix.astype(jnp.bfloat16)
    return high, (matrix - high.astype(np.float64)).astype(jnp.bfloat16)


def np_taps():
    offset = np.arange(-HALO, HALO + 1, dtype=np.float64)
    taper = np.maximum(np.abs(offset) - 0.5 * HALO, 0.0)
    weight = np.cos(np.pi * taper / (HALO + 2.0)) ** 2 / math.sqrt(FRESNEL)
    return weight * np.exp(1j * np.pi * offset * offset / FRESNEL)


def np_band(out_pos, in_pos):
    offset = out_pos[:, None] - in_pos[None, :]
    inside = np.abs(offset) <= HALO
    return np.where(inside, np_taps()[np.clip(offset, -HALO, HALO) + HALO], 0.0)


def row_constant(height):
    matrices = []
    for core in range(2):
        pos = (np.arange(height) + core * (height // 2)) % height
        band = np_band(pos, pos)
        whole = np.block([[band.real, -band.imag], [band.imag, band.real]])
        matrices.append(np.concatenate(np_halves(whole), axis=1))
    return np.stack(matrices)


def col_constant():
    lane = np.arange(LANES)
    turned = np.where((lane >= HALO) & (lane < LANES - HALO), lane ^ (LANES // 2), lane)
    edge_pos = np.where(turned < LANES // 2, turned + LANES, turned - LANES)
    parts = []
    for position in (lane, edge_pos):
        band = np_band(lane, position).T
        parts.append(np.block([[band.real, band.imag], [-band.imag, band.real]]))
    return np.concatenate(np_halves(np.concatenate(parts, axis=0)), axis=1)


def both_rows(near_ref, far_ref, where):
    return jnp.concatenate([near_ref[where], far_ref[where]], axis=0)


def turned(slice_index, block, screens, wave):
    near_cos, near_sin, far_cos, far_sin = screens
    cos = both_rows(near_cos, far_cos, (slice_index, block))
    sin = both_rows(near_sin, far_sin, (slice_index, block))
    real, imag = wave
    return cos * real - sin * imag, cos * imag + sin * real


def row_product(row_matrix, columns):
    high, low = halves(columns)
    whole, width = columns.shape
    wide = jnp.dot(
        row_matrix[:, :whole], jnp.concatenate([high, low], axis=1), preferred_element_type=jnp.float32
    )
    rest = jnp.dot(row_matrix[:, whole:], high, preferred_element_type=jnp.float32)
    return wide[:, :width] + wide[:, width:] + rest


def col_product(high, low, col_ref):
    wide = jnp.dot(high, col_ref[...], preferred_element_type=jnp.float32)
    rest = jnp.dot(low, col_ref[: 2 * LANES, : 2 * LANES], preferred_element_type=jnp.float32)
    return wide[:, : 2 * LANES] + wide[:, 2 * LANES :] + rest


def three_parts(value):
    high = value.astype(jnp.bfloat16)
    rest = value - high.astype(jnp.float32)
    return high, rest.astype(jnp.bfloat16), pltpu.roll(rest, LANES // 2, 1).astype(jnp.bfloat16)


def advance(slice_index, start, waves, screens, row_matrix, col_ref, edge_ref):
    size, height = len(waves), waves[0][0].shape[0]
    chunks = [range(place, min(place + 2, size)) for place in range(0, size, 2)]
    highs, lows = [], []
    for chunk in chunks:
        columns = [
            jnp.concatenate(turned(slice_index, start + place, screens, waves[place]), axis=0) for place in chunk
        ]
        done = row_product(row_matrix, jnp.concatenate(columns, axis=1))
        for sub, place in enumerate(chunk):
            own_high, own_low = [], []
            for part in range(2):
                value = done[part * height : (part + 1) * height, sub * LANES : (sub + 1) * LANES]
                high, low, swung = three_parts(value)
                own_high.append(high)
                own_low.append(low)
                edge = part * LANES
                if place > 0:
                    edge_ref[place - 1, :, pl.ds(edge, HALO)] = high[:, :HALO]
                    edge_ref[place - 1, :, pl.ds(edge + 2 * HALO, HALO)] = swung[:, 2 * HALO : 3 * HALO]
                if place < size - 1:
                    edge_ref[place + 1, :, pl.ds(edge + 3 * HALO, HALO)] = high[:, 3 * HALO :]
                    edge_ref[place + 1, :, pl.ds(edge + HALO, HALO)] = swung[:, HALO : 2 * HALO]
            highs.append(jnp.concatenate(own_high, axis=1))
            lows.append(jnp.concatenate(own_low, axis=1))
    results = []
    for chunk in chunks:
        rows = len(chunk) * height
        edges = edge_ref[pl.ds(chunk[0], len(chunk))].reshape(rows, 2 * LANES)
        own = jnp.concatenate([highs[place] for place in chunk], axis=0)
        total = col_product(
            jnp.concatenate([own, edges], axis=1),
            jnp.concatenate([lows[place] for place in chunk], axis=0),
            col_ref,
        )
        for sub in range(len(chunk)):
            block = total[sub * height : (sub + 1) * height]
            results.append((block[:, :LANES], block[:, LANES:]))
    return results


def clear_edge(edge_ref, place, right):
    for part in range(2):
        for begin in (0, 2 * HALO) if right else (HALO, 3 * HALO):
            cells = pl.ds(part * LANES + begin, HALO)
            edge_ref[place, :, cells] = jnp.zeros((edge_ref.shape[1], HALO), edge_ref.dtype)


def keep(wave_ref, waves):
    for place, wave in enumerate(waves):
        wave_ref[place, 0], wave_ref[place, 1] = wave


def prepare_kernel(tilt_ref, near_own, near_rest, wave_ref, cos_ref, sin_ref):
    blocks, _, height, _ = wave_ref.shape
    count = cos_ref.shape[0] - 1
    core, own_section, own_place = lax.axis_index("row"), lax.axis_index("depth"), lax.axis_index("col")

    def screens(col, carry):
        held = col ^ own_place
        for bits in range(count):
            angle = near_own[held, 0] if bits == 0 else near_rest[held, bits - 1]
            cos_ref[bits ^ own_section, col], sin_ref[bits ^ own_section, col] = cos_sin(angle)
        return carry

    lax.fori_loop(0, blocks, screens, 0)
    cos_ref[count] = jnp.ones(cos_ref.shape[1:], jnp.float32)
    sin_ref[count] = jnp.zeros(cos_ref.shape[1:], jnp.float32)

    def cycles(number, position, extent):
        fraction = (number * position).astype(jnp.float32) / extent
        return turn(fraction - jnp.round(fraction))

    row = lax.broadcasted_iota(jnp.int32, (height, LANES), 0) + core * (height // 2)
    row = jnp.where(row >= height, row - height, row)
    row_cos, row_sin = cycles(tilt_ref[core, 0], row, float(height))
    for block in range(blocks):
        col_cos, col_sin = cycles(
            tilt_ref[core, 1],
            lax.broadcasted_iota(jnp.int32, (8, LANES), 1) + block * LANES,
            float(blocks * LANES),
        )
        col_cos, col_sin = col_cos[:1], col_sin[:1]
        wave_ref[block, 0] = row_cos * col_cos - row_sin * col_sin
        wave_ref[block, 1] = row_sin * col_cos + row_cos * col_sin


def wave_kernel(
    wave_ref, near_cos, near_sin, near_own, far_own, far_rest, row_ref, col_ref,
    mine_ref, theirs_ref, far_cos, far_sin, kept_ref, moved_ref, left_ref, grad_ref, even_edge, odd_edge,
):
    blocks, _, height, _ = wave_ref.shape
    count = near_cos.shape[0] - 1
    core, own_section, own_place = lax.axis_index("row"), lax.axis_index("depth"), lax.axis_index("col")
    near, far = pl.ds(0, height // 2), pl.ds(height // 2, height // 2)
    screens = (near_cos, near_sin, far_cos, far_sin)
    row_matrix = row_ref[core]
    window = min(3, blocks)
    window_start = jnp.clip(own_place - 1, 0, blocks - window)
    own_in_window = own_place - window_start
    edges = (even_edge, odd_edge)

    def far_screens(slice_index):
        bits = slice_index ^ own_section
        for col in range(blocks):
            held = col ^ own_place
            angle = jnp.where(bits == 0, far_own[held, 0], far_rest[held, jnp.maximum(bits - 1, 0)])
            far_cos[slice_index, col], far_sin[slice_index, col] = cos_sin(angle)

    for edge_ref in edges:
        clear_edge(edge_ref, 0, False)
        clear_edge(edge_ref, blocks - 1, True)
    far_cos[count] = jnp.ones(far_cos.shape[1:], jnp.float32)
    far_sin[count] = jnp.zeros(far_cos.shape[1:], jnp.float32)
    far_screens(0)

    waves = [(wave_ref[place, 0], wave_ref[place, 1]) for place in range(blocks)]
    for tick in range(count):
        entering = (wave_ref if tick == 0 else kept_ref)[own_place]
        moved_ref[tick, 0], moved_ref[tick, 1] = turned(tick, own_place, screens, (entering[0], entering[1]))
        waves = advance(tick, 0, waves, screens, row_matrix, col_ref, edges[tick % 2])
        if tick + 1 < count:
            far_screens(tick + 1)
        keep(kept_ref, waves)
        left_ref[tick] = kept_ref[own_place]

    for edge_ref in edges:
        clear_edge(edge_ref, window - 1, True)
    waves = []
    for place in range(window):
        block = window_start + place
        held = block ^ own_place
        measured = jnp.concatenate([near_own[held, 1 + core], far_own[held, 1]], axis=0)
        real, imag = kept_ref[block, 0], kept_ref[block, 1]
        misfit = 2.0 * (real * real + imag * imag - measured)
        waves.append((misfit * real, -misfit * imag))

    for tick in range(count - 1):
        waves = advance(count - tick, window_start, waves, screens, row_matrix, col_ref, edges[tick % 2])
        keep(kept_ref, waves)
        arrived = count - 1 - tick
        pulled = kept_ref[own_in_window]
        grad_ref[arrived] = -(pulled[1] * moved_ref[arrived, 0] + pulled[0] * moved_ref[arrived, 1])

    left, right = jnp.maximum(own_place - 1, 0), jnp.minimum(own_place + 1, blocks - 1)
    lane = lax.broadcasted_iota(jnp.int32, (2 * height, LANES), 1)
    has_left, has_right = own_place > 0, own_place < blocks - 1

    def cells(block):
        wave = kept_ref[block - window_start]
        return jnp.concatenate(turned(1, block, screens, (wave[0], wave[1])), axis=0)

    edge_cells = jnp.where(
        lane < LANES // 2, jnp.where(has_right, cells(right), 0.0), jnp.where(has_left, cells(left), 0.0)
    )
    done = row_product(row_matrix, jnp.concatenate([cells(own_place), edge_cells], axis=1))
    lane = lax.broadcasted_iota(jnp.int32, (height, LANES), 1)
    between = (lane >= HALO) & (lane < LANES - HALO)
    highs, lows, edges = [], [], []
    for part in range(2):
        high, low, _ = three_parts(done[part * height : (part + 1) * height, :LANES])
        highs.append(high)
        lows.append(low)
        value = done[part * height : (part + 1) * height, LANES:]
        whole_high = value.astype(jnp.bfloat16).astype(jnp.float32)
        edge = jnp.where(between, pltpu.roll(value - whole_high, LANES // 2, 1), whole_high)
        edges.append(edge.astype(jnp.bfloat16))
    pulled = col_product(jnp.concatenate(highs + edges, axis=1), jnp.concatenate(lows, axis=1), col_ref)
    grad_ref[0] = -(pulled[:, LANES:] * moved_ref[0, 0] + pulled[:, :LANES] * moved_ref[0, 1])

    for target, row in ((mine_ref, near), (theirs_ref, far)):
        for part in range(2):
            target[0, part] = left_ref[own_section, part, row]
        target[0, 2] = grad_ref[own_section, row]


def finish_kernel(mine_ref, received_ref, grad_ref, exit_ref, total_ref, sems):
    core = lax.axis_index("row")
    copies = []
    for source, item in ((mine_ref, core), (received_ref, 1 - core)):
        copies.append(pltpu.make_async_copy(source.at[:, pl.ds(0, 2)], exit_ref.at[item], sems.at[len(copies)]))
    for copy in copies:
        copy.start()
    total_ref[...] = mine_ref[:, 2] + received_ref[:, 2]
    copies.append(pltpu.make_async_copy(total_ref, grad_ref, sems.at[2]))
    copies[2].start()
    for copy in copies:
        copy.wait()


def spread(shard, axis):
    size = lax.axis_size(axis)
    return [lax.ppermute(shard, axis, [(i, i ^ bits) for i in range(size)]) for bits in range(1, size)]


def exchange(value, pairs):
    return lax.ppermute(value, "col", pairs)


def swap_cores(value):
    return lax.ppermute(value, "row", [(0, 1), (1, 0)])


def whole_field_body(phase, tilt, intensity):
    _, tile_r, tile_c = phase.shape
    count, blocks = lax.axis_size("depth"), lax.axis_size("col")
    core = lax.axis_index("row")
    height = 2 * tile_r
    vmem = pl.BlockSpec(memory_space=pltpu.VMEM)
    smem = pl.BlockSpec(memory_space=pltpu.SMEM)
    hbm = pl.BlockSpec(memory_space=pl.ANY)

    def array(*shape):
        return jax.ShapeDtypeStruct(shape, jnp.float32)

    def params(mebibytes):
        return pltpu.CompilerParams(vmem_limit_bytes=mebibytes * 2**20)

    other_depths = spread(phase, "depth")
    other_depths[0], measured, slab = lax.optimization_barrier((other_depths[0], intensity, phase))
    other_depths = jnp.concatenate(other_depths, axis=0)
    packet = jnp.concatenate([slab, measured], axis=0)
    by_one, by_two, corner = [(i, i ^ 1) for i in range(4)], [(i, i ^ 2) for i in range(4)], [(1, 2), (2, 1)]
    packet_near, packet_next = exchange(packet, by_one), exchange(packet, by_two)
    arriving = [exchange(other_depths, pairs) for pairs in (by_one, by_two, corner)]
    packet_near, packet_next = lax.optimization_barrier((packet_near, packet_next))
    packet_corner = exchange(packet_next, [(0, 1), (3, 2)])
    near_own = jnp.stack([packet, packet_near, packet_next, packet_corner])
    near_rest = jnp.stack([other_depths] + arriving)
    wanted = lax.dynamic_slice_in_dim(near_own, 2 - core, 1, 1)
    far_own = swap_cores(jnp.concatenate([near_own[:, :1], wanted], axis=1))
    far_rest = swap_cores(near_rest)

    half_screens = (count + 1, blocks, tile_r, tile_c)
    field = (blocks, 2, height, tile_c)
    wave, near_cos, near_sin = pl.pallas_call(
        prepare_kernel,
        out_shape=(array(*field), array(*half_screens), array(*half_screens)),
        in_specs=[smem, vmem, vmem],
        out_specs=(vmem,) * 3,
        compiler_params=params(8),
        cost_estimate=pl.CostEstimate(flops=5 * 10**8, bytes_accessed=2**20, transcendentals=0),
    )(tilt, near_own, near_rest)
    mine, theirs = pl.pallas_call(
        wave_kernel,
        out_shape=(array(1, 3, tile_r, tile_c),) * 2,
        in_specs=[vmem] * 8,
        out_specs=(vmem,) * 2,
        scratch_shapes=[pltpu.VMEM(half_screens, jnp.float32)] * 2
        + [pltpu.VMEM(field, jnp.float32)]
        + [pltpu.VMEM((count, 2, height, tile_c), jnp.float32)] * 2
        + [pltpu.VMEM((count, height, tile_c), jnp.float32)]
        + [pltpu.VMEM((blocks, height, 2 * LANES), jnp.bfloat16)] * 2,
        compiler_params=params(24),
    )(
        wave, near_cos, near_sin, near_own, far_own, far_rest,
        jnp.asarray(row_constant(height)), jnp.asarray(col_constant()),
    )
    return pl.pallas_call(
        finish_kernel,
        out_shape=(array(*phase.shape), array(2, 1, 2, tile_r, tile_c)),
        in_specs=[vmem, vmem],
        out_specs=(hbm, hbm),
        scratch_shapes=[pltpu.VMEM(phase.shape, jnp.float32), pltpu.SemaphoreType.DMA((3,))],
        compiler_params=params(4),
    )(mine, swap_cores(theirs))


def extended_2(cells, sides, width):
    for axis, dim in sides:
        count = lax.axis_size(axis)
        ends = count - 1
        head = lax.slice_in_dim(cells, 0, width, axis=dim)
        tail = lax.slice_in_dim(cells, cells.shape[dim] - width, cells.shape[dim], axis=dim)
        cells = jnp.concatenate(
            [
                lax.ppermute(tail, axis, [(i, (i + 1) % count) for i in range(ends)]),
                cells,
                lax.ppermute(head, axis, [((i + 1) % count, i) for i in range(ends)]),
            ],
            axis=dim,
        )
    return cells


def from_behind(value, axis, steps):
    count = lax.axis_size(axis)
    leading, last = (max(0, -steps), min(count, count - steps))
    return lax.ppermute(value, axis, [(source, source + steps) for source in range(leading, last)])


def band_matrix(block_size, margin, fresnel, adjoint):
    shape_full = (block_size, block_size + 2 * margin)
    out_idx = lax.broadcasted_iota(jnp.int32, shape_full, 0)
    in_idx = lax.broadcasted_iota(jnp.int32, shape_full, 1)
    offset = (out_idx + margin - in_idx).astype(jnp.float32)
    inside = jnp.abs(offset) <= margin
    taper_dist = jnp.maximum(jnp.abs(offset) - 0.5 * margin, 0.0)
    profile = jnp.cos(jnp.pi * taper_dist / (margin + 2.0))
    weight = profile * profile / math.sqrt(fresnel)
    phase_angle = jnp.pi * offset * offset / fresnel
    real_part = jnp.where(inside, jnp.cos(phase_angle) * weight, 0.0)
    imag_part = jnp.where(inside, jnp.sin(phase_angle) * weight, 0.0)
    if adjoint:
        imag_part = -imag_part
    upper = jnp.stack([real_part, -imag_part])
    lower = jnp.stack([imag_part, real_part])
    return jnp.stack([upper, lower])


def along_rows(extended, matrix):
    pieces = [jnp.einsum("pqij,gqjc->gpic", matrix, extended, precision=lax.Precision.HIGHEST)]
    return jnp.concatenate(pieces, axis=2)


def along_cols(extended, matrix, margin):
    block_size = matrix.shape[2]
    extent = extended.shape[3] - 2 * margin
    pieces = []
    for block_start in range(0, extent, block_size):
        window = extended[:, :, :, block_start : block_start + block_size + 2 * margin]
        pieces.append(
            jnp.einsum("pqij,gqrj->gpri", matrix, window, precision=lax.Precision.HIGHEST)
        )
    return jnp.concatenate(pieces, axis=3)


def propagate(current, row_matrix, col_matrix):
    with_rows = extended_2(current, (("row", 2),), HALO)
    row_done = along_rows(with_rows, row_matrix)
    with_cols = extended_2(row_done, (("col", 3),), HALO)
    return along_cols(with_cols, col_matrix, HALO)


def transmit(screen, current, adjoint):
    screen_re = screen[0][None]
    screen_im = screen[1][None]
    if adjoint:
        screen_im = -screen_im
    real_part = screen_re * current[:, 0] - screen_im * current[:, 1]
    imag_part = screen_re * current[:, 1] + screen_im * current[:, 0]
    return jnp.stack([real_part, imag_part], axis=1)


def store_item(store, current, first_item, slice_index, active):
    begin = (first_item, jnp.int32(slice_index), jnp.int32(0), jnp.int32(0), jnp.int32(0))
    sizes_now = (current.shape[0], 1) + current.shape[1:]
    previous = lax.dynamic_slice(store, begin, sizes_now)
    fresh = jnp.where(active, current[:, None], previous)
    return lax.dynamic_update_slice(store, fresh, begin)


def staged_body(phase, tilt, intensity):
    slices, tile_r, tile_c = phase.shape
    batch_size = tilt.shape[0]
    sections = lax.axis_size("depth")
    section_index = lax.axis_index("depth")
    group_size = 1
    groups = batch_size // group_size
    tick_count = sections + groups - 1
    block_r = 64
    block_c = 128
    fwd_rows = band_matrix(block_r, HALO, FRESNEL, False)
    fwd_cols = band_matrix(block_c, HALO, FRESNEL, False)
    adj_rows = band_matrix(block_r, HALO, FRESNEL, True)
    adj_cols = band_matrix(block_c, HALO, FRESNEL, True)
    row_pos = (
        lax.axis_index("row") * tile_r + lax.broadcasted_iota(jnp.int32, (tile_r, tile_c), 0)
    ).astype(jnp.float32)
    col_pos = (
        lax.axis_index("col") * tile_c + lax.broadcasted_iota(jnp.int32, (tile_r, tile_c), 1)
    ).astype(jnp.float32)
    height = float(tile_r * lax.axis_size("row"))
    width_all = float(tile_c * lax.axis_size("col"))
    tilt_f = tilt.astype(jnp.float32)
    phase_angle = (
        2.0
        * jnp.pi
        * (
            tilt_f[:, 0, None, None] * row_pos / height
            + tilt_f[:, 1, None, None] * col_pos / width_all
        )
    )
    incident = jnp.stack([jnp.cos(phase_angle), jnp.sin(phase_angle)], axis=1)
    screens = jnp.stack([jnp.cos(phase), jnp.sin(phase)], axis=1)

    def forward_tick(tick_now, carry):
        incoming, entering, leaving = carry
        group_index = tick_now - section_index
        active = (group_index >= 0) & (group_index < groups)
        first_item = jnp.clip(group_index, 0, groups - 1) * group_size
        current = jnp.where(
            section_index == 0,
            lax.dynamic_slice_in_dim(incident, first_item, group_size, 0),
            incoming,
        )
        entering = store_item(entering, current, first_item, 0, active)
        current = propagate(transmit(screens[0], current, False), fwd_rows, fwd_cols)
        leaving = store_item(leaving, current, first_item, 0, active)
        incoming = from_behind(current, "depth", 1)
        return (incoming, entering, leaving)

    store_zero = jnp.zeros((batch_size, slices, 2, tile_r, tile_c), jnp.float32)
    start_wave = jnp.zeros((group_size, 2, tile_r, tile_c), jnp.float32)
    _, entering, leaving = lax.fori_loop(
        0, tick_count, forward_tick, (start_wave, store_zero, store_zero)
    )
    final_wave = leaving[:, slices - 1]
    misfit = final_wave[:, 0] * final_wave[:, 0] + final_wave[:, 1] * final_wave[:, 1] - intensity
    seed_adjoint = 2.0 * misfit[:, None] * final_wave

    def backward_tick(tick_now, carry):
        incoming, gradient = carry
        group_index = tick_now - (sections - 1 - section_index)
        active = (group_index >= 0) & (group_index < groups)
        first_item = jnp.clip(group_index, 0, groups - 1) * group_size
        adjoint_wave = jnp.where(
            section_index == sections - 1,
            lax.dynamic_slice_in_dim(seed_adjoint, first_item, group_size, 0),
            incoming,
        )
        for slice_index in reversed(range(slices)):
            pulled = propagate(adjoint_wave, adj_rows, adj_cols)
            arrived = lax.dynamic_slice_in_dim(entering[:, slice_index], first_item, group_size, 0)
            moved = transmit(screens[slice_index], arrived, False)
            contribution = jnp.sum(pulled[:, 1] * moved[:, 0] - pulled[:, 0] * moved[:, 1], axis=0)
            gradient = gradient.at[slice_index].add(jnp.where(active, contribution, 0.0))
            adjoint_wave = transmit(screens[slice_index], pulled, True)
        incoming = from_behind(adjoint_wave, "depth", -1)
        return (incoming, gradient)

    grad_zero = jnp.zeros((slices, tile_r, tile_c), jnp.float32)
    _, gradient = lax.fori_loop(0, tick_count, backward_tick, (start_wave, grad_zero))
    return (gradient, leaving)


def fits_whole(phase_shape, batch, mesh):
    slices, height, width = phase_shape
    rows, cols, sections = mesh.shape["row"], mesh.shape["col"], mesh.shape["depth"]
    return (
        4 * height * width * (slices + batch) <= GATHER_BUDGET
        and batch == rows == 2
        and slices == sections
        and sections & (sections - 1) == 0
        and cols == 4
        and height == LANES
        and width == cols * LANES
        and sections > 1
        and sections * HALO <= LANES
    )


def solution(mesh):
    placed = (P("depth", "row", "col"), P(), P(None, "row", "col"))

    def run(phase, tilt, intensity):
        if fits_whole(phase.shape, tilt.shape[0], mesh):
            body = whole_field_body
        else:
            body = staged_body
        return jax.shard_map(
            body,
            mesh=mesh,
            in_specs=placed,
            out_specs=(P("depth", "row", "col"), P(None, "depth", None, "row", "col")),
            check_vma=False,
        )(phase, tilt, intensity)

    return run
```

```python
import math

import jax
import jax.numpy as jnp
import numpy as np
from jax import lax
from jax.experimental import pallas as pl
from jax.experimental.pallas import tpu as pltpu
from jax.sharding import PartitionSpec as P

HALO = 32
FRESNEL = 64
LANES = 128
GATHER_BUDGET = 4 * 2**20
SIN = (
    0.9999999980536763,
    -0.1666666530009577,
    0.008333305907073658,
    -0.00019838908256358006,
    2.745822627876341e-06,
    -2.3043562782810933e-08,
)
COS = (
    0.9999999961345007,
    -0.4999999301617528,
    0.04166646215023687,
    -0.0013886696163545999,
    2.4695045482778703e-05,
    -2.5154931690000354e-07,
)


def horner(coefficients, square):
    total = jnp.full_like(square, coefficients[-1])
    for coefficient in coefficients[-2::-1]:
        total = total * square + coefficient
    return total


def cos_sin(angle):
    square = angle * angle
    return horner(COS, square), horner(SIN, square) * angle


def turn(fraction):
    half_cos, half_sin = cos_sin(fraction * math.pi)
    return half_cos * half_cos - half_sin * half_sin, 2.0 * half_cos * half_sin


def halves(value):
    high = value.astype(jnp.bfloat16)
    return high, (value - high.astype(jnp.float32)).astype(jnp.bfloat16)


def np_halves(matrix):
    high = matrix.astype(jnp.bfloat16)
    return high, (matrix - high.astype(np.float64)).astype(jnp.bfloat16)


def np_taps():
    offset = np.arange(-HALO, HALO + 1, dtype=np.float64)
    taper = np.maximum(np.abs(offset) - 0.5 * HALO, 0.0)
    weight = np.cos(np.pi * taper / (HALO + 2.0)) ** 2 / math.sqrt(FRESNEL)
    return weight * np.exp(1j * np.pi * offset * offset / FRESNEL)


def np_band(out_pos, in_pos):
    offset = out_pos[:, None] - in_pos[None, :]
    inside = np.abs(offset) <= HALO
    return np.where(inside, np_taps()[np.clip(offset, -HALO, HALO) + HALO], 0.0)


def row_constant(height):
    matrices = []
    for core in range(2):
        pos = (np.arange(height) + core * (height // 2)) % height
        band = np_band(pos, pos)
        whole = np.block([[band.real, -band.imag], [band.imag, band.real]])
        matrices.append(np.concatenate(np_halves(whole), axis=1))
    return np.stack(matrices)


def col_constant():
    lane = np.arange(LANES)
    turned = np.where((lane >= HALO) & (lane < LANES - HALO), lane ^ (LANES // 2), lane)
    edge_pos = np.where(turned < LANES // 2, turned + LANES, turned - LANES)
    parts = []
    for position in (lane, edge_pos):
        band = np_band(lane, position).T
        parts.append(np.block([[band.real, band.imag], [-band.imag, band.real]]))
    return np.concatenate(np_halves(np.concatenate(parts, axis=0)), axis=1)


def both_rows(near_ref, far_ref, where):
    return jnp.concatenate([near_ref[where], far_ref[where]], axis=0)


def turned(slice_index, block, screens, wave):
    near_cos, near_sin, far_cos, far_sin = screens
    cos = both_rows(near_cos, far_cos, (slice_index, block))
    sin = both_rows(near_sin, far_sin, (slice_index, block))
    real, imag = wave
    return cos * real - sin * imag, cos * imag + sin * real


def row_product(row_matrix, columns):
    high, low = halves(columns)
    whole, width = columns.shape
    wide = jnp.dot(
        row_matrix[:, :whole], jnp.concatenate([high, low], axis=1), preferred_element_type=jnp.float32
    )
    rest = jnp.dot(row_matrix[:, whole:], high, preferred_element_type=jnp.float32)
    return wide[:, :width] + wide[:, width:] + rest


def col_product(high, low, col_ref):
    wide = jnp.dot(high, col_ref[...], preferred_element_type=jnp.float32)
    rest = jnp.dot(low, col_ref[: 2 * LANES, : 2 * LANES], preferred_element_type=jnp.float32)
    return wide[:, : 2 * LANES] + wide[:, 2 * LANES :] + rest


def three_parts(value):
    high = value.astype(jnp.bfloat16)
    rest = value - high.astype(jnp.float32)
    return high, rest.astype(jnp.bfloat16), pltpu.roll(rest, LANES // 2, 1).astype(jnp.bfloat16)


def advance(slice_index, start, waves, screens, row_matrix, col_ref, edge_ref):
    size, height = len(waves), waves[0][0].shape[0]
    chunks = [range(place, min(place + 2, size)) for place in range(0, size, 2)]
    highs, lows = [], []
    for chunk in chunks:
        columns = [
            jnp.concatenate(turned(slice_index, start + place, screens, waves[place]), axis=0) for place in chunk
        ]
        done = row_product(row_matrix, jnp.concatenate(columns, axis=1))
        for sub, place in enumerate(chunk):
            own_high, own_low = [], []
            for part in range(2):
                value = done[part * height : (part + 1) * height, sub * LANES : (sub + 1) * LANES]
                high, low, swung = three_parts(value)
                own_high.append(high)
                own_low.append(low)
                edge = part * LANES
                if place > 0:
                    edge_ref[place - 1, :, pl.ds(edge, HALO)] = high[:, :HALO]
                    edge_ref[place - 1, :, pl.ds(edge + 2 * HALO, HALO)] = swung[:, 2 * HALO : 3 * HALO]
                if place < size - 1:
                    edge_ref[place + 1, :, pl.ds(edge + 3 * HALO, HALO)] = high[:, 3 * HALO :]
                    edge_ref[place + 1, :, pl.ds(edge + HALO, HALO)] = swung[:, HALO : 2 * HALO]
            highs.append(jnp.concatenate(own_high, axis=1))
            lows.append(jnp.concatenate(own_low, axis=1))
    results = []
    for chunk in chunks:
        rows = len(chunk) * height
        edges = edge_ref[pl.ds(chunk[0], len(chunk))].reshape(rows, 2 * LANES)
        own = jnp.concatenate([highs[place] for place in chunk], axis=0)
        total = col_product(
            jnp.concatenate([own, edges], axis=1),
            jnp.concatenate([lows[place] for place in chunk], axis=0),
            col_ref,
        )
        for sub in range(len(chunk)):
            block = total[sub * height : (sub + 1) * height]
            results.append((block[:, :LANES], block[:, LANES:]))
    return results


def clear_edge(edge_ref, place, right):
    for part in range(2):
        for begin in (0, 2 * HALO) if right else (HALO, 3 * HALO):
            cells = pl.ds(part * LANES + begin, HALO)
            edge_ref[place, :, cells] = jnp.zeros((edge_ref.shape[1], HALO), edge_ref.dtype)


def keep(wave_ref, waves):
    for place, wave in enumerate(waves):
        wave_ref[place, 0], wave_ref[place, 1] = wave


def first_kernel(tilt_ref, near_own, far_own, wave_ref, measured_ref, cos_ref, sin_ref):
    blocks, _, height, _ = wave_ref.shape
    core, own_place = lax.axis_index("row"), lax.axis_index("col")
    for col in range(blocks):
        held = col ^ own_place
        measured_ref[col] = jnp.concatenate([near_own[held, 1 + core], far_own[held, 1]], axis=0)
        cos_ref[col], sin_ref[col] = cos_sin(near_own[held, 0])

    def cycles(number, position, extent):
        fraction = (number * position).astype(jnp.float32) / extent
        return turn(fraction - jnp.round(fraction))

    row = lax.broadcasted_iota(jnp.int32, (height, LANES), 0) + core * (height // 2)
    row = jnp.where(row >= height, row - height, row)
    row_cos, row_sin = cycles(tilt_ref[core, 0], row, float(height))
    for block in range(blocks):
        col_cos, col_sin = cycles(
            tilt_ref[core, 1],
            lax.broadcasted_iota(jnp.int32, (8, LANES), 1) + block * LANES,
            float(blocks * LANES),
        )
        col_cos, col_sin = col_cos[:1], col_sin[:1]
        wave_ref[block, 0] = row_cos * col_cos - row_sin * col_sin
        wave_ref[block, 1] = row_sin * col_cos + row_cos * col_sin


def second_kernel(near_rest, own_cos, own_sin, cos_ref, sin_ref):
    blocks = own_cos.shape[0]
    count = cos_ref.shape[0] - 1
    own_section, own_place = lax.axis_index("depth"), lax.axis_index("col")

    def screens(col, carry):
        held = col ^ own_place
        cos_ref[own_section, col], sin_ref[own_section, col] = own_cos[col], own_sin[col]
        for bits in range(1, count):
            cos_ref[bits ^ own_section, col], sin_ref[bits ^ own_section, col] = cos_sin(near_rest[held, bits - 1])
        return carry

    lax.fori_loop(0, blocks, screens, 0)
    cos_ref[count] = jnp.ones(cos_ref.shape[1:], jnp.float32)
    sin_ref[count] = jnp.zeros(cos_ref.shape[1:], jnp.float32)


def wave_kernel(
    wave_ref, near_cos, near_sin, measured_ref, far_own, far_rest, row_ref, col_ref,
    mine_ref, theirs_ref, far_cos, far_sin, kept_ref, moved_ref, left_ref, grad_ref, even_edge, odd_edge,
):
    blocks, _, height, _ = wave_ref.shape
    count = near_cos.shape[0] - 1
    core, own_section, own_place = lax.axis_index("row"), lax.axis_index("depth"), lax.axis_index("col")
    near, far = pl.ds(0, height // 2), pl.ds(height // 2, height // 2)
    screens = (near_cos, near_sin, far_cos, far_sin)
    row_matrix = row_ref[core]
    window = min(3, blocks)
    window_start = jnp.clip(own_place - 1, 0, blocks - window)
    own_in_window = own_place - window_start
    edges = (even_edge, odd_edge)

    def far_screens(slice_index):
        bits = slice_index ^ own_section
        for col in range(blocks):
            held = col ^ own_place
            angle = jnp.where(bits == 0, far_own[held, 0], far_rest[held, jnp.maximum(bits - 1, 0)])
            far_cos[slice_index, col], far_sin[slice_index, col] = cos_sin(angle)

    for edge_ref in edges:
        clear_edge(edge_ref, 0, False)
        clear_edge(edge_ref, blocks - 1, True)
    far_cos[count] = jnp.ones(far_cos.shape[1:], jnp.float32)
    far_sin[count] = jnp.zeros(far_cos.shape[1:], jnp.float32)
    far_screens(0)

    waves = [(wave_ref[place, 0], wave_ref[place, 1]) for place in range(blocks)]
    for tick in range(count):
        entering = (wave_ref if tick == 0 else kept_ref)[own_place]
        moved_ref[tick, 0], moved_ref[tick, 1] = turned(tick, own_place, screens, (entering[0], entering[1]))
        waves = advance(tick, 0, waves, screens, row_matrix, col_ref, edges[tick % 2])
        if tick + 1 < count:
            far_screens(tick + 1)
        keep(kept_ref, waves)
        left_ref[tick] = kept_ref[own_place]

    for edge_ref in edges:
        clear_edge(edge_ref, window - 1, True)
    waves = []
    for place in range(window):
        block = window_start + place
        real, imag = kept_ref[block, 0], kept_ref[block, 1]
        misfit = 2.0 * (real * real + imag * imag - measured_ref[block])
        waves.append((misfit * real, -misfit * imag))

    for tick in range(count - 1):
        waves = advance(count - tick, window_start, waves, screens, row_matrix, col_ref, edges[tick % 2])
        keep(kept_ref, waves)
        arrived = count - 1 - tick
        pulled = kept_ref[own_in_window]
        grad_ref[arrived] = -(pulled[1] * moved_ref[arrived, 0] + pulled[0] * moved_ref[arrived, 1])

    left, right = jnp.maximum(own_place - 1, 0), jnp.minimum(own_place + 1, blocks - 1)
    lane = lax.broadcasted_iota(jnp.int32, (2 * height, LANES), 1)
    has_left, has_right = own_place > 0, own_place < blocks - 1

    def cells(block):
        wave = kept_ref[block - window_start]
        return jnp.concatenate(turned(1, block, screens, (wave[0], wave[1])), axis=0)

    edge_cells = jnp.where(
        lane < LANES // 2, jnp.where(has_right, cells(right), 0.0), jnp.where(has_left, cells(left), 0.0)
    )
    done = row_product(row_matrix, jnp.concatenate([cells(own_place), edge_cells], axis=1))
    lane = lax.broadcasted_iota(jnp.int32, (height, LANES), 1)
    between = (lane >= HALO) & (lane < LANES - HALO)
    highs, lows, edges = [], [], []
    for part in range(2):
        high, low, _ = three_parts(done[part * height : (part + 1) * height, :LANES])
        highs.append(high)
        lows.append(low)
        value = done[part * height : (part + 1) * height, LANES:]
        whole_high = value.astype(jnp.bfloat16).astype(jnp.float32)
        edge = jnp.where(between, pltpu.roll(value - whole_high, LANES // 2, 1), whole_high)
        edges.append(edge.astype(jnp.bfloat16))
    pulled = col_product(jnp.concatenate(highs + edges, axis=1), jnp.concatenate(lows, axis=1), col_ref)
    grad_ref[0] = -(pulled[:, LANES:] * moved_ref[0, 0] + pulled[:, :LANES] * moved_ref[0, 1])

    for target, row in ((mine_ref, near), (theirs_ref, far)):
        for part in range(2):
            target[0, part] = left_ref[own_section, part, row]
        target[0, 2] = grad_ref[own_section, row]


def finish_kernel(mine_ref, received_ref, grad_ref, exit_ref, total_ref, sems):
    core = lax.axis_index("row")
    copies = []
    for source, item in ((mine_ref, core), (received_ref, 1 - core)):
        copies.append(pltpu.make_async_copy(source.at[:, pl.ds(0, 2)], exit_ref.at[item], sems.at[len(copies)]))
    for copy in copies:
        copy.start()
    total_ref[...] = mine_ref[:, 2] + received_ref[:, 2]
    copies.append(pltpu.make_async_copy(total_ref, grad_ref, sems.at[2]))
    copies[2].start()
    for copy in copies:
        copy.wait()


def spread(shard, axis, reach=None):
    size = lax.axis_size(axis)
    reach = size if reach is None else reach
    pieces = []
    for bits in range(1, size):
        pairs = [(i, i ^ bits) for i in range(size) if abs(i - (i ^ bits)) <= reach]
        pieces.append(lax.ppermute(shard, axis, pairs) if pairs else jnp.zeros_like(shard))
    return pieces


def swap_cores(value):
    return lax.ppermute(value, "row", [(0, 1), (1, 0)])


def whole_field_body(phase, tilt, intensity):
    _, tile_r, tile_c = phase.shape
    count, blocks = lax.axis_size("depth"), lax.axis_size("col")
    core = lax.axis_index("row")
    height = 2 * tile_r
    vmem = pl.BlockSpec(memory_space=pltpu.VMEM)
    smem = pl.BlockSpec(memory_space=pltpu.SMEM)
    hbm = pl.BlockSpec(memory_space=pl.ANY)

    def array(*shape):
        return jax.ShapeDtypeStruct(shape, jnp.float32)

    def params(mebibytes):
        return pltpu.CompilerParams(vmem_limit_bytes=mebibytes * 2**20)

    other_depths = spread(phase, "depth")
    other_depths[0], measured, slab = lax.optimization_barrier((other_depths[0], intensity, phase))
    other_depths = jnp.concatenate(other_depths, axis=0)
    packet = jnp.concatenate([slab, measured], axis=0)
    near_own = [packet]
    for bits in range(1, blocks):
        pairs = [(i, i ^ bits) for i in range(blocks)]
        close = [(i, j) for i, j in pairs if abs(i - j) <= 1]
        if close:
            near_own.append(lax.ppermute(packet, "col", close))
        else:
            further = [(i, j) for i, j in pairs if abs(i - j) <= 2]
            arrived = lax.ppermute(slab, "col", further) if further else jnp.zeros_like(slab)
            near_own.append(jnp.concatenate([arrived, jnp.zeros_like(measured)], axis=0))
    near_own = jnp.stack(near_own)
    arriving = spread(other_depths, "col", 2)
    arriving[2], near_own = lax.optimization_barrier((arriving[2], near_own))
    near_rest = jnp.stack([other_depths] + arriving)
    wanted = lax.dynamic_slice_in_dim(near_own, 2 - core, 1, 1)
    far_own = swap_cores(jnp.concatenate([near_own[:, :1], wanted], axis=1))
    far_rest = swap_cores(near_rest)

    half_screens = (count + 1, blocks, tile_r, tile_c)
    field = (blocks, 2, height, tile_c)
    wave, measured, own_cos, own_sin = pl.pallas_call(
        first_kernel,
        out_shape=(array(*field), array(blocks, height, tile_c)) + (array(blocks, tile_r, tile_c),) * 2,
        in_specs=[smem, vmem, vmem],
        out_specs=(vmem,) * 4,
        compiler_params=params(8),
        cost_estimate=pl.CostEstimate(flops=2 * 10**9, bytes_accessed=2**20, transcendentals=0),
    )(tilt, near_own, far_own)
    near_cos, near_sin = pl.pallas_call(
        second_kernel,
        out_shape=(array(*half_screens),) * 2,
        in_specs=[vmem] * 3,
        out_specs=(vmem,) * 2,
        compiler_params=params(8),
        cost_estimate=pl.CostEstimate(flops=5 * 10**8, bytes_accessed=2**20, transcendentals=0),
    )(near_rest, own_cos, own_sin)
    mine, theirs = pl.pallas_call(
        wave_kernel,
        out_shape=(array(1, 3, tile_r, tile_c),) * 2,
        in_specs=[vmem] * 8,
        out_specs=(vmem,) * 2,
        scratch_shapes=[pltpu.VMEM(half_screens, jnp.float32)] * 2
        + [pltpu.VMEM(field, jnp.float32)]
        + [pltpu.VMEM((count, 2, height, tile_c), jnp.float32)] * 2
        + [pltpu.VMEM((count, height, tile_c), jnp.float32)]
        + [pltpu.VMEM((blocks, height, 2 * LANES), jnp.bfloat16)] * 2,
        compiler_params=params(24),
    )(
        wave, near_cos, near_sin, measured, far_own, far_rest,
        jnp.asarray(row_constant(height)), jnp.asarray(col_constant()),
    )
    return pl.pallas_call(
        finish_kernel,
        out_shape=(array(*phase.shape), array(2, 1, 2, tile_r, tile_c)),
        in_specs=[vmem, vmem],
        out_specs=(hbm, hbm),
        scratch_shapes=[pltpu.VMEM(phase.shape, jnp.float32), pltpu.SemaphoreType.DMA((3,))],
        compiler_params=params(4),
    )(mine, swap_cores(theirs))


def extended_2(cells, sides, width):
    for axis, dim in sides:
        count = lax.axis_size(axis)
        ends = count - 1
        head = lax.slice_in_dim(cells, 0, width, axis=dim)
        tail = lax.slice_in_dim(cells, cells.shape[dim] - width, cells.shape[dim], axis=dim)
        cells = jnp.concatenate(
            [
                lax.ppermute(tail, axis, [(i, (i + 1) % count) for i in range(ends)]),
                cells,
                lax.ppermute(head, axis, [((i + 1) % count, i) for i in range(ends)]),
            ],
            axis=dim,
        )
    return cells


def from_behind(value, axis, steps):
    count = lax.axis_size(axis)
    leading, last = (max(0, -steps), min(count, count - steps))
    return lax.ppermute(value, axis, [(source, source + steps) for source in range(leading, last)])


def band_matrix(block_size, margin, fresnel, adjoint):
    shape_full = (block_size, block_size + 2 * margin)
    out_idx = lax.broadcasted_iota(jnp.int32, shape_full, 0)
    in_idx = lax.broadcasted_iota(jnp.int32, shape_full, 1)
    offset = (out_idx + margin - in_idx).astype(jnp.float32)
    inside = jnp.abs(offset) <= margin
    taper_dist = jnp.maximum(jnp.abs(offset) - 0.5 * margin, 0.0)
    profile = jnp.cos(jnp.pi * taper_dist / (margin + 2.0))
    weight = profile * profile / math.sqrt(fresnel)
    phase_angle = jnp.pi * offset * offset / fresnel
    real_part = jnp.where(inside, jnp.cos(phase_angle) * weight, 0.0)
    imag_part = jnp.where(inside, jnp.sin(phase_angle) * weight, 0.0)
    if adjoint:
        imag_part = -imag_part
    upper = jnp.stack([real_part, -imag_part])
    lower = jnp.stack([imag_part, real_part])
    return jnp.stack([upper, lower])


def along_rows(extended, matrix):
    pieces = [jnp.einsum("pqij,gqjc->gpic", matrix, extended, precision=lax.Precision.HIGHEST)]
    return jnp.concatenate(pieces, axis=2)


def along_cols(extended, matrix, margin):
    block_size = matrix.shape[2]
    extent = extended.shape[3] - 2 * margin
    pieces = []
    for block_start in range(0, extent, block_size):
        window = extended[:, :, :, block_start : block_start + block_size + 2 * margin]
        pieces.append(
            jnp.einsum("pqij,gqrj->gpri", matrix, window, precision=lax.Precision.HIGHEST)
        )
    return jnp.concatenate(pieces, axis=3)


def propagate(current, row_matrix, col_matrix):
    with_rows = extended_2(current, (("row", 2),), HALO)
    row_done = along_rows(with_rows, row_matrix)
    with_cols = extended_2(row_done, (("col", 3),), HALO)
    return along_cols(with_cols, col_matrix, HALO)


def transmit(screen, current, adjoint):
    screen_re = screen[0][None]
    screen_im = screen[1][None]
    if adjoint:
        screen_im = -screen_im
    real_part = screen_re * current[:, 0] - screen_im * current[:, 1]
    imag_part = screen_re * current[:, 1] + screen_im * current[:, 0]
    return jnp.stack([real_part, imag_part], axis=1)


def store_item(store, current, first_item, slice_index, active):
    begin = (first_item, jnp.int32(slice_index), jnp.int32(0), jnp.int32(0), jnp.int32(0))
    sizes_now = (current.shape[0], 1) + current.shape[1:]
    previous = lax.dynamic_slice(store, begin, sizes_now)
    fresh = jnp.where(active, current[:, None], previous)
    return lax.dynamic_update_slice(store, fresh, begin)


def staged_body(phase, tilt, intensity):
    slices, tile_r, tile_c = phase.shape
    batch_size = tilt.shape[0]
    sections = lax.axis_size("depth")
    section_index = lax.axis_index("depth")
    group_size = 1
    groups = batch_size // group_size
    tick_count = sections + groups - 1
    block_r = 64
    block_c = 128
    fwd_rows = band_matrix(block_r, HALO, FRESNEL, False)
    fwd_cols = band_matrix(block_c, HALO, FRESNEL, False)
    adj_rows = band_matrix(block_r, HALO, FRESNEL, True)
    adj_cols = band_matrix(block_c, HALO, FRESNEL, True)
    row_pos = (
        lax.axis_index("row") * tile_r + lax.broadcasted_iota(jnp.int32, (tile_r, tile_c), 0)
    ).astype(jnp.float32)
    col_pos = (
        lax.axis_index("col") * tile_c + lax.broadcasted_iota(jnp.int32, (tile_r, tile_c), 1)
    ).astype(jnp.float32)
    height = float(tile_r * lax.axis_size("row"))
    width_all = float(tile_c * lax.axis_size("col"))
    tilt_f = tilt.astype(jnp.float32)
    phase_angle = (
        2.0
        * jnp.pi
        * (
            tilt_f[:, 0, None, None] * row_pos / height
            + tilt_f[:, 1, None, None] * col_pos / width_all
        )
    )
    incident = jnp.stack([jnp.cos(phase_angle), jnp.sin(phase_angle)], axis=1)
    screens = jnp.stack([jnp.cos(phase), jnp.sin(phase)], axis=1)

    def forward_tick(tick_now, carry):
        incoming, entering, leaving = carry
        group_index = tick_now - section_index
        active = (group_index >= 0) & (group_index < groups)
        first_item = jnp.clip(group_index, 0, groups - 1) * group_size
        current = jnp.where(
            section_index == 0,
            lax.dynamic_slice_in_dim(incident, first_item, group_size, 0),
            incoming,
        )
        entering = store_item(entering, current, first_item, 0, active)
        current = propagate(transmit(screens[0], current, False), fwd_rows, fwd_cols)
        leaving = store_item(leaving, current, first_item, 0, active)
        incoming = from_behind(current, "depth", 1)
        return (incoming, entering, leaving)

    store_zero = jnp.zeros((batch_size, slices, 2, tile_r, tile_c), jnp.float32)
    start_wave = jnp.zeros((group_size, 2, tile_r, tile_c), jnp.float32)
    _, entering, leaving = lax.fori_loop(
        0, tick_count, forward_tick, (start_wave, store_zero, store_zero)
    )
    final_wave = leaving[:, slices - 1]
    misfit = final_wave[:, 0] * final_wave[:, 0] + final_wave[:, 1] * final_wave[:, 1] - intensity
    seed_adjoint = 2.0 * misfit[:, None] * final_wave

    def backward_tick(tick_now, carry):
        incoming, gradient = carry
        group_index = tick_now - (sections - 1 - section_index)
        active = (group_index >= 0) & (group_index < groups)
        first_item = jnp.clip(group_index, 0, groups - 1) * group_size
        adjoint_wave = jnp.where(
            section_index == sections - 1,
            lax.dynamic_slice_in_dim(seed_adjoint, first_item, group_size, 0),
            incoming,
        )
        for slice_index in reversed(range(slices)):
            pulled = propagate(adjoint_wave, adj_rows, adj_cols)
            arrived = lax.dynamic_slice_in_dim(entering[:, slice_index], first_item, group_size, 0)
            moved = transmit(screens[slice_index], arrived, False)
            contribution = jnp.sum(pulled[:, 1] * moved[:, 0] - pulled[:, 0] * moved[:, 1], axis=0)
            gradient = gradient.at[slice_index].add(jnp.where(active, contribution, 0.0))
            adjoint_wave = transmit(screens[slice_index], pulled, True)
        incoming = from_behind(adjoint_wave, "depth", -1)
        return (incoming, gradient)

    grad_zero = jnp.zeros((slices, tile_r, tile_c), jnp.float32)
    _, gradient = lax.fori_loop(0, tick_count, backward_tick, (start_wave, grad_zero))
    return (gradient, leaving)


def fits_whole(phase_shape, batch, mesh):
    slices, height, width = phase_shape
    rows, cols, sections = mesh.shape["row"], mesh.shape["col"], mesh.shape["depth"]
    return (
        4 * height * width * (slices + batch) <= GATHER_BUDGET
        and batch == rows == 2
        and slices == sections
        and sections & (sections - 1) == 0
        and cols & (cols - 1) == 0
        and height == LANES
        and width == cols * LANES
        and cols > 1
        and sections > 1
        and sections * HALO <= LANES
    )


def solution(mesh):
    placed = (P("depth", "row", "col"), P(), P(None, "row", "col"))

    def run(phase, tilt, intensity):
        if fits_whole(phase.shape, tilt.shape[0], mesh):
            body = whole_field_body
        else:
            body = staged_body
        return jax.shard_map(
            body,
            mesh=mesh,
            in_specs=placed,
            out_specs=(P("depth", "row", "col"), P(None, "depth", None, "row", "col")),
            check_vma=False,
        )(phase, tilt, intensity)

    return run
```

```python
import math

import jax
import jax.numpy as jnp
import numpy as np
from jax import lax
from jax.experimental import pallas as pl
from jax.experimental.pallas import tpu as pltpu
from jax.sharding import PartitionSpec as P

HALO = 32
FRESNEL = 64
LANES = 128
GATHER_BUDGET = 4 * 2**20
SIN = (
    0.9999999980536763,
    -0.1666666530009577,
    0.008333305907073658,
    -0.00019838908256358006,
    2.745822627876341e-06,
    -2.3043562782810933e-08,
)
COS = (
    0.9999999961345007,
    -0.4999999301617528,
    0.04166646215023687,
    -0.0013886696163545999,
    2.4695045482778703e-05,
    -2.5154931690000354e-07,
)


def horner(coefficients, square):
    total = jnp.full_like(square, coefficients[-1])
    for coefficient in coefficients[-2::-1]:
        total = total * square + coefficient
    return total


def cos_sin(angle):
    square = angle * angle
    return horner(COS, square), horner(SIN, square) * angle


def turn(fraction):
    half_cos, half_sin = cos_sin(fraction * math.pi)
    return half_cos * half_cos - half_sin * half_sin, 2.0 * half_cos * half_sin


def halves(value):
    high = value.astype(jnp.bfloat16)
    return high, (value - high.astype(jnp.float32)).astype(jnp.bfloat16)


def np_halves(matrix):
    high = matrix.astype(jnp.bfloat16)
    return high, (matrix - high.astype(np.float64)).astype(jnp.bfloat16)


def np_taps():
    offset = np.arange(-HALO, HALO + 1, dtype=np.float64)
    taper = np.maximum(np.abs(offset) - 0.5 * HALO, 0.0)
    weight = np.cos(np.pi * taper / (HALO + 2.0)) ** 2 / math.sqrt(FRESNEL)
    return weight * np.exp(1j * np.pi * offset * offset / FRESNEL)


def np_band(out_pos, in_pos):
    offset = out_pos[:, None] - in_pos[None, :]
    inside = np.abs(offset) <= HALO
    return np.where(inside, np_taps()[np.clip(offset, -HALO, HALO) + HALO], 0.0)


def row_constant(height):
    matrices = []
    for core in range(2):
        pos = (np.arange(height) + core * (height // 2)) % height
        band = np_band(pos, pos)
        whole = np.block([[band.real, -band.imag], [band.imag, band.real]])
        matrices.append(np.concatenate(np_halves(whole), axis=1))
    return np.stack(matrices)


def col_constant():
    lane = np.arange(LANES)
    turned = np.where((lane >= HALO) & (lane < LANES - HALO), lane ^ (LANES // 2), lane)
    edge_pos = np.where(turned < LANES // 2, turned + LANES, turned - LANES)
    parts = []
    for position in (lane, edge_pos):
        band = np_band(lane, position).T
        parts.append(np.block([[band.real, band.imag], [-band.imag, band.real]]))
    return np.concatenate(np_halves(np.concatenate(parts, axis=0)), axis=1)


def both_rows(near_ref, far_ref, where):
    return jnp.concatenate([near_ref[where], far_ref[where]], axis=0)


def turned(slice_index, block, screens, wave):
    near_cos, near_sin, far_cos, far_sin = screens
    cos = both_rows(near_cos, far_cos, (slice_index, block))
    sin = both_rows(near_sin, far_sin, (slice_index, block))
    real, imag = wave
    return cos * real - sin * imag, cos * imag + sin * real


def row_product(row_matrix, columns):
    high, low = halves(columns)
    whole, width = columns.shape
    wide = jnp.dot(
        row_matrix[:, :whole], jnp.concatenate([high, low], axis=1), preferred_element_type=jnp.float32
    )
    rest = jnp.dot(row_matrix[:, whole:], high, preferred_element_type=jnp.float32)
    return wide[:, :width] + wide[:, width:] + rest


def col_product(high, low, col_ref):
    wide = jnp.dot(high, col_ref[...], preferred_element_type=jnp.float32)
    rest = jnp.dot(low, col_ref[: 2 * LANES, : 2 * LANES], preferred_element_type=jnp.float32)
    return wide[:, : 2 * LANES] + wide[:, 2 * LANES :] + rest


def three_parts(value):
    high = value.astype(jnp.bfloat16)
    rest = value - high.astype(jnp.float32)
    return high, rest.astype(jnp.bfloat16), pltpu.roll(rest, LANES // 2, 1).astype(jnp.bfloat16)


def advance(slice_index, start, waves, screens, row_matrix, col_ref, edge_ref):
    size, height = len(waves), waves[0][0].shape[0]
    chunks = [range(place, min(place + 2, size)) for place in range(0, size, 2)]
    highs, lows = [], []
    for chunk in chunks:
        columns = [
            jnp.concatenate(turned(slice_index, start + place, screens, waves[place]), axis=0) for place in chunk
        ]
        done = row_product(row_matrix, jnp.concatenate(columns, axis=1))
        for sub, place in enumerate(chunk):
            own_high, own_low = [], []
            for part in range(2):
                value = done[part * height : (part + 1) * height, sub * LANES : (sub + 1) * LANES]
                high, low, swung = three_parts(value)
                own_high.append(high)
                own_low.append(low)
                edge = part * LANES
                if place > 0:
                    edge_ref[place - 1, :, pl.ds(edge, HALO)] = high[:, :HALO]
                    edge_ref[place - 1, :, pl.ds(edge + 2 * HALO, HALO)] = swung[:, 2 * HALO : 3 * HALO]
                if place < size - 1:
                    edge_ref[place + 1, :, pl.ds(edge + 3 * HALO, HALO)] = high[:, 3 * HALO :]
                    edge_ref[place + 1, :, pl.ds(edge + HALO, HALO)] = swung[:, HALO : 2 * HALO]
            highs.append(jnp.concatenate(own_high, axis=1))
            lows.append(jnp.concatenate(own_low, axis=1))
    results = []
    for chunk in chunks:
        rows = len(chunk) * height
        edges = edge_ref[pl.ds(chunk[0], len(chunk))].reshape(rows, 2 * LANES)
        own = jnp.concatenate([highs[place] for place in chunk], axis=0)
        total = col_product(
            jnp.concatenate([own, edges], axis=1),
            jnp.concatenate([lows[place] for place in chunk], axis=0),
            col_ref,
        )
        for sub in range(len(chunk)):
            block = total[sub * height : (sub + 1) * height]
            results.append((block[:, :LANES], block[:, LANES:]))
    return results


def clear_edge(edge_ref, place, right):
    for part in range(2):
        for begin in (0, 2 * HALO) if right else (HALO, 3 * HALO):
            cells = pl.ds(part * LANES + begin, HALO)
            edge_ref[place, :, cells] = jnp.zeros((edge_ref.shape[1], HALO), edge_ref.dtype)


def keep(wave_ref, waves):
    for place, wave in enumerate(waves):
        wave_ref[place, 0], wave_ref[place, 1] = wave


def load_kernel(row_from, col_from, row_to, col_to, sems):
    copies = [
        pltpu.make_async_copy(row_from.at[lax.axis_index("row")], row_to, sems.at[0]),
        pltpu.make_async_copy(col_from, col_to, sems.at[1]),
    ]
    for copy in copies:
        copy.start()
    for copy in copies:
        copy.wait()


def first_kernel(tilt_ref, near_own, far_own, wave_ref, measured_ref, cos_ref, sin_ref):
    blocks, _, height, _ = wave_ref.shape
    core, own_place = lax.axis_index("row"), lax.axis_index("col")
    for col in range(blocks):
        held = col ^ own_place
        measured_ref[col] = jnp.concatenate([near_own[held, 1 + core], far_own[held, 1]], axis=0)
        cos_ref[col], sin_ref[col] = cos_sin(near_own[held, 0])

    def cycles(number, position, extent):
        fraction = (number * position).astype(jnp.float32) / extent
        return turn(fraction - jnp.round(fraction))

    row = lax.broadcasted_iota(jnp.int32, (height, LANES), 0) + core * (height // 2)
    row = jnp.where(row >= height, row - height, row)
    row_cos, row_sin = cycles(tilt_ref[core, 0], row, float(height))
    for block in range(blocks):
        col_cos, col_sin = cycles(
            tilt_ref[core, 1],
            lax.broadcasted_iota(jnp.int32, (8, LANES), 1) + block * LANES,
            float(blocks * LANES),
        )
        col_cos, col_sin = col_cos[:1], col_sin[:1]
        wave_ref[block, 0] = row_cos * col_cos - row_sin * col_sin
        wave_ref[block, 1] = row_sin * col_cos + row_cos * col_sin


def second_kernel(near_rest, own_cos, own_sin, cos_ref, sin_ref):
    blocks = own_cos.shape[0]
    count = cos_ref.shape[0] - 1
    own_section, own_place = lax.axis_index("depth"), lax.axis_index("col")

    def screens(col, carry):
        held = col ^ own_place
        cos_ref[own_section, col], sin_ref[own_section, col] = own_cos[col], own_sin[col]
        for bits in range(1, count):
            cos_ref[bits ^ own_section, col], sin_ref[bits ^ own_section, col] = cos_sin(near_rest[held, bits - 1])
        return carry

    lax.fori_loop(0, blocks, screens, 0)
    cos_ref[count] = jnp.ones(cos_ref.shape[1:], jnp.float32)
    sin_ref[count] = jnp.zeros(cos_ref.shape[1:], jnp.float32)


def wave_kernel(
    wave_ref, near_cos, near_sin, measured_ref, far_own, far_rest, row_ref, col_ref,
    mine_ref, theirs_ref, far_cos, far_sin, kept_ref, moved_ref, left_ref, grad_ref, even_edge, odd_edge,
):
    blocks, _, height, _ = wave_ref.shape
    count = near_cos.shape[0] - 1
    core, own_section, own_place = lax.axis_index("row"), lax.axis_index("depth"), lax.axis_index("col")
    near, far = pl.ds(0, height // 2), pl.ds(height // 2, height // 2)
    screens = (near_cos, near_sin, far_cos, far_sin)
    row_matrix = row_ref[...]
    window = min(3, blocks)
    window_start = jnp.clip(own_place - 1, 0, blocks - window)
    own_in_window = own_place - window_start
    edges = (even_edge, odd_edge)

    def far_screens(slice_index):
        bits = slice_index ^ own_section
        for col in range(blocks):
            held = col ^ own_place
            angle = jnp.where(bits == 0, far_own[held, 0], far_rest[held, jnp.maximum(bits - 1, 0)])
            far_cos[slice_index, col], far_sin[slice_index, col] = cos_sin(angle)

    for edge_ref in edges:
        clear_edge(edge_ref, 0, False)
        clear_edge(edge_ref, blocks - 1, True)
    far_cos[count] = jnp.ones(far_cos.shape[1:], jnp.float32)
    far_sin[count] = jnp.zeros(far_cos.shape[1:], jnp.float32)
    far_screens(0)

    waves = [(wave_ref[place, 0], wave_ref[place, 1]) for place in range(blocks)]
    for tick in range(count):
        entering = (wave_ref if tick == 0 else kept_ref)[own_place]
        moved_ref[tick, 0], moved_ref[tick, 1] = turned(tick, own_place, screens, (entering[0], entering[1]))
        waves = advance(tick, 0, waves, screens, row_matrix, col_ref, edges[tick % 2])
        if tick + 1 < count:
            far_screens(tick + 1)
        keep(kept_ref, waves)
        left_ref[tick] = kept_ref[own_place]

    for edge_ref in edges:
        clear_edge(edge_ref, window - 1, True)
    waves = []
    for place in range(window):
        block = window_start + place
        real, imag = kept_ref[block, 0], kept_ref[block, 1]
        misfit = 2.0 * (real * real + imag * imag - measured_ref[block])
        waves.append((misfit * real, -misfit * imag))

    for tick in range(count - 1):
        waves = advance(count - tick, window_start, waves, screens, row_matrix, col_ref, edges[tick % 2])
        keep(kept_ref, waves)
        arrived = count - 1 - tick
        pulled = kept_ref[own_in_window]
        grad_ref[arrived] = -(pulled[1] * moved_ref[arrived, 0] + pulled[0] * moved_ref[arrived, 1])

    left, right = jnp.maximum(own_place - 1, 0), jnp.minimum(own_place + 1, blocks - 1)
    lane = lax.broadcasted_iota(jnp.int32, (2 * height, LANES), 1)
    has_left, has_right = own_place > 0, own_place < blocks - 1

    def cells(block):
        wave = kept_ref[block - window_start]
        return jnp.concatenate(turned(1, block, screens, (wave[0], wave[1])), axis=0)

    edge_cells = jnp.where(
        lane < LANES // 2, jnp.where(has_right, cells(right), 0.0), jnp.where(has_left, cells(left), 0.0)
    )
    done = row_product(row_matrix, jnp.concatenate([cells(own_place), edge_cells], axis=1))
    lane = lax.broadcasted_iota(jnp.int32, (height, LANES), 1)
    between = (lane >= HALO) & (lane < LANES - HALO)
    highs, lows, edges = [], [], []
    for part in range(2):
        high, low, _ = three_parts(done[part * height : (part + 1) * height, :LANES])
        highs.append(high)
        lows.append(low)
        value = done[part * height : (part + 1) * height, LANES:]
        whole_high = value.astype(jnp.bfloat16).astype(jnp.float32)
        edge = jnp.where(between, pltpu.roll(value - whole_high, LANES // 2, 1), whole_high)
        edges.append(edge.astype(jnp.bfloat16))
    pulled = col_product(jnp.concatenate(highs + edges, axis=1), jnp.concatenate(lows, axis=1), col_ref)
    grad_ref[0] = -(pulled[:, LANES:] * moved_ref[0, 0] + pulled[:, :LANES] * moved_ref[0, 1])

    for target, row in ((mine_ref, near), (theirs_ref, far)):
        for part in range(2):
            target[0, part] = left_ref[own_section, part, row]
        target[0, 2] = grad_ref[own_section, row]


def finish_kernel(mine_ref, received_ref, grad_ref, exit_ref, total_ref, sems):
    core = lax.axis_index("row")
    copies = []
    for source, item in ((mine_ref, core), (received_ref, 1 - core)):
        copies.append(pltpu.make_async_copy(source.at[:, pl.ds(0, 2)], exit_ref.at[item], sems.at[len(copies)]))
    for copy in copies:
        copy.start()
    total_ref[...] = mine_ref[:, 2] + received_ref[:, 2]
    copies.append(pltpu.make_async_copy(total_ref, grad_ref, sems.at[2]))
    copies[2].start()
    for copy in copies:
        copy.wait()


def spread(shard, axis, reach=None):
    size = lax.axis_size(axis)
    reach = size if reach is None else reach
    pieces = []
    for bits in range(1, size):
        pairs = [(i, i ^ bits) for i in range(size) if abs(i - (i ^ bits)) <= reach]
        pieces.append(lax.ppermute(shard, axis, pairs) if pairs else jnp.zeros_like(shard))
    return pieces


def swap_cores(value):
    return lax.ppermute(value, "row", [(0, 1), (1, 0)])


def whole_field_body(phase, tilt, intensity):
    _, tile_r, tile_c = phase.shape
    count, blocks = lax.axis_size("depth"), lax.axis_size("col")
    core = lax.axis_index("row")
    height = 2 * tile_r
    vmem = pl.BlockSpec(memory_space=pltpu.VMEM)
    smem = pl.BlockSpec(memory_space=pltpu.SMEM)
    hbm = pl.BlockSpec(memory_space=pl.ANY)

    def array(*shape):
        return jax.ShapeDtypeStruct(shape, jnp.float32)

    def params(mebibytes):
        return pltpu.CompilerParams(vmem_limit_bytes=mebibytes * 2**20)

    other_depths = spread(phase, "depth")
    other_depths[0], measured, slab = lax.optimization_barrier((other_depths[0], intensity, phase))
    other_depths = jnp.concatenate(other_depths, axis=0)
    packet = jnp.concatenate([slab, measured], axis=0)
    near_own = [packet]
    for bits in range(1, blocks):
        pairs = [(i, i ^ bits) for i in range(blocks)]
        close = [(i, j) for i, j in pairs if abs(i - j) <= 1]
        if close:
            near_own.append(lax.ppermute(packet, "col", close))
        else:
            further = [(i, j) for i, j in pairs if abs(i - j) <= 2]
            arrived = lax.ppermute(slab, "col", further) if further else jnp.zeros_like(slab)
            near_own.append(jnp.concatenate([arrived, jnp.zeros_like(measured)], axis=0))
    near_own = jnp.stack(near_own)
    arriving = spread(other_depths, "col", 2)
    row_all, col_all = jnp.asarray(row_constant(height)), jnp.asarray(col_constant())
    arriving[2], near_own, row_all, col_all = lax.optimization_barrier((arriving[2], near_own, row_all, col_all))
    row_matrix, col_matrix = pl.pallas_call(
        load_kernel,
        out_shape=(
            jax.ShapeDtypeStruct(row_all.shape[1:], row_all.dtype),
            jax.ShapeDtypeStruct(col_all.shape, col_all.dtype),
        ),
        in_specs=[hbm, hbm],
        out_specs=(vmem, vmem),
        scratch_shapes=[pltpu.SemaphoreType.DMA((2,))],
        compiler_params=params(2),
        cost_estimate=pl.CostEstimate(flops=10**8, bytes_accessed=2**20, transcendentals=0),
    )(row_all, col_all)
    arriving[1], row_matrix, col_matrix = lax.optimization_barrier((arriving[1], row_matrix, col_matrix))
    near_rest = jnp.stack([other_depths] + arriving)
    wanted = lax.dynamic_slice_in_dim(near_own, 2 - core, 1, 1)
    far_own = swap_cores(jnp.concatenate([near_own[:, :1], wanted], axis=1))
    far_rest = swap_cores(near_rest)

    half_screens = (count + 1, blocks, tile_r, tile_c)
    field = (blocks, 2, height, tile_c)
    wave, measured, own_cos, own_sin = pl.pallas_call(
        first_kernel,
        out_shape=(array(*field), array(blocks, height, tile_c)) + (array(blocks, tile_r, tile_c),) * 2,
        in_specs=[smem, vmem, vmem],
        out_specs=(vmem,) * 4,
        compiler_params=params(8),
        cost_estimate=pl.CostEstimate(flops=2 * 10**9, bytes_accessed=2**20, transcendentals=0),
    )(tilt, near_own, far_own)
    near_cos, near_sin = pl.pallas_call(
        second_kernel,
        out_shape=(array(*half_screens),) * 2,
        in_specs=[vmem] * 3,
        out_specs=(vmem,) * 2,
        compiler_params=params(8),
        cost_estimate=pl.CostEstimate(flops=5 * 10**8, bytes_accessed=2**20, transcendentals=0),
    )(near_rest, own_cos, own_sin)
    mine, theirs = pl.pallas_call(
        wave_kernel,
        out_shape=(array(1, 3, tile_r, tile_c),) * 2,
        in_specs=[vmem] * 8,
        out_specs=(vmem,) * 2,
        scratch_shapes=[pltpu.VMEM(half_screens, jnp.float32)] * 2
        + [pltpu.VMEM(field, jnp.float32)]
        + [pltpu.VMEM((count, 2, height, tile_c), jnp.float32)] * 2
        + [pltpu.VMEM((count, height, tile_c), jnp.float32)]
        + [pltpu.VMEM((blocks, height, 2 * LANES), jnp.bfloat16)] * 2,
        compiler_params=params(24),
    )(
        wave, near_cos, near_sin, measured, far_own, far_rest,
        row_matrix, col_matrix,
    )
    return pl.pallas_call(
        finish_kernel,
        out_shape=(array(*phase.shape), array(2, 1, 2, tile_r, tile_c)),
        in_specs=[vmem, vmem],
        out_specs=(hbm, hbm),
        scratch_shapes=[pltpu.VMEM(phase.shape, jnp.float32), pltpu.SemaphoreType.DMA((3,))],
        compiler_params=params(4),
    )(mine, swap_cores(theirs))


def extended_2(cells, sides, width):
    for axis, dim in sides:
        count = lax.axis_size(axis)
        ends = count - 1
        head = lax.slice_in_dim(cells, 0, width, axis=dim)
        tail = lax.slice_in_dim(cells, cells.shape[dim] - width, cells.shape[dim], axis=dim)
        cells = jnp.concatenate(
            [
                lax.ppermute(tail, axis, [(i, (i + 1) % count) for i in range(ends)]),
                cells,
                lax.ppermute(head, axis, [((i + 1) % count, i) for i in range(ends)]),
            ],
            axis=dim,
        )
    return cells


def from_behind(value, axis, steps):
    count = lax.axis_size(axis)
    leading, last = (max(0, -steps), min(count, count - steps))
    return lax.ppermute(value, axis, [(source, source + steps) for source in range(leading, last)])


def band_matrix(block_size, margin, fresnel, adjoint):
    shape_full = (block_size, block_size + 2 * margin)
    out_idx = lax.broadcasted_iota(jnp.int32, shape_full, 0)
    in_idx = lax.broadcasted_iota(jnp.int32, shape_full, 1)
    offset = (out_idx + margin - in_idx).astype(jnp.float32)
    inside = jnp.abs(offset) <= margin
    taper_dist = jnp.maximum(jnp.abs(offset) - 0.5 * margin, 0.0)
    profile = jnp.cos(jnp.pi * taper_dist / (margin + 2.0))
    weight = profile * profile / math.sqrt(fresnel)
    phase_angle = jnp.pi * offset * offset / fresnel
    real_part = jnp.where(inside, jnp.cos(phase_angle) * weight, 0.0)
    imag_part = jnp.where(inside, jnp.sin(phase_angle) * weight, 0.0)
    if adjoint:
        imag_part = -imag_part
    upper = jnp.stack([real_part, -imag_part])
    lower = jnp.stack([imag_part, real_part])
    return jnp.stack([upper, lower])


def along_rows(extended, matrix):
    pieces = [jnp.einsum("pqij,gqjc->gpic", matrix, extended, precision=lax.Precision.HIGHEST)]
    return jnp.concatenate(pieces, axis=2)


def along_cols(extended, matrix, margin):
    block_size = matrix.shape[2]
    extent = extended.shape[3] - 2 * margin
    pieces = []
    for block_start in range(0, extent, block_size):
        window = extended[:, :, :, block_start : block_start + block_size + 2 * margin]
        pieces.append(
            jnp.einsum("pqij,gqrj->gpri", matrix, window, precision=lax.Precision.HIGHEST)
        )
    return jnp.concatenate(pieces, axis=3)


def propagate(current, row_matrix, col_matrix):
    with_rows = extended_2(current, (("row", 2),), HALO)
    row_done = along_rows(with_rows, row_matrix)
    with_cols = extended_2(row_done, (("col", 3),), HALO)
    return along_cols(with_cols, col_matrix, HALO)


def transmit(screen, current, adjoint):
    screen_re = screen[0][None]
    screen_im = screen[1][None]
    if adjoint:
        screen_im = -screen_im
    real_part = screen_re * current[:, 0] - screen_im * current[:, 1]
    imag_part = screen_re * current[:, 1] + screen_im * current[:, 0]
    return jnp.stack([real_part, imag_part], axis=1)


def store_item(store, current, first_item, slice_index, active):
    begin = (first_item, jnp.int32(slice_index), jnp.int32(0), jnp.int32(0), jnp.int32(0))
    sizes_now = (current.shape[0], 1) + current.shape[1:]
    previous = lax.dynamic_slice(store, begin, sizes_now)
    fresh = jnp.where(active, current[:, None], previous)
    return lax.dynamic_update_slice(store, fresh, begin)


def staged_body(phase, tilt, intensity):
    slices, tile_r, tile_c = phase.shape
    batch_size = tilt.shape[0]
    sections = lax.axis_size("depth")
    section_index = lax.axis_index("depth")
    group_size = 1
    groups = batch_size // group_size
    tick_count = sections + groups - 1
    block_r = 64
    block_c = 128
    fwd_rows = band_matrix(block_r, HALO, FRESNEL, False)
    fwd_cols = band_matrix(block_c, HALO, FRESNEL, False)
    adj_rows = band_matrix(block_r, HALO, FRESNEL, True)
    adj_cols = band_matrix(block_c, HALO, FRESNEL, True)
    row_pos = (
        lax.axis_index("row") * tile_r + lax.broadcasted_iota(jnp.int32, (tile_r, tile_c), 0)
    ).astype(jnp.float32)
    col_pos = (
        lax.axis_index("col") * tile_c + lax.broadcasted_iota(jnp.int32, (tile_r, tile_c), 1)
    ).astype(jnp.float32)
    height = float(tile_r * lax.axis_size("row"))
    width_all = float(tile_c * lax.axis_size("col"))
    tilt_f = tilt.astype(jnp.float32)
    phase_angle = (
        2.0
        * jnp.pi
        * (
            tilt_f[:, 0, None, None] * row_pos / height
            + tilt_f[:, 1, None, None] * col_pos / width_all
        )
    )
    incident = jnp.stack([jnp.cos(phase_angle), jnp.sin(phase_angle)], axis=1)
    screens = jnp.stack([jnp.cos(phase), jnp.sin(phase)], axis=1)

    def forward_tick(tick_now, carry):
        incoming, entering, leaving = carry
        group_index = tick_now - section_index
        active = (group_index >= 0) & (group_index < groups)
        first_item = jnp.clip(group_index, 0, groups - 1) * group_size
        current = jnp.where(
            section_index == 0,
            lax.dynamic_slice_in_dim(incident, first_item, group_size, 0),
            incoming,
        )
        entering = store_item(entering, current, first_item, 0, active)
        current = propagate(transmit(screens[0], current, False), fwd_rows, fwd_cols)
        leaving = store_item(leaving, current, first_item, 0, active)
        incoming = from_behind(current, "depth", 1)
        return (incoming, entering, leaving)

    store_zero = jnp.zeros((batch_size, slices, 2, tile_r, tile_c), jnp.float32)
    start_wave = jnp.zeros((group_size, 2, tile_r, tile_c), jnp.float32)
    _, entering, leaving = lax.fori_loop(
        0, tick_count, forward_tick, (start_wave, store_zero, store_zero)
    )
    final_wave = leaving[:, slices - 1]
    misfit = final_wave[:, 0] * final_wave[:, 0] + final_wave[:, 1] * final_wave[:, 1] - intensity
    seed_adjoint = 2.0 * misfit[:, None] * final_wave

    def backward_tick(tick_now, carry):
        incoming, gradient = carry
        group_index = tick_now - (sections - 1 - section_index)
        active = (group_index >= 0) & (group_index < groups)
        first_item = jnp.clip(group_index, 0, groups - 1) * group_size
        adjoint_wave = jnp.where(
            section_index == sections - 1,
            lax.dynamic_slice_in_dim(seed_adjoint, first_item, group_size, 0),
            incoming,
        )
        for slice_index in reversed(range(slices)):
            pulled = propagate(adjoint_wave, adj_rows, adj_cols)
            arrived = lax.dynamic_slice_in_dim(entering[:, slice_index], first_item, group_size, 0)
            moved = transmit(screens[slice_index], arrived, False)
            contribution = jnp.sum(pulled[:, 1] * moved[:, 0] - pulled[:, 0] * moved[:, 1], axis=0)
            gradient = gradient.at[slice_index].add(jnp.where(active, contribution, 0.0))
            adjoint_wave = transmit(screens[slice_index], pulled, True)
        incoming = from_behind(adjoint_wave, "depth", -1)
        return (incoming, gradient)

    grad_zero = jnp.zeros((slices, tile_r, tile_c), jnp.float32)
    _, gradient = lax.fori_loop(0, tick_count, backward_tick, (start_wave, grad_zero))
    return (gradient, leaving)


def fits_whole(phase_shape, batch, mesh):
    slices, height, width = phase_shape
    rows, cols, sections = mesh.shape["row"], mesh.shape["col"], mesh.shape["depth"]
    return (
        4 * height * width * (slices + batch) <= GATHER_BUDGET
        and batch == rows == 2
        and slices == sections
        and sections & (sections - 1) == 0
        and cols & (cols - 1) == 0
        and height == LANES
        and width == cols * LANES
        and cols > 1
        and sections > 1
        and sections * HALO <= LANES
    )


def solution(mesh):
    placed = (P("depth", "row", "col"), P(), P(None, "row", "col"))

    def run(phase, tilt, intensity):
        if fits_whole(phase.shape, tilt.shape[0], mesh):
            body = whole_field_body
        else:
            body = staged_body
        return jax.shard_map(
            body,
            mesh=mesh,
            in_specs=placed,
            out_specs=(P("depth", "row", "col"), P(None, "depth", None, "row", "col")),
            check_vma=False,
        )(phase, tilt, intensity)

    return run
```

```python
import math

import jax
import jax.numpy as jnp
import numpy as np
from jax import lax
from jax.experimental import pallas as pl
from jax.experimental.pallas import tpu as pltpu
from jax.sharding import PartitionSpec as P

HALO = 32
FRESNEL = 64
LANES = 128
GATHER_BUDGET = 4 * 2**20
SIN = (
    0.9999999980536763,
    -0.1666666530009577,
    0.008333305907073658,
    -0.00019838908256358006,
    2.745822627876341e-06,
    -2.3043562782810933e-08,
)
COS = (
    0.9999999961345007,
    -0.4999999301617528,
    0.04166646215023687,
    -0.0013886696163545999,
    2.4695045482778703e-05,
    -2.5154931690000354e-07,
)


def horner(coefficients, square):
    total = jnp.full_like(square, coefficients[-1])
    for coefficient in coefficients[-2::-1]:
        total = total * square + coefficient
    return total


def cos_sin(angle):
    square = angle * angle
    return horner(COS, square), horner(SIN, square) * angle


def turn(fraction):
    half_cos, half_sin = cos_sin(fraction * math.pi)
    return half_cos * half_cos - half_sin * half_sin, 2.0 * half_cos * half_sin


def halves(value):
    high = value.astype(jnp.bfloat16)
    return high, (value - high.astype(jnp.float32)).astype(jnp.bfloat16)


def np_halves(matrix):
    high = matrix.astype(jnp.bfloat16)
    return high, (matrix - high.astype(np.float64)).astype(jnp.bfloat16)


def np_taps():
    offset = np.arange(-HALO, HALO + 1, dtype=np.float64)
    taper = np.maximum(np.abs(offset) - 0.5 * HALO, 0.0)
    weight = np.cos(np.pi * taper / (HALO + 2.0)) ** 2 / math.sqrt(FRESNEL)
    return weight * np.exp(1j * np.pi * offset * offset / FRESNEL)


def np_band(out_pos, in_pos):
    offset = out_pos[:, None] - in_pos[None, :]
    inside = np.abs(offset) <= HALO
    return np.where(inside, np_taps()[np.clip(offset, -HALO, HALO) + HALO], 0.0)


def row_constant(height):
    matrices = []
    for core in range(2):
        pos = (np.arange(height) + core * (height // 2)) % height
        band = np_band(pos, pos)
        whole = np.block([[band.real, -band.imag], [band.imag, band.real]])
        matrices.append(np.concatenate(np_halves(whole), axis=1))
    return np.stack(matrices)


def col_constant():
    lane = np.arange(LANES)
    turned = np.where((lane >= HALO) & (lane < LANES - HALO), lane ^ (LANES // 2), lane)
    edge_pos = np.where(turned < LANES // 2, turned + LANES, turned - LANES)
    parts = []
    for position in (lane, edge_pos):
        band = np_band(lane, position).T
        parts.append(np.block([[band.real, band.imag], [-band.imag, band.real]]))
    return np.concatenate(np_halves(np.concatenate(parts, axis=0)), axis=1)


def both_rows(near_ref, far_ref, where):
    return jnp.concatenate([near_ref[where], far_ref[where]], axis=0)


def turned(slice_index, block, screens, wave):
    near_cos, near_sin, far_cos, far_sin = screens
    cos = both_rows(near_cos, far_cos, (slice_index, block))
    sin = both_rows(near_sin, far_sin, (slice_index, block))
    real, imag = wave
    return cos * real - sin * imag, cos * imag + sin * real


def row_product(row_matrix, columns):
    high, low = halves(columns)
    whole, width = columns.shape
    wide = jnp.dot(
        row_matrix[:, :whole], jnp.concatenate([high, low], axis=1), preferred_element_type=jnp.float32
    )
    rest = jnp.dot(row_matrix[:, whole:], high, preferred_element_type=jnp.float32)
    return wide[:, :width] + wide[:, width:] + rest


def col_product(high, low, col_ref):
    wide = jnp.dot(high, col_ref[...], preferred_element_type=jnp.float32)
    rest = jnp.dot(low, col_ref[: 2 * LANES, : 2 * LANES], preferred_element_type=jnp.float32)
    return wide[:, : 2 * LANES] + wide[:, 2 * LANES :] + rest


def three_parts(value):
    high = value.astype(jnp.bfloat16)
    rest = value - high.astype(jnp.float32)
    return high, rest.astype(jnp.bfloat16), pltpu.roll(rest, LANES // 2, 1).astype(jnp.bfloat16)


def advance(slice_index, start, waves, screens, row_matrix, col_ref, edge_ref):
    size, height = len(waves), waves[0][0].shape[0]
    chunks = [range(place, min(place + 2, size)) for place in range(0, size, 2)]
    highs, lows = [], []
    for chunk in chunks:
        columns = [
            jnp.concatenate(turned(slice_index, start + place, screens, waves[place]), axis=0) for place in chunk
        ]
        done = row_product(row_matrix, jnp.concatenate(columns, axis=1))
        for sub, place in enumerate(chunk):
            own_high, own_low = [], []
            for part in range(2):
                value = done[part * height : (part + 1) * height, sub * LANES : (sub + 1) * LANES]
                high, low, swung = three_parts(value)
                own_high.append(high)
                own_low.append(low)
                edge = part * LANES
                if place > 0:
                    edge_ref[place - 1, :, pl.ds(edge, HALO)] = high[:, :HALO]
                    edge_ref[place - 1, :, pl.ds(edge + 2 * HALO, HALO)] = swung[:, 2 * HALO : 3 * HALO]
                if place < size - 1:
                    edge_ref[place + 1, :, pl.ds(edge + 3 * HALO, HALO)] = high[:, 3 * HALO :]
                    edge_ref[place + 1, :, pl.ds(edge + HALO, HALO)] = swung[:, HALO : 2 * HALO]
            highs.append(jnp.concatenate(own_high, axis=1))
            lows.append(jnp.concatenate(own_low, axis=1))
    results = []
    for chunk in chunks:
        rows = len(chunk) * height
        edges = edge_ref[pl.ds(chunk[0], len(chunk))].reshape(rows, 2 * LANES)
        own = jnp.concatenate([highs[place] for place in chunk], axis=0)
        total = col_product(
            jnp.concatenate([own, edges], axis=1),
            jnp.concatenate([lows[place] for place in chunk], axis=0),
            col_ref,
        )
        for sub in range(len(chunk)):
            block = total[sub * height : (sub + 1) * height]
            results.append((block[:, :LANES], block[:, LANES:]))
    return results


def clear_edge(edge_ref, place, right):
    for part in range(2):
        for begin in (0, 2 * HALO) if right else (HALO, 3 * HALO):
            cells = pl.ds(part * LANES + begin, HALO)
            edge_ref[place, :, cells] = jnp.zeros((edge_ref.shape[1], HALO), edge_ref.dtype)


def keep(wave_ref, waves):
    for place, wave in enumerate(waves):
        wave_ref[place, 0], wave_ref[place, 1] = wave


def load_kernel(tilt_ref, row_from, col_from, row_to, col_to, wave_ref, sems):
    blocks, _, height, _ = wave_ref.shape
    core = lax.axis_index("row")
    copies = [
        pltpu.make_async_copy(row_from.at[core], row_to, sems.at[0]),
        pltpu.make_async_copy(col_from, col_to, sems.at[1]),
    ]
    for copy in copies:
        copy.start()

    def cycles(number, position, extent):
        fraction = (number * position).astype(jnp.float32) / extent
        return turn(fraction - jnp.round(fraction))

    row = lax.broadcasted_iota(jnp.int32, (height, LANES), 0) + core * (height // 2)
    row = jnp.where(row >= height, row - height, row)
    row_cos, row_sin = cycles(tilt_ref[core, 0], row, float(height))
    for block in range(blocks):
        col_cos, col_sin = cycles(
            tilt_ref[core, 1],
            lax.broadcasted_iota(jnp.int32, (8, LANES), 1) + block * LANES,
            float(blocks * LANES),
        )
        col_cos, col_sin = col_cos[:1], col_sin[:1]
        wave_ref[block, 0] = row_cos * col_cos - row_sin * col_sin
        wave_ref[block, 1] = row_sin * col_cos + row_cos * col_sin
    for copy in copies:
        copy.wait()


def first_kernel(near_own, far_own, measured_ref, cos_ref, sin_ref):
    core, own_place = lax.axis_index("row"), lax.axis_index("col")
    for col in range(measured_ref.shape[0]):
        held = col ^ own_place
        measured_ref[col] = jnp.concatenate([near_own[held, 1 + core], far_own[held, 1]], axis=0)
        cos_ref[col], sin_ref[col] = cos_sin(near_own[held, 0])


def second_kernel(near_rest, own_cos, own_sin, cos_ref, sin_ref):
    blocks = own_cos.shape[0]
    count = cos_ref.shape[0] - 1
    own_section, own_place = lax.axis_index("depth"), lax.axis_index("col")

    def screens(col, carry):
        held = col ^ own_place
        cos_ref[own_section, col], sin_ref[own_section, col] = own_cos[col], own_sin[col]
        for bits in range(1, count):
            cos_ref[bits ^ own_section, col], sin_ref[bits ^ own_section, col] = cos_sin(near_rest[held, bits - 1])
        return carry

    lax.fori_loop(0, blocks, screens, 0)
    cos_ref[count] = jnp.ones(cos_ref.shape[1:], jnp.float32)
    sin_ref[count] = jnp.zeros(cos_ref.shape[1:], jnp.float32)


def wave_kernel(
    wave_ref, near_cos, near_sin, measured_ref, far_own, far_rest, row_ref, col_ref,
    mine_ref, theirs_ref, far_cos, far_sin, kept_ref, moved_ref, left_ref, grad_ref, even_edge, odd_edge,
):
    blocks, _, height, _ = wave_ref.shape
    count = near_cos.shape[0] - 1
    core, own_section, own_place = lax.axis_index("row"), lax.axis_index("depth"), lax.axis_index("col")
    near, far = pl.ds(0, height // 2), pl.ds(height // 2, height // 2)
    screens = (near_cos, near_sin, far_cos, far_sin)
    row_matrix = row_ref[...]
    window = min(3, blocks)
    window_start = jnp.clip(own_place - 1, 0, blocks - window)
    own_in_window = own_place - window_start
    edges = (even_edge, odd_edge)

    def far_screens(slice_index):
        bits = slice_index ^ own_section
        for col in range(blocks):
            held = col ^ own_place
            angle = jnp.where(bits == 0, far_own[held, 0], far_rest[held, jnp.maximum(bits - 1, 0)])
            far_cos[slice_index, col], far_sin[slice_index, col] = cos_sin(angle)

    for edge_ref in edges:
        clear_edge(edge_ref, 0, False)
        clear_edge(edge_ref, blocks - 1, True)
    far_cos[count] = jnp.ones(far_cos.shape[1:], jnp.float32)
    far_sin[count] = jnp.zeros(far_cos.shape[1:], jnp.float32)
    far_screens(0)

    waves = [(wave_ref[place, 0], wave_ref[place, 1]) for place in range(blocks)]
    for tick in range(count):
        entering = (wave_ref if tick == 0 else kept_ref)[own_place]
        moved_ref[tick, 0], moved_ref[tick, 1] = turned(tick, own_place, screens, (entering[0], entering[1]))
        waves = advance(tick, 0, waves, screens, row_matrix, col_ref, edges[tick % 2])
        if tick + 1 < count:
            far_screens(tick + 1)
        keep(kept_ref, waves)
        left_ref[tick] = kept_ref[own_place]

    for edge_ref in edges:
        clear_edge(edge_ref, window - 1, True)
    waves = []
    for place in range(window):
        block = window_start + place
        real, imag = kept_ref[block, 0], kept_ref[block, 1]
        misfit = 2.0 * (real * real + imag * imag - measured_ref[block])
        waves.append((misfit * real, -misfit * imag))

    for tick in range(count - 1):
        waves = advance(count - tick, window_start, waves, screens, row_matrix, col_ref, edges[tick % 2])
        keep(kept_ref, waves)
        arrived = count - 1 - tick
        pulled = kept_ref[own_in_window]
        grad_ref[arrived] = -(pulled[1] * moved_ref[arrived, 0] + pulled[0] * moved_ref[arrived, 1])

    left, right = jnp.maximum(own_place - 1, 0), jnp.minimum(own_place + 1, blocks - 1)
    lane = lax.broadcasted_iota(jnp.int32, (2 * height, LANES), 1)
    has_left, has_right = own_place > 0, own_place < blocks - 1

    def cells(block):
        wave = kept_ref[block - window_start]
        return jnp.concatenate(turned(1, block, screens, (wave[0], wave[1])), axis=0)

    edge_cells = jnp.where(
        lane < LANES // 2, jnp.where(has_right, cells(right), 0.0), jnp.where(has_left, cells(left), 0.0)
    )
    done = row_product(row_matrix, jnp.concatenate([cells(own_place), edge_cells], axis=1))
    lane = lax.broadcasted_iota(jnp.int32, (height, LANES), 1)
    between = (lane >= HALO) & (lane < LANES - HALO)
    highs, lows, edges = [], [], []
    for part in range(2):
        high, low, _ = three_parts(done[part * height : (part + 1) * height, :LANES])
        highs.append(high)
        lows.append(low)
        value = done[part * height : (part + 1) * height, LANES:]
        whole_high = value.astype(jnp.bfloat16).astype(jnp.float32)
        edge = jnp.where(between, pltpu.roll(value - whole_high, LANES // 2, 1), whole_high)
        edges.append(edge.astype(jnp.bfloat16))
    pulled = col_product(jnp.concatenate(highs + edges, axis=1), jnp.concatenate(lows, axis=1), col_ref)
    grad_ref[0] = -(pulled[:, LANES:] * moved_ref[0, 0] + pulled[:, :LANES] * moved_ref[0, 1])

    for target, row in ((mine_ref, near), (theirs_ref, far)):
        for part in range(2):
            target[0, part] = left_ref[own_section, part, row]
        target[0, 2] = grad_ref[own_section, row]


def finish_kernel(mine_ref, received_ref, grad_ref, exit_ref, total_ref, sems):
    core = lax.axis_index("row")
    copies = []
    for source, item in ((mine_ref, core), (received_ref, 1 - core)):
        copies.append(pltpu.make_async_copy(source.at[:, pl.ds(0, 2)], exit_ref.at[item], sems.at[len(copies)]))
    for copy in copies:
        copy.start()
    total_ref[...] = mine_ref[:, 2] + received_ref[:, 2]
    copies.append(pltpu.make_async_copy(total_ref, grad_ref, sems.at[2]))
    copies[2].start()
    for copy in copies:
        copy.wait()


def spread(shard, axis, reach=None):
    size = lax.axis_size(axis)
    reach = size if reach is None else reach
    pieces = []
    for bits in range(1, size):
        pairs = [(i, i ^ bits) for i in range(size) if abs(i - (i ^ bits)) <= reach]
        pieces.append(lax.ppermute(shard, axis, pairs) if pairs else jnp.zeros_like(shard))
    return pieces


def swap_cores(value):
    return lax.ppermute(value, "row", [(0, 1), (1, 0)])


def whole_field_body(phase, tilt, intensity):
    _, tile_r, tile_c = phase.shape
    count, blocks = lax.axis_size("depth"), lax.axis_size("col")
    core = lax.axis_index("row")
    height = 2 * tile_r
    vmem = pl.BlockSpec(memory_space=pltpu.VMEM)
    smem = pl.BlockSpec(memory_space=pltpu.SMEM)
    hbm = pl.BlockSpec(memory_space=pl.ANY)

    def array(*shape):
        return jax.ShapeDtypeStruct(shape, jnp.float32)

    def params(mebibytes):
        return pltpu.CompilerParams(vmem_limit_bytes=mebibytes * 2**20)

    other_depths = spread(phase, "depth")
    other_depths[0], measured, slab = lax.optimization_barrier((other_depths[0], intensity, phase))
    other_depths = jnp.concatenate(other_depths, axis=0)
    packet = jnp.concatenate([slab, measured], axis=0)
    near_own = [packet]
    for bits in range(1, blocks):
        pairs = [(i, i ^ bits) for i in range(blocks)]
        close = [(i, j) for i, j in pairs if abs(i - j) <= 1]
        if close:
            near_own.append(lax.ppermute(packet, "col", close))
        else:
            further = [(i, j) for i, j in pairs if abs(i - j) <= 2]
            arrived = lax.ppermute(slab, "col", further) if further else jnp.zeros_like(slab)
            near_own.append(jnp.concatenate([arrived, jnp.zeros_like(measured)], axis=0))
    near_own = jnp.stack(near_own)
    arriving = spread(other_depths, "col", 2)
    row_all, col_all = jnp.asarray(row_constant(height)), jnp.asarray(col_constant())
    arriving[2], near_own, row_all, col_all = lax.optimization_barrier((arriving[2], near_own, row_all, col_all))
    half_screens = (count + 1, blocks, tile_r, tile_c)
    field = (blocks, 2, height, tile_c)
    row_matrix, col_matrix, wave = pl.pallas_call(
        load_kernel,
        out_shape=(
            jax.ShapeDtypeStruct(row_all.shape[1:], row_all.dtype),
            jax.ShapeDtypeStruct(col_all.shape, col_all.dtype),
            array(*field),
        ),
        in_specs=[smem, hbm, hbm],
        out_specs=(vmem, vmem, vmem),
        scratch_shapes=[pltpu.SemaphoreType.DMA((2,))],
        compiler_params=params(4),
        cost_estimate=pl.CostEstimate(flops=10**8, bytes_accessed=2**20, transcendentals=0),
    )(tilt, row_all, col_all)
    arriving[1], row_matrix, col_matrix = lax.optimization_barrier((arriving[1], row_matrix, col_matrix))
    near_rest = jnp.stack([other_depths] + arriving)
    wanted = lax.dynamic_slice_in_dim(near_own, 2 - core, 1, 1)
    far_own = swap_cores(jnp.concatenate([near_own[:, :1], wanted], axis=1))
    far_rest = swap_cores(near_rest)

    measured, own_cos, own_sin = pl.pallas_call(
        first_kernel,
        out_shape=(array(blocks, height, tile_c),) + (array(blocks, tile_r, tile_c),) * 2,
        in_specs=[vmem, vmem],
        out_specs=(vmem,) * 3,
        compiler_params=params(8),
        cost_estimate=pl.CostEstimate(flops=3 * 10**9, bytes_accessed=2**20, transcendentals=0),
    )(near_own, far_own)
    near_cos, near_sin = pl.pallas_call(
        second_kernel,
        out_shape=(array(*half_screens),) * 2,
        in_specs=[vmem] * 3,
        out_specs=(vmem,) * 2,
        compiler_params=params(8),
        cost_estimate=pl.CostEstimate(flops=5 * 10**8, bytes_accessed=2**20, transcendentals=0),
    )(near_rest, own_cos, own_sin)
    mine, theirs = pl.pallas_call(
        wave_kernel,
        out_shape=(array(1, 3, tile_r, tile_c),) * 2,
        in_specs=[vmem] * 8,
        out_specs=(vmem,) * 2,
        scratch_shapes=[pltpu.VMEM(half_screens, jnp.float32)] * 2
        + [pltpu.VMEM(field, jnp.float32)]
        + [pltpu.VMEM((count, 2, height, tile_c), jnp.float32)] * 2
        + [pltpu.VMEM((count, height, tile_c), jnp.float32)]
        + [pltpu.VMEM((blocks, height, 2 * LANES), jnp.bfloat16)] * 2,
        compiler_params=params(24),
    )(
        wave, near_cos, near_sin, measured, far_own, far_rest,
        row_matrix, col_matrix,
    )
    return pl.pallas_call(
        finish_kernel,
        out_shape=(array(*phase.shape), array(2, 1, 2, tile_r, tile_c)),
        in_specs=[vmem, vmem],
        out_specs=(hbm, hbm),
        scratch_shapes=[pltpu.VMEM(phase.shape, jnp.float32), pltpu.SemaphoreType.DMA((3,))],
        compiler_params=params(4),
    )(mine, swap_cores(theirs))


def extended_2(cells, sides, width):
    for axis, dim in sides:
        count = lax.axis_size(axis)
        ends = count - 1
        head = lax.slice_in_dim(cells, 0, width, axis=dim)
        tail = lax.slice_in_dim(cells, cells.shape[dim] - width, cells.shape[dim], axis=dim)
        cells = jnp.concatenate(
            [
                lax.ppermute(tail, axis, [(i, (i + 1) % count) for i in range(ends)]),
                cells,
                lax.ppermute(head, axis, [((i + 1) % count, i) for i in range(ends)]),
            ],
            axis=dim,
        )
    return cells


def from_behind(value, axis, steps):
    count = lax.axis_size(axis)
    leading, last = (max(0, -steps), min(count, count - steps))
    return lax.ppermute(value, axis, [(source, source + steps) for source in range(leading, last)])


def band_matrix(block_size, margin, fresnel, adjoint):
    shape_full = (block_size, block_size + 2 * margin)
    out_idx = lax.broadcasted_iota(jnp.int32, shape_full, 0)
    in_idx = lax.broadcasted_iota(jnp.int32, shape_full, 1)
    offset = (out_idx + margin - in_idx).astype(jnp.float32)
    inside = jnp.abs(offset) <= margin
    taper_dist = jnp.maximum(jnp.abs(offset) - 0.5 * margin, 0.0)
    profile = jnp.cos(jnp.pi * taper_dist / (margin + 2.0))
    weight = profile * profile / math.sqrt(fresnel)
    phase_angle = jnp.pi * offset * offset / fresnel
    real_part = jnp.where(inside, jnp.cos(phase_angle) * weight, 0.0)
    imag_part = jnp.where(inside, jnp.sin(phase_angle) * weight, 0.0)
    if adjoint:
        imag_part = -imag_part
    upper = jnp.stack([real_part, -imag_part])
    lower = jnp.stack([imag_part, real_part])
    return jnp.stack([upper, lower])


def along_rows(extended, matrix):
    pieces = [jnp.einsum("pqij,gqjc->gpic", matrix, extended, precision=lax.Precision.HIGHEST)]
    return jnp.concatenate(pieces, axis=2)


def along_cols(extended, matrix, margin):
    block_size = matrix.shape[2]
    extent = extended.shape[3] - 2 * margin
    pieces = []
    for block_start in range(0, extent, block_size):
        window = extended[:, :, :, block_start : block_start + block_size + 2 * margin]
        pieces.append(
            jnp.einsum("pqij,gqrj->gpri", matrix, window, precision=lax.Precision.HIGHEST)
        )
    return jnp.concatenate(pieces, axis=3)


def propagate(current, row_matrix, col_matrix):
    with_rows = extended_2(current, (("row", 2),), HALO)
    row_done = along_rows(with_rows, row_matrix)
    with_cols = extended_2(row_done, (("col", 3),), HALO)
    return along_cols(with_cols, col_matrix, HALO)


def transmit(screen, current, adjoint):
    screen_re = screen[0][None]
    screen_im = screen[1][None]
    if adjoint:
        screen_im = -screen_im
    real_part = screen_re * current[:, 0] - screen_im * current[:, 1]
    imag_part = screen_re * current[:, 1] + screen_im * current[:, 0]
    return jnp.stack([real_part, imag_part], axis=1)


def store_item(store, current, first_item, slice_index, active):
    begin = (first_item, jnp.int32(slice_index), jnp.int32(0), jnp.int32(0), jnp.int32(0))
    sizes_now = (current.shape[0], 1) + current.shape[1:]
    previous = lax.dynamic_slice(store, begin, sizes_now)
    fresh = jnp.where(active, current[:, None], previous)
    return lax.dynamic_update_slice(store, fresh, begin)


def staged_body(phase, tilt, intensity):
    slices, tile_r, tile_c = phase.shape
    batch_size = tilt.shape[0]
    sections = lax.axis_size("depth")
    section_index = lax.axis_index("depth")
    group_size = 1
    groups = batch_size // group_size
    tick_count = sections + groups - 1
    block_r = 64
    block_c = 128
    fwd_rows = band_matrix(block_r, HALO, FRESNEL, False)
    fwd_cols = band_matrix(block_c, HALO, FRESNEL, False)
    adj_rows = band_matrix(block_r, HALO, FRESNEL, True)
    adj_cols = band_matrix(block_c, HALO, FRESNEL, True)
    row_pos = (
        lax.axis_index("row") * tile_r + lax.broadcasted_iota(jnp.int32, (tile_r, tile_c), 0)
    ).astype(jnp.float32)
    col_pos = (
        lax.axis_index("col") * tile_c + lax.broadcasted_iota(jnp.int32, (tile_r, tile_c), 1)
    ).astype(jnp.float32)
    height = float(tile_r * lax.axis_size("row"))
    width_all = float(tile_c * lax.axis_size("col"))
    tilt_f = tilt.astype(jnp.float32)
    phase_angle = (
        2.0
        * jnp.pi
        * (
            tilt_f[:, 0, None, None] * row_pos / height
            + tilt_f[:, 1, None, None] * col_pos / width_all
        )
    )
    incident = jnp.stack([jnp.cos(phase_angle), jnp.sin(phase_angle)], axis=1)
    screens = jnp.stack([jnp.cos(phase), jnp.sin(phase)], axis=1)

    def forward_tick(tick_now, carry):
        incoming, entering, leaving = carry
        group_index = tick_now - section_index
        active = (group_index >= 0) & (group_index < groups)
        first_item = jnp.clip(group_index, 0, groups - 1) * group_size
        current = jnp.where(
            section_index == 0,
            lax.dynamic_slice_in_dim(incident, first_item, group_size, 0),
            incoming,
        )
        entering = store_item(entering, current, first_item, 0, active)
        current = propagate(transmit(screens[0], current, False), fwd_rows, fwd_cols)
        leaving = store_item(leaving, current, first_item, 0, active)
        incoming = from_behind(current, "depth", 1)
        return (incoming, entering, leaving)

    store_zero = jnp.zeros((batch_size, slices, 2, tile_r, tile_c), jnp.float32)
    start_wave = jnp.zeros((group_size, 2, tile_r, tile_c), jnp.float32)
    _, entering, leaving = lax.fori_loop(
        0, tick_count, forward_tick, (start_wave, store_zero, store_zero)
    )
    final_wave = leaving[:, slices - 1]
    misfit = final_wave[:, 0] * final_wave[:, 0] + final_wave[:, 1] * final_wave[:, 1] - intensity
    seed_adjoint = 2.0 * misfit[:, None] * final_wave

    def backward_tick(tick_now, carry):
        incoming, gradient = carry
        group_index = tick_now - (sections - 1 - section_index)
        active = (group_index >= 0) & (group_index < groups)
        first_item = jnp.clip(group_index, 0, groups - 1) * group_size
        adjoint_wave = jnp.where(
            section_index == sections - 1,
            lax.dynamic_slice_in_dim(seed_adjoint, first_item, group_size, 0),
            incoming,
        )
        for slice_index in reversed(range(slices)):
            pulled = propagate(adjoint_wave, adj_rows, adj_cols)
            arrived = lax.dynamic_slice_in_dim(entering[:, slice_index], first_item, group_size, 0)
            moved = transmit(screens[slice_index], arrived, False)
            contribution = jnp.sum(pulled[:, 1] * moved[:, 0] - pulled[:, 0] * moved[:, 1], axis=0)
            gradient = gradient.at[slice_index].add(jnp.where(active, contribution, 0.0))
            adjoint_wave = transmit(screens[slice_index], pulled, True)
        incoming = from_behind(adjoint_wave, "depth", -1)
        return (incoming, gradient)

    grad_zero = jnp.zeros((slices, tile_r, tile_c), jnp.float32)
    _, gradient = lax.fori_loop(0, tick_count, backward_tick, (start_wave, grad_zero))
    return (gradient, leaving)


def fits_whole(phase_shape, batch, mesh):
    slices, height, width = phase_shape
    rows, cols, sections = mesh.shape["row"], mesh.shape["col"], mesh.shape["depth"]
    return (
        4 * height * width * (slices + batch) <= GATHER_BUDGET
        and batch == rows == 2
        and slices == sections
        and sections & (sections - 1) == 0
        and cols & (cols - 1) == 0
        and height == LANES
        and width == cols * LANES
        and cols > 1
        and sections > 1
        and sections * HALO <= LANES
    )


def solution(mesh):
    placed = (P("depth", "row", "col"), P(), P(None, "row", "col"))

    def run(phase, tilt, intensity):
        if fits_whole(phase.shape, tilt.shape[0], mesh):
            body = whole_field_body
        else:
            body = staged_body
        return jax.shard_map(
            body,
            mesh=mesh,
            in_specs=placed,
            out_specs=(P("depth", "row", "col"), P(None, "depth", None, "row", "col")),
            check_vma=False,
        )(phase, tilt, intensity)

    return run
```

```python
import math

import jax
import jax.numpy as jnp
import numpy as np
from jax import lax
from jax.experimental import pallas as pl
from jax.experimental.pallas import tpu as pltpu
from jax.sharding import PartitionSpec as P

HALO = 32
FRESNEL = 64
LANES = 128
GATHER_BUDGET = 4 * 2**20
SIN = (
    0.9999999980536763,
    -0.1666666530009577,
    0.008333305907073658,
    -0.00019838908256358006,
    2.745822627876341e-06,
    -2.3043562782810933e-08,
)
COS = (
    0.9999999961345007,
    -0.4999999301617528,
    0.04166646215023687,
    -0.0013886696163545999,
    2.4695045482778703e-05,
    -2.5154931690000354e-07,
)


def horner(coefficients, square):
    total = jnp.full_like(square, coefficients[-1])
    for coefficient in coefficients[-2::-1]:
        total = total * square + coefficient
    return total


def cos_sin(angle):
    square = angle * angle
    return horner(COS, square), horner(SIN, square) * angle


def turn(fraction):
    half_cos, half_sin = cos_sin(fraction * math.pi)
    return half_cos * half_cos - half_sin * half_sin, 2.0 * half_cos * half_sin


def halves(value):
    high = value.astype(jnp.bfloat16)
    return high, (value - high.astype(jnp.float32)).astype(jnp.bfloat16)


def np_halves(matrix):
    high = matrix.astype(jnp.bfloat16)
    return high, (matrix - high.astype(np.float64)).astype(jnp.bfloat16)


def np_taps():
    offset = np.arange(-HALO, HALO + 1, dtype=np.float64)
    taper = np.maximum(np.abs(offset) - 0.5 * HALO, 0.0)
    weight = np.cos(np.pi * taper / (HALO + 2.0)) ** 2 / math.sqrt(FRESNEL)
    return weight * np.exp(1j * np.pi * offset * offset / FRESNEL)


def np_band(out_pos, in_pos):
    offset = out_pos[:, None] - in_pos[None, :]
    inside = np.abs(offset) <= HALO
    return np.where(inside, np_taps()[np.clip(offset, -HALO, HALO) + HALO], 0.0)


def row_constant(height):
    matrices = []
    for core in range(2):
        pos = (np.arange(height) + core * (height // 2)) % height
        band = np_band(pos, pos)
        whole = np.block([[band.real, -band.imag], [band.imag, band.real]])
        matrices.append(np.concatenate(np_halves(whole), axis=1))
    return np.stack(matrices)


def col_constant():
    lane = np.arange(LANES)
    turned = np.where((lane >= HALO) & (lane < LANES - HALO), lane ^ (LANES // 2), lane)
    edge_pos = np.where(turned < LANES // 2, turned + LANES, turned - LANES)
    parts = []
    for position in (lane, edge_pos):
        band = np_band(lane, position).T
        parts.append(np.block([[band.real, band.imag], [-band.imag, band.real]]))
    return np.concatenate(np_halves(np.concatenate(parts, axis=0)), axis=1)


def both_rows(near_ref, far_ref, where):
    return jnp.concatenate([near_ref[where], far_ref[where]], axis=0)


def turned(slice_index, block, screens, wave):
    near_cos, near_sin, far_cos, far_sin = screens
    cos = both_rows(near_cos, far_cos, (slice_index, block))
    sin = both_rows(near_sin, far_sin, (slice_index, block))
    real, imag = wave
    return cos * real - sin * imag, cos * imag + sin * real


def row_product(row_matrix, columns):
    high, low = halves(columns)
    whole, width = columns.shape
    wide = jnp.dot(
        row_matrix[:, :whole], jnp.concatenate([high, low], axis=1), preferred_element_type=jnp.float32
    )
    rest = jnp.dot(row_matrix[:, whole:], high, preferred_element_type=jnp.float32)
    return wide[:, :width] + wide[:, width:] + rest


def col_product(high, low, col_ref):
    wide = jnp.dot(high, col_ref[...], preferred_element_type=jnp.float32)
    rest = jnp.dot(low, col_ref[: 2 * LANES, : 2 * LANES], preferred_element_type=jnp.float32)
    return wide[:, : 2 * LANES] + wide[:, 2 * LANES :] + rest


def three_parts(value):
    high = value.astype(jnp.bfloat16)
    rest = value - high.astype(jnp.float32)
    return high, rest.astype(jnp.bfloat16), pltpu.roll(rest, LANES // 2, 1).astype(jnp.bfloat16)


def advance(slice_index, start, waves, screens, row_matrix, col_ref, edge_ref):
    size, height = len(waves), waves[0][0].shape[0]
    chunks = [range(place, min(place + 2, size)) for place in range(0, size, 2)]
    highs, lows = [], []
    for chunk in chunks:
        columns = [
            jnp.concatenate(turned(slice_index, start + place, screens, waves[place]), axis=0) for place in chunk
        ]
        done = row_product(row_matrix, jnp.concatenate(columns, axis=1))
        for sub, place in enumerate(chunk):
            own_high, own_low = [], []
            for part in range(2):
                value = done[part * height : (part + 1) * height, sub * LANES : (sub + 1) * LANES]
                high, low, swung = three_parts(value)
                own_high.append(high)
                own_low.append(low)
                edge = part * LANES
                if place > 0:
                    edge_ref[place - 1, :, pl.ds(edge, HALO)] = high[:, :HALO]
                    edge_ref[place - 1, :, pl.ds(edge + 2 * HALO, HALO)] = swung[:, 2 * HALO : 3 * HALO]
                if place < size - 1:
                    edge_ref[place + 1, :, pl.ds(edge + 3 * HALO, HALO)] = high[:, 3 * HALO :]
                    edge_ref[place + 1, :, pl.ds(edge + HALO, HALO)] = swung[:, HALO : 2 * HALO]
            highs.append(jnp.concatenate(own_high, axis=1))
            lows.append(jnp.concatenate(own_low, axis=1))
    results = []
    for chunk in chunks:
        rows = len(chunk) * height
        edges = edge_ref[pl.ds(chunk[0], len(chunk))].reshape(rows, 2 * LANES)
        own = jnp.concatenate([highs[place] for place in chunk], axis=0)
        total = col_product(
            jnp.concatenate([own, edges], axis=1),
            jnp.concatenate([lows[place] for place in chunk], axis=0),
            col_ref,
        )
        for sub in range(len(chunk)):
            block = total[sub * height : (sub + 1) * height]
            results.append((block[:, :LANES], block[:, LANES:]))
    return results


def clear_edge(edge_ref, place, right):
    for part in range(2):
        for begin in (0, 2 * HALO) if right else (HALO, 3 * HALO):
            cells = pl.ds(part * LANES + begin, HALO)
            edge_ref[place, :, cells] = jnp.zeros((edge_ref.shape[1], HALO), edge_ref.dtype)


def keep(wave_ref, waves):
    for place, wave in enumerate(waves):
        wave_ref[place, 0], wave_ref[place, 1] = wave


def load_kernel(tilt_ref, row_from, col_from, row_to, col_to, wave_ref, sems):
    blocks, _, height, _ = wave_ref.shape
    core = lax.axis_index("row")
    copies = [
        pltpu.make_async_copy(row_from.at[core], row_to, sems.at[0]),
        pltpu.make_async_copy(col_from, col_to, sems.at[1]),
    ]
    for copy in copies:
        copy.start()

    def cycles(number, position, extent):
        fraction = (number * position).astype(jnp.float32) / extent
        return turn(fraction - jnp.round(fraction))

    row = lax.broadcasted_iota(jnp.int32, (height, LANES), 0) + core * (height // 2)
    row = jnp.where(row >= height, row - height, row)
    row_cos, row_sin = cycles(tilt_ref[core, 0], row, float(height))
    for block in range(blocks):
        col_cos, col_sin = cycles(
            tilt_ref[core, 1],
            lax.broadcasted_iota(jnp.int32, (8, LANES), 1) + block * LANES,
            float(blocks * LANES),
        )
        col_cos, col_sin = col_cos[:1], col_sin[:1]
        wave_ref[block, 0] = row_cos * col_cos - row_sin * col_sin
        wave_ref[block, 1] = row_sin * col_cos + row_cos * col_sin
    for copy in copies:
        copy.wait()


def first_kernel(near_own, far_own, measured_ref, cos_ref, sin_ref):
    core, own_place = lax.axis_index("row"), lax.axis_index("col")
    for col in range(measured_ref.shape[0]):
        held = col ^ own_place
        measured_ref[col] = jnp.concatenate([near_own[held, 1 + core], far_own[held, 1]], axis=0)
        cos_ref[col], sin_ref[col] = cos_sin(near_own[held, 0])


def second_kernel(near_rest, own_cos, own_sin, cos_ref, sin_ref):
    blocks = own_cos.shape[0]
    count = cos_ref.shape[0] - 1
    own_section, own_place = lax.axis_index("depth"), lax.axis_index("col")

    def screens(col, carry):
        held = col ^ own_place
        cos_ref[own_section, col], sin_ref[own_section, col] = own_cos[col], own_sin[col]
        for bits in range(1, count):
            cos_ref[bits ^ own_section, col], sin_ref[bits ^ own_section, col] = cos_sin(near_rest[held, bits - 1])
        return carry

    lax.fori_loop(0, blocks, screens, 0)
    cos_ref[count] = jnp.ones(cos_ref.shape[1:], jnp.float32)
    sin_ref[count] = jnp.zeros(cos_ref.shape[1:], jnp.float32)


def wave_kernel(
    wave_ref, near_cos, near_sin, measured_ref, far_own, far_rest, row_ref, col_ref,
    mine_ref, theirs_ref, far_cos, far_sin, kept_ref, moved_ref, left_ref, grad_ref, even_edge, odd_edge,
):
    blocks, _, height, _ = wave_ref.shape
    count = near_cos.shape[0] - 1
    core, own_section, own_place = lax.axis_index("row"), lax.axis_index("depth"), lax.axis_index("col")
    near, far = pl.ds(0, height // 2), pl.ds(height // 2, height // 2)
    screens = (near_cos, near_sin, far_cos, far_sin)
    row_matrix = row_ref[...]
    window = min(3, blocks)
    window_start = jnp.clip(own_place - 1, 0, blocks - window)
    own_in_window = own_place - window_start
    edges = (even_edge, odd_edge)

    def far_screens(slice_index):
        bits = slice_index ^ own_section
        for col in range(blocks):
            held = col ^ own_place
            angle = jnp.where(bits == 0, far_own[held, 0], far_rest[held, jnp.maximum(bits - 1, 0)])
            far_cos[slice_index, col], far_sin[slice_index, col] = cos_sin(angle)

    for edge_ref in edges:
        clear_edge(edge_ref, 0, False)
        clear_edge(edge_ref, blocks - 1, True)
    far_cos[count] = jnp.ones(far_cos.shape[1:], jnp.float32)
    far_sin[count] = jnp.zeros(far_cos.shape[1:], jnp.float32)
    far_screens(0)

    waves = [(wave_ref[place, 0], wave_ref[place, 1]) for place in range(blocks)]
    for tick in range(count):
        entering = (wave_ref if tick == 0 else kept_ref)[own_place]
        moved_ref[tick, 0], moved_ref[tick, 1] = turned(tick, own_place, screens, (entering[0], entering[1]))
        waves = advance(tick, 0, waves, screens, row_matrix, col_ref, edges[tick % 2])
        if tick + 1 < count:
            far_screens(tick + 1)
        keep(kept_ref, waves)
        left_ref[tick] = kept_ref[own_place]

    for edge_ref in edges:
        clear_edge(edge_ref, window - 1, True)
    waves = []
    for place in range(window):
        block = window_start + place
        real, imag = kept_ref[block, 0], kept_ref[block, 1]
        misfit = 2.0 * (real * real + imag * imag - measured_ref[block])
        waves.append((misfit * real, -misfit * imag))

    for tick in range(count - 1):
        waves = advance(count - tick, window_start, waves, screens, row_matrix, col_ref, edges[tick % 2])
        keep(kept_ref, waves)
        arrived = count - 1 - tick
        pulled = kept_ref[own_in_window]
        grad_ref[arrived] = -(pulled[1] * moved_ref[arrived, 0] + pulled[0] * moved_ref[arrived, 1])

    left, right = jnp.maximum(own_place - 1, 0), jnp.minimum(own_place + 1, blocks - 1)
    lane = lax.broadcasted_iota(jnp.int32, (2 * height, LANES), 1)
    has_left, has_right = own_place > 0, own_place < blocks - 1

    def cells(block):
        wave = kept_ref[block - window_start]
        return jnp.concatenate(turned(1, block, screens, (wave[0], wave[1])), axis=0)

    edge_cells = jnp.where(
        lane < LANES // 2, jnp.where(has_right, cells(right), 0.0), jnp.where(has_left, cells(left), 0.0)
    )
    done = row_product(row_matrix, jnp.concatenate([cells(own_place), edge_cells], axis=1))
    lane = lax.broadcasted_iota(jnp.int32, (height, LANES), 1)
    between = (lane >= HALO) & (lane < LANES - HALO)
    highs, lows, edges = [], [], []
    for part in range(2):
        high, low, _ = three_parts(done[part * height : (part + 1) * height, :LANES])
        highs.append(high)
        lows.append(low)
        value = done[part * height : (part + 1) * height, LANES:]
        whole_high = value.astype(jnp.bfloat16).astype(jnp.float32)
        edge = jnp.where(between, pltpu.roll(value - whole_high, LANES // 2, 1), whole_high)
        edges.append(edge.astype(jnp.bfloat16))
    pulled = col_product(jnp.concatenate(highs + edges, axis=1), jnp.concatenate(lows, axis=1), col_ref)
    grad_ref[0] = -(pulled[:, LANES:] * moved_ref[0, 0] + pulled[:, :LANES] * moved_ref[0, 1])

    for target, row in ((mine_ref, near), (theirs_ref, far)):
        for part in range(2):
            target[0, part] = left_ref[own_section, part, row]
        target[0, 2] = grad_ref[own_section, row]


def finish_kernel(mine_ref, received_ref, grad_ref, exit_ref, total_ref, sems):
    core = lax.axis_index("row")
    copies = []
    for source, item in ((mine_ref, core), (received_ref, 1 - core)):
        copies.append(pltpu.make_async_copy(source.at[:, pl.ds(0, 2)], exit_ref.at[item], sems.at[len(copies)]))
    for copy in copies:
        copy.start()
    total_ref[...] = mine_ref[:, 2] + received_ref[:, 2]
    copies.append(pltpu.make_async_copy(total_ref, grad_ref, sems.at[2]))
    copies[2].start()
    for copy in copies:
        copy.wait()


def spread(shard, axis, reach=None):
    size = lax.axis_size(axis)
    reach = size if reach is None else reach
    pieces = []
    for bits in range(1, size):
        pairs = [(i, i ^ bits) for i in range(size) if abs(i - (i ^ bits)) <= reach]
        pieces.append(lax.ppermute(shard, axis, pairs) if pairs else jnp.zeros_like(shard))
    return pieces


def swap_cores(value):
    return lax.ppermute(value, "row", [(0, 1), (1, 0)])


def whole_field_body(phase, tilt, intensity):
    _, tile_r, tile_c = phase.shape
    count, blocks = lax.axis_size("depth"), lax.axis_size("col")
    core = lax.axis_index("row")
    height = 2 * tile_r
    vmem = pl.BlockSpec(memory_space=pltpu.VMEM)
    smem = pl.BlockSpec(memory_space=pltpu.SMEM)
    hbm = pl.BlockSpec(memory_space=pl.ANY)

    def array(*shape):
        return jax.ShapeDtypeStruct(shape, jnp.float32)

    def params(mebibytes):
        return pltpu.CompilerParams(vmem_limit_bytes=mebibytes * 2**20)

    other_depths = spread(phase, "depth")
    other_depths[0], measured, slab = lax.optimization_barrier((other_depths[0], intensity, phase))
    other_depths = jnp.concatenate(other_depths, axis=0)
    packet = jnp.concatenate([slab, measured], axis=0)
    near_own = [packet]
    for bits in range(1, blocks):
        pairs = [(i, i ^ bits) for i in range(blocks)]
        close = [(i, j) for i, j in pairs if abs(i - j) <= 1]
        if close:
            near_own.append(lax.ppermute(packet, "col", close))
        else:
            further = [(i, j) for i, j in pairs if abs(i - j) <= 2]
            arrived = lax.ppermute(slab, "col", further) if further else jnp.zeros_like(slab)
            near_own.append(jnp.concatenate([arrived, jnp.zeros_like(measured)], axis=0))
    near_own = jnp.stack(near_own)
    arriving = spread(other_depths, "col", 2)
    row_all, col_all = jnp.asarray(row_constant(height)), jnp.asarray(col_constant())
    near_own, row_all, col_all = lax.optimization_barrier((near_own, row_all, col_all))
    half_screens = (count + 1, blocks, tile_r, tile_c)
    field = (blocks, 2, height, tile_c)
    row_matrix, col_matrix, wave = pl.pallas_call(
        load_kernel,
        out_shape=(
            jax.ShapeDtypeStruct(row_all.shape[1:], row_all.dtype),
            jax.ShapeDtypeStruct(col_all.shape, col_all.dtype),
            array(*field),
        ),
        in_specs=[smem, hbm, hbm],
        out_specs=(vmem, vmem, vmem),
        scratch_shapes=[pltpu.SemaphoreType.DMA((2,))],
        compiler_params=params(4),
        cost_estimate=pl.CostEstimate(flops=10**8, bytes_accessed=2**20, transcendentals=0),
    )(tilt, row_all, col_all)
    arriving[2], near_own, row_matrix, col_matrix, wave = lax.optimization_barrier(
        (arriving[2], near_own, row_matrix, col_matrix, wave)
    )
    near_rest = jnp.stack([other_depths] + arriving)
    wanted = lax.dynamic_slice_in_dim(near_own, 2 - core, 1, 1)
    far_own = swap_cores(jnp.concatenate([near_own[:, :1], wanted], axis=1))
    far_rest = swap_cores(near_rest)

    measured, own_cos, own_sin = pl.pallas_call(
        first_kernel,
        out_shape=(array(blocks, height, tile_c),) + (array(blocks, tile_r, tile_c),) * 2,
        in_specs=[vmem, vmem],
        out_specs=(vmem,) * 3,
        compiler_params=params(8),
        cost_estimate=pl.CostEstimate(flops=2 * 10**9, bytes_accessed=2**20, transcendentals=0),
    )(near_own, far_own)
    near_cos, near_sin = pl.pallas_call(
        second_kernel,
        out_shape=(array(*half_screens),) * 2,
        in_specs=[vmem] * 3,
        out_specs=(vmem,) * 2,
        compiler_params=params(8),
        cost_estimate=pl.CostEstimate(flops=5 * 10**8, bytes_accessed=2**20, transcendentals=0),
    )(near_rest, own_cos, own_sin)
    mine, theirs = pl.pallas_call(
        wave_kernel,
        out_shape=(array(1, 3, tile_r, tile_c),) * 2,
        in_specs=[vmem] * 8,
        out_specs=(vmem,) * 2,
        scratch_shapes=[pltpu.VMEM(half_screens, jnp.float32)] * 2
        + [pltpu.VMEM(field, jnp.float32)]
        + [pltpu.VMEM((count, 2, height, tile_c), jnp.float32)] * 2
        + [pltpu.VMEM((count, height, tile_c), jnp.float32)]
        + [pltpu.VMEM((blocks, height, 2 * LANES), jnp.bfloat16)] * 2,
        compiler_params=params(24),
    )(
        wave, near_cos, near_sin, measured, far_own, far_rest,
        row_matrix, col_matrix,
    )
    return pl.pallas_call(
        finish_kernel,
        out_shape=(array(*phase.shape), array(2, 1, 2, tile_r, tile_c)),
        in_specs=[vmem, vmem],
        out_specs=(hbm, hbm),
        scratch_shapes=[pltpu.VMEM(phase.shape, jnp.float32), pltpu.SemaphoreType.DMA((3,))],
        compiler_params=params(4),
    )(mine, swap_cores(theirs))


def extended_2(cells, sides, width):
    for axis, dim in sides:
        count = lax.axis_size(axis)
        ends = count - 1
        head = lax.slice_in_dim(cells, 0, width, axis=dim)
        tail = lax.slice_in_dim(cells, cells.shape[dim] - width, cells.shape[dim], axis=dim)
        cells = jnp.concatenate(
            [
                lax.ppermute(tail, axis, [(i, (i + 1) % count) for i in range(ends)]),
                cells,
                lax.ppermute(head, axis, [((i + 1) % count, i) for i in range(ends)]),
            ],
            axis=dim,
        )
    return cells


def from_behind(value, axis, steps):
    count = lax.axis_size(axis)
    leading, last = (max(0, -steps), min(count, count - steps))
    return lax.ppermute(value, axis, [(source, source + steps) for source in range(leading, last)])


def band_matrix(block_size, margin, fresnel, adjoint):
    shape_full = (block_size, block_size + 2 * margin)
    out_idx = lax.broadcasted_iota(jnp.int32, shape_full, 0)
    in_idx = lax.broadcasted_iota(jnp.int32, shape_full, 1)
    offset = (out_idx + margin - in_idx).astype(jnp.float32)
    inside = jnp.abs(offset) <= margin
    taper_dist = jnp.maximum(jnp.abs(offset) - 0.5 * margin, 0.0)
    profile = jnp.cos(jnp.pi * taper_dist / (margin + 2.0))
    weight = profile * profile / math.sqrt(fresnel)
    phase_angle = jnp.pi * offset * offset / fresnel
    real_part = jnp.where(inside, jnp.cos(phase_angle) * weight, 0.0)
    imag_part = jnp.where(inside, jnp.sin(phase_angle) * weight, 0.0)
    if adjoint:
        imag_part = -imag_part
    upper = jnp.stack([real_part, -imag_part])
    lower = jnp.stack([imag_part, real_part])
    return jnp.stack([upper, lower])


def along_rows(extended, matrix):
    pieces = [jnp.einsum("pqij,gqjc->gpic", matrix, extended, precision=lax.Precision.HIGHEST)]
    return jnp.concatenate(pieces, axis=2)


def along_cols(extended, matrix, margin):
    block_size = matrix.shape[2]
    extent = extended.shape[3] - 2 * margin
    pieces = []
    for block_start in range(0, extent, block_size):
        window = extended[:, :, :, block_start : block_start + block_size + 2 * margin]
        pieces.append(
            jnp.einsum("pqij,gqrj->gpri", matrix, window, precision=lax.Precision.HIGHEST)
        )
    return jnp.concatenate(pieces, axis=3)


def propagate(current, row_matrix, col_matrix):
    with_rows = extended_2(current, (("row", 2),), HALO)
    row_done = along_rows(with_rows, row_matrix)
    with_cols = extended_2(row_done, (("col", 3),), HALO)
    return along_cols(with_cols, col_matrix, HALO)


def transmit(screen, current, adjoint):
    screen_re = screen[0][None]
    screen_im = screen[1][None]
    if adjoint:
        screen_im = -screen_im
    real_part = screen_re * current[:, 0] - screen_im * current[:, 1]
    imag_part = screen_re * current[:, 1] + screen_im * current[:, 0]
    return jnp.stack([real_part, imag_part], axis=1)


def store_item(store, current, first_item, slice_index, active):
    begin = (first_item, jnp.int32(slice_index), jnp.int32(0), jnp.int32(0), jnp.int32(0))
    sizes_now = (current.shape[0], 1) + current.shape[1:]
    previous = lax.dynamic_slice(store, begin, sizes_now)
    fresh = jnp.where(active, current[:, None], previous)
    return lax.dynamic_update_slice(store, fresh, begin)


def staged_body(phase, tilt, intensity):
    slices, tile_r, tile_c = phase.shape
    batch_size = tilt.shape[0]
    sections = lax.axis_size("depth")
    section_index = lax.axis_index("depth")
    group_size = 1
    groups = batch_size // group_size
    tick_count = sections + groups - 1
    block_r = 64
    block_c = 128
    fwd_rows = band_matrix(block_r, HALO, FRESNEL, False)
    fwd_cols = band_matrix(block_c, HALO, FRESNEL, False)
    adj_rows = band_matrix(block_r, HALO, FRESNEL, True)
    adj_cols = band_matrix(block_c, HALO, FRESNEL, True)
    row_pos = (
        lax.axis_index("row") * tile_r + lax.broadcasted_iota(jnp.int32, (tile_r, tile_c), 0)
    ).astype(jnp.float32)
    col_pos = (
        lax.axis_index("col") * tile_c + lax.broadcasted_iota(jnp.int32, (tile_r, tile_c), 1)
    ).astype(jnp.float32)
    height = float(tile_r * lax.axis_size("row"))
    width_all = float(tile_c * lax.axis_size("col"))
    tilt_f = tilt.astype(jnp.float32)
    phase_angle = (
        2.0
        * jnp.pi
        * (
            tilt_f[:, 0, None, None] * row_pos / height
            + tilt_f[:, 1, None, None] * col_pos / width_all
        )
    )
    incident = jnp.stack([jnp.cos(phase_angle), jnp.sin(phase_angle)], axis=1)
    screens = jnp.stack([jnp.cos(phase), jnp.sin(phase)], axis=1)

    def forward_tick(tick_now, carry):
        incoming, entering, leaving = carry
        group_index = tick_now - section_index
        active = (group_index >= 0) & (group_index < groups)
        first_item = jnp.clip(group_index, 0, groups - 1) * group_size
        current = jnp.where(
            section_index == 0,
            lax.dynamic_slice_in_dim(incident, first_item, group_size, 0),
            incoming,
        )
        entering = store_item(entering, current, first_item, 0, active)
        current = propagate(transmit(screens[0], current, False), fwd_rows, fwd_cols)
        leaving = store_item(leaving, current, first_item, 0, active)
        incoming = from_behind(current, "depth", 1)
        return (incoming, entering, leaving)

    store_zero = jnp.zeros((batch_size, slices, 2, tile_r, tile_c), jnp.float32)
    start_wave = jnp.zeros((group_size, 2, tile_r, tile_c), jnp.float32)
    _, entering, leaving = lax.fori_loop(
        0, tick_count, forward_tick, (start_wave, store_zero, store_zero)
    )
    final_wave = leaving[:, slices - 1]
    misfit = final_wave[:, 0] * final_wave[:, 0] + final_wave[:, 1] * final_wave[:, 1] - intensity
    seed_adjoint = 2.0 * misfit[:, None] * final_wave

    def backward_tick(tick_now, carry):
        incoming, gradient = carry
        group_index = tick_now - (sections - 1 - section_index)
        active = (group_index >= 0) & (group_index < groups)
        first_item = jnp.clip(group_index, 0, groups - 1) * group_size
        adjoint_wave = jnp.where(
            section_index == sections - 1,
            lax.dynamic_slice_in_dim(seed_adjoint, first_item, group_size, 0),
            incoming,
        )
        for slice_index in reversed(range(slices)):
            pulled = propagate(adjoint_wave, adj_rows, adj_cols)
            arrived = lax.dynamic_slice_in_dim(entering[:, slice_index], first_item, group_size, 0)
            moved = transmit(screens[slice_index], arrived, False)
            contribution = jnp.sum(pulled[:, 1] * moved[:, 0] - pulled[:, 0] * moved[:, 1], axis=0)
            gradient = gradient.at[slice_index].add(jnp.where(active, contribution, 0.0))
            adjoint_wave = transmit(screens[slice_index], pulled, True)
        incoming = from_behind(adjoint_wave, "depth", -1)
        return (incoming, gradient)

    grad_zero = jnp.zeros((slices, tile_r, tile_c), jnp.float32)
    _, gradient = lax.fori_loop(0, tick_count, backward_tick, (start_wave, grad_zero))
    return (gradient, leaving)


def fits_whole(phase_shape, batch, mesh):
    slices, height, width = phase_shape
    rows, cols, sections = mesh.shape["row"], mesh.shape["col"], mesh.shape["depth"]
    return (
        4 * height * width * (slices + batch) <= GATHER_BUDGET
        and batch == rows == 2
        and slices == sections
        and sections & (sections - 1) == 0
        and cols & (cols - 1) == 0
        and height == LANES
        and width == cols * LANES
        and cols > 1
        and sections > 1
        and sections * HALO <= LANES
    )


def solution(mesh):
    placed = (P("depth", "row", "col"), P(), P(None, "row", "col"))

    def run(phase, tilt, intensity):
        if fits_whole(phase.shape, tilt.shape[0], mesh):
            body = whole_field_body
        else:
            body = staged_body
        return jax.shard_map(
            body,
            mesh=mesh,
            in_specs=placed,
            out_specs=(P("depth", "row", "col"), P(None, "depth", None, "row", "col")),
            check_vma=False,
        )(phase, tilt, intensity)

    return run
```

```python
import math

import jax
import jax.numpy as jnp
import numpy as np
from jax import lax
from jax.experimental import pallas as pl
from jax.experimental.pallas import tpu as pltpu
from jax.sharding import PartitionSpec as P

HALO = 32
FRESNEL = 64
LANES = 128
GATHER_BUDGET = 4 * 2**20
SIN = (
    0.9999999980536763,
    -0.1666666530009577,
    0.008333305907073658,
    -0.00019838908256358006,
    2.745822627876341e-06,
    -2.3043562782810933e-08,
)
COS = (
    0.9999999961345007,
    -0.4999999301617528,
    0.04166646215023687,
    -0.0013886696163545999,
    2.4695045482778703e-05,
    -2.5154931690000354e-07,
)


def horner(coefficients, square):
    total = jnp.full_like(square, coefficients[-1])
    for coefficient in coefficients[-2::-1]:
        total = total * square + coefficient
    return total


def cos_sin(angle):
    square = angle * angle
    return horner(COS, square), horner(SIN, square) * angle


def turn(fraction):
    half_cos, half_sin = cos_sin(fraction * math.pi)
    return half_cos * half_cos - half_sin * half_sin, 2.0 * half_cos * half_sin


def halves(value):
    high = value.astype(jnp.bfloat16)
    return high, (value - high.astype(jnp.float32)).astype(jnp.bfloat16)


def np_halves(matrix):
    high = matrix.astype(jnp.bfloat16)
    return high, (matrix - high.astype(np.float64)).astype(jnp.bfloat16)


def np_taps():
    offset = np.arange(-HALO, HALO + 1, dtype=np.float64)
    taper = np.maximum(np.abs(offset) - 0.5 * HALO, 0.0)
    weight = np.cos(np.pi * taper / (HALO + 2.0)) ** 2 / math.sqrt(FRESNEL)
    return weight * np.exp(1j * np.pi * offset * offset / FRESNEL)


def np_band(out_pos, in_pos):
    offset = out_pos[:, None] - in_pos[None, :]
    inside = np.abs(offset) <= HALO
    return np.where(inside, np_taps()[np.clip(offset, -HALO, HALO) + HALO], 0.0)


def row_constant(height):
    matrices = []
    for core in range(2):
        pos = (np.arange(height) + core * (height // 2)) % height
        band = np_band(pos, pos)
        whole = np.block([[band.real, -band.imag], [band.imag, band.real]])
        matrices.append(np.concatenate(np_halves(whole), axis=1))
    return np.stack(matrices)


def col_constant():
    lane = np.arange(LANES)
    turned = np.where((lane >= HALO) & (lane < LANES - HALO), lane ^ (LANES // 2), lane)
    edge_pos = np.where(turned < LANES // 2, turned + LANES, turned - LANES)
    parts = []
    for position in (lane, edge_pos):
        band = np_band(lane, position).T
        parts.append(np.block([[band.real, band.imag], [-band.imag, band.real]]))
    return np.concatenate(np_halves(np.concatenate(parts, axis=0)), axis=1)


def both_rows(near_ref, far_ref, where):
    return jnp.concatenate([near_ref[where], far_ref[where]], axis=0)


def turned(slice_index, block, screens, wave):
    near_cos, near_sin, far_cos, far_sin = screens
    cos = both_rows(near_cos, far_cos, (slice_index, block))
    sin = both_rows(near_sin, far_sin, (slice_index, block))
    real, imag = wave
    return cos * real - sin * imag, cos * imag + sin * real


def row_product(row_matrix, columns):
    high, low = halves(columns)
    whole, width = columns.shape
    wide = jnp.dot(
        row_matrix[:, :whole], jnp.concatenate([high, low], axis=1), preferred_element_type=jnp.float32
    )
    rest = jnp.dot(row_matrix[:, whole:], high, preferred_element_type=jnp.float32)
    return wide[:, :width] + wide[:, width:] + rest


def col_product(high, low, col_ref):
    wide = jnp.dot(high, col_ref[...], preferred_element_type=jnp.float32)
    rest = jnp.dot(low, col_ref[: 2 * LANES, : 2 * LANES], preferred_element_type=jnp.float32)
    return wide[:, : 2 * LANES] + wide[:, 2 * LANES :] + rest


def three_parts(value):
    high = value.astype(jnp.bfloat16)
    rest = value - high.astype(jnp.float32)
    return high, rest.astype(jnp.bfloat16), pltpu.roll(rest, LANES // 2, 1).astype(jnp.bfloat16)


def advance(slice_index, start, waves, screens, row_matrix, col_ref, edge_ref):
    size, height = len(waves), waves[0][0].shape[0]
    chunks = [range(place, min(place + 2, size)) for place in range(0, size, 2)]
    highs, lows = [], []
    for chunk in chunks:
        columns = [
            jnp.concatenate(turned(slice_index, start + place, screens, waves[place]), axis=0) for place in chunk
        ]
        done = row_product(row_matrix, jnp.concatenate(columns, axis=1))
        for sub, place in enumerate(chunk):
            own_high, own_low = [], []
            for part in range(2):
                value = done[part * height : (part + 1) * height, sub * LANES : (sub + 1) * LANES]
                high, low, swung = three_parts(value)
                own_high.append(high)
                own_low.append(low)
                edge = part * LANES
                if place > 0:
                    edge_ref[place - 1, :, pl.ds(edge, HALO)] = high[:, :HALO]
                    edge_ref[place - 1, :, pl.ds(edge + 2 * HALO, HALO)] = swung[:, 2 * HALO : 3 * HALO]
                if place < size - 1:
                    edge_ref[place + 1, :, pl.ds(edge + 3 * HALO, HALO)] = high[:, 3 * HALO :]
                    edge_ref[place + 1, :, pl.ds(edge + HALO, HALO)] = swung[:, HALO : 2 * HALO]
            highs.append(jnp.concatenate(own_high, axis=1))
            lows.append(jnp.concatenate(own_low, axis=1))
    results = []
    for chunk in chunks:
        rows = len(chunk) * height
        edges = edge_ref[pl.ds(chunk[0], len(chunk))].reshape(rows, 2 * LANES)
        own = jnp.concatenate([highs[place] for place in chunk], axis=0)
        total = col_product(
            jnp.concatenate([own, edges], axis=1),
            jnp.concatenate([lows[place] for place in chunk], axis=0),
            col_ref,
        )
        for sub in range(len(chunk)):
            block = total[sub * height : (sub + 1) * height]
            results.append((block[:, :LANES], block[:, LANES:]))
    return results


def clear_edge(edge_ref, place, right):
    for part in range(2):
        for begin in (0, 2 * HALO) if right else (HALO, 3 * HALO):
            cells = pl.ds(part * LANES + begin, HALO)
            edge_ref[place, :, cells] = jnp.zeros((edge_ref.shape[1], HALO), edge_ref.dtype)


def keep(wave_ref, waves):
    for place, wave in enumerate(waves):
        wave_ref[place, 0], wave_ref[place, 1] = wave


def load_kernel(tilt_ref, near_own, row_from, col_from, row_to, col_to, wave_ref, cos_ref, sin_ref, sems):
    blocks, _, height, _ = wave_ref.shape
    core = lax.axis_index("row")
    copies = [
        pltpu.make_async_copy(row_from.at[core], row_to, sems.at[0]),
        pltpu.make_async_copy(col_from, col_to, sems.at[1]),
    ]
    for copy in copies:
        copy.start()
    for col in range(blocks):
        cos_ref[col], sin_ref[col] = cos_sin(near_own[col ^ lax.axis_index("col"), 0])

    def cycles(number, position, extent):
        fraction = (number * position).astype(jnp.float32) / extent
        return turn(fraction - jnp.round(fraction))

    row = lax.broadcasted_iota(jnp.int32, (height, LANES), 0) + core * (height // 2)
    row = jnp.where(row >= height, row - height, row)
    row_cos, row_sin = cycles(tilt_ref[core, 0], row, float(height))
    for block in range(blocks):
        col_cos, col_sin = cycles(
            tilt_ref[core, 1],
            lax.broadcasted_iota(jnp.int32, (8, LANES), 1) + block * LANES,
            float(blocks * LANES),
        )
        col_cos, col_sin = col_cos[:1], col_sin[:1]
        wave_ref[block, 0] = row_cos * col_cos - row_sin * col_sin
        wave_ref[block, 1] = row_sin * col_cos + row_cos * col_sin
    for copy in copies:
        copy.wait()


def second_kernel(near_rest, own_cos, own_sin, cos_ref, sin_ref):
    blocks = own_cos.shape[0]
    count = cos_ref.shape[0] - 1
    own_section, own_place = lax.axis_index("depth"), lax.axis_index("col")

    def screens(col, carry):
        held = col ^ own_place
        cos_ref[own_section, col], sin_ref[own_section, col] = own_cos[col], own_sin[col]
        for bits in range(1, count):
            cos_ref[bits ^ own_section, col], sin_ref[bits ^ own_section, col] = cos_sin(near_rest[held, bits - 1])
        return carry

    lax.fori_loop(0, blocks, screens, 0)
    cos_ref[count] = jnp.ones(cos_ref.shape[1:], jnp.float32)
    sin_ref[count] = jnp.zeros(cos_ref.shape[1:], jnp.float32)


def wave_kernel(
    wave_ref, near_cos, near_sin, near_own, far_first, far_second, row_ref, col_ref,
    mine_ref, theirs_ref, far_cos, far_sin, kept_ref, moved_ref, left_ref, grad_ref, even_edge, odd_edge,
):
    blocks, _, height, _ = wave_ref.shape
    count = near_cos.shape[0] - 1
    core, own_section, own_place = lax.axis_index("row"), lax.axis_index("depth"), lax.axis_index("col")
    near, far = pl.ds(0, height // 2), pl.ds(height // 2, height // 2)
    screens = (near_cos, near_sin, far_cos, far_sin)
    row_matrix = row_ref[...]
    window = min(3, blocks)
    window_start = jnp.clip(own_place - 1, 0, blocks - window)
    own_in_window = own_place - window_start
    edges = (even_edge, odd_edge)

    def far_screens(slice_index):
        bits = slice_index ^ own_section
        for col in range(blocks):
            held = col ^ own_place
            others = jnp.maximum(bits - 1, 0)
            in_first = (bits == 0) | (held == 3)
            place = jnp.where(bits == 0, 2 * held, 2 * blocks + others)
            angle = jnp.where(in_first, far_first[place], far_second[jnp.minimum(held, 2) * (count - 1) + others])
            far_cos[slice_index, col], far_sin[slice_index, col] = cos_sin(angle)

    for edge_ref in edges:
        clear_edge(edge_ref, 0, False)
        clear_edge(edge_ref, blocks - 1, True)
    far_cos[count] = jnp.ones(far_cos.shape[1:], jnp.float32)
    far_sin[count] = jnp.zeros(far_cos.shape[1:], jnp.float32)
    far_screens(0)

    waves = [(wave_ref[place, 0], wave_ref[place, 1]) for place in range(blocks)]
    for tick in range(count):
        entering = (wave_ref if tick == 0 else kept_ref)[own_place]
        moved_ref[tick, 0], moved_ref[tick, 1] = turned(tick, own_place, screens, (entering[0], entering[1]))
        waves = advance(tick, 0, waves, screens, row_matrix, col_ref, edges[tick % 2])
        if tick + 1 < count:
            far_screens(tick + 1)
        keep(kept_ref, waves)
        left_ref[tick] = kept_ref[own_place]

    for edge_ref in edges:
        clear_edge(edge_ref, window - 1, True)
    waves = []
    for place in range(window):
        block = window_start + place
        real, imag = kept_ref[block, 0], kept_ref[block, 1]
        held = block ^ own_place
        measured = jnp.concatenate([near_own[held, 1 + core], far_first[2 * held + 1]], axis=0)
        misfit = 2.0 * (real * real + imag * imag - measured)
        waves.append((misfit * real, -misfit * imag))

    for tick in range(count - 1):
        waves = advance(count - tick, window_start, waves, screens, row_matrix, col_ref, edges[tick % 2])
        keep(kept_ref, waves)
        arrived = count - 1 - tick
        pulled = kept_ref[own_in_window]
        grad_ref[arrived] = -(pulled[1] * moved_ref[arrived, 0] + pulled[0] * moved_ref[arrived, 1])

    left, right = jnp.maximum(own_place - 1, 0), jnp.minimum(own_place + 1, blocks - 1)
    lane = lax.broadcasted_iota(jnp.int32, (2 * height, LANES), 1)
    has_left, has_right = own_place > 0, own_place < blocks - 1

    def cells(block):
        wave = kept_ref[block - window_start]
        return jnp.concatenate(turned(1, block, screens, (wave[0], wave[1])), axis=0)

    edge_cells = jnp.where(
        lane < LANES // 2, jnp.where(has_right, cells(right), 0.0), jnp.where(has_left, cells(left), 0.0)
    )
    done = row_product(row_matrix, jnp.concatenate([cells(own_place), edge_cells], axis=1))
    lane = lax.broadcasted_iota(jnp.int32, (height, LANES), 1)
    between = (lane >= HALO) & (lane < LANES - HALO)
    highs, lows, edges = [], [], []
    for part in range(2):
        high, low, _ = three_parts(done[part * height : (part + 1) * height, :LANES])
        highs.append(high)
        lows.append(low)
        value = done[part * height : (part + 1) * height, LANES:]
        whole_high = value.astype(jnp.bfloat16).astype(jnp.float32)
        edge = jnp.where(between, pltpu.roll(value - whole_high, LANES // 2, 1), whole_high)
        edges.append(edge.astype(jnp.bfloat16))
    pulled = col_product(jnp.concatenate(highs + edges, axis=1), jnp.concatenate(lows, axis=1), col_ref)
    grad_ref[0] = -(pulled[:, LANES:] * moved_ref[0, 0] + pulled[:, :LANES] * moved_ref[0, 1])

    for target, row in ((mine_ref, near), (theirs_ref, far)):
        for part in range(2):
            target[0, part] = left_ref[own_section, part, row]
        target[0, 2] = grad_ref[own_section, row]


def finish_kernel(mine_ref, received_ref, grad_ref, exit_ref, total_ref, sems):
    core = lax.axis_index("row")
    copies = []
    for source, item in ((mine_ref, core), (received_ref, 1 - core)):
        copies.append(pltpu.make_async_copy(source.at[:, pl.ds(0, 2)], exit_ref.at[item], sems.at[len(copies)]))
    for copy in copies:
        copy.start()
    total_ref[...] = mine_ref[:, 2] + received_ref[:, 2]
    copies.append(pltpu.make_async_copy(total_ref, grad_ref, sems.at[2]))
    copies[2].start()
    for copy in copies:
        copy.wait()


def spread(shard, axis, reach=None):
    size = lax.axis_size(axis)
    reach = size if reach is None else reach
    pieces = []
    for bits in range(1, size):
        pairs = [(i, i ^ bits) for i in range(size) if abs(i - (i ^ bits)) <= reach]
        pieces.append(lax.ppermute(shard, axis, pairs) if pairs else jnp.zeros_like(shard))
    return pieces


def swap_cores(value):
    return lax.ppermute(value, "row", [(0, 1), (1, 0)])


def whole_field_body(phase, tilt, intensity):
    _, tile_r, tile_c = phase.shape
    count, blocks = lax.axis_size("depth"), lax.axis_size("col")
    core = lax.axis_index("row")
    height = 2 * tile_r
    vmem = pl.BlockSpec(memory_space=pltpu.VMEM)
    smem = pl.BlockSpec(memory_space=pltpu.SMEM)
    hbm = pl.BlockSpec(memory_space=pl.ANY)

    def array(*shape):
        return jax.ShapeDtypeStruct(shape, jnp.float32)

    def params(mebibytes):
        return pltpu.CompilerParams(vmem_limit_bytes=mebibytes * 2**20)

    other_depths = spread(phase, "depth")
    other_depths[0], measured, slab = lax.optimization_barrier((other_depths[0], intensity, phase))
    other_depths = jnp.concatenate(other_depths, axis=0)
    packet = jnp.concatenate([slab, measured], axis=0)
    near_own = [packet]
    for bits in range(1, blocks):
        pairs = [(i, i ^ bits) for i in range(blocks)]
        close = [(i, j) for i, j in pairs if abs(i - j) <= 1]
        if close:
            near_own.append(lax.ppermute(packet, "col", close))
        else:
            further = [(i, j) for i, j in pairs if abs(i - j) <= 2]
            arrived = lax.ppermute(slab, "col", further) if further else jnp.zeros_like(slab)
            near_own.append(jnp.concatenate([arrived, jnp.zeros_like(measured)], axis=0))
    near_own = jnp.stack(near_own)
    arriving = spread(other_depths, "col", 2)
    row_all, col_all = jnp.asarray(row_constant(height)), jnp.asarray(col_constant())
    near_own, row_all, col_all = lax.optimization_barrier((near_own, row_all, col_all))
    half_screens = (count + 1, blocks, tile_r, tile_c)
    field = (blocks, 2, height, tile_c)
    row_matrix, col_matrix, wave, own_cos, own_sin = pl.pallas_call(
        load_kernel,
        out_shape=(
            jax.ShapeDtypeStruct(row_all.shape[1:], row_all.dtype),
            jax.ShapeDtypeStruct(col_all.shape, col_all.dtype),
            array(*field),
            array(blocks, tile_r, tile_c),
            array(blocks, tile_r, tile_c),
        ),
        in_specs=[smem, vmem, hbm, hbm],
        out_specs=(vmem,) * 5,
        scratch_shapes=[pltpu.SemaphoreType.DMA((2,))],
        compiler_params=params(4),
        cost_estimate=pl.CostEstimate(flops=10**8, bytes_accessed=2**20, transcendentals=0),
    )(tilt, near_own, row_all, col_all)
    arriving[2], near_own, row_matrix, col_matrix, wave, own_cos, own_sin = lax.optimization_barrier(
        (arriving[2], near_own, row_matrix, col_matrix, wave, own_cos, own_sin)
    )
    wanted = lax.dynamic_slice_in_dim(near_own, 2 - core, 1, 1)
    packets = jnp.concatenate([near_own[:, :1], wanted], axis=1).reshape(2 * blocks, tile_r, tile_c)
    far_first = swap_cores(jnp.concatenate([packets, arriving[2]], axis=0))
    far_second = swap_cores(jnp.concatenate([other_depths] + arriving[:2], axis=0))
    near_rest = jnp.stack([other_depths] + arriving)

    near_cos, near_sin = pl.pallas_call(
        second_kernel,
        out_shape=(array(*half_screens),) * 2,
        in_specs=[vmem] * 3,
        out_specs=(vmem,) * 2,
        compiler_params=params(8),
        cost_estimate=pl.CostEstimate(flops=5 * 10**8, bytes_accessed=2**20, transcendentals=0),
    )(near_rest, own_cos, own_sin)
    mine, theirs = pl.pallas_call(
        wave_kernel,
        out_shape=(array(1, 3, tile_r, tile_c),) * 2,
        in_specs=[vmem] * 8,
        out_specs=(vmem,) * 2,
        scratch_shapes=[pltpu.VMEM(half_screens, jnp.float32)] * 2
        + [pltpu.VMEM(field, jnp.float32)]
        + [pltpu.VMEM((count, 2, height, tile_c), jnp.float32)] * 2
        + [pltpu.VMEM((count, height, tile_c), jnp.float32)]
        + [pltpu.VMEM((blocks, height, 2 * LANES), jnp.bfloat16)] * 2,
        compiler_params=params(24),
    )(
        wave, near_cos, near_sin, near_own, far_first, far_second,
        row_matrix, col_matrix,
    )
    return pl.pallas_call(
        finish_kernel,
        out_shape=(array(*phase.shape), array(2, 1, 2, tile_r, tile_c)),
        in_specs=[vmem, vmem],
        out_specs=(hbm, hbm),
        scratch_shapes=[pltpu.VMEM(phase.shape, jnp.float32), pltpu.SemaphoreType.DMA((3,))],
        compiler_params=params(4),
    )(mine, swap_cores(theirs))


def extended_2(cells, sides, width):
    for axis, dim in sides:
        count = lax.axis_size(axis)
        ends = count - 1
        head = lax.slice_in_dim(cells, 0, width, axis=dim)
        tail = lax.slice_in_dim(cells, cells.shape[dim] - width, cells.shape[dim], axis=dim)
        cells = jnp.concatenate(
            [
                lax.ppermute(tail, axis, [(i, (i + 1) % count) for i in range(ends)]),
                cells,
                lax.ppermute(head, axis, [((i + 1) % count, i) for i in range(ends)]),
            ],
            axis=dim,
        )
    return cells


def from_behind(value, axis, steps):
    count = lax.axis_size(axis)
    leading, last = (max(0, -steps), min(count, count - steps))
    return lax.ppermute(value, axis, [(source, source + steps) for source in range(leading, last)])


def band_matrix(block_size, margin, fresnel, adjoint):
    shape_full = (block_size, block_size + 2 * margin)
    out_idx = lax.broadcasted_iota(jnp.int32, shape_full, 0)
    in_idx = lax.broadcasted_iota(jnp.int32, shape_full, 1)
    offset = (out_idx + margin - in_idx).astype(jnp.float32)
    inside = jnp.abs(offset) <= margin
    taper_dist = jnp.maximum(jnp.abs(offset) - 0.5 * margin, 0.0)
    profile = jnp.cos(jnp.pi * taper_dist / (margin + 2.0))
    weight = profile * profile / math.sqrt(fresnel)
    phase_angle = jnp.pi * offset * offset / fresnel
    real_part = jnp.where(inside, jnp.cos(phase_angle) * weight, 0.0)
    imag_part = jnp.where(inside, jnp.sin(phase_angle) * weight, 0.0)
    if adjoint:
        imag_part = -imag_part
    upper = jnp.stack([real_part, -imag_part])
    lower = jnp.stack([imag_part, real_part])
    return jnp.stack([upper, lower])


def along_rows(extended, matrix):
    pieces = [jnp.einsum("pqij,gqjc->gpic", matrix, extended, precision=lax.Precision.HIGHEST)]
    return jnp.concatenate(pieces, axis=2)


def along_cols(extended, matrix, margin):
    block_size = matrix.shape[2]
    extent = extended.shape[3] - 2 * margin
    pieces = []
    for block_start in range(0, extent, block_size):
        window = extended[:, :, :, block_start : block_start + block_size + 2 * margin]
        pieces.append(
            jnp.einsum("pqij,gqrj->gpri", matrix, window, precision=lax.Precision.HIGHEST)
        )
    return jnp.concatenate(pieces, axis=3)


def propagate(current, row_matrix, col_matrix):
    with_rows = extended_2(current, (("row", 2),), HALO)
    row_done = along_rows(with_rows, row_matrix)
    with_cols = extended_2(row_done, (("col", 3),), HALO)
    return along_cols(with_cols, col_matrix, HALO)


def transmit(screen, current, adjoint):
    screen_re = screen[0][None]
    screen_im = screen[1][None]
    if adjoint:
        screen_im = -screen_im
    real_part = screen_re * current[:, 0] - screen_im * current[:, 1]
    imag_part = screen_re * current[:, 1] + screen_im * current[:, 0]
    return jnp.stack([real_part, imag_part], axis=1)


def store_item(store, current, first_item, slice_index, active):
    begin = (first_item, jnp.int32(slice_index), jnp.int32(0), jnp.int32(0), jnp.int32(0))
    sizes_now = (current.shape[0], 1) + current.shape[1:]
    previous = lax.dynamic_slice(store, begin, sizes_now)
    fresh = jnp.where(active, current[:, None], previous)
    return lax.dynamic_update_slice(store, fresh, begin)


def staged_body(phase, tilt, intensity):
    slices, tile_r, tile_c = phase.shape
    batch_size = tilt.shape[0]
    sections = lax.axis_size("depth")
    section_index = lax.axis_index("depth")
    group_size = 1
    groups = batch_size // group_size
    tick_count = sections + groups - 1
    block_r = 64
    block_c = 128
    fwd_rows = band_matrix(block_r, HALO, FRESNEL, False)
    fwd_cols = band_matrix(block_c, HALO, FRESNEL, False)
    adj_rows = band_matrix(block_r, HALO, FRESNEL, True)
    adj_cols = band_matrix(block_c, HALO, FRESNEL, True)
    row_pos = (
        lax.axis_index("row") * tile_r + lax.broadcasted_iota(jnp.int32, (tile_r, tile_c), 0)
    ).astype(jnp.float32)
    col_pos = (
        lax.axis_index("col") * tile_c + lax.broadcasted_iota(jnp.int32, (tile_r, tile_c), 1)
    ).astype(jnp.float32)
    height = float(tile_r * lax.axis_size("row"))
    width_all = float(tile_c * lax.axis_size("col"))
    tilt_f = tilt.astype(jnp.float32)
    phase_angle = (
        2.0
        * jnp.pi
        * (
            tilt_f[:, 0, None, None] * row_pos / height
            + tilt_f[:, 1, None, None] * col_pos / width_all
        )
    )
    incident = jnp.stack([jnp.cos(phase_angle), jnp.sin(phase_angle)], axis=1)
    screens = jnp.stack([jnp.cos(phase), jnp.sin(phase)], axis=1)

    def forward_tick(tick_now, carry):
        incoming, entering, leaving = carry
        group_index = tick_now - section_index
        active = (group_index >= 0) & (group_index < groups)
        first_item = jnp.clip(group_index, 0, groups - 1) * group_size
        current = jnp.where(
            section_index == 0,
            lax.dynamic_slice_in_dim(incident, first_item, group_size, 0),
            incoming,
        )
        entering = store_item(entering, current, first_item, 0, active)
        current = propagate(transmit(screens[0], current, False), fwd_rows, fwd_cols)
        leaving = store_item(leaving, current, first_item, 0, active)
        incoming = from_behind(current, "depth", 1)
        return (incoming, entering, leaving)

    store_zero = jnp.zeros((batch_size, slices, 2, tile_r, tile_c), jnp.float32)
    start_wave = jnp.zeros((group_size, 2, tile_r, tile_c), jnp.float32)
    _, entering, leaving = lax.fori_loop(
        0, tick_count, forward_tick, (start_wave, store_zero, store_zero)
    )
    final_wave = leaving[:, slices - 1]
    misfit = final_wave[:, 0] * final_wave[:, 0] + final_wave[:, 1] * final_wave[:, 1] - intensity
    seed_adjoint = 2.0 * misfit[:, None] * final_wave

    def backward_tick(tick_now, carry):
        incoming, gradient = carry
        group_index = tick_now - (sections - 1 - section_index)
        active = (group_index >= 0) & (group_index < groups)
        first_item = jnp.clip(group_index, 0, groups - 1) * group_size
        adjoint_wave = jnp.where(
            section_index == sections - 1,
            lax.dynamic_slice_in_dim(seed_adjoint, first_item, group_size, 0),
            incoming,
        )
        for slice_index in reversed(range(slices)):
            pulled = propagate(adjoint_wave, adj_rows, adj_cols)
            arrived = lax.dynamic_slice_in_dim(entering[:, slice_index], first_item, group_size, 0)
            moved = transmit(screens[slice_index], arrived, False)
            contribution = jnp.sum(pulled[:, 1] * moved[:, 0] - pulled[:, 0] * moved[:, 1], axis=0)
            gradient = gradient.at[slice_index].add(jnp.where(active, contribution, 0.0))
            adjoint_wave = transmit(screens[slice_index], pulled, True)
        incoming = from_behind(adjoint_wave, "depth", -1)
        return (incoming, gradient)

    grad_zero = jnp.zeros((slices, tile_r, tile_c), jnp.float32)
    _, gradient = lax.fori_loop(0, tick_count, backward_tick, (start_wave, grad_zero))
    return (gradient, leaving)


def fits_whole(phase_shape, batch, mesh):
    slices, height, width = phase_shape
    rows, cols, sections = mesh.shape["row"], mesh.shape["col"], mesh.shape["depth"]
    return (
        4 * height * width * (slices + batch) <= GATHER_BUDGET
        and batch == rows == 2
        and slices == sections
        and sections & (sections - 1) == 0
        and cols & (cols - 1) == 0
        and height == LANES
        and width == cols * LANES
        and cols > 1
        and sections > 1
        and sections * HALO <= LANES
    )


def solution(mesh):
    placed = (P("depth", "row", "col"), P(), P(None, "row", "col"))

    def run(phase, tilt, intensity):
        if fits_whole(phase.shape, tilt.shape[0], mesh):
            body = whole_field_body
        else:
            body = staged_body
        return jax.shard_map(
            body,
            mesh=mesh,
            in_specs=placed,
            out_specs=(P("depth", "row", "col"), P(None, "depth", None, "row", "col")),
            check_vma=False,
        )(phase, tilt, intensity)

    return run
```

```python
import math

import jax
import jax.numpy as jnp
import numpy as np
from jax import lax
from jax.experimental import pallas as pl
from jax.experimental.pallas import tpu as pltpu
from jax.sharding import PartitionSpec as P

HALO = 32
FRESNEL = 64
LANES = 128
GATHER_BUDGET = 4 * 2**20
SIN = (
    0.9999999980536763,
    -0.1666666530009577,
    0.008333305907073658,
    -0.00019838908256358006,
    2.745822627876341e-06,
    -2.3043562782810933e-08,
)
COS = (
    0.9999999961345007,
    -0.4999999301617528,
    0.04166646215023687,
    -0.0013886696163545999,
    2.4695045482778703e-05,
    -2.5154931690000354e-07,
)


def horner(coefficients, square):
    total = jnp.full_like(square, coefficients[-1])
    for coefficient in coefficients[-2::-1]:
        total = total * square + coefficient
    return total


def cos_sin(angle):
    square = angle * angle
    return horner(COS, square), horner(SIN, square) * angle


def turn(fraction):
    half_cos, half_sin = cos_sin(fraction * math.pi)
    return half_cos * half_cos - half_sin * half_sin, 2.0 * half_cos * half_sin


def halves(value):
    high = value.astype(jnp.bfloat16)
    return high, (value - high.astype(jnp.float32)).astype(jnp.bfloat16)


def np_halves(matrix):
    high = matrix.astype(jnp.bfloat16)
    return high, (matrix - high.astype(np.float64)).astype(jnp.bfloat16)


def np_taps():
    offset = np.arange(-HALO, HALO + 1, dtype=np.float64)
    taper = np.maximum(np.abs(offset) - 0.5 * HALO, 0.0)
    weight = np.cos(np.pi * taper / (HALO + 2.0)) ** 2 / math.sqrt(FRESNEL)
    return weight * np.exp(1j * np.pi * offset * offset / FRESNEL)


def np_band(out_pos, in_pos):
    offset = out_pos[:, None] - in_pos[None, :]
    inside = np.abs(offset) <= HALO
    return np.where(inside, np_taps()[np.clip(offset, -HALO, HALO) + HALO], 0.0)


def row_constant(height):
    matrices = []
    for core in range(2):
        pos = (np.arange(height) + core * (height // 2)) % height
        band = np_band(pos, pos)
        whole = np.block([[band.real, -band.imag], [band.imag, band.real]])
        matrices.append(np.concatenate(np_halves(whole), axis=1))
    return np.stack(matrices)


def col_constant():
    lane = np.arange(LANES)
    turned = np.where((lane >= HALO) & (lane < LANES - HALO), lane ^ (LANES // 2), lane)
    edge_pos = np.where(turned < LANES // 2, turned + LANES, turned - LANES)
    parts = []
    for position in (lane, edge_pos):
        band = np_band(lane, position).T
        parts.append(np.block([[band.real, band.imag], [-band.imag, band.real]]))
    return np.concatenate(np_halves(np.concatenate(parts, axis=0)), axis=1)


def both_rows(near_ref, far_ref, where):
    return jnp.concatenate([near_ref[where], far_ref[where]], axis=0)


def turned(slice_index, block, screens, wave):
    near_cos, near_sin, far_cos, far_sin = screens
    cos = both_rows(near_cos, far_cos, (slice_index, block))
    sin = both_rows(near_sin, far_sin, (slice_index, block))
    real, imag = wave
    return cos * real - sin * imag, cos * imag + sin * real


def row_product(row_matrix, columns):
    high, low = halves(columns)
    whole, width = columns.shape
    wide = jnp.dot(
        row_matrix[:, :whole], jnp.concatenate([high, low], axis=1), preferred_element_type=jnp.float32
    )
    rest = jnp.dot(row_matrix[:, whole:], high, preferred_element_type=jnp.float32)
    return wide[:, :width] + wide[:, width:] + rest


def col_product(high, low, col_ref):
    wide = jnp.dot(high, col_ref[...], preferred_element_type=jnp.float32)
    rest = jnp.dot(low, col_ref[: 2 * LANES, : 2 * LANES], preferred_element_type=jnp.float32)
    return wide[:, : 2 * LANES] + wide[:, 2 * LANES :] + rest


def three_parts(value):
    high = value.astype(jnp.bfloat16)
    rest = value - high.astype(jnp.float32)
    return high, rest.astype(jnp.bfloat16), pltpu.roll(rest, LANES // 2, 1).astype(jnp.bfloat16)


def advance(slice_index, start, waves, screens, row_matrix, col_ref, edge_ref):
    size, height = len(waves), waves[0][0].shape[0]
    chunks = [range(place, min(place + 2, size)) for place in range(0, size, 2)]
    highs, lows = [], []
    for chunk in chunks:
        columns = [
            jnp.concatenate(turned(slice_index, start + place, screens, waves[place]), axis=0) for place in chunk
        ]
        done = row_product(row_matrix, jnp.concatenate(columns, axis=1))
        for sub, place in enumerate(chunk):
            own_high, own_low = [], []
            for part in range(2):
                value = done[part * height : (part + 1) * height, sub * LANES : (sub + 1) * LANES]
                high, low, swung = three_parts(value)
                own_high.append(high)
                own_low.append(low)
                edge = part * LANES
                if place > 0:
                    edge_ref[place - 1, :, pl.ds(edge, HALO)] = high[:, :HALO]
                    edge_ref[place - 1, :, pl.ds(edge + 2 * HALO, HALO)] = swung[:, 2 * HALO : 3 * HALO]
                if place < size - 1:
                    edge_ref[place + 1, :, pl.ds(edge + 3 * HALO, HALO)] = high[:, 3 * HALO :]
                    edge_ref[place + 1, :, pl.ds(edge + HALO, HALO)] = swung[:, HALO : 2 * HALO]
            highs.append(jnp.concatenate(own_high, axis=1))
            lows.append(jnp.concatenate(own_low, axis=1))
    results = []
    for chunk in chunks:
        rows = len(chunk) * height
        edges = edge_ref[pl.ds(chunk[0], len(chunk))].reshape(rows, 2 * LANES)
        own = jnp.concatenate([highs[place] for place in chunk], axis=0)
        total = col_product(
            jnp.concatenate([own, edges], axis=1),
            jnp.concatenate([lows[place] for place in chunk], axis=0),
            col_ref,
        )
        for sub in range(len(chunk)):
            block = total[sub * height : (sub + 1) * height]
            results.append((block[:, :LANES], block[:, LANES:]))
    return results


def clear_edge(edge_ref, place, right):
    for part in range(2):
        for begin in (0, 2 * HALO) if right else (HALO, 3 * HALO):
            cells = pl.ds(part * LANES + begin, HALO)
            edge_ref[place, :, cells] = jnp.zeros((edge_ref.shape[1], HALO), edge_ref.dtype)


def keep(wave_ref, waves):
    for place, wave in enumerate(waves):
        wave_ref[place, 0], wave_ref[place, 1] = wave


def load_kernel(tilt_ref, near_own, row_from, col_from, row_to, col_to, wave_ref, cos_ref, sin_ref, sems):
    blocks, _, height, _ = wave_ref.shape
    core = lax.axis_index("row")
    copies = [
        pltpu.make_async_copy(row_from.at[core], row_to, sems.at[0]),
        pltpu.make_async_copy(col_from, col_to, sems.at[1]),
    ]
    for copy in copies:
        copy.start()
    for col in range(blocks):
        cos_ref[col], sin_ref[col] = cos_sin(near_own[col ^ lax.axis_index("col"), 0])

    def cycles(number, position, extent):
        fraction = (number * position).astype(jnp.float32) / extent
        return turn(fraction - jnp.round(fraction))

    row = lax.broadcasted_iota(jnp.int32, (height, LANES), 0) + core * (height // 2)
    row = jnp.where(row >= height, row - height, row)
    row_cos, row_sin = cycles(tilt_ref[core, 0], row, float(height))
    for block in range(blocks):
        col_cos, col_sin = cycles(
            tilt_ref[core, 1],
            lax.broadcasted_iota(jnp.int32, (8, LANES), 1) + block * LANES,
            float(blocks * LANES),
        )
        col_cos, col_sin = col_cos[:1], col_sin[:1]
        wave_ref[block, 0] = row_cos * col_cos - row_sin * col_sin
        wave_ref[block, 1] = row_sin * col_cos + row_cos * col_sin
    for copy in copies:
        copy.wait()


def second_kernel(near_rest, own_cos, own_sin, cos_ref, sin_ref):
    blocks = own_cos.shape[0]
    count = cos_ref.shape[0] - 1
    own_section, own_place = lax.axis_index("depth"), lax.axis_index("col")

    def screens(col, carry):
        held = col ^ own_place
        cos_ref[own_section, col], sin_ref[own_section, col] = own_cos[col], own_sin[col]
        for bits in range(1, count):
            cos_ref[bits ^ own_section, col], sin_ref[bits ^ own_section, col] = cos_sin(near_rest[held, bits - 1])
        return carry

    lax.fori_loop(0, blocks, screens, 0)
    cos_ref[count] = jnp.ones(cos_ref.shape[1:], jnp.float32)
    sin_ref[count] = jnp.zeros(cos_ref.shape[1:], jnp.float32)


def wave_kernel(
    wave_ref, near_cos, near_sin, near_own, far_first, far_second, row_ref, col_ref,
    mine_ref, theirs_ref, far_cos, far_sin, kept_ref, moved_ref, left_ref, grad_ref, even_edge, odd_edge,
):
    blocks, _, height, _ = wave_ref.shape
    count = near_cos.shape[0] - 1
    core, own_section, own_place = lax.axis_index("row"), lax.axis_index("depth"), lax.axis_index("col")
    near, far = pl.ds(0, height // 2), pl.ds(height // 2, height // 2)
    screens = (near_cos, near_sin, far_cos, far_sin)
    row_matrix = row_ref[...]
    window = min(3, blocks)
    window_start = jnp.clip(own_place - 1, 0, blocks - window)
    own_in_window = own_place - window_start
    edges = (even_edge, odd_edge)

    def far_screens(slice_index):
        bits = slice_index ^ own_section
        for col in range(blocks):
            held = col ^ own_place
            others = jnp.maximum(bits - 1, 0)
            in_first = (bits == 0) | (held == 3)
            place = jnp.where(bits == 0, 2 * held, 2 * blocks + others)
            angle = jnp.where(in_first, far_first[place], far_second[jnp.minimum(held, 2) * (count - 1) + others])
            far_cos[slice_index, col], far_sin[slice_index, col] = cos_sin(angle)

    for edge_ref in edges:
        clear_edge(edge_ref, 0, False)
        clear_edge(edge_ref, blocks - 1, True)
    far_cos[count] = jnp.ones(far_cos.shape[1:], jnp.float32)
    far_sin[count] = jnp.zeros(far_cos.shape[1:], jnp.float32)
    far_screens(0)

    waves = [(wave_ref[place, 0], wave_ref[place, 1]) for place in range(blocks)]
    for tick in range(count):
        entering = (wave_ref if tick == 0 else kept_ref)[own_place]
        moved_ref[tick, 0], moved_ref[tick, 1] = turned(tick, own_place, screens, (entering[0], entering[1]))
        waves = advance(tick, 0, waves, screens, row_matrix, col_ref, edges[tick % 2])
        if tick + 1 < count:
            far_screens(tick + 1)
        keep(kept_ref, waves)
        left_ref[tick] = kept_ref[own_place]

    for edge_ref in edges:
        clear_edge(edge_ref, window - 1, True)
    waves = []
    for place in range(window):
        block = window_start + place
        real, imag = kept_ref[block, 0], kept_ref[block, 1]
        held = block ^ own_place
        measured = jnp.concatenate([near_own[held, 1 + core], far_first[2 * held + 1]], axis=0)
        misfit = 2.0 * (real * real + imag * imag - measured)
        waves.append((misfit * real, -misfit * imag))

    for tick in range(count - 1):
        waves = advance(count - tick, window_start, waves, screens, row_matrix, col_ref, edges[tick % 2])
        keep(kept_ref, waves)
        arrived = count - 1 - tick
        pulled = kept_ref[own_in_window]
        grad_ref[arrived] = -(pulled[1] * moved_ref[arrived, 0] + pulled[0] * moved_ref[arrived, 1])

    left, right = jnp.maximum(own_place - 1, 0), jnp.minimum(own_place + 1, blocks - 1)
    lane = lax.broadcasted_iota(jnp.int32, (2 * height, LANES), 1)
    has_left, has_right = own_place > 0, own_place < blocks - 1

    def cells(block):
        wave = kept_ref[block - window_start]
        return jnp.concatenate(turned(1, block, screens, (wave[0], wave[1])), axis=0)

    edge_cells = jnp.where(
        lane < LANES // 2, jnp.where(has_right, cells(right), 0.0), jnp.where(has_left, cells(left), 0.0)
    )
    done = row_product(row_matrix, jnp.concatenate([cells(own_place), edge_cells], axis=1))
    lane = lax.broadcasted_iota(jnp.int32, (height, LANES), 1)
    between = (lane >= HALO) & (lane < LANES - HALO)
    highs, lows, edges = [], [], []
    for part in range(2):
        high, low, _ = three_parts(done[part * height : (part + 1) * height, :LANES])
        highs.append(high)
        lows.append(low)
        value = done[part * height : (part + 1) * height, LANES:]
        whole_high = value.astype(jnp.bfloat16).astype(jnp.float32)
        edge = jnp.where(between, pltpu.roll(value - whole_high, LANES // 2, 1), whole_high)
        edges.append(edge.astype(jnp.bfloat16))
    pulled = col_product(jnp.concatenate(highs + edges, axis=1), jnp.concatenate(lows, axis=1), col_ref)
    grad_ref[0] = -(pulled[:, LANES:] * moved_ref[0, 0] + pulled[:, :LANES] * moved_ref[0, 1])

    for target, row in ((mine_ref, near), (theirs_ref, far)):
        for part in range(2):
            target[0, part] = left_ref[own_section, part, row]
        target[0, 2] = grad_ref[own_section, row]


def finish_kernel(mine_ref, received_ref, grad_ref, exit_ref, total_ref, sems):
    core = lax.axis_index("row")
    copies = []
    for source, item in ((mine_ref, core), (received_ref, 1 - core)):
        copies.append(pltpu.make_async_copy(source.at[:, pl.ds(0, 2)], exit_ref.at[item], sems.at[len(copies)]))
    for copy in copies:
        copy.start()
    total_ref[...] = mine_ref[:, 2] + received_ref[:, 2]
    copies.append(pltpu.make_async_copy(total_ref, grad_ref, sems.at[2]))
    copies[2].start()
    for copy in copies:
        copy.wait()


def spread(shard, axis, all_bits, reach=3):
    pieces = []
    for bits in all_bits:
        pairs = [(i, i ^ bits) for i in range(4) if abs(i - (i ^ bits)) <= reach]
        pieces.append(lax.ppermute(shard, axis, pairs))
    return pieces


def swap_cores(value):
    return lax.ppermute(value, "row", [(0, 1), (1, 0)])


def whole_field_body(phase, tilt, intensity):
    _, tile_r, tile_c = phase.shape
    count, blocks = lax.axis_size("depth"), lax.axis_size("col")
    core = lax.axis_index("row")
    height = 2 * tile_r
    vmem = pl.BlockSpec(memory_space=pltpu.VMEM)
    smem = pl.BlockSpec(memory_space=pltpu.SMEM)
    hbm = pl.BlockSpec(memory_space=pl.ANY)

    def array(*shape):
        return jax.ShapeDtypeStruct(shape, jnp.float32)

    def params(mebibytes):
        return pltpu.CompilerParams(vmem_limit_bytes=mebibytes * 2**20)

    other_depths = spread(phase, "depth", (1, 3))
    other_depths[0], measured, slab = lax.optimization_barrier((other_depths[0], intensity, phase))
    other_depths[1:1] = spread(slab, "depth", (2,))
    other_depths = jnp.concatenate(other_depths, axis=0)
    packet = jnp.concatenate([slab, measured], axis=0)
    near_own = [packet]
    for bits in range(1, blocks):
        pairs = [(i, i ^ bits) for i in range(blocks)]
        close = [(i, j) for i, j in pairs if abs(i - j) <= 1]
        if close:
            near_own.append(lax.ppermute(packet, "col", close))
        else:
            further = [(i, j) for i, j in pairs if abs(i - j) <= 2]
            arrived = lax.ppermute(slab, "col", further) if further else jnp.zeros_like(slab)
            near_own.append(jnp.concatenate([arrived, jnp.zeros_like(measured)], axis=0))
    near_own = jnp.stack(near_own)
    arriving = spread(other_depths, "col", (1, 2, 3), 2)
    row_all, col_all = jnp.asarray(row_constant(height)), jnp.asarray(col_constant())
    near_own, row_all, col_all = lax.optimization_barrier((near_own, row_all, col_all))
    half_screens = (count + 1, blocks, tile_r, tile_c)
    field = (blocks, 2, height, tile_c)
    row_matrix, col_matrix, wave, own_cos, own_sin = pl.pallas_call(
        load_kernel,
        out_shape=(
            jax.ShapeDtypeStruct(row_all.shape[1:], row_all.dtype),
            jax.ShapeDtypeStruct(col_all.shape, col_all.dtype),
            array(*field),
            array(blocks, tile_r, tile_c),
            array(blocks, tile_r, tile_c),
        ),
        in_specs=[smem, vmem, hbm, hbm],
        out_specs=(vmem,) * 5,
        scratch_shapes=[pltpu.SemaphoreType.DMA((2,))],
        compiler_params=params(4),
        cost_estimate=pl.CostEstimate(flops=10**8, bytes_accessed=2**20, transcendentals=0),
    )(tilt, near_own, row_all, col_all)
    arriving[2], near_own, row_matrix, col_matrix, wave, own_cos, own_sin = lax.optimization_barrier(
        (arriving[2], near_own, row_matrix, col_matrix, wave, own_cos, own_sin)
    )
    wanted = lax.dynamic_slice_in_dim(near_own, 2 - core, 1, 1)
    packets = jnp.concatenate([near_own[:, :1], wanted], axis=1).reshape(2 * blocks, tile_r, tile_c)
    far_first = swap_cores(jnp.concatenate([packets, arriving[2]], axis=0))
    far_second = swap_cores(jnp.concatenate([other_depths] + arriving[:2], axis=0))
    near_rest = jnp.stack([other_depths] + arriving)

    near_cos, near_sin = pl.pallas_call(
        second_kernel,
        out_shape=(array(*half_screens),) * 2,
        in_specs=[vmem] * 3,
        out_specs=(vmem,) * 2,
        compiler_params=params(8),
        cost_estimate=pl.CostEstimate(flops=5 * 10**8, bytes_accessed=2**20, transcendentals=0),
    )(near_rest, own_cos, own_sin)
    mine, theirs = pl.pallas_call(
        wave_kernel,
        out_shape=(array(1, 3, tile_r, tile_c),) * 2,
        in_specs=[vmem] * 8,
        out_specs=(vmem,) * 2,
        scratch_shapes=[pltpu.VMEM(half_screens, jnp.float32)] * 2
        + [pltpu.VMEM(field, jnp.float32)]
        + [pltpu.VMEM((count, 2, height, tile_c), jnp.float32)] * 2
        + [pltpu.VMEM((count, height, tile_c), jnp.float32)]
        + [pltpu.VMEM((blocks, height, 2 * LANES), jnp.bfloat16)] * 2,
        compiler_params=params(24),
    )(
        wave, near_cos, near_sin, near_own, far_first, far_second,
        row_matrix, col_matrix,
    )
    return pl.pallas_call(
        finish_kernel,
        out_shape=(array(*phase.shape), array(2, 1, 2, tile_r, tile_c)),
        in_specs=[vmem, vmem],
        out_specs=(hbm, hbm),
        scratch_shapes=[pltpu.VMEM(phase.shape, jnp.float32), pltpu.SemaphoreType.DMA((3,))],
        compiler_params=params(4),
    )(mine, swap_cores(theirs))


def extended_2(cells, sides, width):
    for axis, dim in sides:
        count = lax.axis_size(axis)
        ends = count - 1
        head = lax.slice_in_dim(cells, 0, width, axis=dim)
        tail = lax.slice_in_dim(cells, cells.shape[dim] - width, cells.shape[dim], axis=dim)
        cells = jnp.concatenate(
            [
                lax.ppermute(tail, axis, [(i, (i + 1) % count) for i in range(ends)]),
                cells,
                lax.ppermute(head, axis, [((i + 1) % count, i) for i in range(ends)]),
            ],
            axis=dim,
        )
    return cells


def from_behind(value, axis, steps):
    count = lax.axis_size(axis)
    leading, last = (max(0, -steps), min(count, count - steps))
    return lax.ppermute(value, axis, [(source, source + steps) for source in range(leading, last)])


def band_matrix(block_size, margin, fresnel, adjoint):
    shape_full = (block_size, block_size + 2 * margin)
    out_idx = lax.broadcasted_iota(jnp.int32, shape_full, 0)
    in_idx = lax.broadcasted_iota(jnp.int32, shape_full, 1)
    offset = (out_idx + margin - in_idx).astype(jnp.float32)
    inside = jnp.abs(offset) <= margin
    taper_dist = jnp.maximum(jnp.abs(offset) - 0.5 * margin, 0.0)
    profile = jnp.cos(jnp.pi * taper_dist / (margin + 2.0))
    weight = profile * profile / math.sqrt(fresnel)
    phase_angle = jnp.pi * offset * offset / fresnel
    real_part = jnp.where(inside, jnp.cos(phase_angle) * weight, 0.0)
    imag_part = jnp.where(inside, jnp.sin(phase_angle) * weight, 0.0)
    if adjoint:
        imag_part = -imag_part
    upper = jnp.stack([real_part, -imag_part])
    lower = jnp.stack([imag_part, real_part])
    return jnp.stack([upper, lower])


def along_rows(extended, matrix):
    pieces = [jnp.einsum("pqij,gqjc->gpic", matrix, extended, precision=lax.Precision.HIGHEST)]
    return jnp.concatenate(pieces, axis=2)


def along_cols(extended, matrix, margin):
    block_size = matrix.shape[2]
    extent = extended.shape[3] - 2 * margin
    pieces = []
    for block_start in range(0, extent, block_size):
        window = extended[:, :, :, block_start : block_start + block_size + 2 * margin]
        pieces.append(
            jnp.einsum("pqij,gqrj->gpri", matrix, window, precision=lax.Precision.HIGHEST)
        )
    return jnp.concatenate(pieces, axis=3)


def propagate(current, row_matrix, col_matrix):
    with_rows = extended_2(current, (("row", 2),), HALO)
    row_done = along_rows(with_rows, row_matrix)
    with_cols = extended_2(row_done, (("col", 3),), HALO)
    return along_cols(with_cols, col_matrix, HALO)


def transmit(screen, current, adjoint):
    screen_re = screen[0][None]
    screen_im = screen[1][None]
    if adjoint:
        screen_im = -screen_im
    real_part = screen_re * current[:, 0] - screen_im * current[:, 1]
    imag_part = screen_re * current[:, 1] + screen_im * current[:, 0]
    return jnp.stack([real_part, imag_part], axis=1)


def store_item(store, current, first_item, slice_index, active):
    begin = (first_item, jnp.int32(slice_index), jnp.int32(0), jnp.int32(0), jnp.int32(0))
    sizes_now = (current.shape[0], 1) + current.shape[1:]
    previous = lax.dynamic_slice(store, begin, sizes_now)
    fresh = jnp.where(active, current[:, None], previous)
    return lax.dynamic_update_slice(store, fresh, begin)


def staged_body(phase, tilt, intensity):
    slices, tile_r, tile_c = phase.shape
    batch_size = tilt.shape[0]
    sections = lax.axis_size("depth")
    section_index = lax.axis_index("depth")
    group_size = 1
    groups = batch_size // group_size
    tick_count = sections + groups - 1
    block_r = 64
    block_c = 128
    fwd_rows = band_matrix(block_r, HALO, FRESNEL, False)
    fwd_cols = band_matrix(block_c, HALO, FRESNEL, False)
    adj_rows = band_matrix(block_r, HALO, FRESNEL, True)
    adj_cols = band_matrix(block_c, HALO, FRESNEL, True)
    row_pos = (
        lax.axis_index("row") * tile_r + lax.broadcasted_iota(jnp.int32, (tile_r, tile_c), 0)
    ).astype(jnp.float32)
    col_pos = (
        lax.axis_index("col") * tile_c + lax.broadcasted_iota(jnp.int32, (tile_r, tile_c), 1)
    ).astype(jnp.float32)
    height = float(tile_r * lax.axis_size("row"))
    width_all = float(tile_c * lax.axis_size("col"))
    tilt_f = tilt.astype(jnp.float32)
    phase_angle = (
        2.0
        * jnp.pi
        * (
            tilt_f[:, 0, None, None] * row_pos / height
            + tilt_f[:, 1, None, None] * col_pos / width_all
        )
    )
    incident = jnp.stack([jnp.cos(phase_angle), jnp.sin(phase_angle)], axis=1)
    screens = jnp.stack([jnp.cos(phase), jnp.sin(phase)], axis=1)

    def forward_tick(tick_now, carry):
        incoming, entering, leaving = carry
        group_index = tick_now - section_index
        active = (group_index >= 0) & (group_index < groups)
        first_item = jnp.clip(group_index, 0, groups - 1) * group_size
        current = jnp.where(
            section_index == 0,
            lax.dynamic_slice_in_dim(incident, first_item, group_size, 0),
            incoming,
        )
        entering = store_item(entering, current, first_item, 0, active)
        current = propagate(transmit(screens[0], current, False), fwd_rows, fwd_cols)
        leaving = store_item(leaving, current, first_item, 0, active)
        incoming = from_behind(current, "depth", 1)
        return (incoming, entering, leaving)

    store_zero = jnp.zeros((batch_size, slices, 2, tile_r, tile_c), jnp.float32)
    start_wave = jnp.zeros((group_size, 2, tile_r, tile_c), jnp.float32)
    _, entering, leaving = lax.fori_loop(
        0, tick_count, forward_tick, (start_wave, store_zero, store_zero)
    )
    final_wave = leaving[:, slices - 1]
    misfit = final_wave[:, 0] * final_wave[:, 0] + final_wave[:, 1] * final_wave[:, 1] - intensity
    seed_adjoint = 2.0 * misfit[:, None] * final_wave

    def backward_tick(tick_now, carry):
        incoming, gradient = carry
        group_index = tick_now - (sections - 1 - section_index)
        active = (group_index >= 0) & (group_index < groups)
        first_item = jnp.clip(group_index, 0, groups - 1) * group_size
        adjoint_wave = jnp.where(
            section_index == sections - 1,
            lax.dynamic_slice_in_dim(seed_adjoint, first_item, group_size, 0),
            incoming,
        )
        for slice_index in reversed(range(slices)):
            pulled = propagate(adjoint_wave, adj_rows, adj_cols)
            arrived = lax.dynamic_slice_in_dim(entering[:, slice_index], first_item, group_size, 0)
            moved = transmit(screens[slice_index], arrived, False)
            contribution = jnp.sum(pulled[:, 1] * moved[:, 0] - pulled[:, 0] * moved[:, 1], axis=0)
            gradient = gradient.at[slice_index].add(jnp.where(active, contribution, 0.0))
            adjoint_wave = transmit(screens[slice_index], pulled, True)
        incoming = from_behind(adjoint_wave, "depth", -1)
        return (incoming, gradient)

    grad_zero = jnp.zeros((slices, tile_r, tile_c), jnp.float32)
    _, gradient = lax.fori_loop(0, tick_count, backward_tick, (start_wave, grad_zero))
    return (gradient, leaving)


def fits_whole(phase_shape, batch, mesh):
    slices, height, width = phase_shape
    rows, cols, sections = mesh.shape["row"], mesh.shape["col"], mesh.shape["depth"]
    return (
        4 * height * width * (slices + batch) <= GATHER_BUDGET
        and batch == rows == 2
        and slices == sections
        and sections == 4
        and cols == 4
        and height == LANES
        and width == cols * LANES
        and sections * HALO <= LANES
    )


def solution(mesh):
    placed = (P("depth", "row", "col"), P(), P(None, "row", "col"))

    def run(phase, tilt, intensity):
        if fits_whole(phase.shape, tilt.shape[0], mesh):
            body = whole_field_body
        else:
            body = staged_body
        return jax.shard_map(
            body,
            mesh=mesh,
            in_specs=placed,
            out_specs=(P("depth", "row", "col"), P(None, "depth", None, "row", "col")),
            check_vma=False,
        )(phase, tilt, intensity)

    return run
```

```python
import math

import jax
import jax.numpy as jnp
import numpy as np
from jax import lax
from jax.experimental import pallas as pl
from jax.experimental.pallas import tpu as pltpu
from jax.sharding import PartitionSpec as P

HALO = 32
FRESNEL = 64
LANES = 128
GATHER_BUDGET = 4 * 2**20
SIN = (
    0.9999999980536763,
    -0.1666666530009577,
    0.008333305907073658,
    -0.00019838908256358006,
    2.745822627876341e-06,
    -2.3043562782810933e-08,
)
COS = (
    0.9999999961345007,
    -0.4999999301617528,
    0.04166646215023687,
    -0.0013886696163545999,
    2.4695045482778703e-05,
    -2.5154931690000354e-07,
)


def horner(coefficients, square):
    total = jnp.full_like(square, coefficients[-1])
    for coefficient in coefficients[-2::-1]:
        total = total * square + coefficient
    return total


def cos_sin(angle):
    square = angle * angle
    return horner(COS, square), horner(SIN, square) * angle


def turn(fraction):
    half_cos, half_sin = cos_sin(fraction * math.pi)
    return half_cos * half_cos - half_sin * half_sin, 2.0 * half_cos * half_sin


def halves(value):
    high = value.astype(jnp.bfloat16)
    return high, (value - high.astype(jnp.float32)).astype(jnp.bfloat16)


def np_halves(matrix):
    high = matrix.astype(jnp.bfloat16)
    return high, (matrix - high.astype(np.float64)).astype(jnp.bfloat16)


def np_taps():
    offset = np.arange(-HALO, HALO + 1, dtype=np.float64)
    taper = np.maximum(np.abs(offset) - 0.5 * HALO, 0.0)
    weight = np.cos(np.pi * taper / (HALO + 2.0)) ** 2 / math.sqrt(FRESNEL)
    return weight * np.exp(1j * np.pi * offset * offset / FRESNEL)


def np_band(out_pos, in_pos):
    offset = out_pos[:, None] - in_pos[None, :]
    inside = np.abs(offset) <= HALO
    return np.where(inside, np_taps()[np.clip(offset, -HALO, HALO) + HALO], 0.0)


def row_constant(height):
    matrices = []
    for core in range(2):
        pos = (np.arange(height) + core * (height // 2)) % height
        band = np_band(pos, pos)
        whole = np.block([[band.real, -band.imag], [band.imag, band.real]])
        matrices.append(np.concatenate(np_halves(whole), axis=1))
    return np.stack(matrices)


def col_constant():
    lane = np.arange(LANES)
    turned = np.where((lane >= HALO) & (lane < LANES - HALO), lane ^ (LANES // 2), lane)
    edge_pos = np.where(turned < LANES // 2, turned + LANES, turned - LANES)
    parts = []
    for position in (lane, edge_pos):
        band = np_band(lane, position).T
        parts.append(np.block([[band.real, band.imag], [-band.imag, band.real]]))
    return np.concatenate(np_halves(np.concatenate(parts, axis=0)), axis=1)


def both_rows(near_ref, far_ref, where):
    return jnp.concatenate([near_ref[where], far_ref[where]], axis=0)


def turned(slice_index, block, screens, wave):
    near_cos, near_sin, far_cos, far_sin = screens
    cos = both_rows(near_cos, far_cos, (slice_index, block))
    sin = both_rows(near_sin, far_sin, (slice_index, block))
    real, imag = wave
    return cos * real - sin * imag, cos * imag + sin * real


def row_product(row_matrix, columns):
    high, low = halves(columns)
    whole, width = columns.shape
    wide = jnp.dot(
        row_matrix[:, :whole], jnp.concatenate([high, low], axis=1), preferred_element_type=jnp.float32
    )
    rest = jnp.dot(row_matrix[:, whole:], high, preferred_element_type=jnp.float32)
    return wide[:, :width] + wide[:, width:] + rest


def col_product(high, low, col_ref):
    wide = jnp.dot(high, col_ref[...], preferred_element_type=jnp.float32)
    rest = jnp.dot(low, col_ref[: 2 * LANES, : 2 * LANES], preferred_element_type=jnp.float32)
    return wide[:, : 2 * LANES] + wide[:, 2 * LANES :] + rest


def three_parts(value):
    high = value.astype(jnp.bfloat16)
    rest = value - high.astype(jnp.float32)
    return high, rest.astype(jnp.bfloat16), pltpu.roll(rest, LANES // 2, 1).astype(jnp.bfloat16)


def advance(slice_index, start, waves, screens, row_matrix, col_ref, edge_ref):
    size, height = len(waves), waves[0][0].shape[0]
    chunks = [range(place, min(place + 2, size)) for place in range(0, size, 2)]
    highs, lows = [], []
    for chunk in chunks:
        columns = [
            jnp.concatenate(turned(slice_index, start + place, screens, waves[place]), axis=0) for place in chunk
        ]
        done = row_product(row_matrix, jnp.concatenate(columns, axis=1))
        for sub, place in enumerate(chunk):
            own_high, own_low = [], []
            for part in range(2):
                value = done[part * height : (part + 1) * height, sub * LANES : (sub + 1) * LANES]
                high, low, swung = three_parts(value)
                own_high.append(high)
                own_low.append(low)
                edge = part * LANES
                if place > 0:
                    edge_ref[place - 1, :, pl.ds(edge, HALO)] = high[:, :HALO]
                    edge_ref[place - 1, :, pl.ds(edge + 2 * HALO, HALO)] = swung[:, 2 * HALO : 3 * HALO]
                if place < size - 1:
                    edge_ref[place + 1, :, pl.ds(edge + 3 * HALO, HALO)] = high[:, 3 * HALO :]
                    edge_ref[place + 1, :, pl.ds(edge + HALO, HALO)] = swung[:, HALO : 2 * HALO]
            highs.append(jnp.concatenate(own_high, axis=1))
            lows.append(jnp.concatenate(own_low, axis=1))
    results = []
    for chunk in chunks:
        rows = len(chunk) * height
        edges = edge_ref[pl.ds(chunk[0], len(chunk))].reshape(rows, 2 * LANES)
        own = jnp.concatenate([highs[place] for place in chunk], axis=0)
        total = col_product(
            jnp.concatenate([own, edges], axis=1),
            jnp.concatenate([lows[place] for place in chunk], axis=0),
            col_ref,
        )
        for sub in range(len(chunk)):
            block = total[sub * height : (sub + 1) * height]
            results.append((block[:, :LANES], block[:, LANES:]))
    return results


def clear_edge(edge_ref, place, right):
    for part in range(2):
        for begin in (0, 2 * HALO) if right else (HALO, 3 * HALO):
            cells = pl.ds(part * LANES + begin, HALO)
            edge_ref[place, :, cells] = jnp.zeros((edge_ref.shape[1], HALO), edge_ref.dtype)


def keep(wave_ref, waves):
    for place, wave in enumerate(waves):
        wave_ref[place, 0], wave_ref[place, 1] = wave


def load_kernel(tilt_ref, near_own, row_from, col_from, row_to, col_to, wave_ref, cos_ref, sin_ref, sems):
    blocks, _, height, _ = wave_ref.shape
    core = lax.axis_index("row")
    copies = [
        pltpu.make_async_copy(row_from.at[core], row_to, sems.at[0]),
        pltpu.make_async_copy(col_from, col_to, sems.at[1]),
    ]
    for copy in copies:
        copy.start()
    for col in range(blocks):
        cos_ref[col], sin_ref[col] = cos_sin(near_own[col ^ lax.axis_index("col"), 0])

    def cycles(number, position, extent):
        fraction = (number * position).astype(jnp.float32) / extent
        return turn(fraction - jnp.round(fraction))

    row = lax.broadcasted_iota(jnp.int32, (height, LANES), 0) + core * (height // 2)
    row = jnp.where(row >= height, row - height, row)
    row_cos, row_sin = cycles(tilt_ref[core, 0], row, float(height))
    for block in range(blocks):
        col_cos, col_sin = cycles(
            tilt_ref[core, 1],
            lax.broadcasted_iota(jnp.int32, (8, LANES), 1) + block * LANES,
            float(blocks * LANES),
        )
        col_cos, col_sin = col_cos[:1], col_sin[:1]
        wave_ref[block, 0] = row_cos * col_cos - row_sin * col_sin
        wave_ref[block, 1] = row_sin * col_cos + row_cos * col_sin
    for copy in copies:
        copy.wait()


def second_kernel(near_rest, own_cos, own_sin, cos_ref, sin_ref):
    blocks = own_cos.shape[0]
    count = cos_ref.shape[0] - 1
    own_section, own_place = lax.axis_index("depth"), lax.axis_index("col")

    def screens(col, carry):
        held = col ^ own_place
        cos_ref[own_section, col], sin_ref[own_section, col] = own_cos[col], own_sin[col]
        for bits in range(1, count):
            cos_ref[bits ^ own_section, col], sin_ref[bits ^ own_section, col] = cos_sin(near_rest[held, (4 - bits) % 3])
        return carry

    lax.fori_loop(0, blocks, screens, 0)
    cos_ref[count] = jnp.ones(cos_ref.shape[1:], jnp.float32)
    sin_ref[count] = jnp.zeros(cos_ref.shape[1:], jnp.float32)


def wave_kernel(
    wave_ref, near_cos, near_sin, near_own, far_first, far_second, row_ref, col_ref,
    mine_ref, theirs_ref, far_cos, far_sin, kept_ref, moved_ref, left_ref, grad_ref, even_edge, odd_edge,
):
    blocks, _, height, _ = wave_ref.shape
    count = near_cos.shape[0] - 1
    core, own_section, own_place = lax.axis_index("row"), lax.axis_index("depth"), lax.axis_index("col")
    near, far = pl.ds(0, height // 2), pl.ds(height // 2, height // 2)
    screens = (near_cos, near_sin, far_cos, far_sin)
    row_matrix = row_ref[...]
    window = min(3, blocks)
    window_start = jnp.clip(own_place - 1, 0, blocks - window)
    own_in_window = own_place - window_start
    edges = (even_edge, odd_edge)

    def far_screens(slice_index):
        bits = slice_index ^ own_section
        for col in range(blocks):
            held = col ^ own_place
            others = lax.rem(4 - bits, 3)
            in_first = (bits == 0) | (held == 3)
            place = jnp.where(bits == 0, 2 * held, 2 * blocks + others)
            angle = jnp.where(in_first, far_first[place], far_second[jnp.minimum(held, 2) * (count - 1) + others])
            far_cos[slice_index, col], far_sin[slice_index, col] = cos_sin(angle)

    for edge_ref in edges:
        clear_edge(edge_ref, 0, False)
        clear_edge(edge_ref, blocks - 1, True)
    far_cos[count] = jnp.ones(far_cos.shape[1:], jnp.float32)
    far_sin[count] = jnp.zeros(far_cos.shape[1:], jnp.float32)
    far_screens(0)

    waves = [(wave_ref[place, 0], wave_ref[place, 1]) for place in range(blocks)]
    for tick in range(count):
        entering = (wave_ref if tick == 0 else kept_ref)[own_place]
        moved_ref[tick, 0], moved_ref[tick, 1] = turned(tick, own_place, screens, (entering[0], entering[1]))
        waves = advance(tick, 0, waves, screens, row_matrix, col_ref, edges[tick % 2])
        if tick + 1 < count:
            far_screens(tick + 1)
        keep(kept_ref, waves)
        left_ref[tick] = kept_ref[own_place]

    for edge_ref in edges:
        clear_edge(edge_ref, window - 1, True)
    waves = []
    for place in range(window):
        block = window_start + place
        real, imag = kept_ref[block, 0], kept_ref[block, 1]
        held = block ^ own_place
        measured = jnp.concatenate([near_own[held, 1 + core], far_first[2 * held + 1]], axis=0)
        misfit = 2.0 * (real * real + imag * imag - measured)
        waves.append((misfit * real, -misfit * imag))

    for tick in range(count - 1):
        waves = advance(count - tick, window_start, waves, screens, row_matrix, col_ref, edges[tick % 2])
        keep(kept_ref, waves)
        arrived = count - 1 - tick
        pulled = kept_ref[own_in_window]
        grad_ref[arrived] = -(pulled[1] * moved_ref[arrived, 0] + pulled[0] * moved_ref[arrived, 1])

    left, right = jnp.maximum(own_place - 1, 0), jnp.minimum(own_place + 1, blocks - 1)
    lane = lax.broadcasted_iota(jnp.int32, (2 * height, LANES), 1)
    has_left, has_right = own_place > 0, own_place < blocks - 1

    def cells(block):
        wave = kept_ref[block - window_start]
        return jnp.concatenate(turned(1, block, screens, (wave[0], wave[1])), axis=0)

    edge_cells = jnp.where(
        lane < LANES // 2, jnp.where(has_right, cells(right), 0.0), jnp.where(has_left, cells(left), 0.0)
    )
    done = row_product(row_matrix, jnp.concatenate([cells(own_place), edge_cells], axis=1))
    lane = lax.broadcasted_iota(jnp.int32, (height, LANES), 1)
    between = (lane >= HALO) & (lane < LANES - HALO)
    highs, lows, edges = [], [], []
    for part in range(2):
        high, low, _ = three_parts(done[part * height : (part + 1) * height, :LANES])
        highs.append(high)
        lows.append(low)
        value = done[part * height : (part + 1) * height, LANES:]
        whole_high = value.astype(jnp.bfloat16).astype(jnp.float32)
        edge = jnp.where(between, pltpu.roll(value - whole_high, LANES // 2, 1), whole_high)
        edges.append(edge.astype(jnp.bfloat16))
    pulled = col_product(jnp.concatenate(highs + edges, axis=1), jnp.concatenate(lows, axis=1), col_ref)
    grad_ref[0] = -(pulled[:, LANES:] * moved_ref[0, 0] + pulled[:, :LANES] * moved_ref[0, 1])

    for target, row in ((mine_ref, near), (theirs_ref, far)):
        for part in range(2):
            target[0, part] = left_ref[own_section, part, row]
        target[0, 2] = grad_ref[own_section, row]


def finish_kernel(mine_ref, received_ref, grad_ref, exit_ref, total_ref, sems):
    core = lax.axis_index("row")
    copies = []
    for source, item in ((mine_ref, core), (received_ref, 1 - core)):
        copies.append(pltpu.make_async_copy(source.at[:, pl.ds(0, 2)], exit_ref.at[item], sems.at[len(copies)]))
    for copy in copies:
        copy.start()
    total_ref[...] = mine_ref[:, 2] + received_ref[:, 2]
    copies.append(pltpu.make_async_copy(total_ref, grad_ref, sems.at[2]))
    copies[2].start()
    for copy in copies:
        copy.wait()


def spread(shard, axis, all_bits, reach=3):
    pieces = []
    for bits in all_bits:
        pairs = [(i, i ^ bits) for i in range(4) if abs(i - (i ^ bits)) <= reach]
        pieces.append(lax.ppermute(shard, axis, pairs))
    return pieces


def swap_cores(value):
    return lax.ppermute(value, "row", [(0, 1), (1, 0)])


def whole_field_body(phase, tilt, intensity):
    _, tile_r, tile_c = phase.shape
    count, blocks = lax.axis_size("depth"), lax.axis_size("col")
    core = lax.axis_index("row")
    height = 2 * tile_r
    vmem = pl.BlockSpec(memory_space=pltpu.VMEM)
    smem = pl.BlockSpec(memory_space=pltpu.SMEM)
    hbm = pl.BlockSpec(memory_space=pl.ANY)

    def array(*shape):
        return jax.ShapeDtypeStruct(shape, jnp.float32)

    def params(mebibytes):
        return pltpu.CompilerParams(vmem_limit_bytes=mebibytes * 2**20)

    first_depth, farthest, two_away = spread(phase, "depth", (1, 3, 2))
    first_depth, measured, slab = lax.optimization_barrier((first_depth, intensity, phase))
    other_depths = [first_depth, farthest, two_away]
    other_depths = jnp.concatenate(other_depths, axis=0)
    packet = jnp.concatenate([slab, measured], axis=0)
    near_own = [packet]
    for bits in range(1, blocks):
        pairs = [(i, i ^ bits) for i in range(blocks)]
        close = [(i, j) for i, j in pairs if abs(i - j) <= 1]
        if close:
            near_own.append(lax.ppermute(packet, "col", close))
        else:
            further = [(i, j) for i, j in pairs if abs(i - j) <= 2]
            arrived = lax.ppermute(slab, "col", further) if further else jnp.zeros_like(slab)
            near_own.append(jnp.concatenate([arrived, jnp.zeros_like(measured)], axis=0))
    near_own = jnp.stack(near_own)
    arriving = spread(other_depths, "col", (1, 2, 3), 2)
    row_all, col_all = jnp.asarray(row_constant(height)), jnp.asarray(col_constant())
    near_own, row_all, col_all = lax.optimization_barrier((near_own, row_all, col_all))
    half_screens = (count + 1, blocks, tile_r, tile_c)
    field = (blocks, 2, height, tile_c)
    row_matrix, col_matrix, wave, own_cos, own_sin = pl.pallas_call(
        load_kernel,
        out_shape=(
            jax.ShapeDtypeStruct(row_all.shape[1:], row_all.dtype),
            jax.ShapeDtypeStruct(col_all.shape, col_all.dtype),
            array(*field),
            array(blocks, tile_r, tile_c),
            array(blocks, tile_r, tile_c),
        ),
        in_specs=[smem, vmem, hbm, hbm],
        out_specs=(vmem,) * 5,
        scratch_shapes=[pltpu.SemaphoreType.DMA((2,))],
        compiler_params=params(4),
        cost_estimate=pl.CostEstimate(flops=10**8, bytes_accessed=2**20, transcendentals=0),
    )(tilt, near_own, row_all, col_all)
    arriving[2], near_own, row_matrix, col_matrix, wave, own_cos, own_sin = lax.optimization_barrier(
        (arriving[2], near_own, row_matrix, col_matrix, wave, own_cos, own_sin)
    )
    wanted = lax.dynamic_slice_in_dim(near_own, 2 - core, 1, 1)
    packets = jnp.concatenate([near_own[:, :1], wanted], axis=1).reshape(2 * blocks, tile_r, tile_c)
    far_first = swap_cores(jnp.concatenate([packets, arriving[2]], axis=0))
    far_second = swap_cores(jnp.concatenate([other_depths] + arriving[:2], axis=0))
    near_rest = jnp.stack([other_depths] + arriving)

    near_cos, near_sin = pl.pallas_call(
        second_kernel,
        out_shape=(array(*half_screens),) * 2,
        in_specs=[vmem] * 3,
        out_specs=(vmem,) * 2,
        compiler_params=params(8),
        cost_estimate=pl.CostEstimate(flops=5 * 10**8, bytes_accessed=2**20, transcendentals=0),
    )(near_rest, own_cos, own_sin)
    mine, theirs = pl.pallas_call(
        wave_kernel,
        out_shape=(array(1, 3, tile_r, tile_c),) * 2,
        in_specs=[vmem] * 8,
        out_specs=(vmem,) * 2,
        scratch_shapes=[pltpu.VMEM(half_screens, jnp.float32)] * 2
        + [pltpu.VMEM(field, jnp.float32)]
        + [pltpu.VMEM((count, 2, height, tile_c), jnp.float32)] * 2
        + [pltpu.VMEM((count, height, tile_c), jnp.float32)]
        + [pltpu.VMEM((blocks, height, 2 * LANES), jnp.bfloat16)] * 2,
        compiler_params=params(24),
    )(
        wave, near_cos, near_sin, near_own, far_first, far_second,
        row_matrix, col_matrix,
    )
    return pl.pallas_call(
        finish_kernel,
        out_shape=(array(*phase.shape), array(2, 1, 2, tile_r, tile_c)),
        in_specs=[vmem, vmem],
        out_specs=(hbm, hbm),
        scratch_shapes=[pltpu.VMEM(phase.shape, jnp.float32), pltpu.SemaphoreType.DMA((3,))],
        compiler_params=params(4),
    )(mine, swap_cores(theirs))


def extended_2(cells, sides, width):
    for axis, dim in sides:
        count = lax.axis_size(axis)
        ends = count - 1
        head = lax.slice_in_dim(cells, 0, width, axis=dim)
        tail = lax.slice_in_dim(cells, cells.shape[dim] - width, cells.shape[dim], axis=dim)
        cells = jnp.concatenate(
            [
                lax.ppermute(tail, axis, [(i, (i + 1) % count) for i in range(ends)]),
                cells,
                lax.ppermute(head, axis, [((i + 1) % count, i) for i in range(ends)]),
            ],
            axis=dim,
        )
    return cells


def from_behind(value, axis, steps):
    count = lax.axis_size(axis)
    leading, last = (max(0, -steps), min(count, count - steps))
    return lax.ppermute(value, axis, [(source, source + steps) for source in range(leading, last)])


def band_matrix(block_size, margin, fresnel, adjoint):
    shape_full = (block_size, block_size + 2 * margin)
    out_idx = lax.broadcasted_iota(jnp.int32, shape_full, 0)
    in_idx = lax.broadcasted_iota(jnp.int32, shape_full, 1)
    offset = (out_idx + margin - in_idx).astype(jnp.float32)
    inside = jnp.abs(offset) <= margin
    taper_dist = jnp.maximum(jnp.abs(offset) - 0.5 * margin, 0.0)
    profile = jnp.cos(jnp.pi * taper_dist / (margin + 2.0))
    weight = profile * profile / math.sqrt(fresnel)
    phase_angle = jnp.pi * offset * offset / fresnel
    real_part = jnp.where(inside, jnp.cos(phase_angle) * weight, 0.0)
    imag_part = jnp.where(inside, jnp.sin(phase_angle) * weight, 0.0)
    if adjoint:
        imag_part = -imag_part
    upper = jnp.stack([real_part, -imag_part])
    lower = jnp.stack([imag_part, real_part])
    return jnp.stack([upper, lower])


def along_rows(extended, matrix):
    pieces = [jnp.einsum("pqij,gqjc->gpic", matrix, extended, precision=lax.Precision.HIGHEST)]
    return jnp.concatenate(pieces, axis=2)


def along_cols(extended, matrix, margin):
    block_size = matrix.shape[2]
    extent = extended.shape[3] - 2 * margin
    pieces = []
    for block_start in range(0, extent, block_size):
        window = extended[:, :, :, block_start : block_start + block_size + 2 * margin]
        pieces.append(
            jnp.einsum("pqij,gqrj->gpri", matrix, window, precision=lax.Precision.HIGHEST)
        )
    return jnp.concatenate(pieces, axis=3)


def propagate(current, row_matrix, col_matrix):
    with_rows = extended_2(current, (("row", 2),), HALO)
    row_done = along_rows(with_rows, row_matrix)
    with_cols = extended_2(row_done, (("col", 3),), HALO)
    return along_cols(with_cols, col_matrix, HALO)


def transmit(screen, current, adjoint):
    screen_re = screen[0][None]
    screen_im = screen[1][None]
    if adjoint:
        screen_im = -screen_im
    real_part = screen_re * current[:, 0] - screen_im * current[:, 1]
    imag_part = screen_re * current[:, 1] + screen_im * current[:, 0]
    return jnp.stack([real_part, imag_part], axis=1)


def store_item(store, current, first_item, slice_index, active):
    begin = (first_item, jnp.int32(slice_index), jnp.int32(0), jnp.int32(0), jnp.int32(0))
    sizes_now = (current.shape[0], 1) + current.shape[1:]
    previous = lax.dynamic_slice(store, begin, sizes_now)
    fresh = jnp.where(active, current[:, None], previous)
    return lax.dynamic_update_slice(store, fresh, begin)


def staged_body(phase, tilt, intensity):
    slices, tile_r, tile_c = phase.shape
    batch_size = tilt.shape[0]
    sections = lax.axis_size("depth")
    section_index = lax.axis_index("depth")
    group_size = 1
    groups = batch_size // group_size
    tick_count = sections + groups - 1
    block_r = 64
    block_c = 128
    fwd_rows = band_matrix(block_r, HALO, FRESNEL, False)
    fwd_cols = band_matrix(block_c, HALO, FRESNEL, False)
    adj_rows = band_matrix(block_r, HALO, FRESNEL, True)
    adj_cols = band_matrix(block_c, HALO, FRESNEL, True)
    row_pos = (
        lax.axis_index("row") * tile_r + lax.broadcasted_iota(jnp.int32, (tile_r, tile_c), 0)
    ).astype(jnp.float32)
    col_pos = (
        lax.axis_index("col") * tile_c + lax.broadcasted_iota(jnp.int32, (tile_r, tile_c), 1)
    ).astype(jnp.float32)
    height = float(tile_r * lax.axis_size("row"))
    width_all = float(tile_c * lax.axis_size("col"))
    tilt_f = tilt.astype(jnp.float32)
    phase_angle = (
        2.0
        * jnp.pi
        * (
            tilt_f[:, 0, None, None] * row_pos / height
            + tilt_f[:, 1, None, None] * col_pos / width_all
        )
    )
    incident = jnp.stack([jnp.cos(phase_angle), jnp.sin(phase_angle)], axis=1)
    screens = jnp.stack([jnp.cos(phase), jnp.sin(phase)], axis=1)

    def forward_tick(tick_now, carry):
        incoming, entering, leaving = carry
        group_index = tick_now - section_index
        active = (group_index >= 0) & (group_index < groups)
        first_item = jnp.clip(group_index, 0, groups - 1) * group_size
        current = jnp.where(
            section_index == 0,
            lax.dynamic_slice_in_dim(incident, first_item, group_size, 0),
            incoming,
        )
        entering = store_item(entering, current, first_item, 0, active)
        current = propagate(transmit(screens[0], current, False), fwd_rows, fwd_cols)
        leaving = store_item(leaving, current, first_item, 0, active)
        incoming = from_behind(current, "depth", 1)
        return (incoming, entering, leaving)

    store_zero = jnp.zeros((batch_size, slices, 2, tile_r, tile_c), jnp.float32)
    start_wave = jnp.zeros((group_size, 2, tile_r, tile_c), jnp.float32)
    _, entering, leaving = lax.fori_loop(
        0, tick_count, forward_tick, (start_wave, store_zero, store_zero)
    )
    final_wave = leaving[:, slices - 1]
    misfit = final_wave[:, 0] * final_wave[:, 0] + final_wave[:, 1] * final_wave[:, 1] - intensity
    seed_adjoint = 2.0 * misfit[:, None] * final_wave

    def backward_tick(tick_now, carry):
        incoming, gradient = carry
        group_index = tick_now - (sections - 1 - section_index)
        active = (group_index >= 0) & (group_index < groups)
        first_item = jnp.clip(group_index, 0, groups - 1) * group_size
        adjoint_wave = jnp.where(
            section_index == sections - 1,
            lax.dynamic_slice_in_dim(seed_adjoint, first_item, group_size, 0),
            incoming,
        )
        for slice_index in reversed(range(slices)):
            pulled = propagate(adjoint_wave, adj_rows, adj_cols)
            arrived = lax.dynamic_slice_in_dim(entering[:, slice_index], first_item, group_size, 0)
            moved = transmit(screens[slice_index], arrived, False)
            contribution = jnp.sum(pulled[:, 1] * moved[:, 0] - pulled[:, 0] * moved[:, 1], axis=0)
            gradient = gradient.at[slice_index].add(jnp.where(active, contribution, 0.0))
            adjoint_wave = transmit(screens[slice_index], pulled, True)
        incoming = from_behind(adjoint_wave, "depth", -1)
        return (incoming, gradient)

    grad_zero = jnp.zeros((slices, tile_r, tile_c), jnp.float32)
    _, gradient = lax.fori_loop(0, tick_count, backward_tick, (start_wave, grad_zero))
    return (gradient, leaving)


def fits_whole(phase_shape, batch, mesh):
    slices, height, width = phase_shape
    rows, cols, sections = mesh.shape["row"], mesh.shape["col"], mesh.shape["depth"]
    return (
        4 * height * width * (slices + batch) <= GATHER_BUDGET
        and batch == rows == 2
        and slices == sections
        and sections == 4
        and cols == 4
        and height == LANES
        and width == cols * LANES
        and sections * HALO <= LANES
    )


def solution(mesh):
    placed = (P("depth", "row", "col"), P(), P(None, "row", "col"))

    def run(phase, tilt, intensity):
        if fits_whole(phase.shape, tilt.shape[0], mesh):
            body = whole_field_body
        else:
            body = staged_body
        return jax.shard_map(
            body,
            mesh=mesh,
            in_specs=placed,
            out_specs=(P("depth", "row", "col"), P(None, "depth", None, "row", "col")),
            check_vma=False,
        )(phase, tilt, intensity)

    return run
```

```python
import math

import jax
import jax.numpy as jnp
import numpy as np
from jax import lax
from jax.experimental import pallas as pl
from jax.experimental.pallas import tpu as pltpu
from jax.sharding import PartitionSpec as P

HALO = 32
FRESNEL = 64
LANES = 128
GATHER_BUDGET = 4 * 2**20
SIN = (
    0.9999999980536763,
    -0.1666666530009577,
    0.008333305907073658,
    -0.00019838908256358006,
    2.745822627876341e-06,
    -2.3043562782810933e-08,
)
COS = (
    0.9999999961345007,
    -0.4999999301617528,
    0.04166646215023687,
    -0.0013886696163545999,
    2.4695045482778703e-05,
    -2.5154931690000354e-07,
)


def horner(coefficients, square):
    total = jnp.full_like(square, coefficients[-1])
    for coefficient in coefficients[-2::-1]:
        total = total * square + coefficient
    return total


def cos_sin(angle):
    square = angle * angle
    return horner(COS, square), horner(SIN, square) * angle


def turn(fraction):
    half_cos, half_sin = cos_sin(fraction * math.pi)
    return half_cos * half_cos - half_sin * half_sin, 2.0 * half_cos * half_sin


def halves(value):
    high = value.astype(jnp.bfloat16)
    return high, (value - high.astype(jnp.float32)).astype(jnp.bfloat16)


def np_halves(matrix):
    high = matrix.astype(jnp.bfloat16)
    return high, (matrix - high.astype(np.float64)).astype(jnp.bfloat16)


def np_taps():
    offset = np.arange(-HALO, HALO + 1, dtype=np.float64)
    taper = np.maximum(np.abs(offset) - 0.5 * HALO, 0.0)
    weight = np.cos(np.pi * taper / (HALO + 2.0)) ** 2 / math.sqrt(FRESNEL)
    return weight * np.exp(1j * np.pi * offset * offset / FRESNEL)


def np_band(out_pos, in_pos):
    offset = out_pos[:, None] - in_pos[None, :]
    inside = np.abs(offset) <= HALO
    return np.where(inside, np_taps()[np.clip(offset, -HALO, HALO) + HALO], 0.0)


def row_constant(height):
    matrices = []
    for core in range(2):
        pos = (np.arange(height) + core * (height // 2)) % height
        band = np_band(pos, pos)
        whole = np.block([[band.real, -band.imag], [band.imag, band.real]])
        matrices.append(np.concatenate(np_halves(whole), axis=1))
    return np.stack(matrices)


def col_constant():
    lane = np.arange(LANES)
    turned = np.where((lane >= HALO) & (lane < LANES - HALO), lane ^ (LANES // 2), lane)
    edge_pos = np.where(turned < LANES // 2, turned + LANES, turned - LANES)
    parts = []
    for position in (lane, edge_pos):
        band = np_band(lane, position).T
        parts.append(np.block([[band.real, band.imag], [-band.imag, band.real]]))
    return np.concatenate(np_halves(np.concatenate(parts, axis=0)), axis=1)


def both_rows(near_ref, far_ref, where):
    return jnp.concatenate([near_ref[where], far_ref[where]], axis=0)


def turned(slice_index, block, screens, wave):
    near_cos, near_sin, far_cos, far_sin = screens
    cos = both_rows(near_cos, far_cos, (slice_index, block))
    sin = both_rows(near_sin, far_sin, (slice_index, block))
    real, imag = wave
    return cos * real - sin * imag, cos * imag + sin * real


def row_product(row_matrix, columns):
    high, low = halves(columns)
    whole, width = columns.shape
    wide = jnp.dot(
        row_matrix[:, :whole], jnp.concatenate([high, low], axis=1), preferred_element_type=jnp.float32
    )
    rest = jnp.dot(row_matrix[:, whole:], high, preferred_element_type=jnp.float32)
    return wide[:, :width] + wide[:, width:] + rest


def col_product(high, low, col_ref):
    wide = jnp.dot(high, col_ref[...], preferred_element_type=jnp.float32)
    rest = jnp.dot(low, col_ref[: 2 * LANES, : 2 * LANES], preferred_element_type=jnp.float32)
    return wide[:, : 2 * LANES] + wide[:, 2 * LANES :] + rest


def three_parts(value):
    high = value.astype(jnp.bfloat16)
    rest = value - high.astype(jnp.float32)
    return high, rest.astype(jnp.bfloat16), pltpu.roll(rest, LANES // 2, 1).astype(jnp.bfloat16)


def advance(slice_index, start, waves, screens, row_matrix, col_ref, edge_ref):
    size, height = len(waves), waves[0][0].shape[0]
    chunks = [range(place, min(place + 2, size)) for place in range(0, size, 2)]
    highs, lows = [], []
    for chunk in chunks:
        columns = [
            jnp.concatenate(turned(slice_index, start + place, screens, waves[place]), axis=0) for place in chunk
        ]
        done = row_product(row_matrix, jnp.concatenate(columns, axis=1))
        for sub, place in enumerate(chunk):
            own_high, own_low = [], []
            for part in range(2):
                value = done[part * height : (part + 1) * height, sub * LANES : (sub + 1) * LANES]
                high, low, swung = three_parts(value)
                own_high.append(high)
                own_low.append(low)
                edge = part * LANES
                if place > 0:
                    edge_ref[place - 1, :, pl.ds(edge, HALO)] = high[:, :HALO]
                    edge_ref[place - 1, :, pl.ds(edge + 2 * HALO, HALO)] = swung[:, 2 * HALO : 3 * HALO]
                if place < size - 1:
                    edge_ref[place + 1, :, pl.ds(edge + 3 * HALO, HALO)] = high[:, 3 * HALO :]
                    edge_ref[place + 1, :, pl.ds(edge + HALO, HALO)] = swung[:, HALO : 2 * HALO]
            highs.append(jnp.concatenate(own_high, axis=1))
            lows.append(jnp.concatenate(own_low, axis=1))
    results = []
    for chunk in chunks:
        rows = len(chunk) * height
        edges = edge_ref[pl.ds(chunk[0], len(chunk))].reshape(rows, 2 * LANES)
        own = jnp.concatenate([highs[place] for place in chunk], axis=0)
        total = col_product(
            jnp.concatenate([own, edges], axis=1),
            jnp.concatenate([lows[place] for place in chunk], axis=0),
            col_ref,
        )
        for sub in range(len(chunk)):
            block = total[sub * height : (sub + 1) * height]
            results.append((block[:, :LANES], block[:, LANES:]))
    return results


def clear_edge(edge_ref, place, right):
    for part in range(2):
        for begin in (0, 2 * HALO) if right else (HALO, 3 * HALO):
            cells = pl.ds(part * LANES + begin, HALO)
            edge_ref[place, :, cells] = jnp.zeros((edge_ref.shape[1], HALO), edge_ref.dtype)


def keep(wave_ref, waves):
    for place, wave in enumerate(waves):
        wave_ref[place, 0], wave_ref[place, 1] = wave


def load_kernel(tilt_ref, near_own, row_from, col_from, row_to, col_to, wave_ref, cos_ref, sin_ref, sems):
    blocks, _, height, _ = wave_ref.shape
    core = lax.axis_index("row")
    copies = [
        pltpu.make_async_copy(row_from.at[core], row_to, sems.at[0]),
        pltpu.make_async_copy(col_from, col_to, sems.at[1]),
    ]
    for copy in copies:
        copy.start()
    for col in range(blocks):
        cos_ref[col], sin_ref[col] = cos_sin(near_own[col ^ lax.axis_index("col"), 0])

    def cycles(number, position, extent):
        fraction = (number * position).astype(jnp.float32) / extent
        return turn(fraction - jnp.round(fraction))

    row = lax.broadcasted_iota(jnp.int32, (height, LANES), 0) + core * (height // 2)
    row = jnp.where(row >= height, row - height, row)
    row_cos, row_sin = cycles(tilt_ref[core, 0], row, float(height))
    for block in range(blocks):
        col_cos, col_sin = cycles(
            tilt_ref[core, 1],
            lax.broadcasted_iota(jnp.int32, (8, LANES), 1) + block * LANES,
            float(blocks * LANES),
        )
        col_cos, col_sin = col_cos[:1], col_sin[:1]
        wave_ref[block, 0] = row_cos * col_cos - row_sin * col_sin
        wave_ref[block, 1] = row_sin * col_cos + row_cos * col_sin
    for copy in copies:
        copy.wait()


def second_kernel(near_rest, own_cos, own_sin, cos_ref, sin_ref):
    blocks = own_cos.shape[0]
    count = cos_ref.shape[0] - 1
    own_section, own_place = lax.axis_index("depth"), lax.axis_index("col")

    def screens(col, carry):
        held = col ^ own_place
        cos_ref[own_section, col], sin_ref[own_section, col] = own_cos[col], own_sin[col]
        for bits in range(1, count):
            cos_ref[bits ^ own_section, col], sin_ref[bits ^ own_section, col] = cos_sin(near_rest[held, (4 - bits) % 3])
        return carry

    lax.fori_loop(0, blocks, screens, 0)
    cos_ref[count] = jnp.ones(cos_ref.shape[1:], jnp.float32)
    sin_ref[count] = jnp.zeros(cos_ref.shape[1:], jnp.float32)


def wave_kernel(
    wave_ref, near_cos, near_sin, near_own, far_first, far_second, row_ref, col_ref,
    mine_ref, theirs_ref, far_cos, far_sin, kept_ref, moved_ref, left_ref, grad_ref, even_edge, odd_edge,
):
    blocks, _, height, _ = wave_ref.shape
    count = near_cos.shape[0] - 1
    core, own_section, own_place = lax.axis_index("row"), lax.axis_index("depth"), lax.axis_index("col")
    near, far = pl.ds(0, height // 2), pl.ds(height // 2, height // 2)
    screens = (near_cos, near_sin, far_cos, far_sin)
    row_matrix = row_ref[...]
    window = min(3, blocks)
    window_start = jnp.clip(own_place - 1, 0, blocks - window)
    own_in_window = own_place - window_start
    edges = (even_edge, odd_edge)

    def far_screens(slice_index):
        bits = slice_index ^ own_section
        for col in range(blocks):
            held = col ^ own_place
            others = lax.rem(4 - bits, 3)
            in_first = (bits == 0) | (held == 3)
            place = jnp.where(bits == 0, 2 * held, 2 * blocks + others)
            angle = jnp.where(in_first, far_first[place], far_second[jnp.minimum(held, 2) * (count - 1) + others])
            far_cos[slice_index, col], far_sin[slice_index, col] = cos_sin(angle)

    for edge_ref in edges:
        clear_edge(edge_ref, 0, False)
        clear_edge(edge_ref, blocks - 1, True)
    far_cos[count] = jnp.ones(far_cos.shape[1:], jnp.float32)
    far_sin[count] = jnp.zeros(far_cos.shape[1:], jnp.float32)
    far_screens(0)

    waves = [(wave_ref[place, 0], wave_ref[place, 1]) for place in range(blocks)]
    for tick in range(count):
        entering = (wave_ref if tick == 0 else kept_ref)[own_place]
        moved_ref[tick, 0], moved_ref[tick, 1] = turned(tick, own_place, screens, (entering[0], entering[1]))
        waves = advance(tick, 0, waves, screens, row_matrix, col_ref, edges[tick % 2])
        if tick + 1 < count:
            far_screens(tick + 1)
        keep(kept_ref, waves)
        left_ref[tick] = kept_ref[own_place]

    for edge_ref in edges:
        clear_edge(edge_ref, window - 1, True)
    waves = []
    for place in range(window):
        block = window_start + place
        real, imag = kept_ref[block, 0], kept_ref[block, 1]
        held = block ^ own_place
        measured = jnp.concatenate([near_own[held, 1 + core], far_first[2 * held + 1]], axis=0)
        misfit = 2.0 * (real * real + imag * imag - measured)
        waves.append((misfit * real, -misfit * imag))

    for tick in range(count - 1):
        waves = advance(count - tick, window_start, waves, screens, row_matrix, col_ref, edges[tick % 2])
        keep(kept_ref, waves)
        arrived = count - 1 - tick
        pulled = kept_ref[own_in_window]
        grad_ref[arrived] = -(pulled[1] * moved_ref[arrived, 0] + pulled[0] * moved_ref[arrived, 1])

    left, right = jnp.maximum(own_place - 1, 0), jnp.minimum(own_place + 1, blocks - 1)
    lane = lax.broadcasted_iota(jnp.int32, (2 * height, LANES), 1)
    has_left, has_right = own_place > 0, own_place < blocks - 1

    def cells(block):
        wave = kept_ref[block - window_start]
        return jnp.concatenate(turned(1, block, screens, (wave[0], wave[1])), axis=0)

    edge_cells = jnp.where(
        lane < LANES // 2, jnp.where(has_right, cells(right), 0.0), jnp.where(has_left, cells(left), 0.0)
    )
    done = row_product(row_matrix, jnp.concatenate([cells(own_place), edge_cells], axis=1))
    lane = lax.broadcasted_iota(jnp.int32, (height, LANES), 1)
    between = (lane >= HALO) & (lane < LANES - HALO)
    highs, lows, edges = [], [], []
    for part in range(2):
        high, low, _ = three_parts(done[part * height : (part + 1) * height, :LANES])
        highs.append(high)
        lows.append(low)
        value = done[part * height : (part + 1) * height, LANES:]
        whole_high = value.astype(jnp.bfloat16).astype(jnp.float32)
        edge = jnp.where(between, pltpu.roll(value - whole_high, LANES // 2, 1), whole_high)
        edges.append(edge.astype(jnp.bfloat16))
    pulled = col_product(jnp.concatenate(highs + edges, axis=1), jnp.concatenate(lows, axis=1), col_ref)
    grad_ref[0] = -(pulled[:, LANES:] * moved_ref[0, 0] + pulled[:, :LANES] * moved_ref[0, 1])

    for target, row in ((mine_ref, near), (theirs_ref, far)):
        for part in range(2):
            target[0, part] = left_ref[own_section, part, row]
        target[0, 2] = grad_ref[own_section, row]


def finish_kernel(mine_ref, received_ref, grad_ref, exit_ref, total_ref, sems):
    core = lax.axis_index("row")
    copies = []
    for source, item in ((mine_ref, core), (received_ref, 1 - core)):
        copies.append(pltpu.make_async_copy(source.at[:, pl.ds(0, 2)], exit_ref.at[item], sems.at[len(copies)]))
    for copy in copies:
        copy.start()
    total_ref[...] = mine_ref[:, 2] + received_ref[:, 2]
    copies.append(pltpu.make_async_copy(total_ref, grad_ref, sems.at[2]))
    copies[2].start()
    for copy in copies:
        copy.wait()


def spread(shard, axis, all_bits, reach=3):
    pieces = []
    for bits in all_bits:
        pairs = [(i, i ^ bits) for i in range(4) if abs(i - (i ^ bits)) <= reach]
        pieces.append(lax.ppermute(shard, axis, pairs))
    return pieces


def swap_cores(value):
    return lax.ppermute(value, "row", [(0, 1), (1, 0)])


def whole_field_body(phase, tilt, intensity):
    _, tile_r, tile_c = phase.shape
    count, blocks = lax.axis_size("depth"), lax.axis_size("col")
    core = lax.axis_index("row")
    height = 2 * tile_r
    vmem = pl.BlockSpec(memory_space=pltpu.VMEM)
    smem = pl.BlockSpec(memory_space=pltpu.SMEM)
    hbm = pl.BlockSpec(memory_space=pl.ANY)

    def array(*shape):
        return jax.ShapeDtypeStruct(shape, jnp.float32)

    def params(mebibytes):
        return pltpu.CompilerParams(vmem_limit_bytes=mebibytes * 2**20)

    first_depth, farthest, two_away = spread(phase, "depth", (1, 3, 2))
    first_depth, measured, slab = lax.optimization_barrier((first_depth, intensity, phase))
    other_depths = [first_depth, farthest, two_away]
    other_depths = jnp.concatenate(other_depths, axis=0)
    packet = jnp.concatenate([slab, measured], axis=0)
    near_own = [packet] + spread(packet, "col", (1, 2, 3), 2)
    near_own = jnp.stack(near_own)
    arriving = spread(other_depths, "col", (1, 2, 3), 2)
    row_all, col_all = jnp.asarray(row_constant(height)), jnp.asarray(col_constant())
    near_own, row_all, col_all = lax.optimization_barrier((near_own, row_all, col_all))
    half_screens = (count + 1, blocks, tile_r, tile_c)
    field = (blocks, 2, height, tile_c)
    row_matrix, col_matrix, wave, own_cos, own_sin = pl.pallas_call(
        load_kernel,
        out_shape=(
            jax.ShapeDtypeStruct(row_all.shape[1:], row_all.dtype),
            jax.ShapeDtypeStruct(col_all.shape, col_all.dtype),
            array(*field),
            array(blocks, tile_r, tile_c),
            array(blocks, tile_r, tile_c),
        ),
        in_specs=[smem, vmem, hbm, hbm],
        out_specs=(vmem,) * 5,
        scratch_shapes=[pltpu.SemaphoreType.DMA((2,))],
        compiler_params=params(4),
        cost_estimate=pl.CostEstimate(flops=10**8, bytes_accessed=2**20, transcendentals=0),
    )(tilt, near_own, row_all, col_all)
    arriving[2], near_own, row_matrix, col_matrix, wave, own_cos, own_sin = lax.optimization_barrier(
        (arriving[2], near_own, row_matrix, col_matrix, wave, own_cos, own_sin)
    )
    wanted = lax.dynamic_slice_in_dim(near_own, 2 - core, 1, 1)
    packets = jnp.concatenate([near_own[:, :1], wanted], axis=1).reshape(2 * blocks, tile_r, tile_c)
    far_first = swap_cores(jnp.concatenate([packets, arriving[2]], axis=0))
    far_second = swap_cores(jnp.concatenate([other_depths] + arriving[:2], axis=0))
    near_rest = jnp.stack([other_depths] + arriving)

    near_cos, near_sin = pl.pallas_call(
        second_kernel,
        out_shape=(array(*half_screens),) * 2,
        in_specs=[vmem] * 3,
        out_specs=(vmem,) * 2,
        compiler_params=params(8),
        cost_estimate=pl.CostEstimate(flops=5 * 10**8, bytes_accessed=2**20, transcendentals=0),
    )(near_rest, own_cos, own_sin)
    mine, theirs = pl.pallas_call(
        wave_kernel,
        out_shape=(array(1, 3, tile_r, tile_c),) * 2,
        in_specs=[vmem] * 8,
        out_specs=(vmem,) * 2,
        scratch_shapes=[pltpu.VMEM(half_screens, jnp.float32)] * 2
        + [pltpu.VMEM(field, jnp.float32)]
        + [pltpu.VMEM((count, 2, height, tile_c), jnp.float32)] * 2
        + [pltpu.VMEM((count, height, tile_c), jnp.float32)]
        + [pltpu.VMEM((blocks, height, 2 * LANES), jnp.bfloat16)] * 2,
        compiler_params=params(24),
    )(
        wave, near_cos, near_sin, near_own, far_first, far_second,
        row_matrix, col_matrix,
    )
    return pl.pallas_call(
        finish_kernel,
        out_shape=(array(*phase.shape), array(2, 1, 2, tile_r, tile_c)),
        in_specs=[vmem, vmem],
        out_specs=(hbm, hbm),
        scratch_shapes=[pltpu.VMEM(phase.shape, jnp.float32), pltpu.SemaphoreType.DMA((3,))],
        compiler_params=params(4),
    )(mine, swap_cores(theirs))


def extended_2(cells, sides, width):
    for axis, dim in sides:
        count = lax.axis_size(axis)
        ends = count - 1
        head = lax.slice_in_dim(cells, 0, width, axis=dim)
        tail = lax.slice_in_dim(cells, cells.shape[dim] - width, cells.shape[dim], axis=dim)
        cells = jnp.concatenate(
            [
                lax.ppermute(tail, axis, [(i, (i + 1) % count) for i in range(ends)]),
                cells,
                lax.ppermute(head, axis, [((i + 1) % count, i) for i in range(ends)]),
            ],
            axis=dim,
        )
    return cells


def from_behind(value, axis, steps):
    count = lax.axis_size(axis)
    leading, last = (max(0, -steps), min(count, count - steps))
    return lax.ppermute(value, axis, [(source, source + steps) for source in range(leading, last)])


def band_matrix(block_size, margin, fresnel, adjoint):
    shape_full = (block_size, block_size + 2 * margin)
    out_idx = lax.broadcasted_iota(jnp.int32, shape_full, 0)
    in_idx = lax.broadcasted_iota(jnp.int32, shape_full, 1)
    offset = (out_idx + margin - in_idx).astype(jnp.float32)
    inside = jnp.abs(offset) <= margin
    taper_dist = jnp.maximum(jnp.abs(offset) - 0.5 * margin, 0.0)
    profile = jnp.cos(jnp.pi * taper_dist / (margin + 2.0))
    weight = profile * profile / math.sqrt(fresnel)
    phase_angle = jnp.pi * offset * offset / fresnel
    real_part = jnp.where(inside, jnp.cos(phase_angle) * weight, 0.0)
    imag_part = jnp.where(inside, jnp.sin(phase_angle) * weight, 0.0)
    if adjoint:
        imag_part = -imag_part
    upper = jnp.stack([real_part, -imag_part])
    lower = jnp.stack([imag_part, real_part])
    return jnp.stack([upper, lower])


def along_rows(extended, matrix):
    pieces = [jnp.einsum("pqij,gqjc->gpic", matrix, extended, precision=lax.Precision.HIGHEST)]
    return jnp.concatenate(pieces, axis=2)


def along_cols(extended, matrix, margin):
    block_size = matrix.shape[2]
    extent = extended.shape[3] - 2 * margin
    pieces = []
    for block_start in range(0, extent, block_size):
        window = extended[:, :, :, block_start : block_start + block_size + 2 * margin]
        pieces.append(
            jnp.einsum("pqij,gqrj->gpri", matrix, window, precision=lax.Precision.HIGHEST)
        )
    return jnp.concatenate(pieces, axis=3)


def propagate(current, row_matrix, col_matrix):
    with_rows = extended_2(current, (("row", 2),), HALO)
    row_done = along_rows(with_rows, row_matrix)
    with_cols = extended_2(row_done, (("col", 3),), HALO)
    return along_cols(with_cols, col_matrix, HALO)


def transmit(screen, current, adjoint):
    screen_re = screen[0][None]
    screen_im = screen[1][None]
    if adjoint:
        screen_im = -screen_im
    real_part = screen_re * current[:, 0] - screen_im * current[:, 1]
    imag_part = screen_re * current[:, 1] + screen_im * current[:, 0]
    return jnp.stack([real_part, imag_part], axis=1)


def store_item(store, current, first_item, slice_index, active):
    begin = (first_item, jnp.int32(slice_index), jnp.int32(0), jnp.int32(0), jnp.int32(0))
    sizes_now = (current.shape[0], 1) + current.shape[1:]
    previous = lax.dynamic_slice(store, begin, sizes_now)
    fresh = jnp.where(active, current[:, None], previous)
    return lax.dynamic_update_slice(store, fresh, begin)


def staged_body(phase, tilt, intensity):
    slices, tile_r, tile_c = phase.shape
    batch_size = tilt.shape[0]
    sections = lax.axis_size("depth")
    section_index = lax.axis_index("depth")
    group_size = 1
    groups = batch_size // group_size
    tick_count = sections + groups - 1
    block_r = 64
    block_c = 128
    fwd_rows = band_matrix(block_r, HALO, FRESNEL, False)
    fwd_cols = band_matrix(block_c, HALO, FRESNEL, False)
    adj_rows = band_matrix(block_r, HALO, FRESNEL, True)
    adj_cols = band_matrix(block_c, HALO, FRESNEL, True)
    row_pos = (
        lax.axis_index("row") * tile_r + lax.broadcasted_iota(jnp.int32, (tile_r, tile_c), 0)
    ).astype(jnp.float32)
    col_pos = (
        lax.axis_index("col") * tile_c + lax.broadcasted_iota(jnp.int32, (tile_r, tile_c), 1)
    ).astype(jnp.float32)
    height = float(tile_r * lax.axis_size("row"))
    width_all = float(tile_c * lax.axis_size("col"))
    tilt_f = tilt.astype(jnp.float32)
    phase_angle = (
        2.0
        * jnp.pi
        * (
            tilt_f[:, 0, None, None] * row_pos / height
            + tilt_f[:, 1, None, None] * col_pos / width_all
        )
    )
    incident = jnp.stack([jnp.cos(phase_angle), jnp.sin(phase_angle)], axis=1)
    screens = jnp.stack([jnp.cos(phase), jnp.sin(phase)], axis=1)

    def forward_tick(tick_now, carry):
        incoming, entering, leaving = carry
        group_index = tick_now - section_index
        active = (group_index >= 0) & (group_index < groups)
        first_item = jnp.clip(group_index, 0, groups - 1) * group_size
        current = jnp.where(
            section_index == 0,
            lax.dynamic_slice_in_dim(incident, first_item, group_size, 0),
            incoming,
        )
        entering = store_item(entering, current, first_item, 0, active)
        current = propagate(transmit(screens[0], current, False), fwd_rows, fwd_cols)
        leaving = store_item(leaving, current, first_item, 0, active)
        incoming = from_behind(current, "depth", 1)
        return (incoming, entering, leaving)

    store_zero = jnp.zeros((batch_size, slices, 2, tile_r, tile_c), jnp.float32)
    start_wave = jnp.zeros((group_size, 2, tile_r, tile_c), jnp.float32)
    _, entering, leaving = lax.fori_loop(
        0, tick_count, forward_tick, (start_wave, store_zero, store_zero)
    )
    final_wave = leaving[:, slices - 1]
    misfit = final_wave[:, 0] * final_wave[:, 0] + final_wave[:, 1] * final_wave[:, 1] - intensity
    seed_adjoint = 2.0 * misfit[:, None] * final_wave

    def backward_tick(tick_now, carry):
        incoming, gradient = carry
        group_index = tick_now - (sections - 1 - section_index)
        active = (group_index >= 0) & (group_index < groups)
        first_item = jnp.clip(group_index, 0, groups - 1) * group_size
        adjoint_wave = jnp.where(
            section_index == sections - 1,
            lax.dynamic_slice_in_dim(seed_adjoint, first_item, group_size, 0),
            incoming,
        )
        for slice_index in reversed(range(slices)):
            pulled = propagate(adjoint_wave, adj_rows, adj_cols)
            arrived = lax.dynamic_slice_in_dim(entering[:, slice_index], first_item, group_size, 0)
            moved = transmit(screens[slice_index], arrived, False)
            contribution = jnp.sum(pulled[:, 1] * moved[:, 0] - pulled[:, 0] * moved[:, 1], axis=0)
            gradient = gradient.at[slice_index].add(jnp.where(active, contribution, 0.0))
            adjoint_wave = transmit(screens[slice_index], pulled, True)
        incoming = from_behind(adjoint_wave, "depth", -1)
        return (incoming, gradient)

    grad_zero = jnp.zeros((slices, tile_r, tile_c), jnp.float32)
    _, gradient = lax.fori_loop(0, tick_count, backward_tick, (start_wave, grad_zero))
    return (gradient, leaving)


def fits_whole(phase_shape, batch, mesh):
    slices, height, width = phase_shape
    rows, cols, sections = mesh.shape["row"], mesh.shape["col"], mesh.shape["depth"]
    return (
        4 * height * width * (slices + batch) <= GATHER_BUDGET
        and batch == rows == 2
        and slices == sections
        and sections == 4
        and cols == 4
        and height == LANES
        and width == cols * LANES
        and sections * HALO <= LANES
    )


def solution(mesh):
    placed = (P("depth", "row", "col"), P(), P(None, "row", "col"))

    def run(phase, tilt, intensity):
        if fits_whole(phase.shape, tilt.shape[0], mesh):
            body = whole_field_body
        else:
            body = staged_body
        return jax.shard_map(
            body,
            mesh=mesh,
            in_specs=placed,
            out_specs=(P("depth", "row", "col"), P(None, "depth", None, "row", "col")),
            check_vma=False,
        )(phase, tilt, intensity)

    return run
```

```python
import math

import jax
import jax.numpy as jnp
import numpy as np
from jax import lax
from jax.experimental import pallas as pl
from jax.experimental.pallas import tpu as pltpu
from jax.sharding import PartitionSpec as P

HALO = 32
FRESNEL = 64
LANES = 128
GATHER_BUDGET = 4 * 2**20
SIN = (
    0.9999999980536763,
    -0.1666666530009577,
    0.008333305907073658,
    -0.00019838908256358006,
    2.745822627876341e-06,
    -2.3043562782810933e-08,
)
COS = (
    0.9999999961345007,
    -0.4999999301617528,
    0.04166646215023687,
    -0.0013886696163545999,
    2.4695045482778703e-05,
    -2.5154931690000354e-07,
)


def horner(coefficients, square):
    total = jnp.full_like(square, coefficients[-1])
    for coefficient in coefficients[-2::-1]:
        total = total * square + coefficient
    return total


def cos_sin(angle):
    square = angle * angle
    return horner(COS, square), horner(SIN, square) * angle


def turn(fraction):
    half_cos, half_sin = cos_sin(fraction * math.pi)
    return half_cos * half_cos - half_sin * half_sin, 2.0 * half_cos * half_sin


def halves(value):
    high = value.astype(jnp.bfloat16)
    return high, (value - high.astype(jnp.float32)).astype(jnp.bfloat16)


def np_halves(matrix):
    high = matrix.astype(jnp.bfloat16)
    return high, (matrix - high.astype(np.float64)).astype(jnp.bfloat16)


def np_taps():
    offset = np.arange(-HALO, HALO + 1, dtype=np.float64)
    taper = np.maximum(np.abs(offset) - 0.5 * HALO, 0.0)
    weight = np.cos(np.pi * taper / (HALO + 2.0)) ** 2 / math.sqrt(FRESNEL)
    return weight * np.exp(1j * np.pi * offset * offset / FRESNEL)


def np_band(out_pos, in_pos):
    offset = out_pos[:, None] - in_pos[None, :]
    inside = np.abs(offset) <= HALO
    return np.where(inside, np_taps()[np.clip(offset, -HALO, HALO) + HALO], 0.0)


def row_constant(height):
    matrices = []
    for core in range(2):
        pos = (np.arange(height) + core * (height // 2)) % height
        band = np_band(pos, pos)
        whole = np.block([[band.real, -band.imag], [band.imag, band.real]])
        matrices.append(np.concatenate(np_halves(whole), axis=1))
    return np.stack(matrices)


def col_constant():
    lane = np.arange(LANES)
    turned = np.where((lane >= HALO) & (lane < LANES - HALO), lane ^ (LANES // 2), lane)
    edge_pos = np.where(turned < LANES // 2, turned + LANES, turned - LANES)
    parts = []
    for position in (lane, edge_pos):
        band = np_band(lane, position).T
        parts.append(np.block([[band.real, band.imag], [-band.imag, band.real]]))
    return np.concatenate(np_halves(np.concatenate(parts, axis=0)), axis=1)


def both_rows(near_ref, far_ref, where):
    return jnp.concatenate([near_ref[where], far_ref[where]], axis=0)


def turned(slice_index, block, screens, wave):
    near_cos, near_sin, far_cos, far_sin = screens
    cos = both_rows(near_cos, far_cos, (slice_index, block))
    sin = both_rows(near_sin, far_sin, (slice_index, block))
    real, imag = wave
    return cos * real - sin * imag, cos * imag + sin * real


def row_products(row_matrix, chunks):
    whole = row_matrix.shape[0]
    highs, wides = [], []
    for columns in chunks:
        high, low = halves(columns)
        highs.append(high)
        wide = jnp.dot(
            row_matrix[:, :whole], jnp.concatenate([high, low], axis=1), preferred_element_type=jnp.float32
        )
        wides.append(wide[:, : columns.shape[1]] + wide[:, columns.shape[1] :])
    rest = jnp.dot(row_matrix[:, whole:], jnp.concatenate(highs, axis=1), preferred_element_type=jnp.float32)
    done, begin = [], 0
    for wide in wides:
        done.append(wide + rest[:, begin : begin + wide.shape[1]])
        begin += wide.shape[1]
    return done


def col_product(high, low, col_ref):
    wide = jnp.dot(high, col_ref[...], preferred_element_type=jnp.float32)
    rest = jnp.dot(low, col_ref[: 2 * LANES, : 2 * LANES], preferred_element_type=jnp.float32)
    return wide[:, : 2 * LANES] + wide[:, 2 * LANES :] + rest


def three_parts(value):
    high = value.astype(jnp.bfloat16)
    rest = value - high.astype(jnp.float32)
    return high, rest.astype(jnp.bfloat16), pltpu.roll(rest, LANES // 2, 1).astype(jnp.bfloat16)


def advance(slice_index, start, waves, screens, row_matrix, col_ref, edge_ref):
    size, height = len(waves), waves[0][0].shape[0]
    chunks = [range(place, min(place + 2, size)) for place in range(0, size, 2)]
    highs, lows = [], []
    columns = [
        jnp.concatenate(
            [jnp.concatenate(turned(slice_index, start + place, screens, waves[place]), axis=0) for place in chunk],
            axis=1,
        )
        for chunk in chunks
    ]
    for chunk, done in zip(chunks, row_products(row_matrix, columns)):
        for sub, place in enumerate(chunk):
            own_high, own_low = [], []
            for part in range(2):
                value = done[part * height : (part + 1) * height, sub * LANES : (sub + 1) * LANES]
                high, low, swung = three_parts(value)
                own_high.append(high)
                own_low.append(low)
                edge = part * LANES
                if place > 0:
                    edge_ref[place - 1, :, pl.ds(edge, HALO)] = high[:, :HALO]
                    edge_ref[place - 1, :, pl.ds(edge + 2 * HALO, HALO)] = swung[:, 2 * HALO : 3 * HALO]
                if place < size - 1:
                    edge_ref[place + 1, :, pl.ds(edge + 3 * HALO, HALO)] = high[:, 3 * HALO :]
                    edge_ref[place + 1, :, pl.ds(edge + HALO, HALO)] = swung[:, HALO : 2 * HALO]
            highs.append(jnp.concatenate(own_high, axis=1))
            lows.append(jnp.concatenate(own_low, axis=1))
    results = []
    for chunk in chunks:
        rows = len(chunk) * height
        edges = edge_ref[pl.ds(chunk[0], len(chunk))].reshape(rows, 2 * LANES)
        own = jnp.concatenate([highs[place] for place in chunk], axis=0)
        total = col_product(
            jnp.concatenate([own, edges], axis=1),
            jnp.concatenate([lows[place] for place in chunk], axis=0),
            col_ref,
        )
        for sub in range(len(chunk)):
            block = total[sub * height : (sub + 1) * height]
            results.append((block[:, :LANES], block[:, LANES:]))
    return results


def clear_edge(edge_ref, place, right):
    for part in range(2):
        for begin in (0, 2 * HALO) if right else (HALO, 3 * HALO):
            cells = pl.ds(part * LANES + begin, HALO)
            edge_ref[place, :, cells] = jnp.zeros((edge_ref.shape[1], HALO), edge_ref.dtype)


def keep(wave_ref, waves):
    for place, wave in enumerate(waves):
        wave_ref[place, 0], wave_ref[place, 1] = wave


def load_kernel(tilt_ref, near_own, row_from, col_from, row_to, col_to, wave_ref, cos_ref, sin_ref, sems):
    blocks, _, height, _ = wave_ref.shape
    core = lax.axis_index("row")
    copies = [
        pltpu.make_async_copy(row_from.at[core], row_to, sems.at[0]),
        pltpu.make_async_copy(col_from, col_to, sems.at[1]),
    ]
    for copy in copies:
        copy.start()
    for col in range(blocks):
        cos_ref[col], sin_ref[col] = cos_sin(near_own[col ^ lax.axis_index("col"), 0])

    def cycles(number, position, extent):
        fraction = (number * position).astype(jnp.float32) / extent
        return turn(fraction - jnp.round(fraction))

    row = lax.broadcasted_iota(jnp.int32, (height, LANES), 0) + core * (height // 2)
    row = jnp.where(row >= height, row - height, row)
    row_cos, row_sin = cycles(tilt_ref[core, 0], row, float(height))
    for block in range(blocks):
        col_cos, col_sin = cycles(
            tilt_ref[core, 1],
            lax.broadcasted_iota(jnp.int32, (8, LANES), 1) + block * LANES,
            float(blocks * LANES),
        )
        col_cos, col_sin = col_cos[:1], col_sin[:1]
        wave_ref[block, 0] = row_cos * col_cos - row_sin * col_sin
        wave_ref[block, 1] = row_sin * col_cos + row_cos * col_sin
    for copy in copies:
        copy.wait()


def second_kernel(near_rest, own_cos, own_sin, cos_ref, sin_ref):
    blocks = own_cos.shape[0]
    count = cos_ref.shape[0] - 1
    own_section, own_place = lax.axis_index("depth"), lax.axis_index("col")

    def screens(col, carry):
        held = col ^ own_place
        cos_ref[own_section, col], sin_ref[own_section, col] = own_cos[col], own_sin[col]
        for bits in range(1, count):
            cos_ref[bits ^ own_section, col], sin_ref[bits ^ own_section, col] = cos_sin(near_rest[held, (4 - bits) % 3])
        return carry

    lax.fori_loop(0, blocks, screens, 0)
    cos_ref[count] = jnp.ones(cos_ref.shape[1:], jnp.float32)
    sin_ref[count] = jnp.zeros(cos_ref.shape[1:], jnp.float32)


def wave_kernel(
    wave_ref, near_cos, near_sin, near_own, far_first, far_second, row_ref, col_ref,
    mine_ref, theirs_ref, far_cos, far_sin, kept_ref, moved_ref, left_ref, grad_ref, even_edge, odd_edge,
):
    blocks, _, height, _ = wave_ref.shape
    count = near_cos.shape[0] - 1
    core, own_section, own_place = lax.axis_index("row"), lax.axis_index("depth"), lax.axis_index("col")
    near, far = pl.ds(0, height // 2), pl.ds(height // 2, height // 2)
    screens = (near_cos, near_sin, far_cos, far_sin)
    row_matrix = row_ref[...]
    window = min(3, blocks)
    window_start = jnp.clip(own_place - 1, 0, blocks - window)
    own_in_window = own_place - window_start
    edges = (even_edge, odd_edge)

    def far_screens(slice_index):
        bits = slice_index ^ own_section
        for col in range(blocks):
            held = col ^ own_place
            others = lax.rem(4 - bits, 3)
            in_first = (bits == 0) | (held == 3)
            place = jnp.where(bits == 0, 2 * held, 2 * blocks + others)
            angle = jnp.where(in_first, far_first[place], far_second[jnp.minimum(held, 2) * (count - 1) + others])
            far_cos[slice_index, col], far_sin[slice_index, col] = cos_sin(angle)

    for edge_ref in edges:
        clear_edge(edge_ref, 0, False)
        clear_edge(edge_ref, blocks - 1, True)
    far_cos[count] = jnp.ones(far_cos.shape[1:], jnp.float32)
    far_sin[count] = jnp.zeros(far_cos.shape[1:], jnp.float32)
    far_screens(0)

    waves = [(wave_ref[place, 0], wave_ref[place, 1]) for place in range(blocks)]
    for tick in range(count):
        entering = (wave_ref if tick == 0 else kept_ref)[own_place]
        moved_ref[tick, 0], moved_ref[tick, 1] = turned(tick, own_place, screens, (entering[0], entering[1]))
        waves = advance(tick, 0, waves, screens, row_matrix, col_ref, edges[tick % 2])
        if tick + 1 < count:
            far_screens(tick + 1)
        keep(kept_ref, waves)
        left_ref[tick] = kept_ref[own_place]

    for edge_ref in edges:
        clear_edge(edge_ref, window - 1, True)
    waves = []
    for place in range(window):
        block = window_start + place
        real, imag = kept_ref[block, 0], kept_ref[block, 1]
        held = block ^ own_place
        measured = jnp.concatenate([near_own[held, 1 + core], far_first[2 * held + 1]], axis=0)
        misfit = 2.0 * (real * real + imag * imag - measured)
        waves.append((misfit * real, -misfit * imag))

    for tick in range(count - 1):
        waves = advance(count - tick, window_start, waves, screens, row_matrix, col_ref, edges[tick % 2])
        keep(kept_ref, waves)
        arrived = count - 1 - tick
        pulled = kept_ref[own_in_window]
        grad_ref[arrived] = -(pulled[1] * moved_ref[arrived, 0] + pulled[0] * moved_ref[arrived, 1])

    left, right = jnp.maximum(own_place - 1, 0), jnp.minimum(own_place + 1, blocks - 1)
    lane = lax.broadcasted_iota(jnp.int32, (2 * height, LANES), 1)
    has_left, has_right = own_place > 0, own_place < blocks - 1

    def cells(block):
        wave = kept_ref[block - window_start]
        return jnp.concatenate(turned(1, block, screens, (wave[0], wave[1])), axis=0)

    edge_cells = jnp.where(
        lane < LANES // 2, jnp.where(has_right, cells(right), 0.0), jnp.where(has_left, cells(left), 0.0)
    )
    done = row_products(row_matrix, [jnp.concatenate([cells(own_place), edge_cells], axis=1)])[0]
    lane = lax.broadcasted_iota(jnp.int32, (height, LANES), 1)
    between = (lane >= HALO) & (lane < LANES - HALO)
    highs, lows, edges = [], [], []
    for part in range(2):
        high, low, _ = three_parts(done[part * height : (part + 1) * height, :LANES])
        highs.append(high)
        lows.append(low)
        value = done[part * height : (part + 1) * height, LANES:]
        whole_high = value.astype(jnp.bfloat16).astype(jnp.float32)
        edge = jnp.where(between, pltpu.roll(value - whole_high, LANES // 2, 1), whole_high)
        edges.append(edge.astype(jnp.bfloat16))
    pulled = col_product(jnp.concatenate(highs + edges, axis=1), jnp.concatenate(lows, axis=1), col_ref)
    grad_ref[0] = -(pulled[:, LANES:] * moved_ref[0, 0] + pulled[:, :LANES] * moved_ref[0, 1])

    for target, row in ((mine_ref, near), (theirs_ref, far)):
        for part in range(2):
            target[0, part] = left_ref[own_section, part, row]
        target[0, 2] = grad_ref[own_section, row]


def finish_kernel(mine_ref, received_ref, grad_ref, exit_ref, total_ref, sems):
    core = lax.axis_index("row")
    copies = []
    for source, item in ((mine_ref, core), (received_ref, 1 - core)):
        copies.append(pltpu.make_async_copy(source.at[:, pl.ds(0, 2)], exit_ref.at[item], sems.at[len(copies)]))
    for copy in copies:
        copy.start()
    total_ref[...] = mine_ref[:, 2] + received_ref[:, 2]
    copies.append(pltpu.make_async_copy(total_ref, grad_ref, sems.at[2]))
    copies[2].start()
    for copy in copies:
        copy.wait()


def spread(shard, axis, all_bits, reach=3):
    pieces = []
    for bits in all_bits:
        pairs = [(i, i ^ bits) for i in range(4) if abs(i - (i ^ bits)) <= reach]
        pieces.append(lax.ppermute(shard, axis, pairs))
    return pieces


def swap_cores(value):
    return lax.ppermute(value, "row", [(0, 1), (1, 0)])


def whole_field_body(phase, tilt, intensity):
    _, tile_r, tile_c = phase.shape
    count, blocks = lax.axis_size("depth"), lax.axis_size("col")
    core = lax.axis_index("row")
    height = 2 * tile_r
    vmem = pl.BlockSpec(memory_space=pltpu.VMEM)
    smem = pl.BlockSpec(memory_space=pltpu.SMEM)
    hbm = pl.BlockSpec(memory_space=pl.ANY)

    def array(*shape):
        return jax.ShapeDtypeStruct(shape, jnp.float32)

    def params(mebibytes):
        return pltpu.CompilerParams(vmem_limit_bytes=mebibytes * 2**20)

    first_depth, farthest, two_away = spread(phase, "depth", (1, 3, 2))
    first_depth, measured, slab = lax.optimization_barrier((first_depth, intensity, phase))
    other_depths = [first_depth, farthest, two_away]
    other_depths = jnp.concatenate(other_depths, axis=0)
    packet = jnp.concatenate([slab, measured], axis=0)
    near_own = [packet]
    for bits in range(1, blocks):
        pairs = [(i, i ^ bits) for i in range(blocks)]
        close = [(i, j) for i, j in pairs if abs(i - j) <= 1]
        if close:
            near_own.append(lax.ppermute(packet, "col", close))
        else:
            further = [(i, j) for i, j in pairs if abs(i - j) <= 2]
            arrived = lax.ppermute(slab, "col", further) if further else jnp.zeros_like(slab)
            near_own.append(jnp.concatenate([arrived, jnp.zeros_like(measured)], axis=0))
    near_own = jnp.stack(near_own)
    arriving = spread(other_depths, "col", (1, 2, 3), 2)
    row_all, col_all = jnp.asarray(row_constant(height)), jnp.asarray(col_constant())
    near_own, row_all, col_all = lax.optimization_barrier((near_own, row_all, col_all))
    half_screens = (count + 1, blocks, tile_r, tile_c)
    field = (blocks, 2, height, tile_c)
    row_matrix, col_matrix, wave, own_cos, own_sin = pl.pallas_call(
        load_kernel,
        out_shape=(
            jax.ShapeDtypeStruct(row_all.shape[1:], row_all.dtype),
            jax.ShapeDtypeStruct(col_all.shape, col_all.dtype),
            array(*field),
            array(blocks, tile_r, tile_c),
            array(blocks, tile_r, tile_c),
        ),
        in_specs=[smem, vmem, hbm, hbm],
        out_specs=(vmem,) * 5,
        scratch_shapes=[pltpu.SemaphoreType.DMA((2,))],
        compiler_params=params(4),
        cost_estimate=pl.CostEstimate(flops=10**8, bytes_accessed=2**20, transcendentals=0),
    )(tilt, near_own, row_all, col_all)
    arriving[2], near_own, row_matrix, col_matrix, wave, own_cos, own_sin = lax.optimization_barrier(
        (arriving[2], near_own, row_matrix, col_matrix, wave, own_cos, own_sin)
    )
    wanted = lax.dynamic_slice_in_dim(near_own, 2 - core, 1, 1)
    packets = jnp.concatenate([near_own[:, :1], wanted], axis=1).reshape(2 * blocks, tile_r, tile_c)
    far_first = swap_cores(jnp.concatenate([packets, arriving[2]], axis=0))
    far_second = swap_cores(jnp.concatenate([other_depths] + arriving[:2], axis=0))
    near_rest = jnp.stack([other_depths] + arriving)

    near_cos, near_sin = pl.pallas_call(
        second_kernel,
        out_shape=(array(*half_screens),) * 2,
        in_specs=[vmem] * 3,
        out_specs=(vmem,) * 2,
        compiler_params=params(8),
        cost_estimate=pl.CostEstimate(flops=5 * 10**8, bytes_accessed=2**20, transcendentals=0),
    )(near_rest, own_cos, own_sin)
    mine, theirs = pl.pallas_call(
        wave_kernel,
        out_shape=(array(1, 3, tile_r, tile_c),) * 2,
        in_specs=[vmem] * 8,
        out_specs=(vmem,) * 2,
        scratch_shapes=[pltpu.VMEM(half_screens, jnp.float32)] * 2
        + [pltpu.VMEM(field, jnp.float32)]
        + [pltpu.VMEM((count, 2, height, tile_c), jnp.float32)] * 2
        + [pltpu.VMEM((count, height, tile_c), jnp.float32)]
        + [pltpu.VMEM((blocks, height, 2 * LANES), jnp.bfloat16)] * 2,
        compiler_params=params(24),
    )(
        wave, near_cos, near_sin, near_own, far_first, far_second,
        row_matrix, col_matrix,
    )
    return pl.pallas_call(
        finish_kernel,
        out_shape=(array(*phase.shape), array(2, 1, 2, tile_r, tile_c)),
        in_specs=[vmem, vmem],
        out_specs=(hbm, hbm),
        scratch_shapes=[pltpu.VMEM(phase.shape, jnp.float32), pltpu.SemaphoreType.DMA((3,))],
        compiler_params=params(4),
    )(mine, swap_cores(theirs))


def extended_2(cells, sides, width):
    for axis, dim in sides:
        count = lax.axis_size(axis)
        ends = count - 1
        head = lax.slice_in_dim(cells, 0, width, axis=dim)
        tail = lax.slice_in_dim(cells, cells.shape[dim] - width, cells.shape[dim], axis=dim)
        cells = jnp.concatenate(
            [
                lax.ppermute(tail, axis, [(i, (i + 1) % count) for i in range(ends)]),
                cells,
                lax.ppermute(head, axis, [((i + 1) % count, i) for i in range(ends)]),
            ],
            axis=dim,
        )
    return cells


def from_behind(value, axis, steps):
    count = lax.axis_size(axis)
    leading, last = (max(0, -steps), min(count, count - steps))
    return lax.ppermute(value, axis, [(source, source + steps) for source in range(leading, last)])


def band_matrix(block_size, margin, fresnel, adjoint):
    shape_full = (block_size, block_size + 2 * margin)
    out_idx = lax.broadcasted_iota(jnp.int32, shape_full, 0)
    in_idx = lax.broadcasted_iota(jnp.int32, shape_full, 1)
    offset = (out_idx + margin - in_idx).astype(jnp.float32)
    inside = jnp.abs(offset) <= margin
    taper_dist = jnp.maximum(jnp.abs(offset) - 0.5 * margin, 0.0)
    profile = jnp.cos(jnp.pi * taper_dist / (margin + 2.0))
    weight = profile * profile / math.sqrt(fresnel)
    phase_angle = jnp.pi * offset * offset / fresnel
    real_part = jnp.where(inside, jnp.cos(phase_angle) * weight, 0.0)
    imag_part = jnp.where(inside, jnp.sin(phase_angle) * weight, 0.0)
    if adjoint:
        imag_part = -imag_part
    upper = jnp.stack([real_part, -imag_part])
    lower = jnp.stack([imag_part, real_part])
    return jnp.stack([upper, lower])


def along_rows(extended, matrix):
    pieces = [jnp.einsum("pqij,gqjc->gpic", matrix, extended, precision=lax.Precision.HIGHEST)]
    return jnp.concatenate(pieces, axis=2)


def along_cols(extended, matrix, margin):
    block_size = matrix.shape[2]
    extent = extended.shape[3] - 2 * margin
    pieces = []
    for block_start in range(0, extent, block_size):
        window = extended[:, :, :, block_start : block_start + block_size + 2 * margin]
        pieces.append(
            jnp.einsum("pqij,gqrj->gpri", matrix, window, precision=lax.Precision.HIGHEST)
        )
    return jnp.concatenate(pieces, axis=3)


def propagate(current, row_matrix, col_matrix):
    with_rows = extended_2(current, (("row", 2),), HALO)
    row_done = along_rows(with_rows, row_matrix)
    with_cols = extended_2(row_done, (("col", 3),), HALO)
    return along_cols(with_cols, col_matrix, HALO)


def transmit(screen, current, adjoint):
    screen_re = screen[0][None]
    screen_im = screen[1][None]
    if adjoint:
        screen_im = -screen_im
    real_part = screen_re * current[:, 0] - screen_im * current[:, 1]
    imag_part = screen_re * current[:, 1] + screen_im * current[:, 0]
    return jnp.stack([real_part, imag_part], axis=1)


def store_item(store, current, first_item, slice_index, active):
    begin = (first_item, jnp.int32(slice_index), jnp.int32(0), jnp.int32(0), jnp.int32(0))
    sizes_now = (current.shape[0], 1) + current.shape[1:]
    previous = lax.dynamic_slice(store, begin, sizes_now)
    fresh = jnp.where(active, current[:, None], previous)
    return lax.dynamic_update_slice(store, fresh, begin)


def staged_body(phase, tilt, intensity):
    slices, tile_r, tile_c = phase.shape
    batch_size = tilt.shape[0]
    sections = lax.axis_size("depth")
    section_index = lax.axis_index("depth")
    group_size = 1
    groups = batch_size // group_size
    tick_count = sections + groups - 1
    block_r = 64
    block_c = 128
    fwd_rows = band_matrix(block_r, HALO, FRESNEL, False)
    fwd_cols = band_matrix(block_c, HALO, FRESNEL, False)
    adj_rows = band_matrix(block_r, HALO, FRESNEL, True)
    adj_cols = band_matrix(block_c, HALO, FRESNEL, True)
    row_pos = (
        lax.axis_index("row") * tile_r + lax.broadcasted_iota(jnp.int32, (tile_r, tile_c), 0)
    ).astype(jnp.float32)
    col_pos = (
        lax.axis_index("col") * tile_c + lax.broadcasted_iota(jnp.int32, (tile_r, tile_c), 1)
    ).astype(jnp.float32)
    height = float(tile_r * lax.axis_size("row"))
    width_all = float(tile_c * lax.axis_size("col"))
    tilt_f = tilt.astype(jnp.float32)
    phase_angle = (
        2.0
        * jnp.pi
        * (
            tilt_f[:, 0, None, None] * row_pos / height
            + tilt_f[:, 1, None, None] * col_pos / width_all
        )
    )
    incident = jnp.stack([jnp.cos(phase_angle), jnp.sin(phase_angle)], axis=1)
    screens = jnp.stack([jnp.cos(phase), jnp.sin(phase)], axis=1)

    def forward_tick(tick_now, carry):
        incoming, entering, leaving = carry
        group_index = tick_now - section_index
        active = (group_index >= 0) & (group_index < groups)
        first_item = jnp.clip(group_index, 0, groups - 1) * group_size
        current = jnp.where(
            section_index == 0,
            lax.dynamic_slice_in_dim(incident, first_item, group_size, 0),
            incoming,
        )
        entering = store_item(entering, current, first_item, 0, active)
        current = propagate(transmit(screens[0], current, False), fwd_rows, fwd_cols)
        leaving = store_item(leaving, current, first_item, 0, active)
        incoming = from_behind(current, "depth", 1)
        return (incoming, entering, leaving)

    store_zero = jnp.zeros((batch_size, slices, 2, tile_r, tile_c), jnp.float32)
    start_wave = jnp.zeros((group_size, 2, tile_r, tile_c), jnp.float32)
    _, entering, leaving = lax.fori_loop(
        0, tick_count, forward_tick, (start_wave, store_zero, store_zero)
    )
    final_wave = leaving[:, slices - 1]
    misfit = final_wave[:, 0] * final_wave[:, 0] + final_wave[:, 1] * final_wave[:, 1] - intensity
    seed_adjoint = 2.0 * misfit[:, None] * final_wave

    def backward_tick(tick_now, carry):
        incoming, gradient = carry
        group_index = tick_now - (sections - 1 - section_index)
        active = (group_index >= 0) & (group_index < groups)
        first_item = jnp.clip(group_index, 0, groups - 1) * group_size
        adjoint_wave = jnp.where(
            section_index == sections - 1,
            lax.dynamic_slice_in_dim(seed_adjoint, first_item, group_size, 0),
            incoming,
        )
        for slice_index in reversed(range(slices)):
            pulled = propagate(adjoint_wave, adj_rows, adj_cols)
            arrived = lax.dynamic_slice_in_dim(entering[:, slice_index], first_item, group_size, 0)
            moved = transmit(screens[slice_index], arrived, False)
            contribution = jnp.sum(pulled[:, 1] * moved[:, 0] - pulled[:, 0] * moved[:, 1], axis=0)
            gradient = gradient.at[slice_index].add(jnp.where(active, contribution, 0.0))
            adjoint_wave = transmit(screens[slice_index], pulled, True)
        incoming = from_behind(adjoint_wave, "depth", -1)
        return (incoming, gradient)

    grad_zero = jnp.zeros((slices, tile_r, tile_c), jnp.float32)
    _, gradient = lax.fori_loop(0, tick_count, backward_tick, (start_wave, grad_zero))
    return (gradient, leaving)


def fits_whole(phase_shape, batch, mesh):
    slices, height, width = phase_shape
    rows, cols, sections = mesh.shape["row"], mesh.shape["col"], mesh.shape["depth"]
    return (
        4 * height * width * (slices + batch) <= GATHER_BUDGET
        and batch == rows == 2
        and slices == sections
        and sections == 4
        and cols == 4
        and height == LANES
        and width == cols * LANES
        and sections * HALO <= LANES
    )


def solution(mesh):
    placed = (P("depth", "row", "col"), P(), P(None, "row", "col"))

    def run(phase, tilt, intensity):
        if fits_whole(phase.shape, tilt.shape[0], mesh):
            body = whole_field_body
        else:
            body = staged_body
        return jax.shard_map(
            body,
            mesh=mesh,
            in_specs=placed,
            out_specs=(P("depth", "row", "col"), P(None, "depth", None, "row", "col")),
            check_vma=False,
        )(phase, tilt, intensity)

    return run
```

```python
import math

import jax
import jax.numpy as jnp
import numpy as np
from jax import lax
from jax.experimental import pallas as pl
from jax.experimental.pallas import tpu as pltpu
from jax.sharding import PartitionSpec as P

HALO = 32
FRESNEL = 64
LANES = 128
GATHER_BUDGET = 4 * 2**20
SIN = (
    0.9999999980536763,
    -0.1666666530009577,
    0.008333305907073658,
    -0.00019838908256358006,
    2.745822627876341e-06,
    -2.3043562782810933e-08,
)
COS = (
    0.9999999961345007,
    -0.4999999301617528,
    0.04166646215023687,
    -0.0013886696163545999,
    2.4695045482778703e-05,
    -2.5154931690000354e-07,
)


def horner(coefficients, square):
    total = jnp.full_like(square, coefficients[-1])
    for coefficient in coefficients[-2::-1]:
        total = total * square + coefficient
    return total


def cos_sin(angle):
    square = angle * angle
    return horner(COS, square), horner(SIN, square) * angle


def turn(fraction):
    half_cos, half_sin = cos_sin(fraction * math.pi)
    return half_cos * half_cos - half_sin * half_sin, 2.0 * half_cos * half_sin


def halves(value):
    high = value.astype(jnp.bfloat16)
    return high, (value - high.astype(jnp.float32)).astype(jnp.bfloat16)


def np_halves(matrix):
    high = matrix.astype(jnp.bfloat16)
    return high, (matrix - high.astype(np.float64)).astype(jnp.bfloat16)


def np_taps():
    offset = np.arange(-HALO, HALO + 1, dtype=np.float64)
    taper = np.maximum(np.abs(offset) - 0.5 * HALO, 0.0)
    weight = np.cos(np.pi * taper / (HALO + 2.0)) ** 2 / math.sqrt(FRESNEL)
    return weight * np.exp(1j * np.pi * offset * offset / FRESNEL)


def np_band(out_pos, in_pos):
    offset = out_pos[:, None] - in_pos[None, :]
    inside = np.abs(offset) <= HALO
    return np.where(inside, np_taps()[np.clip(offset, -HALO, HALO) + HALO], 0.0)


def row_constant(height):
    matrices = []
    for core in range(2):
        pos = (np.arange(height) + core * (height // 2)) % height
        band = np_band(pos, pos)
        whole = np.block([[band.real, -band.imag], [band.imag, band.real]])
        matrices.append(np.concatenate(np_halves(whole), axis=1))
    return np.stack(matrices)


def col_constant():
    lane = np.arange(LANES)
    turned = np.where((lane >= HALO) & (lane < LANES - HALO), lane ^ (LANES // 2), lane)
    edge_pos = np.where(turned < LANES // 2, turned + LANES, turned - LANES)
    parts = []
    for position in (lane, edge_pos):
        band = np_band(lane, position).T
        parts.append(np.block([[band.real, band.imag], [-band.imag, band.real]]))
    return np.concatenate(np_halves(np.concatenate(parts, axis=0)), axis=1)


def both_rows(near_ref, far_ref, where):
    return jnp.concatenate([near_ref[where], far_ref[where]], axis=0)


def turned(slice_index, block, screens, wave):
    near_cos, near_sin, far_cos, far_sin = screens
    cos = both_rows(near_cos, far_cos, (slice_index, block))
    sin = both_rows(near_sin, far_sin, (slice_index, block))
    real, imag = wave
    return cos * real - sin * imag, cos * imag + sin * real


def row_products(row_matrix, chunks):
    whole = row_matrix.shape[0]
    highs, wides = [], []
    for columns in chunks:
        high, low = halves(columns)
        highs.append(high)
        wide = jnp.dot(
            row_matrix[:, :whole], jnp.concatenate([high, low], axis=1), preferred_element_type=jnp.float32
        )
        wides.append(wide[:, : columns.shape[1]] + wide[:, columns.shape[1] :])
    rest = jnp.dot(row_matrix[:, whole:], jnp.concatenate(highs, axis=1), preferred_element_type=jnp.float32)
    done, begin = [], 0
    for wide in wides:
        done.append(wide + rest[:, begin : begin + wide.shape[1]])
        begin += wide.shape[1]
    return done


def col_product(high, low, col_ref):
    wide = jnp.dot(high, col_ref[...], preferred_element_type=jnp.float32)
    rest = jnp.dot(low, col_ref[: 2 * LANES, : 2 * LANES], preferred_element_type=jnp.float32)
    return wide[:, : 2 * LANES] + wide[:, 2 * LANES :] + rest


def three_parts(value):
    high = value.astype(jnp.bfloat16)
    rest = value - high.astype(jnp.float32)
    return high, rest.astype(jnp.bfloat16), pltpu.roll(rest, LANES // 2, 1).astype(jnp.bfloat16)


def advance(slice_index, start, waves, screens, row_matrix, col_ref, edge_ref, outer=None):
    size, height = len(waves), waves[0][0].shape[0]
    chunks = [range(place, min(place + 2, size)) for place in range(0, size, 2)]
    highs, lows = [], []
    columns = [
        jnp.concatenate(
            [
                jnp.concatenate(
                    waves[place] if slice_index is None else turned(slice_index, start + place, screens, waves[place]),
                    axis=0,
                )
                for place in chunk
            ],
            axis=1,
        )
        for chunk in chunks
    ]
    for chunk, done in zip(chunks, row_products(row_matrix, columns)):
        for sub, place in enumerate(chunk):
            own_high, own_low = [], []
            for part in range(2):
                value = done[part * height : (part + 1) * height, sub * LANES : (sub + 1) * LANES]
                high, low, swung = three_parts(value)
                own_high.append(high)
                own_low.append(low)
                edge = part * LANES
                if place > 0:
                    edge_ref[place - 1, :, pl.ds(edge, HALO)] = high[:, :HALO]
                    edge_ref[place - 1, :, pl.ds(edge + 2 * HALO, HALO)] = swung[:, 2 * HALO : 3 * HALO]
                if place < size - 1:
                    edge_ref[place + 1, :, pl.ds(edge + 3 * HALO, HALO)] = high[:, 3 * HALO :]
                    edge_ref[place + 1, :, pl.ds(edge + HALO, HALO)] = swung[:, HALO : 2 * HALO]
            highs.append(jnp.concatenate(own_high, axis=1))
            lows.append(jnp.concatenate(own_low, axis=1))
    edge_parts = [edge_ref[place] for place in range(size)]
    if outer is not None:
        index, high_ref, low_ref = outer
        for end, place in enumerate((0, size - 1)):
            high_ref[end], low_ref[end] = highs[place], lows[place]
        highs = highs[1:-1] + [high_ref[index]]
        lows = lows[1:-1] + [low_ref[index]]
        edge_parts = edge_parts[1:-1] + [edge_ref[index * (size - 1)]]
        chunks = [range(place, min(place + 2, size - 1)) for place in range(0, size - 1, 2)]
    results = []
    for chunk in chunks:
        edges = jnp.concatenate([edge_parts[place] for place in chunk], axis=0)
        own = jnp.concatenate([highs[place] for place in chunk], axis=0)
        total = col_product(
            jnp.concatenate([own, edges], axis=1),
            jnp.concatenate([lows[place] for place in chunk], axis=0),
            col_ref,
        )
        for sub in range(len(chunk)):
            block = total[sub * height : (sub + 1) * height]
            results.append((block[:, :LANES], block[:, LANES:]))
    return results


def clear_edge(edge_ref, place, right):
    for part in range(2):
        for begin in (0, 2 * HALO) if right else (HALO, 3 * HALO):
            cells = pl.ds(part * LANES + begin, HALO)
            edge_ref[place, :, cells] = jnp.zeros((edge_ref.shape[1], HALO), edge_ref.dtype)


def keep(wave_ref, waves):
    for place, wave in enumerate(waves):
        wave_ref[place, 0], wave_ref[place, 1] = wave


def load_kernel(tilt_ref, near_own, row_from, col_from, row_to, col_to, wave_ref, cos_ref, sin_ref, sems):
    blocks, _, height, _ = wave_ref.shape
    core = lax.axis_index("row")
    copies = [
        pltpu.make_async_copy(row_from.at[core], row_to, sems.at[0]),
        pltpu.make_async_copy(col_from, col_to, sems.at[1]),
    ]
    for copy in copies:
        copy.start()
    for col in range(blocks):
        cos_ref[col], sin_ref[col] = cos_sin(near_own[col ^ lax.axis_index("col"), 0])

    def cycles(number, position, extent):
        fraction = (number * position).astype(jnp.float32) / extent
        return turn(fraction - jnp.round(fraction))

    row = lax.broadcasted_iota(jnp.int32, (height, LANES), 0) + core * (height // 2)
    row = jnp.where(row >= height, row - height, row)
    row_cos, row_sin = cycles(tilt_ref[core, 0], row, float(height))
    for block in range(blocks):
        col_cos, col_sin = cycles(
            tilt_ref[core, 1],
            lax.broadcasted_iota(jnp.int32, (8, LANES), 1) + block * LANES,
            float(blocks * LANES),
        )
        col_cos, col_sin = col_cos[:1], col_sin[:1]
        wave_ref[block, 0] = row_cos * col_cos - row_sin * col_sin
        wave_ref[block, 1] = row_sin * col_cos + row_cos * col_sin
    for copy in copies:
        copy.wait()


def second_kernel(near_rest, own_cos, own_sin, cos_ref, sin_ref):
    blocks = own_cos.shape[0]
    count = cos_ref.shape[0]
    own_section, own_place = lax.axis_index("depth"), lax.axis_index("col")

    def screens(col, carry):
        held = col ^ own_place
        cos_ref[own_section, col], sin_ref[own_section, col] = own_cos[col], own_sin[col]
        for bits in range(1, count):
            cos_ref[bits ^ own_section, col], sin_ref[bits ^ own_section, col] = cos_sin(near_rest[held, (4 - bits) % 3])
        return carry

    lax.fori_loop(0, blocks, screens, 0)


def wave_kernel(
    wave_ref, near_cos, near_sin, near_own, far_first, far_second, row_ref, col_ref,
    mine_ref, theirs_ref, far_cos, far_sin, kept_ref, moved_ref, left_ref, grad_ref, even_edge, odd_edge,
    outer_high, outer_low,
):
    blocks, _, height, _ = wave_ref.shape
    count = near_cos.shape[0]
    core, own_section, own_place = lax.axis_index("row"), lax.axis_index("depth"), lax.axis_index("col")
    near, far = pl.ds(0, height // 2), pl.ds(height // 2, height // 2)
    screens = (near_cos, near_sin, far_cos, far_sin)
    row_matrix = row_ref[...]
    window = min(3, blocks)
    window_start = jnp.clip(own_place - 1, 0, blocks - window)
    own_in_window = own_place - window_start
    edges = (even_edge, odd_edge)

    def far_screens(slice_index):
        bits = slice_index ^ own_section
        for col in range(blocks):
            held = col ^ own_place
            others = lax.rem(4 - bits, 3)
            in_first = (bits == 0) | (held == 3)
            place = jnp.where(bits == 0, 2 * held, 2 * blocks + others)
            angle = jnp.where(in_first, far_first[place], far_second[jnp.minimum(held, 2) * (count - 1) + others])
            far_cos[slice_index, col], far_sin[slice_index, col] = cos_sin(angle)

    for edge_ref in edges:
        clear_edge(edge_ref, 0, False)
        clear_edge(edge_ref, blocks - 1, True)
    far_screens(0)

    waves = [(wave_ref[place, 0], wave_ref[place, 1]) for place in range(blocks)]
    for tick in range(count):
        entering = (wave_ref if tick == 0 else kept_ref)[own_place]
        moved_ref[tick, 0], moved_ref[tick, 1] = turned(tick, own_place, screens, (entering[0], entering[1]))
        outer = (window_start, outer_high, outer_low) if tick + 1 == count else None
        waves = advance(tick, 0, waves, screens, row_matrix, col_ref, edges[tick % 2], outer)
        if tick + 1 < count:
            far_screens(tick + 1)
            keep(kept_ref, waves)
        else:
            for place, wave in zip((1, 2, window_start * (blocks - 1)), waves):
                kept_ref[place, 0], kept_ref[place, 1] = wave
        left_ref[tick] = kept_ref[own_place]

    for edge_ref in edges:
        clear_edge(edge_ref, window - 1, True)
    waves = []
    for place in range(window):
        block = window_start + place
        real, imag = kept_ref[block, 0], kept_ref[block, 1]
        held = block ^ own_place
        measured = jnp.concatenate([near_own[held, 1 + core], far_first[2 * held + 1]], axis=0)
        misfit = 2.0 * (real * real + imag * imag - measured)
        waves.append((misfit * real, -misfit * imag))

    for tick in range(count - 1):
        passed = count - tick if tick else None
        waves = advance(passed, window_start, waves, screens, row_matrix, col_ref, edges[tick % 2])
        keep(kept_ref, waves)
        arrived = count - 1 - tick
        pulled = kept_ref[own_in_window]
        grad_ref[arrived] = -(pulled[1] * moved_ref[arrived, 0] + pulled[0] * moved_ref[arrived, 1])

    left, right = jnp.maximum(own_place - 1, 0), jnp.minimum(own_place + 1, blocks - 1)
    lane = lax.broadcasted_iota(jnp.int32, (2 * height, LANES), 1)
    has_left, has_right = own_place > 0, own_place < blocks - 1

    def cells(block):
        wave = kept_ref[block - window_start]
        return jnp.concatenate(turned(1, block, screens, (wave[0], wave[1])), axis=0)

    edge_cells = jnp.where(
        lane < LANES // 2, jnp.where(has_right, cells(right), 0.0), jnp.where(has_left, cells(left), 0.0)
    )
    done = row_products(row_matrix, [jnp.concatenate([cells(own_place), edge_cells], axis=1)])[0]
    lane = lax.broadcasted_iota(jnp.int32, (height, LANES), 1)
    between = (lane >= HALO) & (lane < LANES - HALO)
    highs, lows, edges = [], [], []
    for part in range(2):
        high, low, _ = three_parts(done[part * height : (part + 1) * height, :LANES])
        highs.append(high)
        lows.append(low)
        value = done[part * height : (part + 1) * height, LANES:]
        whole_high = value.astype(jnp.bfloat16).astype(jnp.float32)
        edge = jnp.where(between, pltpu.roll(value - whole_high, LANES // 2, 1), whole_high)
        edges.append(edge.astype(jnp.bfloat16))
    pulled = col_product(jnp.concatenate(highs + edges, axis=1), jnp.concatenate(lows, axis=1), col_ref)
    grad_ref[0] = -(pulled[:, LANES:] * moved_ref[0, 0] + pulled[:, :LANES] * moved_ref[0, 1])

    for target, row in ((mine_ref, near), (theirs_ref, far)):
        for part in range(2):
            target[0, part] = left_ref[own_section, part, row]
        target[0, 2] = grad_ref[own_section, row]


def finish_kernel(mine_ref, received_ref, grad_ref, exit_ref, total_ref, sems):
    core = lax.axis_index("row")
    copies = []
    for source, item in ((mine_ref, core), (received_ref, 1 - core)):
        copies.append(pltpu.make_async_copy(source.at[:, pl.ds(0, 2)], exit_ref.at[item], sems.at[len(copies)]))
    for copy in copies:
        copy.start()
    total_ref[...] = mine_ref[:, 2] + received_ref[:, 2]
    copies.append(pltpu.make_async_copy(total_ref, grad_ref, sems.at[2]))
    copies[2].start()
    for copy in copies:
        copy.wait()


def spread(shard, axis, all_bits, reach=3):
    pieces = []
    for bits in all_bits:
        pairs = [(i, i ^ bits) for i in range(4) if abs(i - (i ^ bits)) <= reach]
        pieces.append(lax.ppermute(shard, axis, pairs))
    return pieces


def swap_cores(value):
    return lax.ppermute(value, "row", [(0, 1), (1, 0)])


def whole_field_body(phase, tilt, intensity):
    _, tile_r, tile_c = phase.shape
    count, blocks = lax.axis_size("depth"), lax.axis_size("col")
    core = lax.axis_index("row")
    height = 2 * tile_r
    vmem = pl.BlockSpec(memory_space=pltpu.VMEM)
    smem = pl.BlockSpec(memory_space=pltpu.SMEM)
    hbm = pl.BlockSpec(memory_space=pl.ANY)

    def array(*shape):
        return jax.ShapeDtypeStruct(shape, jnp.float32)

    def params(mebibytes):
        return pltpu.CompilerParams(vmem_limit_bytes=mebibytes * 2**20)

    first_depth, farthest, two_away = spread(phase, "depth", (1, 3, 2))
    first_depth, measured, slab = lax.optimization_barrier((first_depth, intensity, phase))
    other_depths = [first_depth, farthest, two_away]
    other_depths = jnp.concatenate(other_depths, axis=0)
    packet = jnp.concatenate([slab, measured], axis=0)
    near_own = [packet]
    for bits in range(1, blocks):
        pairs = [(i, i ^ bits) for i in range(blocks)]
        close = [(i, j) for i, j in pairs if abs(i - j) <= 1]
        if close:
            near_own.append(lax.ppermute(packet, "col", close))
        else:
            further = [(i, j) for i, j in pairs if abs(i - j) <= 2]
            arrived = lax.ppermute(slab, "col", further) if further else jnp.zeros_like(slab)
            near_own.append(jnp.concatenate([arrived, jnp.zeros_like(measured)], axis=0))
    near_own = jnp.stack(near_own)
    arriving = spread(other_depths, "col", (1, 2, 3), 2)
    row_all, col_all = jnp.asarray(row_constant(height)), jnp.asarray(col_constant())
    near_own, row_all, col_all = lax.optimization_barrier((near_own, row_all, col_all))
    half_screens = (count, blocks, tile_r, tile_c)
    field = (blocks, 2, height, tile_c)
    row_matrix, col_matrix, wave, own_cos, own_sin = pl.pallas_call(
        load_kernel,
        out_shape=(
            jax.ShapeDtypeStruct(row_all.shape[1:], row_all.dtype),
            jax.ShapeDtypeStruct(col_all.shape, col_all.dtype),
            array(*field),
            array(blocks, tile_r, tile_c),
            array(blocks, tile_r, tile_c),
        ),
        in_specs=[smem, vmem, hbm, hbm],
        out_specs=(vmem,) * 5,
        scratch_shapes=[pltpu.SemaphoreType.DMA((2,))],
        compiler_params=params(4),
        cost_estimate=pl.CostEstimate(flops=10**8, bytes_accessed=2**20, transcendentals=0),
    )(tilt, near_own, row_all, col_all)
    arriving[2], near_own, row_matrix, col_matrix, wave, own_cos, own_sin = lax.optimization_barrier(
        (arriving[2], near_own, row_matrix, col_matrix, wave, own_cos, own_sin)
    )
    wanted = lax.dynamic_slice_in_dim(near_own, 2 - core, 1, 1)
    packets = jnp.concatenate([near_own[:, :1], wanted], axis=1).reshape(2 * blocks, tile_r, tile_c)
    far_first = swap_cores(jnp.concatenate([packets, arriving[2]], axis=0))
    far_second = swap_cores(jnp.concatenate([other_depths] + arriving[:2], axis=0))
    near_rest = jnp.stack([other_depths] + arriving)

    near_cos, near_sin = pl.pallas_call(
        second_kernel,
        out_shape=(array(*half_screens),) * 2,
        in_specs=[vmem] * 3,
        out_specs=(vmem,) * 2,
        compiler_params=params(8),
        cost_estimate=pl.CostEstimate(flops=5 * 10**8, bytes_accessed=2**20, transcendentals=0),
    )(near_rest, own_cos, own_sin)
    mine, theirs = pl.pallas_call(
        wave_kernel,
        out_shape=(array(1, 3, tile_r, tile_c),) * 2,
        in_specs=[vmem] * 8,
        out_specs=(vmem,) * 2,
        scratch_shapes=[pltpu.VMEM(half_screens, jnp.float32)] * 2
        + [pltpu.VMEM(field, jnp.float32)]
        + [pltpu.VMEM((count, 2, height, tile_c), jnp.float32)] * 2
        + [pltpu.VMEM((count, height, tile_c), jnp.float32)]
        + [pltpu.VMEM((blocks, height, 2 * LANES), jnp.bfloat16)] * 2
        + [pltpu.VMEM((2, height, 2 * LANES), jnp.bfloat16)] * 2,
        compiler_params=params(24),
    )(
        wave, near_cos, near_sin, near_own, far_first, far_second,
        row_matrix, col_matrix,
    )
    return pl.pallas_call(
        finish_kernel,
        out_shape=(array(*phase.shape), array(2, 1, 2, tile_r, tile_c)),
        in_specs=[vmem, vmem],
        out_specs=(hbm, hbm),
        scratch_shapes=[pltpu.VMEM(phase.shape, jnp.float32), pltpu.SemaphoreType.DMA((3,))],
        compiler_params=params(4),
    )(mine, swap_cores(theirs))


def extended_2(cells, sides, width):
    for axis, dim in sides:
        count = lax.axis_size(axis)
        ends = count - 1
        head = lax.slice_in_dim(cells, 0, width, axis=dim)
        tail = lax.slice_in_dim(cells, cells.shape[dim] - width, cells.shape[dim], axis=dim)
        cells = jnp.concatenate(
            [
                lax.ppermute(tail, axis, [(i, (i + 1) % count) for i in range(ends)]),
                cells,
                lax.ppermute(head, axis, [((i + 1) % count, i) for i in range(ends)]),
            ],
            axis=dim,
        )
    return cells


def from_behind(value, axis, steps):
    count = lax.axis_size(axis)
    leading, last = (max(0, -steps), min(count, count - steps))
    return lax.ppermute(value, axis, [(source, source + steps) for source in range(leading, last)])


def band_matrix(block_size, margin, fresnel, adjoint):
    shape_full = (block_size, block_size + 2 * margin)
    out_idx = lax.broadcasted_iota(jnp.int32, shape_full, 0)
    in_idx = lax.broadcasted_iota(jnp.int32, shape_full, 1)
    offset = (out_idx + margin - in_idx).astype(jnp.float32)
    inside = jnp.abs(offset) <= margin
    taper_dist = jnp.maximum(jnp.abs(offset) - 0.5 * margin, 0.0)
    profile = jnp.cos(jnp.pi * taper_dist / (margin + 2.0))
    weight = profile * profile / math.sqrt(fresnel)
    phase_angle = jnp.pi * offset * offset / fresnel
    real_part = jnp.where(inside, jnp.cos(phase_angle) * weight, 0.0)
    imag_part = jnp.where(inside, jnp.sin(phase_angle) * weight, 0.0)
    if adjoint:
        imag_part = -imag_part
    upper = jnp.stack([real_part, -imag_part])
    lower = jnp.stack([imag_part, real_part])
    return jnp.stack([upper, lower])


def along_rows(extended, matrix):
    pieces = [jnp.einsum("pqij,gqjc->gpic", matrix, extended, precision=lax.Precision.HIGHEST)]
    return jnp.concatenate(pieces, axis=2)


def along_cols(extended, matrix, margin):
    block_size = matrix.shape[2]
    extent = extended.shape[3] - 2 * margin
    pieces = []
    for block_start in range(0, extent, block_size):
        window = extended[:, :, :, block_start : block_start + block_size + 2 * margin]
        pieces.append(
            jnp.einsum("pqij,gqrj->gpri", matrix, window, precision=lax.Precision.HIGHEST)
        )
    return jnp.concatenate(pieces, axis=3)


def propagate(current, row_matrix, col_matrix):
    with_rows = extended_2(current, (("row", 2),), HALO)
    row_done = along_rows(with_rows, row_matrix)
    with_cols = extended_2(row_done, (("col", 3),), HALO)
    return along_cols(with_cols, col_matrix, HALO)


def transmit(screen, current, adjoint):
    screen_re = screen[0][None]
    screen_im = screen[1][None]
    if adjoint:
        screen_im = -screen_im
    real_part = screen_re * current[:, 0] - screen_im * current[:, 1]
    imag_part = screen_re * current[:, 1] + screen_im * current[:, 0]
    return jnp.stack([real_part, imag_part], axis=1)


def store_item(store, current, first_item, slice_index, active):
    begin = (first_item, jnp.int32(slice_index), jnp.int32(0), jnp.int32(0), jnp.int32(0))
    sizes_now = (current.shape[0], 1) + current.shape[1:]
    previous = lax.dynamic_slice(store, begin, sizes_now)
    fresh = jnp.where(active, current[:, None], previous)
    return lax.dynamic_update_slice(store, fresh, begin)


def staged_body(phase, tilt, intensity):
    slices, tile_r, tile_c = phase.shape
    batch_size = tilt.shape[0]
    sections = lax.axis_size("depth")
    section_index = lax.axis_index("depth")
    group_size = 1
    groups = batch_size // group_size
    tick_count = sections + groups - 1
    block_r = 64
    block_c = 128
    fwd_rows = band_matrix(block_r, HALO, FRESNEL, False)
    fwd_cols = band_matrix(block_c, HALO, FRESNEL, False)
    adj_rows = band_matrix(block_r, HALO, FRESNEL, True)
    adj_cols = band_matrix(block_c, HALO, FRESNEL, True)
    row_pos = (
        lax.axis_index("row") * tile_r + lax.broadcasted_iota(jnp.int32, (tile_r, tile_c), 0)
    ).astype(jnp.float32)
    col_pos = (
        lax.axis_index("col") * tile_c + lax.broadcasted_iota(jnp.int32, (tile_r, tile_c), 1)
    ).astype(jnp.float32)
    height = float(tile_r * lax.axis_size("row"))
    width_all = float(tile_c * lax.axis_size("col"))
    tilt_f = tilt.astype(jnp.float32)
    phase_angle = (
        2.0
        * jnp.pi
        * (
            tilt_f[:, 0, None, None] * row_pos / height
            + tilt_f[:, 1, None, None] * col_pos / width_all
        )
    )
    incident = jnp.stack([jnp.cos(phase_angle), jnp.sin(phase_angle)], axis=1)
    screens = jnp.stack([jnp.cos(phase), jnp.sin(phase)], axis=1)

    def forward_tick(tick_now, carry):
        incoming, entering, leaving = carry
        group_index = tick_now - section_index
        active = (group_index >= 0) & (group_index < groups)
        first_item = jnp.clip(group_index, 0, groups - 1) * group_size
        current = jnp.where(
            section_index == 0,
            lax.dynamic_slice_in_dim(incident, first_item, group_size, 0),
            incoming,
        )
        entering = store_item(entering, current, first_item, 0, active)
        current = propagate(transmit(screens[0], current, False), fwd_rows, fwd_cols)
        leaving = store_item(leaving, current, first_item, 0, active)
        incoming = from_behind(current, "depth", 1)
        return (incoming, entering, leaving)

    store_zero = jnp.zeros((batch_size, slices, 2, tile_r, tile_c), jnp.float32)
    start_wave = jnp.zeros((group_size, 2, tile_r, tile_c), jnp.float32)
    _, entering, leaving = lax.fori_loop(
        0, tick_count, forward_tick, (start_wave, store_zero, store_zero)
    )
    final_wave = leaving[:, slices - 1]
    misfit = final_wave[:, 0] * final_wave[:, 0] + final_wave[:, 1] * final_wave[:, 1] - intensity
    seed_adjoint = 2.0 * misfit[:, None] * final_wave

    def backward_tick(tick_now, carry):
        incoming, gradient = carry
        group_index = tick_now - (sections - 1 - section_index)
        active = (group_index >= 0) & (group_index < groups)
        first_item = jnp.clip(group_index, 0, groups - 1) * group_size
        adjoint_wave = jnp.where(
            section_index == sections - 1,
            lax.dynamic_slice_in_dim(seed_adjoint, first_item, group_size, 0),
            incoming,
        )
        for slice_index in reversed(range(slices)):
            pulled = propagate(adjoint_wave, adj_rows, adj_cols)
            arrived = lax.dynamic_slice_in_dim(entering[:, slice_index], first_item, group_size, 0)
            moved = transmit(screens[slice_index], arrived, False)
            contribution = jnp.sum(pulled[:, 1] * moved[:, 0] - pulled[:, 0] * moved[:, 1], axis=0)
            gradient = gradient.at[slice_index].add(jnp.where(active, contribution, 0.0))
            adjoint_wave = transmit(screens[slice_index], pulled, True)
        incoming = from_behind(adjoint_wave, "depth", -1)
        return (incoming, gradient)

    grad_zero = jnp.zeros((slices, tile_r, tile_c), jnp.float32)
    _, gradient = lax.fori_loop(0, tick_count, backward_tick, (start_wave, grad_zero))
    return (gradient, leaving)


def fits_whole(phase_shape, batch, mesh):
    slices, height, width = phase_shape
    rows, cols, sections = mesh.shape["row"], mesh.shape["col"], mesh.shape["depth"]
    return (
        4 * height * width * (slices + batch) <= GATHER_BUDGET
        and batch == rows == 2
        and slices == sections
        and sections == 4
        and cols == 4
        and height == LANES
        and width == cols * LANES
        and sections * HALO <= LANES
    )


def solution(mesh):
    placed = (P("depth", "row", "col"), P(), P(None, "row", "col"))

    def run(phase, tilt, intensity):
        if fits_whole(phase.shape, tilt.shape[0], mesh):
            body = whole_field_body
        else:
            body = staged_body
        return jax.shard_map(
            body,
            mesh=mesh,
            in_specs=placed,
            out_specs=(P("depth", "row", "col"), P(None, "depth", None, "row", "col")),
            check_vma=False,
        )(phase, tilt, intensity)

    return run
```

```python
import math

import jax
import jax.numpy as jnp
import numpy as np
from jax import lax
from jax.experimental import pallas as pl
from jax.experimental.pallas import tpu as pltpu
from jax.sharding import PartitionSpec as P

HALO = 32
FRESNEL = 64
LANES = 128
GATHER_BUDGET = 4 * 2**20
SIN = (
    0.9999999980536763,
    -0.1666666530009577,
    0.008333305907073658,
    -0.00019838908256358006,
    2.745822627876341e-06,
    -2.3043562782810933e-08,
)
COS = (
    0.9999999961345007,
    -0.4999999301617528,
    0.04166646215023687,
    -0.0013886696163545999,
    2.4695045482778703e-05,
    -2.5154931690000354e-07,
)


def horner(coefficients, square):
    total = jnp.full_like(square, coefficients[-1])
    for coefficient in coefficients[-2::-1]:
        total = total * square + coefficient
    return total


def cos_sin(angle):
    square = angle * angle
    return horner(COS, square), horner(SIN, square) * angle


def turn(fraction):
    half_cos, half_sin = cos_sin(fraction * math.pi)
    return half_cos * half_cos - half_sin * half_sin, 2.0 * half_cos * half_sin


def halves(value):
    high = value.astype(jnp.bfloat16)
    return high, (value - high.astype(jnp.float32)).astype(jnp.bfloat16)


def np_halves(matrix):
    high = matrix.astype(jnp.bfloat16)
    return high, (matrix - high.astype(np.float64)).astype(jnp.bfloat16)


def np_taps():
    offset = np.arange(-HALO, HALO + 1, dtype=np.float64)
    taper = np.maximum(np.abs(offset) - 0.5 * HALO, 0.0)
    weight = np.cos(np.pi * taper / (HALO + 2.0)) ** 2 / math.sqrt(FRESNEL)
    return weight * np.exp(1j * np.pi * offset * offset / FRESNEL)


def np_band(out_pos, in_pos):
    offset = out_pos[:, None] - in_pos[None, :]
    inside = np.abs(offset) <= HALO
    return np.where(inside, np_taps()[np.clip(offset, -HALO, HALO) + HALO], 0.0)


def row_constant(height):
    matrices = []
    for core in range(2):
        pos = (np.arange(height) + core * (height // 2)) % height
        band = np_band(pos, pos)
        whole = np.block([[band.real, -band.imag], [band.imag, band.real]])
        matrices.append(np.concatenate(np_halves(whole), axis=1))
    return np.stack(matrices)


def col_constant():
    lane = np.arange(LANES)
    turned = np.where((lane >= HALO) & (lane < LANES - HALO), lane ^ (LANES // 2), lane)
    edge_pos = np.where(turned < LANES // 2, turned + LANES, turned - LANES)
    parts = []
    for position in (lane, edge_pos):
        band = np_band(lane, position).T
        parts.append(np.block([[band.real, band.imag], [-band.imag, band.real]]))
    return np.concatenate(np_halves(np.concatenate(parts, axis=0)), axis=1)


def both_rows(near_ref, far_ref, where):
    return jnp.concatenate([near_ref[where], far_ref[where]], axis=0)


def turned(slice_index, block, screens, wave):
    near_cos, near_sin, far_cos, far_sin = screens
    cos = both_rows(near_cos, far_cos, (slice_index, block))
    sin = both_rows(near_sin, far_sin, (slice_index, block))
    real, imag = wave
    return cos * real - sin * imag, cos * imag + sin * real


def row_products(row_matrix, chunks):
    whole = row_matrix.shape[0]
    highs, wides = [], []
    for columns in chunks:
        high, low = halves(columns)
        highs.append(high)
        wide = jnp.dot(
            row_matrix[:, :whole], jnp.concatenate([high, low], axis=1), preferred_element_type=jnp.float32
        )
        wides.append(wide[:, : columns.shape[1]] + wide[:, columns.shape[1] :])
    rest = jnp.dot(row_matrix[:, whole:], jnp.concatenate(highs, axis=1), preferred_element_type=jnp.float32)
    done, begin = [], 0
    for wide in wides:
        done.append(wide + rest[:, begin : begin + wide.shape[1]])
        begin += wide.shape[1]
    return done


def col_product(high, low, col_ref):
    wide = jnp.dot(high, col_ref[...], preferred_element_type=jnp.float32)
    rest = jnp.dot(low, col_ref[: 2 * LANES, : 2 * LANES], preferred_element_type=jnp.float32)
    return wide[:, : 2 * LANES] + wide[:, 2 * LANES :] + rest


def three_parts(value):
    high = value.astype(jnp.bfloat16)
    rest = value - high.astype(jnp.float32)
    return high, rest.astype(jnp.bfloat16), pltpu.roll(rest, LANES // 2, 1).astype(jnp.bfloat16)


def advance(slice_index, start, waves, screens, row_matrix, col_ref, edge_ref, outer=None):
    size, height = len(waves), waves[0][0].shape[0]
    chunks = [range(place, min(place + 2, size)) for place in range(0, size, 2)]
    highs, lows = [], []
    columns = [
        jnp.concatenate(
            [
                jnp.concatenate(
                    waves[place] if slice_index is None else turned(slice_index, start + place, screens, waves[place]),
                    axis=0,
                )
                for place in chunk
            ],
            axis=1,
        )
        for chunk in chunks
    ]
    for chunk, done in zip(chunks, row_products(row_matrix, columns)):
        for sub, place in enumerate(chunk):
            own_high, own_low = [], []
            for part in range(2):
                value = done[part * height : (part + 1) * height, sub * LANES : (sub + 1) * LANES]
                high, low, swung = three_parts(value)
                own_high.append(high)
                own_low.append(low)
                edge = part * LANES
                if place > 0:
                    edge_ref[place - 1, :, pl.ds(edge, HALO)] = high[:, :HALO]
                    edge_ref[place - 1, :, pl.ds(edge + 2 * HALO, HALO)] = swung[:, 2 * HALO : 3 * HALO]
                if place < size - 1:
                    edge_ref[place + 1, :, pl.ds(edge + 3 * HALO, HALO)] = high[:, 3 * HALO :]
                    edge_ref[place + 1, :, pl.ds(edge + HALO, HALO)] = swung[:, HALO : 2 * HALO]
            highs.append(jnp.concatenate(own_high, axis=1))
            lows.append(jnp.concatenate(own_low, axis=1))
    edge_parts = [edge_ref[place] for place in range(size)]
    if outer is not None:
        index, high_ref, low_ref = outer
        for end, place in enumerate((0, size - 1)):
            high_ref[end], low_ref[end] = highs[place], lows[place]
        highs = highs[1:-1] + [high_ref[index]]
        lows = lows[1:-1] + [low_ref[index]]
        edge_parts = edge_parts[1:-1] + [edge_ref[index * (size - 1)]]
        chunks = [range(place, min(place + 2, size - 1)) for place in range(0, size - 1, 2)]
    results = []
    rest = jnp.dot(
        jnp.concatenate([lows[place] for chunk in chunks for place in chunk], axis=0),
        col_ref[: 2 * LANES, : 2 * LANES],
        preferred_element_type=jnp.float32,
    )
    for chunk in chunks:
        edges = jnp.concatenate([edge_parts[place] for place in chunk], axis=0)
        own = jnp.concatenate([highs[place] for place in chunk], axis=0)
        wide = jnp.dot(jnp.concatenate([own, edges], axis=1), col_ref[...], preferred_element_type=jnp.float32)
        total = (
            wide[:, : 2 * LANES]
            + wide[:, 2 * LANES :]
            + rest[chunk[0] * height : (chunk[0] + len(chunk)) * height]
        )
        for sub in range(len(chunk)):
            block = total[sub * height : (sub + 1) * height]
            results.append((block[:, :LANES], block[:, LANES:]))
    return results


def clear_edge(edge_ref, place, right):
    for part in range(2):
        for begin in (0, 2 * HALO) if right else (HALO, 3 * HALO):
            cells = pl.ds(part * LANES + begin, HALO)
            edge_ref[place, :, cells] = jnp.zeros((edge_ref.shape[1], HALO), edge_ref.dtype)


def keep(wave_ref, waves):
    for place, wave in enumerate(waves):
        wave_ref[place, 0], wave_ref[place, 1] = wave


def load_kernel(tilt_ref, near_own, row_from, col_from, row_to, col_to, wave_ref, cos_ref, sin_ref, sems):
    blocks, _, height, _ = wave_ref.shape
    core = lax.axis_index("row")
    copies = [
        pltpu.make_async_copy(row_from.at[core], row_to, sems.at[0]),
        pltpu.make_async_copy(col_from, col_to, sems.at[1]),
    ]
    for copy in copies:
        copy.start()
    for col in range(blocks):
        cos_ref[col], sin_ref[col] = cos_sin(near_own[col ^ lax.axis_index("col"), 0])

    def cycles(number, position, extent):
        fraction = (number * position).astype(jnp.float32) / extent
        return turn(fraction - jnp.round(fraction))

    row = lax.broadcasted_iota(jnp.int32, (height, LANES), 0) + core * (height // 2)
    row = jnp.where(row >= height, row - height, row)
    row_cos, row_sin = cycles(tilt_ref[core, 0], row, float(height))
    for block in range(blocks):
        col_cos, col_sin = cycles(
            tilt_ref[core, 1],
            lax.broadcasted_iota(jnp.int32, (8, LANES), 1) + block * LANES,
            float(blocks * LANES),
        )
        col_cos, col_sin = col_cos[:1], col_sin[:1]
        wave_ref[block, 0] = row_cos * col_cos - row_sin * col_sin
        wave_ref[block, 1] = row_sin * col_cos + row_cos * col_sin
    for copy in copies:
        copy.wait()


def second_kernel(near_rest, own_cos, own_sin, cos_ref, sin_ref):
    blocks = own_cos.shape[0]
    count = cos_ref.shape[0]
    own_section, own_place = lax.axis_index("depth"), lax.axis_index("col")

    def screens(col, carry):
        held = col ^ own_place
        cos_ref[own_section, col], sin_ref[own_section, col] = own_cos[col], own_sin[col]
        for bits in range(1, count):
            cos_ref[bits ^ own_section, col], sin_ref[bits ^ own_section, col] = cos_sin(near_rest[held, (4 - bits) % 3])
        return carry

    lax.fori_loop(0, blocks, screens, 0)


def wave_kernel(
    wave_ref, near_cos, near_sin, near_own, far_first, far_second, row_ref, col_ref,
    mine_ref, theirs_ref, far_cos, far_sin, kept_ref, moved_ref, left_ref, grad_ref, even_edge, odd_edge,
    outer_high, outer_low,
):
    blocks, _, height, _ = wave_ref.shape
    count = near_cos.shape[0]
    core, own_section, own_place = lax.axis_index("row"), lax.axis_index("depth"), lax.axis_index("col")
    near, far = pl.ds(0, height // 2), pl.ds(height // 2, height // 2)
    screens = (near_cos, near_sin, far_cos, far_sin)
    row_matrix = row_ref[...]
    window = min(3, blocks)
    window_start = jnp.clip(own_place - 1, 0, blocks - window)
    own_in_window = own_place - window_start
    edges = (even_edge, odd_edge)

    def far_screens(slice_index):
        bits = slice_index ^ own_section
        for col in range(blocks):
            held = col ^ own_place
            others = lax.rem(4 - bits, 3)
            in_first = (bits == 0) | (held == 3)
            place = jnp.where(bits == 0, 2 * held, 2 * blocks + others)
            angle = jnp.where(in_first, far_first[place], far_second[jnp.minimum(held, 2) * (count - 1) + others])
            far_cos[slice_index, col], far_sin[slice_index, col] = cos_sin(angle)

    for edge_ref in edges:
        clear_edge(edge_ref, 0, False)
        clear_edge(edge_ref, blocks - 1, True)
    far_screens(0)

    waves = [(wave_ref[place, 0], wave_ref[place, 1]) for place in range(blocks)]
    for tick in range(count):
        entering = (wave_ref if tick == 0 else kept_ref)[own_place]
        moved_ref[tick, 0], moved_ref[tick, 1] = turned(tick, own_place, screens, (entering[0], entering[1]))
        outer = (window_start, outer_high, outer_low) if tick + 1 == count else None
        waves = advance(tick, 0, waves, screens, row_matrix, col_ref, edges[tick % 2], outer)
        if tick + 1 < count:
            far_screens(tick + 1)
            keep(kept_ref, waves)
        else:
            for place, wave in zip((1, 2, window_start * (blocks - 1)), waves):
                kept_ref[place, 0], kept_ref[place, 1] = wave
        left_ref[tick] = kept_ref[own_place]

    for edge_ref in edges:
        clear_edge(edge_ref, window - 1, True)
    waves = []
    for place in range(window):
        block = window_start + place
        real, imag = kept_ref[block, 0], kept_ref[block, 1]
        held = block ^ own_place
        measured = jnp.concatenate([near_own[held, 1 + core], far_first[2 * held + 1]], axis=0)
        misfit = 2.0 * (real * real + imag * imag - measured)
        waves.append((misfit * real, -misfit * imag))

    for tick in range(count - 1):
        passed = count - tick if tick else None
        waves = advance(passed, window_start, waves, screens, row_matrix, col_ref, edges[tick % 2])
        keep(kept_ref, waves)
        arrived = count - 1 - tick
        pulled = kept_ref[own_in_window]
        grad_ref[arrived] = -(pulled[1] * moved_ref[arrived, 0] + pulled[0] * moved_ref[arrived, 1])

    left, right = jnp.maximum(own_place - 1, 0), jnp.minimum(own_place + 1, blocks - 1)
    lane = lax.broadcasted_iota(jnp.int32, (2 * height, LANES), 1)
    has_left, has_right = own_place > 0, own_place < blocks - 1

    def cells(block):
        wave = kept_ref[block - window_start]
        return jnp.concatenate(turned(1, block, screens, (wave[0], wave[1])), axis=0)

    edge_cells = jnp.where(
        lane < LANES // 2, jnp.where(has_right, cells(right), 0.0), jnp.where(has_left, cells(left), 0.0)
    )
    done = row_products(row_matrix, [jnp.concatenate([cells(own_place), edge_cells], axis=1)])[0]
    lane = lax.broadcasted_iota(jnp.int32, (height, LANES), 1)
    between = (lane >= HALO) & (lane < LANES - HALO)
    highs, lows, edges = [], [], []
    for part in range(2):
        high, low, _ = three_parts(done[part * height : (part + 1) * height, :LANES])
        highs.append(high)
        lows.append(low)
        value = done[part * height : (part + 1) * height, LANES:]
        whole_high = value.astype(jnp.bfloat16).astype(jnp.float32)
        edge = jnp.where(between, pltpu.roll(value - whole_high, LANES // 2, 1), whole_high)
        edges.append(edge.astype(jnp.bfloat16))
    pulled = col_product(jnp.concatenate(highs + edges, axis=1), jnp.concatenate(lows, axis=1), col_ref)
    grad_ref[0] = -(pulled[:, LANES:] * moved_ref[0, 0] + pulled[:, :LANES] * moved_ref[0, 1])

    for target, row in ((mine_ref, near), (theirs_ref, far)):
        for part in range(2):
            target[0, part] = left_ref[own_section, part, row]
        target[0, 2] = grad_ref[own_section, row]


def finish_kernel(mine_ref, received_ref, grad_ref, exit_ref, total_ref, sems):
    core = lax.axis_index("row")
    copies = []
    for source, item in ((mine_ref, core), (received_ref, 1 - core)):
        copies.append(pltpu.make_async_copy(source.at[:, pl.ds(0, 2)], exit_ref.at[item], sems.at[len(copies)]))
    for copy in copies:
        copy.start()
    total_ref[...] = mine_ref[:, 2] + received_ref[:, 2]
    copies.append(pltpu.make_async_copy(total_ref, grad_ref, sems.at[2]))
    copies[2].start()
    for copy in copies:
        copy.wait()


def spread(shard, axis, all_bits, reach=3):
    pieces = []
    for bits in all_bits:
        pairs = [(i, i ^ bits) for i in range(4) if abs(i - (i ^ bits)) <= reach]
        pieces.append(lax.ppermute(shard, axis, pairs))
    return pieces


def swap_cores(value):
    return lax.ppermute(value, "row", [(0, 1), (1, 0)])


def whole_field_body(phase, tilt, intensity):
    _, tile_r, tile_c = phase.shape
    count, blocks = lax.axis_size("depth"), lax.axis_size("col")
    core = lax.axis_index("row")
    height = 2 * tile_r
    vmem = pl.BlockSpec(memory_space=pltpu.VMEM)
    smem = pl.BlockSpec(memory_space=pltpu.SMEM)
    hbm = pl.BlockSpec(memory_space=pl.ANY)

    def array(*shape):
        return jax.ShapeDtypeStruct(shape, jnp.float32)

    def params(mebibytes):
        return pltpu.CompilerParams(vmem_limit_bytes=mebibytes * 2**20)

    first_depth, farthest, two_away = spread(phase, "depth", (1, 3, 2))
    first_depth, measured, slab = lax.optimization_barrier((first_depth, intensity, phase))
    other_depths = [first_depth, farthest, two_away]
    other_depths = jnp.concatenate(other_depths, axis=0)
    packet = jnp.concatenate([slab, measured], axis=0)
    near_own = [packet]
    for bits in range(1, blocks):
        pairs = [(i, i ^ bits) for i in range(blocks)]
        close = [(i, j) for i, j in pairs if abs(i - j) <= 1]
        if close:
            near_own.append(lax.ppermute(packet, "col", close))
        else:
            further = [(i, j) for i, j in pairs if abs(i - j) <= 2]
            arrived = lax.ppermute(slab, "col", further) if further else jnp.zeros_like(slab)
            near_own.append(jnp.concatenate([arrived, jnp.zeros_like(measured)], axis=0))
    near_own = jnp.stack(near_own)
    arriving = spread(other_depths, "col", (1, 2, 3), 2)
    row_all, col_all = jnp.asarray(row_constant(height)), jnp.asarray(col_constant())
    near_own, row_all, col_all = lax.optimization_barrier((near_own, row_all, col_all))
    half_screens = (count, blocks, tile_r, tile_c)
    field = (blocks, 2, height, tile_c)
    row_matrix, col_matrix, wave, own_cos, own_sin = pl.pallas_call(
        load_kernel,
        out_shape=(
            jax.ShapeDtypeStruct(row_all.shape[1:], row_all.dtype),
            jax.ShapeDtypeStruct(col_all.shape, col_all.dtype),
            array(*field),
            array(blocks, tile_r, tile_c),
            array(blocks, tile_r, tile_c),
        ),
        in_specs=[smem, vmem, hbm, hbm],
        out_specs=(vmem,) * 5,
        scratch_shapes=[pltpu.SemaphoreType.DMA((2,))],
        compiler_params=params(4),
        cost_estimate=pl.CostEstimate(flops=10**8, bytes_accessed=2**20, transcendentals=0),
    )(tilt, near_own, row_all, col_all)
    arriving[2], near_own, row_matrix, col_matrix, wave, own_cos, own_sin = lax.optimization_barrier(
        (arriving[2], near_own, row_matrix, col_matrix, wave, own_cos, own_sin)
    )
    wanted = lax.dynamic_slice_in_dim(near_own, 2 - core, 1, 1)
    packets = jnp.concatenate([near_own[:, :1], wanted], axis=1).reshape(2 * blocks, tile_r, tile_c)
    far_first = swap_cores(jnp.concatenate([packets, arriving[2]], axis=0))
    far_second = swap_cores(jnp.concatenate([other_depths] + arriving[:2], axis=0))
    near_rest = jnp.stack([other_depths] + arriving)

    near_cos, near_sin = pl.pallas_call(
        second_kernel,
        out_shape=(array(*half_screens),) * 2,
        in_specs=[vmem] * 3,
        out_specs=(vmem,) * 2,
        compiler_params=params(8),
        cost_estimate=pl.CostEstimate(flops=5 * 10**8, bytes_accessed=2**20, transcendentals=0),
    )(near_rest, own_cos, own_sin)
    mine, theirs = pl.pallas_call(
        wave_kernel,
        out_shape=(array(1, 3, tile_r, tile_c),) * 2,
        in_specs=[vmem] * 8,
        out_specs=(vmem,) * 2,
        scratch_shapes=[pltpu.VMEM(half_screens, jnp.float32)] * 2
        + [pltpu.VMEM(field, jnp.float32)]
        + [pltpu.VMEM((count, 2, height, tile_c), jnp.float32)] * 2
        + [pltpu.VMEM((count, height, tile_c), jnp.float32)]
        + [pltpu.VMEM((blocks, height, 2 * LANES), jnp.bfloat16)] * 2
        + [pltpu.VMEM((2, height, 2 * LANES), jnp.bfloat16)] * 2,
        compiler_params=params(24),
    )(
        wave, near_cos, near_sin, near_own, far_first, far_second,
        row_matrix, col_matrix,
    )
    return pl.pallas_call(
        finish_kernel,
        out_shape=(array(*phase.shape), array(2, 1, 2, tile_r, tile_c)),
        in_specs=[vmem, vmem],
        out_specs=(hbm, hbm),
        scratch_shapes=[pltpu.VMEM(phase.shape, jnp.float32), pltpu.SemaphoreType.DMA((3,))],
        compiler_params=params(4),
    )(mine, swap_cores(theirs))


def extended_2(cells, sides, width):
    for axis, dim in sides:
        count = lax.axis_size(axis)
        ends = count - 1
        head = lax.slice_in_dim(cells, 0, width, axis=dim)
        tail = lax.slice_in_dim(cells, cells.shape[dim] - width, cells.shape[dim], axis=dim)
        cells = jnp.concatenate(
            [
                lax.ppermute(tail, axis, [(i, (i + 1) % count) for i in range(ends)]),
                cells,
                lax.ppermute(head, axis, [((i + 1) % count, i) for i in range(ends)]),
            ],
            axis=dim,
        )
    return cells


def from_behind(value, axis, steps):
    count = lax.axis_size(axis)
    leading, last = (max(0, -steps), min(count, count - steps))
    return lax.ppermute(value, axis, [(source, source + steps) for source in range(leading, last)])


def band_matrix(block_size, margin, fresnel, adjoint):
    shape_full = (block_size, block_size + 2 * margin)
    out_idx = lax.broadcasted_iota(jnp.int32, shape_full, 0)
    in_idx = lax.broadcasted_iota(jnp.int32, shape_full, 1)
    offset = (out_idx + margin - in_idx).astype(jnp.float32)
    inside = jnp.abs(offset) <= margin
    taper_dist = jnp.maximum(jnp.abs(offset) - 0.5 * margin, 0.0)
    profile = jnp.cos(jnp.pi * taper_dist / (margin + 2.0))
    weight = profile * profile / math.sqrt(fresnel)
    phase_angle = jnp.pi * offset * offset / fresnel
    real_part = jnp.where(inside, jnp.cos(phase_angle) * weight, 0.0)
    imag_part = jnp.where(inside, jnp.sin(phase_angle) * weight, 0.0)
    if adjoint:
        imag_part = -imag_part
    upper = jnp.stack([real_part, -imag_part])
    lower = jnp.stack([imag_part, real_part])
    return jnp.stack([upper, lower])


def along_rows(extended, matrix):
    pieces = [jnp.einsum("pqij,gqjc->gpic", matrix, extended, precision=lax.Precision.HIGHEST)]
    return jnp.concatenate(pieces, axis=2)


def along_cols(extended, matrix, margin):
    block_size = matrix.shape[2]
    extent = extended.shape[3] - 2 * margin
    pieces = []
    for block_start in range(0, extent, block_size):
        window = extended[:, :, :, block_start : block_start + block_size + 2 * margin]
        pieces.append(
            jnp.einsum("pqij,gqrj->gpri", matrix, window, precision=lax.Precision.HIGHEST)
        )
    return jnp.concatenate(pieces, axis=3)


def propagate(current, row_matrix, col_matrix):
    with_rows = extended_2(current, (("row", 2),), HALO)
    row_done = along_rows(with_rows, row_matrix)
    with_cols = extended_2(row_done, (("col", 3),), HALO)
    return along_cols(with_cols, col_matrix, HALO)


def transmit(screen, current, adjoint):
    screen_re = screen[0][None]
    screen_im = screen[1][None]
    if adjoint:
        screen_im = -screen_im
    real_part = screen_re * current[:, 0] - screen_im * current[:, 1]
    imag_part = screen_re * current[:, 1] + screen_im * current[:, 0]
    return jnp.stack([real_part, imag_part], axis=1)


def store_item(store, current, first_item, slice_index, active):
    begin = (first_item, jnp.int32(slice_index), jnp.int32(0), jnp.int32(0), jnp.int32(0))
    sizes_now = (current.shape[0], 1) + current.shape[1:]
    previous = lax.dynamic_slice(store, begin, sizes_now)
    fresh = jnp.where(active, current[:, None], previous)
    return lax.dynamic_update_slice(store, fresh, begin)


def staged_body(phase, tilt, intensity):
    slices, tile_r, tile_c = phase.shape
    batch_size = tilt.shape[0]
    sections = lax.axis_size("depth")
    section_index = lax.axis_index("depth")
    group_size = 1
    groups = batch_size // group_size
    tick_count = sections + groups - 1
    block_r = 64
    block_c = 128
    fwd_rows = band_matrix(block_r, HALO, FRESNEL, False)
    fwd_cols = band_matrix(block_c, HALO, FRESNEL, False)
    adj_rows = band_matrix(block_r, HALO, FRESNEL, True)
    adj_cols = band_matrix(block_c, HALO, FRESNEL, True)
    row_pos = (
        lax.axis_index("row") * tile_r + lax.broadcasted_iota(jnp.int32, (tile_r, tile_c), 0)
    ).astype(jnp.float32)
    col_pos = (
        lax.axis_index("col") * tile_c + lax.broadcasted_iota(jnp.int32, (tile_r, tile_c), 1)
    ).astype(jnp.float32)
    height = float(tile_r * lax.axis_size("row"))
    width_all = float(tile_c * lax.axis_size("col"))
    tilt_f = tilt.astype(jnp.float32)
    phase_angle = (
        2.0
        * jnp.pi
        * (
            tilt_f[:, 0, None, None] * row_pos / height
            + tilt_f[:, 1, None, None] * col_pos / width_all
        )
    )
    incident = jnp.stack([jnp.cos(phase_angle), jnp.sin(phase_angle)], axis=1)
    screens = jnp.stack([jnp.cos(phase), jnp.sin(phase)], axis=1)

    def forward_tick(tick_now, carry):
        incoming, entering, leaving = carry
        group_index = tick_now - section_index
        active = (group_index >= 0) & (group_index < groups)
        first_item = jnp.clip(group_index, 0, groups - 1) * group_size
        current = jnp.where(
            section_index == 0,
            lax.dynamic_slice_in_dim(incident, first_item, group_size, 0),
            incoming,
        )
        entering = store_item(entering, current, first_item, 0, active)
        current = propagate(transmit(screens[0], current, False), fwd_rows, fwd_cols)
        leaving = store_item(leaving, current, first_item, 0, active)
        incoming = from_behind(current, "depth", 1)
        return (incoming, entering, leaving)

    store_zero = jnp.zeros((batch_size, slices, 2, tile_r, tile_c), jnp.float32)
    start_wave = jnp.zeros((group_size, 2, tile_r, tile_c), jnp.float32)
    _, entering, leaving = lax.fori_loop(
        0, tick_count, forward_tick, (start_wave, store_zero, store_zero)
    )
    final_wave = leaving[:, slices - 1]
    misfit = final_wave[:, 0] * final_wave[:, 0] + final_wave[:, 1] * final_wave[:, 1] - intensity
    seed_adjoint = 2.0 * misfit[:, None] * final_wave

    def backward_tick(tick_now, carry):
        incoming, gradient = carry
        group_index = tick_now - (sections - 1 - section_index)
        active = (group_index >= 0) & (group_index < groups)
        first_item = jnp.clip(group_index, 0, groups - 1) * group_size
        adjoint_wave = jnp.where(
            section_index == sections - 1,
            lax.dynamic_slice_in_dim(seed_adjoint, first_item, group_size, 0),
            incoming,
        )
        for slice_index in reversed(range(slices)):
            pulled = propagate(adjoint_wave, adj_rows, adj_cols)
            arrived = lax.dynamic_slice_in_dim(entering[:, slice_index], first_item, group_size, 0)
            moved = transmit(screens[slice_index], arrived, False)
            contribution = jnp.sum(pulled[:, 1] * moved[:, 0] - pulled[:, 0] * moved[:, 1], axis=0)
            gradient = gradient.at[slice_index].add(jnp.where(active, contribution, 0.0))
            adjoint_wave = transmit(screens[slice_index], pulled, True)
        incoming = from_behind(adjoint_wave, "depth", -1)
        return (incoming, gradient)

    grad_zero = jnp.zeros((slices, tile_r, tile_c), jnp.float32)
    _, gradient = lax.fori_loop(0, tick_count, backward_tick, (start_wave, grad_zero))
    return (gradient, leaving)


def fits_whole(phase_shape, batch, mesh):
    slices, height, width = phase_shape
    rows, cols, sections = mesh.shape["row"], mesh.shape["col"], mesh.shape["depth"]
    return (
        4 * height * width * (slices + batch) <= GATHER_BUDGET
        and batch == rows == 2
        and slices == sections
        and sections == 4
        and cols == 4
        and height == LANES
        and width == cols * LANES
        and sections * HALO <= LANES
    )


def solution(mesh):
    placed = (P("depth", "row", "col"), P(), P(None, "row", "col"))

    def run(phase, tilt, intensity):
        if fits_whole(phase.shape, tilt.shape[0], mesh):
            body = whole_field_body
        else:
            body = staged_body
        return jax.shard_map(
            body,
            mesh=mesh,
            in_specs=placed,
            out_specs=(P("depth", "row", "col"), P(None, "depth", None, "row", "col")),
            check_vma=False,
        )(phase, tilt, intensity)

    return run
```

```python
import math

import jax
import jax.numpy as jnp
import numpy as np
from jax import lax
from jax.experimental import pallas as pl
from jax.experimental.pallas import tpu as pltpu
from jax.sharding import PartitionSpec as P

HALO = 32
FRESNEL = 64
LANES = 128
GATHER_BUDGET = 4 * 2**20
SIN = (
    0.9999999980536763,
    -0.1666666530009577,
    0.008333305907073658,
    -0.00019838908256358006,
    2.745822627876341e-06,
    -2.3043562782810933e-08,
)
COS = (
    0.9999999961345007,
    -0.4999999301617528,
    0.04166646215023687,
    -0.0013886696163545999,
    2.4695045482778703e-05,
    -2.5154931690000354e-07,
)


def horner(coefficients, square):
    total = jnp.full_like(square, coefficients[-1])
    for coefficient in coefficients[-2::-1]:
        total = total * square + coefficient
    return total


def cos_sin(angle):
    square = angle * angle
    return horner(COS, square), horner(SIN, square) * angle


def turn(fraction):
    half_cos, half_sin = cos_sin(fraction * math.pi)
    return half_cos * half_cos - half_sin * half_sin, 2.0 * half_cos * half_sin


def halves(value):
    high = value.astype(jnp.bfloat16)
    return high, (value - high.astype(jnp.float32)).astype(jnp.bfloat16)


def np_halves(matrix):
    high = matrix.astype(jnp.bfloat16)
    return high, (matrix - high.astype(np.float64)).astype(jnp.bfloat16)


def np_taps():
    offset = np.arange(-HALO, HALO + 1, dtype=np.float64)
    taper = np.maximum(np.abs(offset) - 0.5 * HALO, 0.0)
    weight = np.cos(np.pi * taper / (HALO + 2.0)) ** 2 / math.sqrt(FRESNEL)
    return weight * np.exp(1j * np.pi * offset * offset / FRESNEL)


def np_band(out_pos, in_pos):
    offset = out_pos[:, None] - in_pos[None, :]
    inside = np.abs(offset) <= HALO
    return np.where(inside, np_taps()[np.clip(offset, -HALO, HALO) + HALO], 0.0)


def row_constant(height):
    matrices = []
    for core in range(2):
        pos = (np.arange(height) + core * (height // 2)) % height
        band = np_band(pos, pos)
        whole = np.block([[band.real, -band.imag], [band.imag, band.real]])
        matrices.append(np.concatenate(np_halves(whole), axis=1))
    return np.stack(matrices)


def col_constant():
    lane = np.arange(LANES)
    turned = np.where((lane >= HALO) & (lane < LANES - HALO), lane ^ (LANES // 2), lane)
    edge_pos = np.where(turned < LANES // 2, turned + LANES, turned - LANES)
    parts = []
    for position in (lane, edge_pos):
        band = np_band(lane, position).T
        parts.append(np.block([[band.real, band.imag], [-band.imag, band.real]]))
    return np.concatenate(np_halves(np.concatenate(parts, axis=0)), axis=1)


def both_rows(near_ref, far_ref, where):
    return jnp.concatenate([near_ref[where], far_ref[where]], axis=0)


def turned(slice_index, block, screens, wave):
    near_cos, near_sin, far_cos, far_sin = screens
    cos = both_rows(near_cos, far_cos, (slice_index, block))
    sin = both_rows(near_sin, far_sin, (slice_index, block))
    real, imag = wave
    return cos * real - sin * imag, cos * imag + sin * real


def row_products(row_matrix, chunks):
    whole = row_matrix.shape[0]
    highs, wides = [], []
    for columns in chunks:
        high, low = halves(columns)
        highs.append(high)
        wide = jnp.dot(
            row_matrix[:, :whole], jnp.concatenate([high, low], axis=1), preferred_element_type=jnp.float32
        )
        wides.append(wide[:, : columns.shape[1]] + wide[:, columns.shape[1] :])
    rest = jnp.dot(row_matrix[:, whole:], jnp.concatenate(highs, axis=1), preferred_element_type=jnp.float32)
    done, begin = [], 0
    for wide in wides:
        done.append(wide + rest[:, begin : begin + wide.shape[1]])
        begin += wide.shape[1]
    return done


def col_product(high, low, col_ref):
    wide = jnp.dot(high, col_ref[...], preferred_element_type=jnp.float32)
    rest = jnp.dot(low, col_ref[: 2 * LANES, : 2 * LANES], preferred_element_type=jnp.float32)
    return wide[:, : 2 * LANES] + wide[:, 2 * LANES :] + rest


def three_parts(value):
    high = value.astype(jnp.bfloat16)
    rest = value - high.astype(jnp.float32)
    return high, rest.astype(jnp.bfloat16), pltpu.roll(rest, LANES // 2, 1).astype(jnp.bfloat16)


def advance(slice_index, start, waves, screens, row_matrix, col_ref, edge_ref, outer=None):
    size, height = len(waves), waves[0][0].shape[0]
    chunks = [range(place, min(place + 2, size)) for place in range(0, size, 2)]
    highs, lows = [], []
    columns = [
        jnp.concatenate(
            [
                jnp.concatenate(
                    waves[place] if slice_index is None else turned(slice_index, start + place, screens, waves[place]),
                    axis=0,
                )
                for place in chunk
            ],
            axis=1,
        )
        for chunk in chunks
    ]
    for chunk, done in zip(chunks, row_products(row_matrix, columns)):
        for sub, place in enumerate(chunk):
            own_high, own_low = [], []
            for part in range(2):
                value = done[part * height : (part + 1) * height, sub * LANES : (sub + 1) * LANES]
                high, low, swung = three_parts(value)
                own_high.append(high)
                own_low.append(low)
                edge = part * LANES
                if place > 0:
                    edge_ref[place - 1, :, pl.ds(edge, HALO)] = high[:, :HALO]
                    edge_ref[place - 1, :, pl.ds(edge + 2 * HALO, HALO)] = swung[:, 2 * HALO : 3 * HALO]
                if place < size - 1:
                    edge_ref[place + 1, :, pl.ds(edge + 3 * HALO, HALO)] = high[:, 3 * HALO :]
                    edge_ref[place + 1, :, pl.ds(edge + HALO, HALO)] = swung[:, HALO : 2 * HALO]
            highs.append(jnp.concatenate(own_high, axis=1))
            lows.append(jnp.concatenate(own_low, axis=1))
    edge_parts = [edge_ref[place] for place in range(size)]
    if outer is not None:
        index, high_ref, low_ref = outer
        for end, place in enumerate((0, size - 1)):
            high_ref[end], low_ref[end] = highs[place], lows[place]
        highs = highs[1:-1] + [high_ref[index]]
        lows = lows[1:-1] + [low_ref[index]]
        edge_parts = edge_parts[1:-1] + [edge_ref[index * (size - 1)]]
        chunks = [range(place, min(place + 2, size - 1)) for place in range(0, size - 1, 2)]
    results = []
    for chunk in chunks:
        edges = jnp.concatenate([edge_parts[place] for place in chunk], axis=0)
        own = jnp.concatenate([highs[place] for place in chunk], axis=0)
        total = col_product(
            jnp.concatenate([own, edges], axis=1),
            jnp.concatenate([lows[place] for place in chunk], axis=0),
            col_ref,
        )
        for sub in range(len(chunk)):
            block = total[sub * height : (sub + 1) * height]
            results.append((block[:, :LANES], block[:, LANES:]))
    return results


def clear_edge(edge_ref, place, right):
    for part in range(2):
        for begin in (0, 2 * HALO) if right else (HALO, 3 * HALO):
            cells = pl.ds(part * LANES + begin, HALO)
            edge_ref[place, :, cells] = jnp.zeros((edge_ref.shape[1], HALO), edge_ref.dtype)


def keep(wave_ref, waves):
    for place, wave in enumerate(waves):
        wave_ref[place, 0], wave_ref[place, 1] = wave


def load_kernel(tilt_ref, near_own, row_from, col_from, row_to, col_to, wave_ref, cos_ref, sin_ref, sems):
    blocks, _, height, _ = wave_ref.shape
    core = lax.axis_index("row")
    copies = [
        pltpu.make_async_copy(row_from.at[core], row_to, sems.at[0]),
        pltpu.make_async_copy(col_from, col_to, sems.at[1]),
    ]
    for copy in copies:
        copy.start()
    for col in range(blocks):
        cos_ref[col], sin_ref[col] = cos_sin(near_own[col ^ lax.axis_index("col"), 0])

    def cycles(number, position, extent):
        fraction = (number * position).astype(jnp.float32) / extent
        return turn(fraction - jnp.round(fraction))

    row = lax.broadcasted_iota(jnp.int32, (height, LANES), 0) + core * (height // 2)
    row = jnp.where(row >= height, row - height, row)
    row_cos, row_sin = cycles(tilt_ref[core, 0], row, float(height))
    for block in range(blocks):
        col_cos, col_sin = cycles(
            tilt_ref[core, 1],
            lax.broadcasted_iota(jnp.int32, (8, LANES), 1) + block * LANES,
            float(blocks * LANES),
        )
        col_cos, col_sin = col_cos[:1], col_sin[:1]
        wave_ref[block, 0] = row_cos * col_cos - row_sin * col_sin
        wave_ref[block, 1] = row_sin * col_cos + row_cos * col_sin
    for copy in copies:
        copy.wait()


def second_kernel(near_rest, own_cos, own_sin, cos_ref, sin_ref):
    blocks = own_cos.shape[0]
    count = cos_ref.shape[0]
    own_section, own_place = lax.axis_index("depth"), lax.axis_index("col")

    def screens(col, carry):
        held = col ^ own_place
        cos_ref[own_section, col], sin_ref[own_section, col] = own_cos[col], own_sin[col]
        for bits in range(1, count):
            cos_ref[bits ^ own_section, col], sin_ref[bits ^ own_section, col] = cos_sin(near_rest[held, (4 - bits) % 3])
        return carry

    lax.fori_loop(0, blocks, screens, 0)


def wave_kernel(
    wave_ref, near_cos, near_sin, near_own, far_first, far_second, row_ref, col_ref,
    mine_ref, theirs_ref, far_cos, far_sin, kept_ref, moved_ref, left_ref, grad_ref, even_edge, odd_edge,
    outer_high, outer_low,
):
    blocks, _, height, _ = wave_ref.shape
    count = near_cos.shape[0]
    core, own_section, own_place = lax.axis_index("row"), lax.axis_index("depth"), lax.axis_index("col")
    near, far = pl.ds(0, height // 2), pl.ds(height // 2, height // 2)
    screens = (near_cos, near_sin, far_cos, far_sin)
    row_matrix = row_ref[...]
    window = min(3, blocks)
    window_start = jnp.clip(own_place - 1, 0, blocks - window)
    own_in_window = own_place - window_start
    edges = (even_edge, odd_edge)

    def far_screens(slice_index):
        bits = slice_index ^ own_section
        for col in range(blocks):
            held = col ^ own_place
            others = lax.rem(4 - bits, 3)
            in_first = (bits == 0) | (held == 3)
            place = jnp.where(bits == 0, 2 * held, 2 * blocks + others)
            angle = jnp.where(in_first, far_first[place], far_second[jnp.minimum(held, 2) * (count - 1) + others])
            far_cos[slice_index, col], far_sin[slice_index, col] = cos_sin(angle)

    for edge_ref in edges:
        clear_edge(edge_ref, 0, False)
        clear_edge(edge_ref, blocks - 1, True)
    far_screens(0)

    waves = [(wave_ref[place, 0], wave_ref[place, 1]) for place in range(blocks)]
    for tick in range(count):
        entering = (wave_ref if tick == 0 else kept_ref)[own_place]
        moved_ref[tick, 0], moved_ref[tick, 1] = turned(tick, own_place, screens, (entering[0], entering[1]))
        if tick + 1 < count:
            far_screens(tick + 1)
        outer = (window_start, outer_high, outer_low) if tick + 1 == count else None
        waves = advance(tick, 0, waves, screens, row_matrix, col_ref, edges[tick % 2], outer)
        if tick + 1 < count:
            keep(kept_ref, waves)
        else:
            for place, wave in zip((1, 2, window_start * (blocks - 1)), waves):
                kept_ref[place, 0], kept_ref[place, 1] = wave
        left_ref[tick] = kept_ref[own_place]

    for edge_ref in edges:
        clear_edge(edge_ref, window - 1, True)
    waves = []
    for place in range(window):
        block = window_start + place
        real, imag = kept_ref[block, 0], kept_ref[block, 1]
        held = block ^ own_place
        measured = jnp.concatenate([near_own[held, 1 + core], far_first[2 * held + 1]], axis=0)
        misfit = 2.0 * (real * real + imag * imag - measured)
        waves.append((misfit * real, -misfit * imag))

    for tick in range(count - 1):
        passed = count - tick if tick else None
        waves = advance(passed, window_start, waves, screens, row_matrix, col_ref, edges[tick % 2])
        keep(kept_ref, waves)
        arrived = count - 1 - tick
        pulled = kept_ref[own_in_window]
        grad_ref[arrived] = -(pulled[1] * moved_ref[arrived, 0] + pulled[0] * moved_ref[arrived, 1])

    left, right = jnp.maximum(own_place - 1, 0), jnp.minimum(own_place + 1, blocks - 1)
    lane = lax.broadcasted_iota(jnp.int32, (2 * height, LANES), 1)
    has_left, has_right = own_place > 0, own_place < blocks - 1

    def cells(block):
        wave = kept_ref[block - window_start]
        return jnp.concatenate(turned(1, block, screens, (wave[0], wave[1])), axis=0)

    edge_cells = jnp.where(
        lane < LANES // 2, jnp.where(has_right, cells(right), 0.0), jnp.where(has_left, cells(left), 0.0)
    )
    done = row_products(row_matrix, [jnp.concatenate([cells(own_place), edge_cells], axis=1)])[0]
    lane = lax.broadcasted_iota(jnp.int32, (height, LANES), 1)
    between = (lane >= HALO) & (lane < LANES - HALO)
    highs, lows, edges = [], [], []
    for part in range(2):
        high, low, _ = three_parts(done[part * height : (part + 1) * height, :LANES])
        highs.append(high)
        lows.append(low)
        value = done[part * height : (part + 1) * height, LANES:]
        whole_high = value.astype(jnp.bfloat16).astype(jnp.float32)
        edge = jnp.where(between, pltpu.roll(value - whole_high, LANES // 2, 1), whole_high)
        edges.append(edge.astype(jnp.bfloat16))
    pulled = col_product(jnp.concatenate(highs + edges, axis=1), jnp.concatenate(lows, axis=1), col_ref)
    grad_ref[0] = -(pulled[:, LANES:] * moved_ref[0, 0] + pulled[:, :LANES] * moved_ref[0, 1])

    for target, row in ((mine_ref, near), (theirs_ref, far)):
        for part in range(2):
            target[0, part] = left_ref[own_section, part, row]
        target[0, 2] = grad_ref[own_section, row]


def finish_kernel(mine_ref, received_ref, grad_ref, exit_ref, total_ref, sems):
    core = lax.axis_index("row")
    copies = []
    for source, item in ((mine_ref, core), (received_ref, 1 - core)):
        copies.append(pltpu.make_async_copy(source.at[:, pl.ds(0, 2)], exit_ref.at[item], sems.at[len(copies)]))
    for copy in copies:
        copy.start()
    total_ref[...] = mine_ref[:, 2] + received_ref[:, 2]
    copies.append(pltpu.make_async_copy(total_ref, grad_ref, sems.at[2]))
    copies[2].start()
    for copy in copies:
        copy.wait()


def spread(shard, axis, all_bits, reach=3):
    pieces = []
    for bits in all_bits:
        pairs = [(i, i ^ bits) for i in range(4) if abs(i - (i ^ bits)) <= reach]
        pieces.append(lax.ppermute(shard, axis, pairs))
    return pieces


def swap_cores(value):
    return lax.ppermute(value, "row", [(0, 1), (1, 0)])


def whole_field_body(phase, tilt, intensity):
    _, tile_r, tile_c = phase.shape
    count, blocks = lax.axis_size("depth"), lax.axis_size("col")
    core = lax.axis_index("row")
    height = 2 * tile_r
    vmem = pl.BlockSpec(memory_space=pltpu.VMEM)
    smem = pl.BlockSpec(memory_space=pltpu.SMEM)
    hbm = pl.BlockSpec(memory_space=pl.ANY)

    def array(*shape):
        return jax.ShapeDtypeStruct(shape, jnp.float32)

    def params(mebibytes):
        return pltpu.CompilerParams(vmem_limit_bytes=mebibytes * 2**20)

    first_depth, farthest, two_away = spread(phase, "depth", (1, 3, 2))
    first_depth, measured, slab = lax.optimization_barrier((first_depth, intensity, phase))
    other_depths = [first_depth, farthest, two_away]
    other_depths = jnp.concatenate(other_depths, axis=0)
    packet = jnp.concatenate([slab, measured], axis=0)
    near_own = [packet]
    for bits in range(1, blocks):
        pairs = [(i, i ^ bits) for i in range(blocks)]
        close = [(i, j) for i, j in pairs if abs(i - j) <= 1]
        if close:
            near_own.append(lax.ppermute(packet, "col", close))
        else:
            further = [(i, j) for i, j in pairs if abs(i - j) <= 2]
            arrived = lax.ppermute(slab, "col", further) if further else jnp.zeros_like(slab)
            near_own.append(jnp.concatenate([arrived, jnp.zeros_like(measured)], axis=0))
    near_own = jnp.stack(near_own)
    arriving = spread(other_depths, "col", (1, 2, 3), 2)
    row_all, col_all = jnp.asarray(row_constant(height)), jnp.asarray(col_constant())
    near_own, row_all, col_all = lax.optimization_barrier((near_own, row_all, col_all))
    half_screens = (count, blocks, tile_r, tile_c)
    field = (blocks, 2, height, tile_c)
    row_matrix, col_matrix, wave, own_cos, own_sin = pl.pallas_call(
        load_kernel,
        out_shape=(
            jax.ShapeDtypeStruct(row_all.shape[1:], row_all.dtype),
            jax.ShapeDtypeStruct(col_all.shape, col_all.dtype),
            array(*field),
            array(blocks, tile_r, tile_c),
            array(blocks, tile_r, tile_c),
        ),
        in_specs=[smem, vmem, hbm, hbm],
        out_specs=(vmem,) * 5,
        scratch_shapes=[pltpu.SemaphoreType.DMA((2,))],
        compiler_params=params(4),
        cost_estimate=pl.CostEstimate(flops=10**8, bytes_accessed=2**20, transcendentals=0),
    )(tilt, near_own, row_all, col_all)
    arriving[2], near_own, row_matrix, col_matrix, wave, own_cos, own_sin = lax.optimization_barrier(
        (arriving[2], near_own, row_matrix, col_matrix, wave, own_cos, own_sin)
    )
    wanted = lax.dynamic_slice_in_dim(near_own, 2 - core, 1, 1)
    packets = jnp.concatenate([near_own[:, :1], wanted], axis=1).reshape(2 * blocks, tile_r, tile_c)
    far_first = swap_cores(jnp.concatenate([packets, arriving[2]], axis=0))
    far_second = swap_cores(jnp.concatenate([other_depths] + arriving[:2], axis=0))
    near_rest = jnp.stack([other_depths] + arriving)

    near_cos, near_sin = pl.pallas_call(
        second_kernel,
        out_shape=(array(*half_screens),) * 2,
        in_specs=[vmem] * 3,
        out_specs=(vmem,) * 2,
        compiler_params=params(8),
        cost_estimate=pl.CostEstimate(flops=5 * 10**8, bytes_accessed=2**20, transcendentals=0),
    )(near_rest, own_cos, own_sin)
    mine, theirs = pl.pallas_call(
        wave_kernel,
        out_shape=(array(1, 3, tile_r, tile_c),) * 2,
        in_specs=[vmem] * 8,
        out_specs=(vmem,) * 2,
        scratch_shapes=[pltpu.VMEM(half_screens, jnp.float32)] * 2
        + [pltpu.VMEM(field, jnp.float32)]
        + [pltpu.VMEM((count, 2, height, tile_c), jnp.float32)] * 2
        + [pltpu.VMEM((count, height, tile_c), jnp.float32)]
        + [pltpu.VMEM((blocks, height, 2 * LANES), jnp.bfloat16)] * 2
        + [pltpu.VMEM((2, height, 2 * LANES), jnp.bfloat16)] * 2,
        compiler_params=params(24),
    )(
        wave, near_cos, near_sin, near_own, far_first, far_second,
        row_matrix, col_matrix,
    )
    return pl.pallas_call(
        finish_kernel,
        out_shape=(array(*phase.shape), array(2, 1, 2, tile_r, tile_c)),
        in_specs=[vmem, vmem],
        out_specs=(hbm, hbm),
        scratch_shapes=[pltpu.VMEM(phase.shape, jnp.float32), pltpu.SemaphoreType.DMA((3,))],
        compiler_params=params(4),
    )(mine, swap_cores(theirs))


def extended_2(cells, sides, width):
    for axis, dim in sides:
        count = lax.axis_size(axis)
        ends = count - 1
        head = lax.slice_in_dim(cells, 0, width, axis=dim)
        tail = lax.slice_in_dim(cells, cells.shape[dim] - width, cells.shape[dim], axis=dim)
        cells = jnp.concatenate(
            [
                lax.ppermute(tail, axis, [(i, (i + 1) % count) for i in range(ends)]),
                cells,
                lax.ppermute(head, axis, [((i + 1) % count, i) for i in range(ends)]),
            ],
            axis=dim,
        )
    return cells


def from_behind(value, axis, steps):
    count = lax.axis_size(axis)
    leading, last = (max(0, -steps), min(count, count - steps))
    return lax.ppermute(value, axis, [(source, source + steps) for source in range(leading, last)])


def band_matrix(block_size, margin, fresnel, adjoint):
    shape_full = (block_size, block_size + 2 * margin)
    out_idx = lax.broadcasted_iota(jnp.int32, shape_full, 0)
    in_idx = lax.broadcasted_iota(jnp.int32, shape_full, 1)
    offset = (out_idx + margin - in_idx).astype(jnp.float32)
    inside = jnp.abs(offset) <= margin
    taper_dist = jnp.maximum(jnp.abs(offset) - 0.5 * margin, 0.0)
    profile = jnp.cos(jnp.pi * taper_dist / (margin + 2.0))
    weight = profile * profile / math.sqrt(fresnel)
    phase_angle = jnp.pi * offset * offset / fresnel
    real_part = jnp.where(inside, jnp.cos(phase_angle) * weight, 0.0)
    imag_part = jnp.where(inside, jnp.sin(phase_angle) * weight, 0.0)
    if adjoint:
        imag_part = -imag_part
    upper = jnp.stack([real_part, -imag_part])
    lower = jnp.stack([imag_part, real_part])
    return jnp.stack([upper, lower])


def along_rows(extended, matrix):
    pieces = [jnp.einsum("pqij,gqjc->gpic", matrix, extended, precision=lax.Precision.HIGHEST)]
    return jnp.concatenate(pieces, axis=2)


def along_cols(extended, matrix, margin):
    block_size = matrix.shape[2]
    extent = extended.shape[3] - 2 * margin
    pieces = []
    for block_start in range(0, extent, block_size):
        window = extended[:, :, :, block_start : block_start + block_size + 2 * margin]
        pieces.append(
            jnp.einsum("pqij,gqrj->gpri", matrix, window, precision=lax.Precision.HIGHEST)
        )
    return jnp.concatenate(pieces, axis=3)


def propagate(current, row_matrix, col_matrix):
    with_rows = extended_2(current, (("row", 2),), HALO)
    row_done = along_rows(with_rows, row_matrix)
    with_cols = extended_2(row_done, (("col", 3),), HALO)
    return along_cols(with_cols, col_matrix, HALO)


def transmit(screen, current, adjoint):
    screen_re = screen[0][None]
    screen_im = screen[1][None]
    if adjoint:
        screen_im = -screen_im
    real_part = screen_re * current[:, 0] - screen_im * current[:, 1]
    imag_part = screen_re * current[:, 1] + screen_im * current[:, 0]
    return jnp.stack([real_part, imag_part], axis=1)


def store_item(store, current, first_item, slice_index, active):
    begin = (first_item, jnp.int32(slice_index), jnp.int32(0), jnp.int32(0), jnp.int32(0))
    sizes_now = (current.shape[0], 1) + current.shape[1:]
    previous = lax.dynamic_slice(store, begin, sizes_now)
    fresh = jnp.where(active, current[:, None], previous)
    return lax.dynamic_update_slice(store, fresh, begin)


def staged_body(phase, tilt, intensity):
    slices, tile_r, tile_c = phase.shape
    batch_size = tilt.shape[0]
    sections = lax.axis_size("depth")
    section_index = lax.axis_index("depth")
    group_size = 1
    groups = batch_size // group_size
    tick_count = sections + groups - 1
    block_r = 64
    block_c = 128
    fwd_rows = band_matrix(block_r, HALO, FRESNEL, False)
    fwd_cols = band_matrix(block_c, HALO, FRESNEL, False)
    adj_rows = band_matrix(block_r, HALO, FRESNEL, True)
    adj_cols = band_matrix(block_c, HALO, FRESNEL, True)
    row_pos = (
        lax.axis_index("row") * tile_r + lax.broadcasted_iota(jnp.int32, (tile_r, tile_c), 0)
    ).astype(jnp.float32)
    col_pos = (
        lax.axis_index("col") * tile_c + lax.broadcasted_iota(jnp.int32, (tile_r, tile_c), 1)
    ).astype(jnp.float32)
    height = float(tile_r * lax.axis_size("row"))
    width_all = float(tile_c * lax.axis_size("col"))
    tilt_f = tilt.astype(jnp.float32)
    phase_angle = (
        2.0
        * jnp.pi
        * (
            tilt_f[:, 0, None, None] * row_pos / height
            + tilt_f[:, 1, None, None] * col_pos / width_all
        )
    )
    incident = jnp.stack([jnp.cos(phase_angle), jnp.sin(phase_angle)], axis=1)
    screens = jnp.stack([jnp.cos(phase), jnp.sin(phase)], axis=1)

    def forward_tick(tick_now, carry):
        incoming, entering, leaving = carry
        group_index = tick_now - section_index
        active = (group_index >= 0) & (group_index < groups)
        first_item = jnp.clip(group_index, 0, groups - 1) * group_size
        current = jnp.where(
            section_index == 0,
            lax.dynamic_slice_in_dim(incident, first_item, group_size, 0),
            incoming,
        )
        entering = store_item(entering, current, first_item, 0, active)
        current = propagate(transmit(screens[0], current, False), fwd_rows, fwd_cols)
        leaving = store_item(leaving, current, first_item, 0, active)
        incoming = from_behind(current, "depth", 1)
        return (incoming, entering, leaving)

    store_zero = jnp.zeros((batch_size, slices, 2, tile_r, tile_c), jnp.float32)
    start_wave = jnp.zeros((group_size, 2, tile_r, tile_c), jnp.float32)
    _, entering, leaving = lax.fori_loop(
        0, tick_count, forward_tick, (start_wave, store_zero, store_zero)
    )
    final_wave = leaving[:, slices - 1]
    misfit = final_wave[:, 0] * final_wave[:, 0] + final_wave[:, 1] * final_wave[:, 1] - intensity
    seed_adjoint = 2.0 * misfit[:, None] * final_wave

    def backward_tick(tick_now, carry):
        incoming, gradient = carry
        group_index = tick_now - (sections - 1 - section_index)
        active = (group_index >= 0) & (group_index < groups)
        first_item = jnp.clip(group_index, 0, groups - 1) * group_size
        adjoint_wave = jnp.where(
            section_index == sections - 1,
            lax.dynamic_slice_in_dim(seed_adjoint, first_item, group_size, 0),
            incoming,
        )
        for slice_index in reversed(range(slices)):
            pulled = propagate(adjoint_wave, adj_rows, adj_cols)
            arrived = lax.dynamic_slice_in_dim(entering[:, slice_index], first_item, group_size, 0)
            moved = transmit(screens[slice_index], arrived, False)
            contribution = jnp.sum(pulled[:, 1] * moved[:, 0] - pulled[:, 0] * moved[:, 1], axis=0)
            gradient = gradient.at[slice_index].add(jnp.where(active, contribution, 0.0))
            adjoint_wave = transmit(screens[slice_index], pulled, True)
        incoming = from_behind(adjoint_wave, "depth", -1)
        return (incoming, gradient)

    grad_zero = jnp.zeros((slices, tile_r, tile_c), jnp.float32)
    _, gradient = lax.fori_loop(0, tick_count, backward_tick, (start_wave, grad_zero))
    return (gradient, leaving)


def fits_whole(phase_shape, batch, mesh):
    slices, height, width = phase_shape
    rows, cols, sections = mesh.shape["row"], mesh.shape["col"], mesh.shape["depth"]
    return (
        4 * height * width * (slices + batch) <= GATHER_BUDGET
        and batch == rows == 2
        and slices == sections
        and sections == 4
        and cols == 4
        and height == LANES
        and width == cols * LANES
        and sections * HALO <= LANES
    )


def solution(mesh):
    placed = (P("depth", "row", "col"), P(), P(None, "row", "col"))

    def run(phase, tilt, intensity):
        if fits_whole(phase.shape, tilt.shape[0], mesh):
            body = whole_field_body
        else:
            body = staged_body
        return jax.shard_map(
            body,
            mesh=mesh,
            in_specs=placed,
            out_specs=(P("depth", "row", "col"), P(None, "depth", None, "row", "col")),
            check_vma=False,
        )(phase, tilt, intensity)

    return run
```

```python
import math

import jax
import jax.numpy as jnp
import numpy as np
from jax import lax
from jax.experimental import pallas as pl
from jax.experimental.pallas import tpu as pltpu
from jax.sharding import PartitionSpec as P

HALO = 32
FRESNEL = 64
LANES = 128
GATHER_BUDGET = 4 * 2**20
SIN = (
    0.9999999980536763,
    -0.1666666530009577,
    0.008333305907073658,
    -0.00019838908256358006,
    2.745822627876341e-06,
    -2.3043562782810933e-08,
)
COS = (
    0.9999999961345007,
    -0.4999999301617528,
    0.04166646215023687,
    -0.0013886696163545999,
    2.4695045482778703e-05,
    -2.5154931690000354e-07,
)


def horner(coefficients, square):
    total = jnp.full_like(square, coefficients[-1])
    for coefficient in coefficients[-2::-1]:
        total = total * square + coefficient
    return total


def cos_sin(angle):
    square = angle * angle
    return horner(COS, square), horner(SIN, square) * angle


def turn(fraction):
    half_cos, half_sin = cos_sin(fraction * math.pi)
    return half_cos * half_cos - half_sin * half_sin, 2.0 * half_cos * half_sin


def halves(value):
    high = value.astype(jnp.bfloat16)
    return high, (value - high.astype(jnp.float32)).astype(jnp.bfloat16)


def np_halves(matrix):
    high = matrix.astype(jnp.bfloat16)
    return high, (matrix - high.astype(np.float64)).astype(jnp.bfloat16)


def np_taps():
    offset = np.arange(-HALO, HALO + 1, dtype=np.float64)
    taper = np.maximum(np.abs(offset) - 0.5 * HALO, 0.0)
    weight = np.cos(np.pi * taper / (HALO + 2.0)) ** 2 / math.sqrt(FRESNEL)
    return weight * np.exp(1j * np.pi * offset * offset / FRESNEL)


def np_band(out_pos, in_pos):
    offset = out_pos[:, None] - in_pos[None, :]
    inside = np.abs(offset) <= HALO
    return np.where(inside, np_taps()[np.clip(offset, -HALO, HALO) + HALO], 0.0)


def row_constant(height):
    matrices = []
    for core in range(2):
        pos = (np.arange(height) + core * (height // 2)) % height
        band = np_band(pos, pos)
        whole = np.block([[band.real, -band.imag], [band.imag, band.real]])
        matrices.append(np.concatenate(np_halves(whole), axis=1))
    return np.stack(matrices)


def col_constant():
    lane = np.arange(LANES)
    turned = np.where((lane >= HALO) & (lane < LANES - HALO), lane ^ (LANES // 2), lane)
    edge_pos = np.where(turned < LANES // 2, turned + LANES, turned - LANES)
    parts = []
    for position in (lane, edge_pos):
        band = np_band(lane, position).T
        parts.append(np.block([[band.real, band.imag], [-band.imag, band.real]]))
    return np.concatenate(np_halves(np.concatenate(parts, axis=0)), axis=1)


def both_rows(near_ref, far_ref, where):
    return jnp.concatenate([near_ref[where], far_ref[where]], axis=0)


def turned(slice_index, block, screens, wave):
    near_cos, near_sin, far_cos, far_sin = screens
    cos = both_rows(near_cos, far_cos, (slice_index, block))
    sin = both_rows(near_sin, far_sin, (slice_index, block))
    real, imag = wave
    return cos * real - sin * imag, cos * imag + sin * real


def row_products(row_matrix, chunks):
    whole = row_matrix.shape[0]
    highs, wides = [], []
    for columns in chunks:
        high, low = halves(columns)
        highs.append(high)
        wide = jnp.dot(
            row_matrix[:, :whole], jnp.concatenate([high, low], axis=1), preferred_element_type=jnp.float32
        )
        wides.append(wide[:, : columns.shape[1]] + wide[:, columns.shape[1] :])
    rest = jnp.dot(row_matrix[:, whole:], jnp.concatenate(highs, axis=1), preferred_element_type=jnp.float32)
    done, begin = [], 0
    for wide in wides:
        done.append(wide + rest[:, begin : begin + wide.shape[1]])
        begin += wide.shape[1]
    return done


def col_product(high, low, col_ref):
    wide = jnp.dot(high, col_ref[...], preferred_element_type=jnp.float32)
    rest = jnp.dot(low, col_ref[: 2 * LANES, : 2 * LANES], preferred_element_type=jnp.float32)
    return wide[:, : 2 * LANES] + wide[:, 2 * LANES :] + rest


def three_parts(value):
    high = value.astype(jnp.bfloat16)
    rest = value - high.astype(jnp.float32)
    return high, rest.astype(jnp.bfloat16), pltpu.roll(rest, LANES // 2, 1).astype(jnp.bfloat16)


def advance(slice_index, start, waves, screens, row_matrix, col_ref, edge_ref, outer=None):
    size, height = len(waves), waves[0][0].shape[0]
    chunks = [range(place, min(place + 2, size)) for place in range(0, size, 2)]
    highs, lows = [], []
    columns = [
        jnp.concatenate(
            [
                jnp.concatenate(
                    waves[place] if slice_index is None else turned(slice_index, start + place, screens, waves[place]),
                    axis=0,
                )
                for place in chunk
            ],
            axis=1,
        )
        for chunk in chunks
    ]
    for chunk, done in zip(chunks, row_products(row_matrix, columns)):
        for sub, place in enumerate(chunk):
            own_high, own_low = [], []
            for part in range(2):
                value = done[part * height : (part + 1) * height, sub * LANES : (sub + 1) * LANES]
                high, low, swung = three_parts(value)
                own_high.append(high)
                own_low.append(low)
                edge = part * LANES
                if place > 0:
                    edge_ref[place - 1, :, pl.ds(edge, HALO)] = high[:, :HALO]
                    edge_ref[place - 1, :, pl.ds(edge + 2 * HALO, HALO)] = swung[:, 2 * HALO : 3 * HALO]
                if place < size - 1:
                    edge_ref[place + 1, :, pl.ds(edge + 3 * HALO, HALO)] = high[:, 3 * HALO :]
                    edge_ref[place + 1, :, pl.ds(edge + HALO, HALO)] = swung[:, HALO : 2 * HALO]
            highs.append(jnp.concatenate(own_high, axis=1))
            lows.append(jnp.concatenate(own_low, axis=1))
    edge_parts = [edge_ref[place] for place in range(size)]
    if outer is not None:
        index, high_ref, low_ref = outer
        for end, place in enumerate((0, size - 1)):
            high_ref[end], low_ref[end] = highs[place], lows[place]
        highs = highs[1:-1] + [high_ref[index]]
        lows = lows[1:-1] + [low_ref[index]]
        edge_parts = edge_parts[1:-1] + [edge_ref[index * (size - 1)]]
        chunks = [range(place, min(place + 2, size - 1)) for place in range(0, size - 1, 2)]
    results = []
    for chunk in chunks:
        edges = jnp.concatenate([edge_parts[place] for place in chunk], axis=0)
        own = jnp.concatenate([highs[place] for place in chunk], axis=0)
        total = col_product(
            jnp.concatenate([own, edges], axis=1),
            jnp.concatenate([lows[place] for place in chunk], axis=0),
            col_ref,
        )
        for sub in range(len(chunk)):
            block = total[sub * height : (sub + 1) * height]
            results.append((block[:, :LANES], block[:, LANES:]))
    return results


def clear_edge(edge_ref, place, right):
    for part in range(2):
        for begin in (0, 2 * HALO) if right else (HALO, 3 * HALO):
            cells = pl.ds(part * LANES + begin, HALO)
            edge_ref[place, :, cells] = jnp.zeros((edge_ref.shape[1], HALO), edge_ref.dtype)


def keep(wave_ref, waves):
    for place, wave in enumerate(waves):
        wave_ref[place, 0], wave_ref[place, 1] = wave


def load_kernel(tilt_ref, near_own, row_from, col_from, row_to, col_to, wave_ref, cos_ref, sin_ref, sems):
    blocks, _, height, _ = wave_ref.shape
    core = lax.axis_index("row")
    copies = [
        pltpu.make_async_copy(row_from.at[core], row_to, sems.at[0]),
        pltpu.make_async_copy(col_from, col_to, sems.at[1]),
    ]
    for copy in copies:
        copy.start()
    for col in range(blocks):
        cos_ref[col], sin_ref[col] = cos_sin(near_own[col ^ lax.axis_index("col"), 0])

    def cycles(number, position, extent):
        fraction = (number * position).astype(jnp.float32) / extent
        return turn(fraction - jnp.round(fraction))

    row = lax.broadcasted_iota(jnp.int32, (height, LANES), 0) + core * (height // 2)
    row = jnp.where(row >= height, row - height, row)
    row_cos, row_sin = cycles(tilt_ref[core, 0], row, float(height))
    for block in range(blocks):
        col_cos, col_sin = cycles(
            tilt_ref[core, 1],
            lax.broadcasted_iota(jnp.int32, (8, LANES), 1) + block * LANES,
            float(blocks * LANES),
        )
        col_cos, col_sin = col_cos[:1], col_sin[:1]
        wave_ref[block, 0] = row_cos * col_cos - row_sin * col_sin
        wave_ref[block, 1] = row_sin * col_cos + row_cos * col_sin
    for copy in copies:
        copy.wait()


def second_kernel(near_rest, own_cos, own_sin, cos_ref, sin_ref):
    blocks = own_cos.shape[0]
    count = cos_ref.shape[0]
    own_section, own_place = lax.axis_index("depth"), lax.axis_index("col")

    def screens(col, carry):
        held = col ^ own_place
        cos_ref[own_section, col], sin_ref[own_section, col] = own_cos[col], own_sin[col]
        for bits in range(1, count):
            cos_ref[bits ^ own_section, col], sin_ref[bits ^ own_section, col] = cos_sin(near_rest[held, (4 - bits) % 3])
        return carry

    lax.fori_loop(0, blocks, screens, 0)


def wave_kernel(
    wave_ref, near_cos, near_sin, near_own, far_first, far_second, row_ref, col_ref,
    mine_ref, theirs_ref, far_cos, far_sin, kept_ref, moved_ref, left_ref, grad_ref, even_edge, odd_edge,
    outer_high, outer_low,
):
    blocks, _, height, _ = wave_ref.shape
    count = near_cos.shape[0]
    core, own_section, own_place = lax.axis_index("row"), lax.axis_index("depth"), lax.axis_index("col")
    near, far = pl.ds(0, height // 2), pl.ds(height // 2, height // 2)
    screens = (near_cos, near_sin, far_cos, far_sin)
    row_matrix = row_ref[...]
    window = min(3, blocks)
    window_start = jnp.clip(own_place - 1, 0, blocks - window)
    own_in_window = own_place - window_start
    edges = (even_edge, odd_edge)

    def far_screens(slice_index):
        bits = slice_index ^ own_section
        for col in range(blocks):
            held = col ^ own_place
            others = lax.rem(4 - bits, 3)
            in_first = (bits == 0) | (held == 3)
            place = jnp.where(bits == 0, 2 * held, 2 * blocks + others)
            angle = jnp.where(in_first, far_first[place], far_second[jnp.minimum(held, 2) * (count - 1) + others])
            far_cos[slice_index, col], far_sin[slice_index, col] = cos_sin(angle)

    for edge_ref in edges:
        clear_edge(edge_ref, 0, False)
        clear_edge(edge_ref, blocks - 1, True)
    far_screens(0)

    waves = [(wave_ref[place, 0], wave_ref[place, 1]) for place in range(blocks)]
    entering = wave_ref[own_place]
    for tick in range(count):
        moved_ref[tick, 0], moved_ref[tick, 1] = turned(tick, own_place, screens, (entering[0], entering[1]))
        outer = (window_start, outer_high, outer_low) if tick + 1 == count else None
        waves = advance(tick, 0, waves, screens, row_matrix, col_ref, edges[tick % 2], outer)
        if tick + 1 < count:
            far_screens(tick + 1)
            keep(kept_ref, waves)
        else:
            for place, wave in zip((1, 2, window_start * (blocks - 1)), waves):
                kept_ref[place, 0], kept_ref[place, 1] = wave
        entering = kept_ref[own_place]
        left_ref[tick] = entering

    for edge_ref in edges:
        clear_edge(edge_ref, window - 1, True)
    waves = []
    for place in range(window):
        block = window_start + place
        real, imag = kept_ref[block, 0], kept_ref[block, 1]
        held = block ^ own_place
        measured = jnp.concatenate([near_own[held, 1 + core], far_first[2 * held + 1]], axis=0)
        misfit = 2.0 * (real * real + imag * imag - measured)
        waves.append((misfit * real, -misfit * imag))

    for tick in range(count - 1):
        passed = count - tick if tick else None
        waves = advance(passed, window_start, waves, screens, row_matrix, col_ref, edges[tick % 2])
        keep(kept_ref, waves)
        arrived = count - 1 - tick
        pulled = kept_ref[own_in_window]
        grad_ref[arrived] = -(pulled[1] * moved_ref[arrived, 0] + pulled[0] * moved_ref[arrived, 1])

    left, right = jnp.maximum(own_place - 1, 0), jnp.minimum(own_place + 1, blocks - 1)
    lane = lax.broadcasted_iota(jnp.int32, (2 * height, LANES), 1)
    has_left, has_right = own_place > 0, own_place < blocks - 1

    def cells(block):
        wave = kept_ref[block - window_start]
        return jnp.concatenate(turned(1, block, screens, (wave[0], wave[1])), axis=0)

    edge_cells = jnp.where(
        lane < LANES // 2, jnp.where(has_right, cells(right), 0.0), jnp.where(has_left, cells(left), 0.0)
    )
    done = row_products(row_matrix, [jnp.concatenate([cells(own_place), edge_cells], axis=1)])[0]
    lane = lax.broadcasted_iota(jnp.int32, (height, LANES), 1)
    between = (lane >= HALO) & (lane < LANES - HALO)
    highs, lows, edges = [], [], []
    for part in range(2):
        high, low, _ = three_parts(done[part * height : (part + 1) * height, :LANES])
        highs.append(high)
        lows.append(low)
        value = done[part * height : (part + 1) * height, LANES:]
        whole_high = value.astype(jnp.bfloat16).astype(jnp.float32)
        edge = jnp.where(between, pltpu.roll(value - whole_high, LANES // 2, 1), whole_high)
        edges.append(edge.astype(jnp.bfloat16))
    pulled = col_product(jnp.concatenate(highs + edges, axis=1), jnp.concatenate(lows, axis=1), col_ref)
    grad_ref[0] = -(pulled[:, LANES:] * moved_ref[0, 0] + pulled[:, :LANES] * moved_ref[0, 1])

    for target, row in ((mine_ref, near), (theirs_ref, far)):
        for part in range(2):
            target[0, part] = left_ref[own_section, part, row]
        target[0, 2] = grad_ref[own_section, row]


def finish_kernel(mine_ref, received_ref, grad_ref, exit_ref, total_ref, sems):
    core = lax.axis_index("row")
    copies = []
    for source, item in ((mine_ref, core), (received_ref, 1 - core)):
        copies.append(pltpu.make_async_copy(source.at[:, pl.ds(0, 2)], exit_ref.at[item], sems.at[len(copies)]))
    for copy in copies:
        copy.start()
    total_ref[...] = mine_ref[:, 2] + received_ref[:, 2]
    copies.append(pltpu.make_async_copy(total_ref, grad_ref, sems.at[2]))
    copies[2].start()
    for copy in copies:
        copy.wait()


def spread(shard, axis, all_bits, reach=3):
    pieces = []
    for bits in all_bits:
        pairs = [(i, i ^ bits) for i in range(4) if abs(i - (i ^ bits)) <= reach]
        pieces.append(lax.ppermute(shard, axis, pairs))
    return pieces


def swap_cores(value):
    return lax.ppermute(value, "row", [(0, 1), (1, 0)])


def whole_field_body(phase, tilt, intensity):
    _, tile_r, tile_c = phase.shape
    count, blocks = lax.axis_size("depth"), lax.axis_size("col")
    core = lax.axis_index("row")
    height = 2 * tile_r
    vmem = pl.BlockSpec(memory_space=pltpu.VMEM)
    smem = pl.BlockSpec(memory_space=pltpu.SMEM)
    hbm = pl.BlockSpec(memory_space=pl.ANY)

    def array(*shape):
        return jax.ShapeDtypeStruct(shape, jnp.float32)

    def params(mebibytes):
        return pltpu.CompilerParams(vmem_limit_bytes=mebibytes * 2**20)

    first_depth, farthest, two_away = spread(phase, "depth", (1, 3, 2))
    first_depth, measured, slab = lax.optimization_barrier((first_depth, intensity, phase))
    other_depths = [first_depth, farthest, two_away]
    other_depths = jnp.concatenate(other_depths, axis=0)
    packet = jnp.concatenate([slab, measured], axis=0)
    near_own = [packet]
    for bits in range(1, blocks):
        pairs = [(i, i ^ bits) for i in range(blocks)]
        close = [(i, j) for i, j in pairs if abs(i - j) <= 1]
        if close:
            near_own.append(lax.ppermute(packet, "col", close))
        else:
            further = [(i, j) for i, j in pairs if abs(i - j) <= 2]
            arrived = lax.ppermute(slab, "col", further) if further else jnp.zeros_like(slab)
            near_own.append(jnp.concatenate([arrived, jnp.zeros_like(measured)], axis=0))
    near_own = jnp.stack(near_own)
    arriving = spread(other_depths, "col", (1, 2, 3), 2)
    row_all, col_all = jnp.asarray(row_constant(height)), jnp.asarray(col_constant())
    near_own, row_all, col_all = lax.optimization_barrier((near_own, row_all, col_all))
    half_screens = (count, blocks, tile_r, tile_c)
    field = (blocks, 2, height, tile_c)
    row_matrix, col_matrix, wave, own_cos, own_sin = pl.pallas_call(
        load_kernel,
        out_shape=(
            jax.ShapeDtypeStruct(row_all.shape[1:], row_all.dtype),
            jax.ShapeDtypeStruct(col_all.shape, col_all.dtype),
            array(*field),
            array(blocks, tile_r, tile_c),
            array(blocks, tile_r, tile_c),
        ),
        in_specs=[smem, vmem, hbm, hbm],
        out_specs=(vmem,) * 5,
        scratch_shapes=[pltpu.SemaphoreType.DMA((2,))],
        compiler_params=params(4),
        cost_estimate=pl.CostEstimate(flops=10**8, bytes_accessed=2**20, transcendentals=0),
    )(tilt, near_own, row_all, col_all)
    arriving[2], near_own, row_matrix, col_matrix, wave, own_cos, own_sin = lax.optimization_barrier(
        (arriving[2], near_own, row_matrix, col_matrix, wave, own_cos, own_sin)
    )
    wanted = lax.dynamic_slice_in_dim(near_own, 2 - core, 1, 1)
    packets = jnp.concatenate([near_own[:, :1], wanted], axis=1).reshape(2 * blocks, tile_r, tile_c)
    far_first = swap_cores(jnp.concatenate([packets, arriving[2]], axis=0))
    far_second = swap_cores(jnp.concatenate([other_depths] + arriving[:2], axis=0))
    near_rest = jnp.stack([other_depths] + arriving)

    near_cos, near_sin = pl.pallas_call(
        second_kernel,
        out_shape=(array(*half_screens),) * 2,
        in_specs=[vmem] * 3,
        out_specs=(vmem,) * 2,
        compiler_params=params(8),
        cost_estimate=pl.CostEstimate(flops=5 * 10**8, bytes_accessed=2**20, transcendentals=0),
    )(near_rest, own_cos, own_sin)
    mine, theirs = pl.pallas_call(
        wave_kernel,
        out_shape=(array(1, 3, tile_r, tile_c),) * 2,
        in_specs=[vmem] * 8,
        out_specs=(vmem,) * 2,
        scratch_shapes=[pltpu.VMEM(half_screens, jnp.float32)] * 2
        + [pltpu.VMEM(field, jnp.float32)]
        + [pltpu.VMEM((count, 2, height, tile_c), jnp.float32)] * 2
        + [pltpu.VMEM((count, height, tile_c), jnp.float32)]
        + [pltpu.VMEM((blocks, height, 2 * LANES), jnp.bfloat16)] * 2
        + [pltpu.VMEM((2, height, 2 * LANES), jnp.bfloat16)] * 2,
        compiler_params=params(24),
    )(
        wave, near_cos, near_sin, near_own, far_first, far_second,
        row_matrix, col_matrix,
    )
    return pl.pallas_call(
        finish_kernel,
        out_shape=(array(*phase.shape), array(2, 1, 2, tile_r, tile_c)),
        in_specs=[vmem, vmem],
        out_specs=(hbm, hbm),
        scratch_shapes=[pltpu.VMEM(phase.shape, jnp.float32), pltpu.SemaphoreType.DMA((3,))],
        compiler_params=params(4),
    )(mine, swap_cores(theirs))


def extended_2(cells, sides, width):
    for axis, dim in sides:
        count = lax.axis_size(axis)
        ends = count - 1
        head = lax.slice_in_dim(cells, 0, width, axis=dim)
        tail = lax.slice_in_dim(cells, cells.shape[dim] - width, cells.shape[dim], axis=dim)
        cells = jnp.concatenate(
            [
                lax.ppermute(tail, axis, [(i, (i + 1) % count) for i in range(ends)]),
                cells,
                lax.ppermute(head, axis, [((i + 1) % count, i) for i in range(ends)]),
            ],
            axis=dim,
        )
    return cells


def from_behind(value, axis, steps):
    count = lax.axis_size(axis)
    leading, last = (max(0, -steps), min(count, count - steps))
    return lax.ppermute(value, axis, [(source, source + steps) for source in range(leading, last)])


def band_matrix(block_size, margin, fresnel, adjoint):
    shape_full = (block_size, block_size + 2 * margin)
    out_idx = lax.broadcasted_iota(jnp.int32, shape_full, 0)
    in_idx = lax.broadcasted_iota(jnp.int32, shape_full, 1)
    offset = (out_idx + margin - in_idx).astype(jnp.float32)
    inside = jnp.abs(offset) <= margin
    taper_dist = jnp.maximum(jnp.abs(offset) - 0.5 * margin, 0.0)
    profile = jnp.cos(jnp.pi * taper_dist / (margin + 2.0))
    weight = profile * profile / math.sqrt(fresnel)
    phase_angle = jnp.pi * offset * offset / fresnel
    real_part = jnp.where(inside, jnp.cos(phase_angle) * weight, 0.0)
    imag_part = jnp.where(inside, jnp.sin(phase_angle) * weight, 0.0)
    if adjoint:
        imag_part = -imag_part
    upper = jnp.stack([real_part, -imag_part])
    lower = jnp.stack([imag_part, real_part])
    return jnp.stack([upper, lower])


def along_rows(extended, matrix):
    pieces = [jnp.einsum("pqij,gqjc->gpic", matrix, extended, precision=lax.Precision.HIGHEST)]
    return jnp.concatenate(pieces, axis=2)


def along_cols(extended, matrix, margin):
    block_size = matrix.shape[2]
    extent = extended.shape[3] - 2 * margin
    pieces = []
    for block_start in range(0, extent, block_size):
        window = extended[:, :, :, block_start : block_start + block_size + 2 * margin]
        pieces.append(
            jnp.einsum("pqij,gqrj->gpri", matrix, window, precision=lax.Precision.HIGHEST)
        )
    return jnp.concatenate(pieces, axis=3)


def propagate(current, row_matrix, col_matrix):
    with_rows = extended_2(current, (("row", 2),), HALO)
    row_done = along_rows(with_rows, row_matrix)
    with_cols = extended_2(row_done, (("col", 3),), HALO)
    return along_cols(with_cols, col_matrix, HALO)


def transmit(screen, current, adjoint):
    screen_re = screen[0][None]
    screen_im = screen[1][None]
    if adjoint:
        screen_im = -screen_im
    real_part = screen_re * current[:, 0] - screen_im * current[:, 1]
    imag_part = screen_re * current[:, 1] + screen_im * current[:, 0]
    return jnp.stack([real_part, imag_part], axis=1)


def store_item(store, current, first_item, slice_index, active):
    begin = (first_item, jnp.int32(slice_index), jnp.int32(0), jnp.int32(0), jnp.int32(0))
    sizes_now = (current.shape[0], 1) + current.shape[1:]
    previous = lax.dynamic_slice(store, begin, sizes_now)
    fresh = jnp.where(active, current[:, None], previous)
    return lax.dynamic_update_slice(store, fresh, begin)


def staged_body(phase, tilt, intensity):
    slices, tile_r, tile_c = phase.shape
    batch_size = tilt.shape[0]
    sections = lax.axis_size("depth")
    section_index = lax.axis_index("depth")
    group_size = 1
    groups = batch_size // group_size
    tick_count = sections + groups - 1
    block_r = 64
    block_c = 128
    fwd_rows = band_matrix(block_r, HALO, FRESNEL, False)
    fwd_cols = band_matrix(block_c, HALO, FRESNEL, False)
    adj_rows = band_matrix(block_r, HALO, FRESNEL, True)
    adj_cols = band_matrix(block_c, HALO, FRESNEL, True)
    row_pos = (
        lax.axis_index("row") * tile_r + lax.broadcasted_iota(jnp.int32, (tile_r, tile_c), 0)
    ).astype(jnp.float32)
    col_pos = (
        lax.axis_index("col") * tile_c + lax.broadcasted_iota(jnp.int32, (tile_r, tile_c), 1)
    ).astype(jnp.float32)
    height = float(tile_r * lax.axis_size("row"))
    width_all = float(tile_c * lax.axis_size("col"))
    tilt_f = tilt.astype(jnp.float32)
    phase_angle = (
        2.0
        * jnp.pi
        * (
            tilt_f[:, 0, None, None] * row_pos / height
            + tilt_f[:, 1, None, None] * col_pos / width_all
        )
    )
    incident = jnp.stack([jnp.cos(phase_angle), jnp.sin(phase_angle)], axis=1)
    screens = jnp.stack([jnp.cos(phase), jnp.sin(phase)], axis=1)

    def forward_tick(tick_now, carry):
        incoming, entering, leaving = carry
        group_index = tick_now - section_index
        active = (group_index >= 0) & (group_index < groups)
        first_item = jnp.clip(group_index, 0, groups - 1) * group_size
        current = jnp.where(
            section_index == 0,
            lax.dynamic_slice_in_dim(incident, first_item, group_size, 0),
            incoming,
        )
        entering = store_item(entering, current, first_item, 0, active)
        current = propagate(transmit(screens[0], current, False), fwd_rows, fwd_cols)
        leaving = store_item(leaving, current, first_item, 0, active)
        incoming = from_behind(current, "depth", 1)
        return (incoming, entering, leaving)

    store_zero = jnp.zeros((batch_size, slices, 2, tile_r, tile_c), jnp.float32)
    start_wave = jnp.zeros((group_size, 2, tile_r, tile_c), jnp.float32)
    _, entering, leaving = lax.fori_loop(
        0, tick_count, forward_tick, (start_wave, store_zero, store_zero)
    )
    final_wave = leaving[:, slices - 1]
    misfit = final_wave[:, 0] * final_wave[:, 0] + final_wave[:, 1] * final_wave[:, 1] - intensity
    seed_adjoint = 2.0 * misfit[:, None] * final_wave

    def backward_tick(tick_now, carry):
        incoming, gradient = carry
        group_index = tick_now - (sections - 1 - section_index)
        active = (group_index >= 0) & (group_index < groups)
        first_item = jnp.clip(group_index, 0, groups - 1) * group_size
        adjoint_wave = jnp.where(
            section_index == sections - 1,
            lax.dynamic_slice_in_dim(seed_adjoint, first_item, group_size, 0),
            incoming,
        )
        for slice_index in reversed(range(slices)):
            pulled = propagate(adjoint_wave, adj_rows, adj_cols)
            arrived = lax.dynamic_slice_in_dim(entering[:, slice_index], first_item, group_size, 0)
            moved = transmit(screens[slice_index], arrived, False)
            contribution = jnp.sum(pulled[:, 1] * moved[:, 0] - pulled[:, 0] * moved[:, 1], axis=0)
            gradient = gradient.at[slice_index].add(jnp.where(active, contribution, 0.0))
            adjoint_wave = transmit(screens[slice_index], pulled, True)
        incoming = from_behind(adjoint_wave, "depth", -1)
        return (incoming, gradient)

    grad_zero = jnp.zeros((slices, tile_r, tile_c), jnp.float32)
    _, gradient = lax.fori_loop(0, tick_count, backward_tick, (start_wave, grad_zero))
    return (gradient, leaving)


def fits_whole(phase_shape, batch, mesh):
    slices, height, width = phase_shape
    rows, cols, sections = mesh.shape["row"], mesh.shape["col"], mesh.shape["depth"]
    return (
        4 * height * width * (slices + batch) <= GATHER_BUDGET
        and batch == rows == 2
        and slices == sections
        and sections == 4
        and cols == 4
        and height == LANES
        and width == cols * LANES
        and sections * HALO <= LANES
    )


def solution(mesh):
    placed = (P("depth", "row", "col"), P(), P(None, "row", "col"))

    def run(phase, tilt, intensity):
        if fits_whole(phase.shape, tilt.shape[0], mesh):
            body = whole_field_body
        else:
            body = staged_body
        return jax.shard_map(
            body,
            mesh=mesh,
            in_specs=placed,
            out_specs=(P("depth", "row", "col"), P(None, "depth", None, "row", "col")),
            check_vma=False,
        )(phase, tilt, intensity)

    return run
```

```python
import math

import jax
import jax.numpy as jnp
import numpy as np
from jax import lax
from jax.experimental import pallas as pl
from jax.experimental.pallas import tpu as pltpu
from jax.sharding import PartitionSpec as P

HALO = 32
FRESNEL = 64
LANES = 128
GATHER_BUDGET = 4 * 2**20
SIN = (
    0.9999999980536763,
    -0.1666666530009577,
    0.008333305907073658,
    -0.00019838908256358006,
    2.745822627876341e-06,
    -2.3043562782810933e-08,
)
COS = (
    0.9999999961345007,
    -0.4999999301617528,
    0.04166646215023687,
    -0.0013886696163545999,
    2.4695045482778703e-05,
    -2.5154931690000354e-07,
)


def horner(coefficients, square):
    total = jnp.full_like(square, coefficients[-1])
    for coefficient in coefficients[-2::-1]:
        total = total * square + coefficient
    return total


def cos_sin(angle):
    square = angle * angle
    return horner(COS, square), horner(SIN, square) * angle


def turn(fraction):
    half_cos, half_sin = cos_sin(fraction * math.pi)
    return half_cos * half_cos - half_sin * half_sin, 2.0 * half_cos * half_sin


def halves(value):
    high = value.astype(jnp.bfloat16)
    return high, (value - high.astype(jnp.float32)).astype(jnp.bfloat16)


def np_halves(matrix):
    high = matrix.astype(jnp.bfloat16)
    return high, (matrix - high.astype(np.float64)).astype(jnp.bfloat16)


def np_taps():
    offset = np.arange(-HALO, HALO + 1, dtype=np.float64)
    taper = np.maximum(np.abs(offset) - 0.5 * HALO, 0.0)
    weight = np.cos(np.pi * taper / (HALO + 2.0)) ** 2 / math.sqrt(FRESNEL)
    return weight * np.exp(1j * np.pi * offset * offset / FRESNEL)


def np_band(out_pos, in_pos):
    offset = out_pos[:, None] - in_pos[None, :]
    inside = np.abs(offset) <= HALO
    return np.where(inside, np_taps()[np.clip(offset, -HALO, HALO) + HALO], 0.0)


def row_constant(height):
    matrices = []
    for core in range(2):
        pos = (np.arange(height) + core * (height // 2)) % height
        band = np_band(pos, pos)
        whole = np.block([[band.real, -band.imag], [band.imag, band.real]])
        matrices.append(np.concatenate(np_halves(whole), axis=1))
    return np.stack(matrices)


def col_constant():
    lane = np.arange(LANES)
    turned = np.where((lane >= HALO) & (lane < LANES - HALO), lane ^ (LANES // 2), lane)
    edge_pos = np.where(turned < LANES // 2, turned + LANES, turned - LANES)
    parts = []
    for position in (lane, edge_pos):
        band = np_band(lane, position).T
        parts.append(np.block([[band.real, band.imag], [-band.imag, band.real]]))
    return np.concatenate(np_halves(np.concatenate(parts, axis=0)), axis=1)


def both_rows(near_ref, far_ref, where):
    return jnp.concatenate([near_ref[where], far_ref[where]], axis=0)


def turned(slice_index, block, screens, wave):
    near_cos, near_sin, far_cos, far_sin = screens
    cos = both_rows(near_cos, far_cos, (slice_index, block))
    sin = both_rows(near_sin, far_sin, (slice_index, block))
    real, imag = wave
    return cos * real - sin * imag, cos * imag + sin * real


def row_products(row_matrix, chunks):
    whole = row_matrix.shape[0]
    highs, wides = [], []
    for columns in chunks:
        high, low = halves(columns)
        highs.append(high)
        wide = jnp.dot(
            row_matrix[:, :whole], jnp.concatenate([high, low], axis=1), preferred_element_type=jnp.float32
        )
        wides.append(wide[:, : columns.shape[1]] + wide[:, columns.shape[1] :])
    rest = jnp.dot(row_matrix[:, whole:], jnp.concatenate(highs, axis=1), preferred_element_type=jnp.float32)
    done, begin = [], 0
    for wide in wides:
        done.append(wide + rest[:, begin : begin + wide.shape[1]])
        begin += wide.shape[1]
    return done


def col_product(high, low, col_ref):
    wide = jnp.dot(high, col_ref[...], preferred_element_type=jnp.float32)
    rest = jnp.dot(low, col_ref[: 2 * LANES, : 2 * LANES], preferred_element_type=jnp.float32)
    return wide[:, : 2 * LANES] + wide[:, 2 * LANES :] + rest


def three_parts(value):
    high = value.astype(jnp.bfloat16)
    rest = value - high.astype(jnp.float32)
    return high, rest.astype(jnp.bfloat16), pltpu.roll(rest, LANES // 2, 1).astype(jnp.bfloat16)


def advance(slice_index, start, waves, screens, row_matrix, col_ref, edge_ref, outer=None):
    size, height = len(waves), waves[0][0].shape[0]
    chunks = [range(place, min(place + 2, size)) for place in range(0, size, 2)]
    highs, lows = [], []
    columns = [
        jnp.concatenate(
            [
                jnp.concatenate(
                    waves[place] if slice_index is None else turned(slice_index, start + place, screens, waves[place]),
                    axis=0,
                )
                for place in chunk
            ],
            axis=1,
        )
        for chunk in chunks
    ]
    for chunk, done in zip(chunks, row_products(row_matrix, columns)):
        for sub, place in enumerate(chunk):
            own_high, own_low = [], []
            for part in range(2):
                value = done[part * height : (part + 1) * height, sub * LANES : (sub + 1) * LANES]
                high, low, swung = three_parts(value)
                own_high.append(high)
                own_low.append(low)
                edge = part * LANES
                if place > 0:
                    edge_ref[place - 1, :, pl.ds(edge, HALO)] = high[:, :HALO]
                    edge_ref[place - 1, :, pl.ds(edge + 2 * HALO, HALO)] = swung[:, 2 * HALO : 3 * HALO]
                if place < size - 1:
                    edge_ref[place + 1, :, pl.ds(edge + 3 * HALO, HALO)] = high[:, 3 * HALO :]
                    edge_ref[place + 1, :, pl.ds(edge + HALO, HALO)] = swung[:, HALO : 2 * HALO]
            highs.append(jnp.concatenate(own_high, axis=1))
            lows.append(jnp.concatenate(own_low, axis=1))
    edge_parts = [edge_ref[place] for place in range(size)]
    if outer is not None:
        index, high_ref, low_ref = outer
        for end, place in enumerate((0, size - 1)):
            high_ref[end], low_ref[end] = highs[place], lows[place]
        highs = highs[1:-1] + [high_ref[index]]
        lows = lows[1:-1] + [low_ref[index]]
        edge_parts = edge_parts[1:-1] + [edge_ref[index * (size - 1)]]
        chunks = [range(place, min(place + 2, size - 1)) for place in range(0, size - 1, 2)]
    results = []
    for chunk in chunks:
        edges = jnp.concatenate([edge_parts[place] for place in chunk], axis=0)
        own = jnp.concatenate([highs[place] for place in chunk], axis=0)
        total = col_product(
            jnp.concatenate([own, edges], axis=1),
            jnp.concatenate([lows[place] for place in chunk], axis=0),
            col_ref,
        )
        for sub in range(len(chunk)):
            block = total[sub * height : (sub + 1) * height]
            results.append((block[:, :LANES], block[:, LANES:]))
    return results


def clear_edge(edge_ref, place, right):
    for part in range(2):
        for begin in (0, 2 * HALO) if right else (HALO, 3 * HALO):
            cells = pl.ds(part * LANES + begin, HALO)
            edge_ref[place, :, cells] = jnp.zeros((edge_ref.shape[1], HALO), edge_ref.dtype)


def keep(wave_ref, waves):
    for place, wave in enumerate(waves):
        wave_ref[place, 0], wave_ref[place, 1] = wave


def load_kernel(tilt_ref, near_own, row_from, col_from, row_to, col_to, wave_ref, cos_ref, sin_ref, sems):
    blocks, _, height, _ = wave_ref.shape
    core = lax.axis_index("row")
    copies = [
        pltpu.make_async_copy(row_from.at[core], row_to, sems.at[0]),
        pltpu.make_async_copy(col_from, col_to, sems.at[1]),
    ]
    for copy in copies:
        copy.start()
    for col in range(blocks):
        cos_ref[col], sin_ref[col] = cos_sin(near_own[col ^ lax.axis_index("col"), 0])

    def cycles(number, position, extent):
        fraction = (number * position).astype(jnp.float32) / extent
        return turn(fraction - jnp.round(fraction))

    row = lax.broadcasted_iota(jnp.int32, (height, LANES), 0) + core * (height // 2)
    row = jnp.where(row >= height, row - height, row)
    row_cos, row_sin = cycles(tilt_ref[core, 0], row, float(height))
    for block in range(blocks):
        col_cos, col_sin = cycles(
            tilt_ref[core, 1],
            lax.broadcasted_iota(jnp.int32, (8, LANES), 1) + block * LANES,
            float(blocks * LANES),
        )
        col_cos, col_sin = col_cos[:1], col_sin[:1]
        wave_ref[block, 0] = row_cos * col_cos - row_sin * col_sin
        wave_ref[block, 1] = row_sin * col_cos + row_cos * col_sin
    for copy in copies:
        copy.wait()


def second_kernel(near_rest, own_cos, own_sin, cos_ref, sin_ref):
    blocks = own_cos.shape[0]
    count = cos_ref.shape[0]
    own_section, own_place = lax.axis_index("depth"), lax.axis_index("col")

    def screens(col, carry):
        held = col ^ own_place
        cos_ref[own_section, col], sin_ref[own_section, col] = own_cos[col], own_sin[col]
        for bits in range(1, count):
            cos_ref[bits ^ own_section, col], sin_ref[bits ^ own_section, col] = cos_sin(near_rest[held, (4 - bits) % 3])
        return carry

    lax.fori_loop(0, blocks, screens, 0)


def wave_kernel(
    wave_ref, near_cos, near_sin, near_own, far_first, far_second, row_ref, col_ref,
    mine_ref, theirs_ref, far_cos, far_sin, kept_ref, moved_ref, left_ref, grad_ref, even_edge, odd_edge,
    outer_high, outer_low,
):
    blocks, _, height, _ = wave_ref.shape
    count = near_cos.shape[0]
    core, own_section, own_place = lax.axis_index("row"), lax.axis_index("depth"), lax.axis_index("col")
    near, far = pl.ds(0, height // 2), pl.ds(height // 2, height // 2)
    screens = (near_cos, near_sin, far_cos, far_sin)
    row_matrix = row_ref[...]
    window = min(3, blocks)
    window_start = jnp.clip(own_place - 1, 0, blocks - window)
    own_in_window = own_place - window_start
    edges = (even_edge, odd_edge)

    def far_screens(slice_index):
        bits = slice_index ^ own_section
        for col in range(blocks):
            held = col ^ own_place
            others = lax.rem(4 - bits, 3)
            in_first = (bits == 0) | (held == 3)
            place = jnp.where(bits == 0, 2 * held, 2 * blocks + others)
            angle = jnp.where(in_first, far_first[place], far_second[jnp.minimum(held, 2) * (count - 1) + others])
            far_cos[slice_index, col], far_sin[slice_index, col] = cos_sin(angle)

    for edge_ref in edges:
        clear_edge(edge_ref, 0, False)
        clear_edge(edge_ref, blocks - 1, True)
    far_screens(0)

    waves = [(wave_ref[place, 0], wave_ref[place, 1]) for place in range(blocks)]
    entering = wave_ref[own_place]
    for tick in range(count):
        moved_ref[tick, 0], moved_ref[tick, 1] = turned(tick, own_place, screens, (entering[0], entering[1]))
        if tick + 1 < count:
            far_screens(tick + 1)
        outer = (window_start, outer_high, outer_low) if tick + 1 == count else None
        waves = advance(tick, 0, waves, screens, row_matrix, col_ref, edges[tick % 2], outer)
        if tick + 1 < count:
            keep(kept_ref, waves)
        else:
            for place, wave in zip((1, 2, window_start * (blocks - 1)), waves):
                kept_ref[place, 0], kept_ref[place, 1] = wave
        entering = kept_ref[own_place]
        left_ref[tick] = entering

    for edge_ref in edges:
        clear_edge(edge_ref, window - 1, True)
    waves = []
    for place in range(window):
        block = window_start + place
        real, imag = kept_ref[block, 0], kept_ref[block, 1]
        held = block ^ own_place
        measured = jnp.concatenate([near_own[held, 1 + core], far_first[2 * held + 1]], axis=0)
        misfit = 2.0 * (real * real + imag * imag - measured)
        waves.append((misfit * real, -misfit * imag))

    for tick in range(count - 1):
        passed = count - tick if tick else None
        waves = advance(passed, window_start, waves, screens, row_matrix, col_ref, edges[tick % 2])
        keep(kept_ref, waves)
        arrived = count - 1 - tick
        pulled = kept_ref[own_in_window]
        grad_ref[arrived] = -(pulled[1] * moved_ref[arrived, 0] + pulled[0] * moved_ref[arrived, 1])

    left, right = jnp.maximum(own_place - 1, 0), jnp.minimum(own_place + 1, blocks - 1)
    lane = lax.broadcasted_iota(jnp.int32, (2 * height, LANES), 1)
    has_left, has_right = own_place > 0, own_place < blocks - 1

    def cells(block):
        wave = kept_ref[block - window_start]
        return jnp.concatenate(turned(1, block, screens, (wave[0], wave[1])), axis=0)

    edge_cells = jnp.where(
        lane < LANES // 2, jnp.where(has_right, cells(right), 0.0), jnp.where(has_left, cells(left), 0.0)
    )
    done = row_products(row_matrix, [jnp.concatenate([cells(own_place), edge_cells], axis=1)])[0]
    lane = lax.broadcasted_iota(jnp.int32, (height, LANES), 1)
    between = (lane >= HALO) & (lane < LANES - HALO)
    highs, lows, edges = [], [], []
    for part in range(2):
        high, low, _ = three_parts(done[part * height : (part + 1) * height, :LANES])
        highs.append(high)
        lows.append(low)
        value = done[part * height : (part + 1) * height, LANES:]
        whole_high = value.astype(jnp.bfloat16).astype(jnp.float32)
        edge = jnp.where(between, pltpu.roll(value - whole_high, LANES // 2, 1), whole_high)
        edges.append(edge.astype(jnp.bfloat16))
    pulled = col_product(jnp.concatenate(highs + edges, axis=1), jnp.concatenate(lows, axis=1), col_ref)
    grad_ref[0] = -(pulled[:, LANES:] * moved_ref[0, 0] + pulled[:, :LANES] * moved_ref[0, 1])

    for target, row in ((mine_ref, near), (theirs_ref, far)):
        for part in range(2):
            target[0, part] = left_ref[own_section, part, row]
        target[0, 2] = grad_ref[own_section, row]


def finish_kernel(mine_ref, received_ref, grad_ref, exit_ref, total_ref, sems):
    core = lax.axis_index("row")
    copies = []
    for source, item in ((mine_ref, core), (received_ref, 1 - core)):
        copies.append(pltpu.make_async_copy(source.at[:, pl.ds(0, 2)], exit_ref.at[item], sems.at[len(copies)]))
    for copy in copies:
        copy.start()
    total_ref[...] = mine_ref[:, 2] + received_ref[:, 2]
    copies.append(pltpu.make_async_copy(total_ref, grad_ref, sems.at[2]))
    copies[2].start()
    for copy in copies:
        copy.wait()


def spread(shard, axis, all_bits, reach=3):
    pieces = []
    for bits in all_bits:
        pairs = [(i, i ^ bits) for i in range(4) if abs(i - (i ^ bits)) <= reach]
        pieces.append(lax.ppermute(shard, axis, pairs))
    return pieces


def swap_cores(value):
    return lax.ppermute(value, "row", [(0, 1), (1, 0)])


def whole_field_body(phase, tilt, intensity):
    _, tile_r, tile_c = phase.shape
    count, blocks = lax.axis_size("depth"), lax.axis_size("col")
    core = lax.axis_index("row")
    height = 2 * tile_r
    vmem = pl.BlockSpec(memory_space=pltpu.VMEM)
    smem = pl.BlockSpec(memory_space=pltpu.SMEM)
    hbm = pl.BlockSpec(memory_space=pl.ANY)

    def array(*shape):
        return jax.ShapeDtypeStruct(shape, jnp.float32)

    def params(mebibytes):
        return pltpu.CompilerParams(vmem_limit_bytes=mebibytes * 2**20)

    first_depth, farthest, two_away = spread(phase, "depth", (1, 3, 2))
    first_depth, measured, slab = lax.optimization_barrier((first_depth, intensity, phase))
    other_depths = [first_depth, farthest, two_away]
    other_depths = jnp.concatenate(other_depths, axis=0)
    packet = jnp.concatenate([slab, measured], axis=0)
    near_own = [packet]
    for bits in range(1, blocks):
        pairs = [(i, i ^ bits) for i in range(blocks)]
        close = [(i, j) for i, j in pairs if abs(i - j) <= 1]
        if close:
            near_own.append(lax.ppermute(packet, "col", close))
        else:
            further = [(i, j) for i, j in pairs if abs(i - j) <= 2]
            arrived = lax.ppermute(slab, "col", further) if further else jnp.zeros_like(slab)
            near_own.append(jnp.concatenate([arrived, jnp.zeros_like(measured)], axis=0))
    near_own = jnp.stack(near_own)
    arriving = spread(other_depths, "col", (1, 2, 3), 2)
    row_all, col_all = jnp.asarray(row_constant(height)), jnp.asarray(col_constant())
    near_own, row_all, col_all = lax.optimization_barrier((near_own, row_all, col_all))
    half_screens = (count, blocks, tile_r, tile_c)
    field = (blocks, 2, height, tile_c)
    row_matrix, col_matrix, wave, own_cos, own_sin = pl.pallas_call(
        load_kernel,
        out_shape=(
            jax.ShapeDtypeStruct(row_all.shape[1:], row_all.dtype),
            jax.ShapeDtypeStruct(col_all.shape, col_all.dtype),
            array(*field),
            array(blocks, tile_r, tile_c),
            array(blocks, tile_r, tile_c),
        ),
        in_specs=[smem, vmem, hbm, hbm],
        out_specs=(vmem,) * 5,
        scratch_shapes=[pltpu.SemaphoreType.DMA((2,))],
        compiler_params=params(4),
        cost_estimate=pl.CostEstimate(flops=10**8, bytes_accessed=2**20, transcendentals=0),
    )(tilt, near_own, row_all, col_all)
    arriving[2], near_own, row_matrix, col_matrix, wave, own_cos, own_sin = lax.optimization_barrier(
        (arriving[2], near_own, row_matrix, col_matrix, wave, own_cos, own_sin)
    )
    wanted = lax.dynamic_slice_in_dim(near_own, 2 - core, 1, 1)
    packets = jnp.concatenate([near_own[:, :1], wanted], axis=1).reshape(2 * blocks, tile_r, tile_c)
    far_first = swap_cores(jnp.concatenate([packets, arriving[2]], axis=0))
    far_second = swap_cores(jnp.concatenate([other_depths] + arriving[:2], axis=0))
    near_rest = jnp.stack([other_depths] + arriving)

    near_cos, near_sin = pl.pallas_call(
        second_kernel,
        out_shape=(array(*half_screens),) * 2,
        in_specs=[vmem] * 3,
        out_specs=(vmem,) * 2,
        compiler_params=params(8),
        cost_estimate=pl.CostEstimate(flops=5 * 10**8, bytes_accessed=2**20, transcendentals=0),
    )(near_rest, own_cos, own_sin)
    mine, theirs = pl.pallas_call(
        wave_kernel,
        out_shape=(array(1, 3, tile_r, tile_c),) * 2,
        in_specs=[vmem] * 8,
        out_specs=(vmem,) * 2,
        scratch_shapes=[pltpu.VMEM(half_screens, jnp.float32)] * 2
        + [pltpu.VMEM(field, jnp.float32)]
        + [pltpu.VMEM((count, 2, height, tile_c), jnp.float32)] * 2
        + [pltpu.VMEM((count, height, tile_c), jnp.float32)]
        + [pltpu.VMEM((blocks, height, 2 * LANES), jnp.bfloat16)] * 2
        + [pltpu.VMEM((2, height, 2 * LANES), jnp.bfloat16)] * 2,
        compiler_params=params(24),
    )(
        wave, near_cos, near_sin, near_own, far_first, far_second,
        row_matrix, col_matrix,
    )
    return pl.pallas_call(
        finish_kernel,
        out_shape=(array(*phase.shape), array(2, 1, 2, tile_r, tile_c)),
        in_specs=[vmem, vmem],
        out_specs=(hbm, hbm),
        scratch_shapes=[pltpu.VMEM(phase.shape, jnp.float32), pltpu.SemaphoreType.DMA((3,))],
        compiler_params=params(4),
    )(mine, swap_cores(theirs))


def extended_2(cells, sides, width):
    for axis, dim in sides:
        count = lax.axis_size(axis)
        ends = count - 1
        head = lax.slice_in_dim(cells, 0, width, axis=dim)
        tail = lax.slice_in_dim(cells, cells.shape[dim] - width, cells.shape[dim], axis=dim)
        cells = jnp.concatenate(
            [
                lax.ppermute(tail, axis, [(i, (i + 1) % count) for i in range(ends)]),
                cells,
                lax.ppermute(head, axis, [((i + 1) % count, i) for i in range(ends)]),
            ],
            axis=dim,
        )
    return cells


def from_behind(value, axis, steps):
    count = lax.axis_size(axis)
    leading, last = (max(0, -steps), min(count, count - steps))
    return lax.ppermute(value, axis, [(source, source + steps) for source in range(leading, last)])


def band_matrix(block_size, margin, fresnel, adjoint):
    shape_full = (block_size, block_size + 2 * margin)
    out_idx = lax.broadcasted_iota(jnp.int32, shape_full, 0)
    in_idx = lax.broadcasted_iota(jnp.int32, shape_full, 1)
    offset = (out_idx + margin - in_idx).astype(jnp.float32)
    inside = jnp.abs(offset) <= margin
    taper_dist = jnp.maximum(jnp.abs(offset) - 0.5 * margin, 0.0)
    profile = jnp.cos(jnp.pi * taper_dist / (margin + 2.0))
    weight = profile * profile / math.sqrt(fresnel)
    phase_angle = jnp.pi * offset * offset / fresnel
    real_part = jnp.where(inside, jnp.cos(phase_angle) * weight, 0.0)
    imag_part = jnp.where(inside, jnp.sin(phase_angle) * weight, 0.0)
    if adjoint:
        imag_part = -imag_part
    upper = jnp.stack([real_part, -imag_part])
    lower = jnp.stack([imag_part, real_part])
    return jnp.stack([upper, lower])


def along_rows(extended, matrix):
    pieces = [jnp.einsum("pqij,gqjc->gpic", matrix, extended, precision=lax.Precision.HIGHEST)]
    return jnp.concatenate(pieces, axis=2)


def along_cols(extended, matrix, margin):
    block_size = matrix.shape[2]
    extent = extended.shape[3] - 2 * margin
    pieces = []
    for block_start in range(0, extent, block_size):
        window = extended[:, :, :, block_start : block_start + block_size + 2 * margin]
        pieces.append(
            jnp.einsum("pqij,gqrj->gpri", matrix, window, precision=lax.Precision.HIGHEST)
        )
    return jnp.concatenate(pieces, axis=3)


def propagate(current, row_matrix, col_matrix):
    with_rows = extended_2(current, (("row", 2),), HALO)
    row_done = along_rows(with_rows, row_matrix)
    with_cols = extended_2(row_done, (("col", 3),), HALO)
    return along_cols(with_cols, col_matrix, HALO)


def transmit(screen, current, adjoint):
    screen_re = screen[0][None]
    screen_im = screen[1][None]
    if adjoint:
        screen_im = -screen_im
    real_part = screen_re * current[:, 0] - screen_im * current[:, 1]
    imag_part = screen_re * current[:, 1] + screen_im * current[:, 0]
    return jnp.stack([real_part, imag_part], axis=1)


def store_item(store, current, first_item, slice_index, active):
    begin = (first_item, jnp.int32(slice_index), jnp.int32(0), jnp.int32(0), jnp.int32(0))
    sizes_now = (current.shape[0], 1) + current.shape[1:]
    previous = lax.dynamic_slice(store, begin, sizes_now)
    fresh = jnp.where(active, current[:, None], previous)
    return lax.dynamic_update_slice(store, fresh, begin)


def staged_body(phase, tilt, intensity):
    slices, tile_r, tile_c = phase.shape
    batch_size = tilt.shape[0]
    sections = lax.axis_size("depth")
    section_index = lax.axis_index("depth")
    group_size = 1
    groups = batch_size // group_size
    tick_count = sections + groups - 1
    block_r = 64
    block_c = 128
    fwd_rows = band_matrix(block_r, HALO, FRESNEL, False)
    fwd_cols = band_matrix(block_c, HALO, FRESNEL, False)
    adj_rows = band_matrix(block_r, HALO, FRESNEL, True)
    adj_cols = band_matrix(block_c, HALO, FRESNEL, True)
    row_pos = (
        lax.axis_index("row") * tile_r + lax.broadcasted_iota(jnp.int32, (tile_r, tile_c), 0)
    ).astype(jnp.float32)
    col_pos = (
        lax.axis_index("col") * tile_c + lax.broadcasted_iota(jnp.int32, (tile_r, tile_c), 1)
    ).astype(jnp.float32)
    height = float(tile_r * lax.axis_size("row"))
    width_all = float(tile_c * lax.axis_size("col"))
    tilt_f = tilt.astype(jnp.float32)
    phase_angle = (
        2.0
        * jnp.pi
        * (
            tilt_f[:, 0, None, None] * row_pos / height
            + tilt_f[:, 1, None, None] * col_pos / width_all
        )
    )
    incident = jnp.stack([jnp.cos(phase_angle), jnp.sin(phase_angle)], axis=1)
    screens = jnp.stack([jnp.cos(phase), jnp.sin(phase)], axis=1)

    def forward_tick(tick_now, carry):
        incoming, entering, leaving = carry
        group_index = tick_now - section_index
        active = (group_index >= 0) & (group_index < groups)
        first_item = jnp.clip(group_index, 0, groups - 1) * group_size
        current = jnp.where(
            section_index == 0,
            lax.dynamic_slice_in_dim(incident, first_item, group_size, 0),
            incoming,
        )
        entering = store_item(entering, current, first_item, 0, active)
        current = propagate(transmit(screens[0], current, False), fwd_rows, fwd_cols)
        leaving = store_item(leaving, current, first_item, 0, active)
        incoming = from_behind(current, "depth", 1)
        return (incoming, entering, leaving)

    store_zero = jnp.zeros((batch_size, slices, 2, tile_r, tile_c), jnp.float32)
    start_wave = jnp.zeros((group_size, 2, tile_r, tile_c), jnp.float32)
    _, entering, leaving = lax.fori_loop(
        0, tick_count, forward_tick, (start_wave, store_zero, store_zero)
    )
    final_wave = leaving[:, slices - 1]
    misfit = final_wave[:, 0] * final_wave[:, 0] + final_wave[:, 1] * final_wave[:, 1] - intensity
    seed_adjoint = 2.0 * misfit[:, None] * final_wave

    def backward_tick(tick_now, carry):
        incoming, gradient = carry
        group_index = tick_now - (sections - 1 - section_index)
        active = (group_index >= 0) & (group_index < groups)
        first_item = jnp.clip(group_index, 0, groups - 1) * group_size
        adjoint_wave = jnp.where(
            section_index == sections - 1,
            lax.dynamic_slice_in_dim(seed_adjoint, first_item, group_size, 0),
            incoming,
        )
        for slice_index in reversed(range(slices)):
            pulled = propagate(adjoint_wave, adj_rows, adj_cols)
            arrived = lax.dynamic_slice_in_dim(entering[:, slice_index], first_item, group_size, 0)
            moved = transmit(screens[slice_index], arrived, False)
            contribution = jnp.sum(pulled[:, 1] * moved[:, 0] - pulled[:, 0] * moved[:, 1], axis=0)
            gradient = gradient.at[slice_index].add(jnp.where(active, contribution, 0.0))
            adjoint_wave = transmit(screens[slice_index], pulled, True)
        incoming = from_behind(adjoint_wave, "depth", -1)
        return (incoming, gradient)

    grad_zero = jnp.zeros((slices, tile_r, tile_c), jnp.float32)
    _, gradient = lax.fori_loop(0, tick_count, backward_tick, (start_wave, grad_zero))
    return (gradient, leaving)


def fits_whole(phase_shape, batch, mesh):
    slices, height, width = phase_shape
    rows, cols, sections = mesh.shape["row"], mesh.shape["col"], mesh.shape["depth"]
    return (
        4 * height * width * (slices + batch) <= GATHER_BUDGET
        and batch == rows == 2
        and slices == sections
        and sections == 4
        and cols == 4
        and height == LANES
        and width == cols * LANES
        and sections * HALO <= LANES
    )


def solution(mesh):
    placed = (P("depth", "row", "col"), P(), P(None, "row", "col"))

    def run(phase, tilt, intensity):
        if fits_whole(phase.shape, tilt.shape[0], mesh):
            body = whole_field_body
        else:
            body = staged_body
        return jax.shard_map(
            body,
            mesh=mesh,
            in_specs=placed,
            out_specs=(P("depth", "row", "col"), P(None, "depth", None, "row", "col")),
            check_vma=False,
        )(phase, tilt, intensity)

    return run
```
